32 devices in a mesh: frame: 4 (over y, core), tile: 8 (over z, x).
Axes of the slice: x: 2, y: 2, z: 4, core: 2. Of those that a mesh axis runs over, the one named last changes fastest.
Arguments:
- movie: bfloat16 [32, 2, 512, 512], P('frame', None, 'tile'), may hold values from -6 to 6
- shifts: int32 [32, 2], P('frame'), may hold values from -8 to 8, as said below
- filters: float32 [2, 64], replicated, may hold values from -0.5 to 0.5
- weights: bfloat16 [1024, 16384], P(('frame', 'tile')), may hold values from -0.046875 to 0.046875
- slot_owner: int32 [1024, 1], P(('frame', 'tile')), may hold values from 0 to 31; in each aligned block of 32 rows (0 to 31, 32 to 63, ...) at most 2 rows name the same one
- slot_local: int32 [1024, 1], P(('frame', 'tile')), may hold values from 0 to 31
Outputs:
- traces: float32 [1024, 32], P(('frame', 'tile'))
The draws below stay inside these ranges and needn't reach their ends.
Inputs may be any that keep to these rules, and one draw needn't show every extreme that they name: `shifts`: each offset has magnitude at most 8; a row offset of 8 and one of -8 occur in every draw. `slot_owner`: among the 32 entries of one pixel tile no owner is named more than 2 times.
All inputs are finite; a program needn't handle non-finite values.
Results may differ from the reference program's by a relative error of at most 0.0047.
Values may be sent and summed in bfloat16 or wider, within the bound.
No kernel may reach another device: no remote copies, remote signals or barrier semaphores. Data moves between devices by JAX's collectives and lax.ppermute only.
A program may use at most 128 MiB of HBM per device.

```python
import math
import jax
import jax.numpy as jnp
import numpy as np
from jax import lax

CB = 16
COMP_DEV = 32
TAPS = 64
MAXS = 8
RAD = 3
CAP = 2
FRAMES = 32
HEIGHT = 512
WIDTH = 512
PIXT = 16384
SLOTS = 32
ENTRIES = 1024
COMPONENTS = 1024
DEVICES = 32


def draw_shifts(key, part):
    values = jax.random.randint(key, (FRAMES, 2), -MAXS, MAXS + 1)
    first = jax.random.randint(jax.random.fold_in(key, 1), (), 0, FRAMES)
    second = (first + FRAMES // 2) % FRAMES
    values = values.at[first, 0].set(MAXS)
    values = values.at[second, 0].set(-MAXS)
    return values.astype(jnp.int32)


def set_ends(entries, key, least, largest):
    shape = entries.shape
    place = [jax.random.randint(jax.random.fold_in(key, axis), (), 0, shape[axis]) for axis in range(len(shape))]
    entries = entries.at[tuple(place)].set(least)
    longest = shape.index(max(shape))
    place[longest] = (place[longest] + 1) % shape[longest]
    return entries.at[tuple(place)].set(largest)


def levels(stream_key, extent, shards, low, largest):
    level, own = 1.0, jax.random.fold_in(stream_key, 6)
    for position, shards_of in shards:
        draws = jnp.exp(jax.random.uniform(jax.random.fold_in(own, position), (shards_of,), jnp.float32, low / len(shards), largest / len(shards)))
        level = level * jnp.repeat(draws, extent[position] // shards_of).reshape([-1 if axis == position else 1 for axis in range(len(extent))])
    return level


def routed_block(own_key, own, number, rows, amount, top, bound, slope):
    sequence = jax.random.permutation(own_key, amount)
    heavy_load, usual = load_shares(amount, rows * top, bound, slope, True), load_shares(amount, rows * top, bound, slope, False)
    places = jnp.arange(amount)

    def named(tallies, offset_by):
        used = int((tallies > 0).sum())
        fixed = max(1, used // 4)
        moved = fixed + (places - fixed + offset_by * (used - fixed)) % max(1, amount - fixed)
        return jnp.zeros((amount,), jnp.int32).at[sequence[jnp.where(places < fixed, places, moved)]].set(jnp.asarray(tallies, jnp.int32))

    tallies = jnp.where(number % 4 == 0, named(heavy_load, number // 4), named(usual, number - number // 4 - 1))
    mixed = jax.random.permutation(jax.random.fold_in(own, 3), amount)
    source_of, sink = mixed[0:amount // 2 * 2:2], mixed[1:amount // 2 * 2:2]
    slack = jnp.minimum(tallies[source_of] - 1, bound - tallies[sink]) // 2
    slack = jnp.where((source_of == sequence[0]) | (sink == sequence[0]) | (tallies[sink] == 0), 0, jnp.maximum(slack, 0))
    moved = jax.random.randint(jax.random.fold_in(own, 4), (amount // 2,), 0, 1 << 20) % (slack + 1)
    tallies = tallies.at[source_of].add(-moved).at[sink].add(moved)
    members = jnp.searchsorted(jnp.cumsum(tallies), jnp.arange(rows * top), side="right").astype(jnp.int32)
    grid = members.reshape(top, rows).T
    grid = grid[jax.random.permutation(jax.random.fold_in(own, 1), rows)]
    offset_by = jax.random.randint(jax.random.fold_in(own, 2), (rows, 1), 0, top)
    return jnp.take_along_axis(grid, (jnp.arange(top)[None, :] + offset_by) % top, axis=1)


def load_shares(count, total, bound, lean, full):
    weights = [(1 << 20) // math.isqrt(grade ** lean) + 1 for grade in range(1, count + 1)]
    largest = bound if full else min(bound, max(-(-total // count), total * weights[0] // sum(weights)))
    least = 1 if total - largest >= count - 1 else 0
    given, rest = [largest] + [least] * (count - 1), total - largest - least * (count - 1)
    while rest > 0:
        free = [i for i in range(1, count) if given[i] < largest] or [i for i in range(1, count) if given[i] < bound]
        mass, remaining = sum([weights[i] for i in free]), rest
        for i in free:
            more = min(bound - given[i], max(1, remaining * weights[i] // mass), rest)
            given[i] = given[i] + more
            rest = rest - more
    return np.array(given)


def gaussian(stream_key, shape, scale, most, shards=(), kind=jnp.bfloat16):
    level = levels(stream_key, shape, shards, -0.22, 0.18) if shards else 1.0
    values = jax.random.normal(stream_key, shape, jnp.float32) * scale * level
    return jnp.minimum(jnp.maximum(values, -most), most).astype(kind)


def setup_inputs(seed: int = 0) -> dict:
    arg_keys = jax.random.split(jax.random.key(seed), 7)
    movie = gaussian(arg_keys[0], (FRAMES, 2, HEIGHT, WIDTH), 1.0, 6.0, ((0, 4), (2, 8)))
    shifts = draw_shifts(jax.random.fold_in(arg_keys[6], 71), 0)
    filters = jnp.clip(jax.random.uniform(arg_keys[2], (2, TAPS), jnp.float32, -0.5, 0.5), -0.5, 0.5)
    weights = gaussian(arg_keys[3], (ENTRIES, PIXT), PIXT ** -0.5, 0.046875, ((0, 32),))
    slot_owner_keys = jax.random.split(jax.random.fold_in(arg_keys[4], 1), ENTRIES // SLOTS)
    slot_owner_turns = jax.random.permutation(jax.random.fold_in(arg_keys[4], 3), ENTRIES // SLOTS)
    slot_owner = jax.vmap(lambda own, number: routed_block(jax.random.fold_in(arg_keys[4], 2), own, number, SLOTS, DEVICES, 1, CAP, 1))(slot_owner_keys, slot_owner_turns).reshape((ENTRIES, 1))
    slot_local = set_ends(jax.random.randint(arg_keys[5], (ENTRIES, 1), 0, COMP_DEV), jax.random.fold_in(arg_keys[5], 1), 0, COMP_DEV - 1).astype(jnp.int32)
    return {"movie": movie, "shifts": shifts, "filters": filters, "weights": weights, "slot_owner": slot_owner, "slot_local": slot_local}


smooth_sigma = 1.0


def gauss_taps():
    positions = jnp.arange(-RAD, RAD + 1).astype(jnp.float32)
    values = jnp.exp(-positions * positions / (2.0 * smooth_sigma * smooth_sigma))
    return values / jnp.sum(values)


def build_kernel(filters, count):
    later = jnp.arange(count)[:, None]
    earlier = jnp.arange(count)[None, :]
    offsets = later - earlier
    onehot = (offsets[:, :, None] == jnp.arange(TAPS)[None, None, :]).astype(jnp.float32)
    return jnp.sum(onehot[None] * filters[:, None, None, :].astype(jnp.float32), axis=-1).astype(jnp.bfloat16)


def smooth_frame(frame_data, offset):
    padded = jnp.pad(frame_data, ((0, 0), (MAXS, MAXS), (MAXS, MAXS)))
    starts = (jnp.int32(0), (MAXS - offset[0]).astype(jnp.int32), (MAXS - offset[1]).astype(jnp.int32))
    registered = lax.dynamic_slice(padded, starts, (2, HEIGHT, WIDTH)).astype(jnp.float32)
    wide = jnp.pad(registered, ((0, 0), (RAD, RAD), (RAD, RAD)))
    taps = gauss_taps()
    vertical = taps[0] * wide[:, 0:HEIGHT, :]
    for tap_index in range(1, 2 * RAD + 1):
        vertical = vertical + taps[tap_index] * wide[:, tap_index:tap_index + HEIGHT, :]
    smoothed = taps[0] * vertical[:, :, 0:WIDTH]
    for tap_index in range(1, 2 * RAD + 1):
        smoothed = smoothed + taps[tap_index] * vertical[:, :, tap_index:tap_index + WIDTH]
    return smoothed.astype(jnp.bfloat16)


def reference(movie, shifts, filters, weights, slot_owner, slot_local):
    smoothed = lax.map(lambda pair: smooth_frame(pair[0], pair[1]), (movie, shifts))
    kernel = build_kernel(filters, FRAMES)

    def per_tile(tile_number):
        start = (tile_number * CB).astype(jnp.int32)
        columns = lax.dynamic_slice_in_dim(smoothed, start, CB, 3).reshape(FRAMES, 2, HEIGHT * CB)
        planes_out = [jnp.dot(kernel[plane], columns[:, plane, :], preferred_element_type=jnp.float32) for plane in range(2)]
        filtered = jnp.stack(planes_out, axis=1)
        spikes = jnp.maximum(filtered, 0.0).astype(jnp.bfloat16).reshape(FRAMES, PIXT)
        tile_weights = lax.dynamic_slice_in_dim(weights, (tile_number * SLOTS).astype(jnp.int32), SLOTS, 0)
        return jnp.dot(tile_weights, spikes.T, preferred_element_type=jnp.float32)

    partial_value = lax.map(per_tile, jnp.arange(DEVICES).astype(jnp.int32)).reshape(ENTRIES, FRAMES)
    component = (slot_owner[:, 0] * COMP_DEV + slot_local[:, 0]).astype(jnp.int32)
    return jax.ops.segment_sum(partial_value, component, num_segments=COMPONENTS)
```

```python
import functools

import jax
import jax.numpy as jnp
import numpy as np
from jax import lax
from jax.experimental import pallas as pl
from jax.experimental.pallas import tpu as pltpu
from jax.sharding import PartitionSpec as P

COMP_DEV = 32
TAPS = 64
MAXS = 8
RAD = 3
LANES = 128
GROUP = 16
HALO = 16
OCTET = 8
MIB = 1 << 20


smooth_sigma = 1.0


def gauss_taps():
    positions = np.arange(-RAD, RAD + 1).astype(np.float32)
    values = np.exp(-positions * positions / np.float32(2.0 * smooth_sigma * smooth_sigma))
    return (values / values.sum(dtype=np.float32)).astype(np.float32)


def band_matrix():
    taps = gauss_taps()
    band = np.zeros((3 * LANES, 2 * LANES), np.float32)
    for x in range(2 * LANES):
        band[x + MAXS - RAD : x + MAXS + RAD + 1, x] = taps
    high = band.astype(jnp.bfloat16)
    low = (band - high.astype(np.float32)).astype(jnp.bfloat16)
    return np.stack([high, low])


def build_kernel(filters, count):
    later = jnp.arange(count)[:, None]
    earlier = jnp.arange(count)[None, :]
    offsets = later - earlier
    onehot = (offsets[:, :, None] == jnp.arange(TAPS)[None, None, :]).astype(jnp.float32)
    return jnp.sum(onehot[None] * filters[:, None, None, :], axis=-1).astype(jnp.bfloat16)


def whole_vmem(count):
    return [pl.BlockSpec(memory_space=pltpu.VMEM)] * count


def params(limit):
    return pltpu.CompilerParams(vmem_limit_bytes=limit)


def pack_kernel(tiles, planes, weights_ref, owner_ref, local_ref, out_ref, ids):
    slots, pixels = weights_ref.shape
    octets = pixels // (planes * tiles * LANES)
    for dest in range(tiles):
        for plane in range(planes):
            for octet in range(octets):
                lane = ((plane * tiles + dest) * octets + octet) * LANES
                row = (plane * octets + octet) * slots
                out_ref[dest, row : row + slots, :] = weights_ref[:, lane : lane + LANES]
    ids[...] = jnp.zeros_like(ids)
    ids[0:1, 0:slots] = owner_ref[...].astype(jnp.float32)
    ids[1:2, 0:slots] = local_ref[...].astype(jnp.float32)
    tail = planes * octets * slots
    for dest in range(tiles):
        out_ref[dest, tail : tail + GROUP, :] = ids[...].astype(jnp.bfloat16)


def pack(weights, owner, local, tiles, planes):
    slots, pixels = weights.shape
    rows = pixels // (tiles * LANES) * slots + GROUP
    return pl.pallas_call(
        functools.partial(pack_kernel, tiles, planes),
        out_shape=jax.ShapeDtypeStruct((tiles, rows, LANES), jnp.bfloat16),
        in_specs=whole_vmem(3),
        out_specs=whole_vmem(1)[0],
        scratch_shapes=[pltpu.VMEM((GROUP, LANES), jnp.float32)],
        compiler_params=params(8 * MIB + 5 * weights.size),
        name="pack_weights",
    )(weights, owner, local)


def smooth_kernel(shift_ref, place_ref, movie_ref, top_ref, bottom_ref, band_ref, out_ref, wide):
    frames, planes, rows, width = movie_ref.shape
    blocks = width // LANES
    reach = rows + 2 * HALO
    parts = out_ref.shape[0]
    span = width // parts
    taps = [float(v) for v in gauss_taps()]
    lane = lax.broadcasted_iota(jnp.int32, (reach, LANES), 1)
    row = lax.broadcasted_iota(jnp.int32, (reach, LANES), 0)
    first_row = place_ref[0]
    total_rows = place_ref[1]

    def one(index, carry):
        frame = index // planes
        plane = index % planes
        down = shift_ref[frame, 0]
        right = shift_ref[frame, 1] + MAXS
        moved = []
        for b in range(blocks):
            cells = pl.ds(b * LANES, LANES)
            piece = jnp.concatenate(
                [top_ref[frame, plane, :, cells], movie_ref[frame, plane, :, cells], bottom_ref[frame, plane, :, cells]],
                axis=0,
            ).astype(jnp.float32)
            moved.append(pltpu.roll(piece, right, 1))
        near = lane < right
        zero = jnp.zeros((reach, LANES), jnp.float32)
        shifted = []
        for b in range(blocks + 1):
            before = moved[b - 1] if b > 0 else zero
            own = moved[b] if b < blocks else zero
            cells = jnp.where(near, before, own)
            if b == 0:
                cells = jnp.where(lane < MAXS, 0.0, cells)
            if b == blocks:
                cells = jnp.where(lane < MAXS, cells, 0.0)
            shifted.append(cells.astype(jnp.bfloat16))
        place = first_row + row - HALO + down
        inside = (place >= 0) & (place < total_rows)
        for b in range(0, blocks, 2):
            cells = jnp.concatenate(shifted[b : b + 3], axis=1)
            result = jnp.dot(cells, band_ref[0], preferred_element_type=jnp.float32)
            result = result + jnp.dot(cells, band_ref[1], preferred_element_type=jnp.float32)
            wide[b] = jnp.where(inside, result[:, :LANES], 0.0)
            wide[b + 1] = jnp.where(inside, result[:, LANES:], 0.0)
        start = HALO - RAD - down
        for b in range(blocks):
            total = taps[RAD] * wide[b, pl.ds(start + RAD, rows), :]
            for i in range(RAD):
                pair = wide[b, pl.ds(start + i, rows), :] + wide[b, pl.ds(start + 2 * RAD - i, rows), :]
                total = total + taps[i] * pair
            part, offset = divmod(b * LANES, span)
            out_ref[part, frame, plane, :, offset : offset + LANES] = total.astype(jnp.bfloat16)
        return carry

    lax.fori_loop(0, frames * planes, one, 0)


def smooth(movie, top, bottom, shifts, place, parts):
    frames, planes, rows, width = movie.shape
    reach = rows + 2 * HALO
    band = jnp.asarray(band_matrix())
    smem = pl.BlockSpec(memory_space=pltpu.SMEM)
    return pl.pallas_call(
        smooth_kernel,
        out_shape=jax.ShapeDtypeStruct((parts, frames, planes, rows, width // parts), jnp.bfloat16),
        in_specs=[smem, smem] + whole_vmem(4),
        out_specs=whole_vmem(1)[0],
        scratch_shapes=[pltpu.VMEM((width // LANES, reach, LANES), jnp.float32)],
        compiler_params=params(16 * MIB + 8 * movie.size),
        name="smooth",
    )(shifts, place, movie, top, bottom, band)


def spread_kernel(kernel_ref, out_ref):
    planes, size, _ = out_ref.shape
    frames = size // GROUP
    row = lax.broadcasted_iota(jnp.int32, (size, frames), 0)
    column = lax.broadcasted_iota(jnp.int32, (size, frames), 1)
    tall = (row % frames == column).astype(jnp.bfloat16)
    row = lax.broadcasted_iota(jnp.int32, (frames, size), 0)
    column = lax.broadcasted_iota(jnp.int32, (frames, size), 1)
    flat = (column // GROUP == row).astype(jnp.bfloat16)
    row = lax.broadcasted_iota(jnp.int32, (size, size), 0)
    column = lax.broadcasted_iota(jnp.int32, (size, size), 1)
    same = row // frames == column % GROUP
    for plane in range(planes):
        left = jnp.dot(tall, kernel_ref[plane], preferred_element_type=jnp.float32).astype(jnp.bfloat16)
        full = jnp.dot(left, flat, preferred_element_type=jnp.float32)
        out_ref[plane] = jnp.where(same, full, 0.0).astype(jnp.bfloat16)


def spread(kernel):
    planes, frames, _ = kernel.shape
    size = frames * GROUP
    return pl.pallas_call(
        spread_kernel,
        out_shape=jax.ShapeDtypeStruct((planes, size, size), jnp.bfloat16),
        in_specs=whole_vmem(1),
        out_specs=whole_vmem(1)[0],
        compiler_params=params(8 * MIB + 16 * size * size),
        name="spread_filters",
    )(kernel)


def swap_lanes(pieces):
    count = len(pieces)
    group = LANES // count
    half = count // 2
    lane = lax.broadcasted_iota(jnp.int32, pieces[0].shape, 1) // group
    while half >= 1:
        low = (lane & half) == 0
        result = list(pieces)
        for i in range(count):
            if i & half:
                continue
            a, b = pieces[i], pieces[i + half]
            if 2 * half == count:
                back = pltpu.roll(b, half * group, 1)
                ahead = pltpu.roll(a, half * group, 1)
            else:
                back = pltpu.roll(b, half * group, 1)
                ahead = pltpu.roll(a, LANES - half * group, 1)
            result[i] = jnp.where(low, a, back)
            result[i + half] = jnp.where(low, ahead, b)
        pieces = result
        half //= 2
    return pieces


def contract_kernel(spread_ref, data_ref, weights_ref, out_ref):
    parts, part_frames, planes, rows, width = data_ref.shape
    tiles = weights_ref.shape[0]
    frames = parts * part_frames
    octets = rows // OCTET
    slots = (weights_ref.shape[1] - GROUP) // (planes * octets)
    tail = planes * octets * slots
    near = LANES * tiles // width
    owners, owner_rows, _ = out_ref.shape
    owned = owners * owner_rows
    size = frames * GROUP
    eye = lax.broadcasted_iota(jnp.int32, (slots, LANES), 0) == lax.broadcasted_iota(jnp.int32, (slots, LANES), 1)
    total = jnp.zeros((owned, LANES), jnp.float32)
    for q in range(width // LANES):
        lanes = slice(q * LANES, (q + 1) * LANES)
        pooled = jnp.zeros((near * slots, near * frames), jnp.float32)
        for plane in range(planes):
            for first in range(0, rows // GROUP, 2):
                cells = jnp.concatenate(
                    [
                        data_ref[:, :, plane, a * GROUP : (a + 1) * GROUP, lanes].reshape(size, LANES)
                        for a in (first, first + 1)
                    ],
                    axis=1,
                )
                spikes = jnp.dot(spread_ref[plane], cells, preferred_element_type=jnp.float32)
                spikes = jnp.maximum(spikes, 0.0)
                for a in (0, 1):
                    sides = []
                    for half in (0, 1):
                        pieces = [
                            spikes[(half * OCTET + r) * frames : (half * OCTET + r + 1) * frames, a * LANES : (a + 1) * LANES]
                            for r in range(OCTET)
                        ]
                        pieces = [piece.astype(jnp.bfloat16) for piece in swap_lanes(pieces)]
                        sides.append(jnp.concatenate(pieces, axis=0))
                    right = jnp.concatenate(sides, axis=1)
                    left = []
                    for half in (0, 1):
                        octet = (first + a) * 2 + half
                        row = (plane * octets + octet) * slots
                        block = weights_ref[q * near : (q + 1) * near, row : row + slots, :]
                        left.append(block.reshape(near * slots, LANES))
                    left = jnp.concatenate(left, axis=1)
                    pooled = pooled + lax.dot_general(
                        left, right, (((1,), (1,)), ((), ())), preferred_element_type=jnp.float32
                    )
        row = lax.broadcasted_iota(jnp.int32, pooled.shape, 0) // slots
        column = lax.broadcasted_iota(jnp.int32, pooled.shape, 1) // frames
        pooled = jnp.where(row == column, pooled, 0.0)
        partial = pooled[:, 0:LANES]
        for at in range(LANES, near * frames, LANES):
            partial = partial + pooled[:, at : at + LANES]
        step = LANES // 2
        while step >= frames:
            partial = partial + pltpu.roll(partial, step, 1)
            step //= 2
        keys, groups = [], []
        for j in range(q * near, (q + 1) * near):
            ids = weights_ref[j, tail : tail + GROUP, :].astype(jnp.float32)
            owner = jnp.sum(jnp.where(eye, ids[0:1, :], 0.0), axis=1, keepdims=True).astype(jnp.int32)
            local = jnp.sum(jnp.where(eye, ids[1:2, :], 0.0), axis=1, keepdims=True).astype(jnp.int32)
            keys.append(owner * owner_rows + local % owner_rows)
            groups.append(local // owner_rows)
        key = jnp.concatenate(keys, axis=0)
        group = jnp.concatenate(groups, axis=0)
        lane_group = lax.broadcasted_iota(jnp.int32, partial.shape, 1) // frames
        partial = jnp.where(lane_group == group, partial, 0.0)
        high = partial.astype(jnp.bfloat16)
        low = (partial - high.astype(jnp.float32)).astype(jnp.bfloat16)
        onehot = (lax.broadcasted_iota(jnp.int32, (near * slots, owned), 1) == key).astype(jnp.bfloat16)
        both = lax.dot_general(
            onehot,
            jnp.concatenate([high, low], axis=1),
            (((0,), (0,)), ((), ())),
            preferred_element_type=jnp.float32,
        )
        total = total + both[:, :LANES] + both[:, LANES:]
    out_ref[...] = total.reshape(owners, owner_rows, LANES)


def contract(spread_filters, data, weights, owners):
    frames = data.shape[0] * data.shape[1]
    shape = (owners, COMP_DEV * frames // LANES, LANES)
    return pl.pallas_call(
        contract_kernel,
        out_shape=jax.ShapeDtypeStruct(shape, jnp.float32),
        in_specs=whole_vmem(3),
        out_specs=whole_vmem(1)[0],
        compiler_params=params(12 * MIB + 2 * (spread_filters.size + data.size + weights.size) * 2),
        name="contract",
    )(spread_filters, data, weights)


def finish_kernel(parts_ref, out_ref):
    sources, rows, _ = parts_ref.shape
    frames = out_ref.shape[1]
    total = jnp.sum(parts_ref[...], axis=0)
    for group in range(LANES // frames):
        out_ref[group * rows : (group + 1) * rows, :] = total[:, group * frames : (group + 1) * frames]


def finish(parts, frames):
    return pl.pallas_call(
        finish_kernel,
        out_shape=jax.ShapeDtypeStruct((COMP_DEV, frames), jnp.float32),
        in_specs=whole_vmem(1),
        out_specs=whole_vmem(1)[0],
        compiler_params=params(8 * MIB + 8 * parts.size),
        name="finish",
    )(parts)


def body(movie, shifts, filters, weights, slot_owner, slot_local):
    part_frames, planes, rows, width = movie.shape
    tiles = lax.axis_size("tile")
    parts = lax.axis_size("frame")
    frames = part_frames * parts
    slots = weights.shape[0]
    ends = tiles - 1
    top = lax.ppermute(movie[:, :, rows - HALO :, :], "tile", [(i, i + 1) for i in range(ends)])
    bottom = lax.ppermute(movie[:, :, :HALO, :], "tile", [(i + 1, i) for i in range(ends)])
    packed = pack(weights, slot_owner.reshape(1, slots), slot_local.reshape(1, slots), tiles, planes)
    packed = lax.all_to_all(packed, "tile", split_axis=0, concat_axis=0, tiled=True)
    place = jnp.stack([lax.axis_index("tile") * rows, jnp.int32(tiles * rows)]).astype(jnp.int32)
    pieces = smooth(movie, top, bottom, shifts, place, parts)
    pieces = lax.all_to_all(pieces, "frame", split_axis=0, concat_axis=0, tiled=True)
    traces = contract(spread(build_kernel(filters, frames)), pieces, packed, parts * tiles)
    traces = lax.all_to_all(traces, ("frame", "tile"), split_axis=0, concat_axis=0, tiled=True)
    return finish(traces, frames)


def solution(mesh):
    in_specs = (
        P("frame", None, "tile", None),
        P("frame", None),
        P(),
        P(("frame", "tile"), None),
        P(("frame", "tile"), None),
        P(("frame", "tile"), None),
    )
    out_specs = P(("frame", "tile"), None)
    return jax.shard_map(body, mesh=mesh, in_specs=in_specs, out_specs=out_specs, check_vma=False)
```

```python
import functools

import jax
import jax.numpy as jnp
import numpy as np
from jax import lax
from jax.experimental import pallas as pl
from jax.experimental.pallas import tpu as pltpu
from jax.sharding import PartitionSpec as P

COMP_DEV = 32
TAPS = 64
MAXS = 8
RAD = 3
LANES = 128
GROUP = 16
HALO = 16
OCTET = 8
MIB = 1 << 20


smooth_sigma = 1.0


def gauss_taps():
    positions = np.arange(-RAD, RAD + 1).astype(np.float32)
    values = np.exp(-positions * positions / np.float32(2.0 * smooth_sigma * smooth_sigma))
    return (values / values.sum(dtype=np.float32)).astype(np.float32)


def build_kernel(filters, count):
    later = jnp.arange(count)[:, None]
    earlier = jnp.arange(count)[None, :]
    offsets = later - earlier
    onehot = (offsets[:, :, None] == jnp.arange(TAPS)[None, None, :]).astype(jnp.float32)
    return jnp.sum(onehot[None] * filters[:, None, None, :], axis=-1).astype(jnp.bfloat16)


def whole_vmem(count):
    return [pl.BlockSpec(memory_space=pltpu.VMEM)] * count


def params(limit):
    return pltpu.CompilerParams(vmem_limit_bytes=limit)


def pack_kernel(tiles, planes, weights_ref, owner_ref, local_ref, out_ref, ids):
    slots, pixels = weights_ref.shape
    octets = pixels // (planes * tiles * LANES)
    for dest in range(tiles):
        for plane in range(planes):
            for octet in range(octets):
                lane = ((plane * tiles + dest) * octets + octet) * LANES
                row = (plane * octets + octet) * slots
                out_ref[dest, row : row + slots, :] = weights_ref[:, lane : lane + LANES]
    ids[...] = jnp.zeros_like(ids)
    ids[0:1, 0:slots] = owner_ref[...].astype(jnp.float32)
    ids[1:2, 0:slots] = local_ref[...].astype(jnp.float32)
    tail = planes * octets * slots
    for dest in range(tiles):
        out_ref[dest, tail : tail + GROUP, :] = ids[...].astype(jnp.bfloat16)


def pack(weights, owner, local, tiles, planes):
    slots, pixels = weights.shape
    rows = pixels // (tiles * LANES) * slots + GROUP
    return pl.pallas_call(
        functools.partial(pack_kernel, tiles, planes),
        out_shape=jax.ShapeDtypeStruct((tiles, rows, LANES), jnp.bfloat16),
        in_specs=whole_vmem(3),
        out_specs=whole_vmem(1)[0],
        scratch_shapes=[pltpu.VMEM((GROUP, LANES), jnp.float32)],
        compiler_params=params(8 * MIB + 5 * weights.size),
        name="pack_weights",
    )(weights, owner, local)


def smooth_kernel(shift_ref, place_ref, movie_ref, top_ref, bottom_ref, *refs):
    *out_refs, band, wide = refs
    frames, planes, rows, width = movie_ref.shape
    blocks = width // LANES
    reach = rows + 2 * HALO
    parts = len(out_refs)
    each = blocks // parts
    taps = gauss_taps()
    high = [float(v) for v in taps.astype(jnp.bfloat16)]
    low = [float(v) for v in taps - taps.astype(jnp.bfloat16).astype(np.float32)]
    lane = lax.broadcasted_iota(jnp.int32, (reach, LANES), 1)
    row = lax.broadcasted_iota(jnp.int32, (reach, LANES), 0)
    first_row, total_rows, me = place_ref[0], place_ref[1], place_ref[2]

    tap = lax.broadcasted_iota(jnp.int32, (2 * LANES, LANES), 0) - lax.broadcasted_iota(jnp.int32, (2 * LANES, LANES), 1)
    tap = tap - (MAXS - RAD)
    for side, values in enumerate((high, low)):
        cells = jnp.zeros((2 * LANES, LANES), jnp.float32)
        for i, value in enumerate(values):
            cells = jnp.where(tap == i, value, cells)
        band[:, side * LANES : (side + 1) * LANES] = cells.astype(jnp.bfloat16)

    def one(frame, carry):
        down = shift_ref[0, frame]
        right = shift_ref[1, frame] + MAXS
        near = lane < right
        zero = jnp.zeros((reach, LANES), jnp.float32)
        place = first_row + row - HALO + down
        inside = (place >= 0) & (place < total_rows)
        start = HALO - RAD - down
        for plane in range(planes):
            moved = []
            for b in range(blocks):
                cells = slice(b * LANES, (b + 1) * LANES)
                piece = jnp.concatenate(
                    [top_ref[frame, plane, :, cells], movie_ref[frame, plane, :, cells], bottom_ref[frame, plane, :, cells]],
                    axis=0,
                ).astype(jnp.float32)
                moved.append(pltpu.roll(piece, right, 1))
            shifted = []
            for b in range(blocks + 1):
                before = moved[b - 1] if b > 0 else zero
                own = moved[b] if b < blocks else zero
                cells = jnp.where(near, before, own)
                if b == 0:
                    cells = jnp.where(lane < MAXS, 0.0, cells)
                if b == blocks:
                    cells = jnp.where(lane < MAXS, cells, 0.0)
                shifted.append(cells.astype(jnp.bfloat16))
            cells = jnp.concatenate(
                [jnp.concatenate(shifted[b : b + 2], axis=1) for b in range(blocks)], axis=0
            )
            result = jnp.dot(cells, band[...], preferred_element_type=jnp.float32)
            result = result[:, :LANES] + result[:, LANES:]
            for b in range(blocks):
                wide[plane, b] = jnp.where(inside, result[b * reach : (b + 1) * reach], 0.0)
        for plane in range(planes):
            for k in range(parts):
                for j in range(each):
                    b = (me ^ k) * each + j
                    total = float(taps[RAD]) * wide[plane, b, pl.ds(start + RAD, rows), :]
                    for i in range(RAD):
                        pair = wide[plane, b, pl.ds(start + i, rows), :]
                        pair = pair + wide[plane, b, pl.ds(start + 2 * RAD - i, rows), :]
                        total = total + float(taps[i]) * pair
                    out_refs[k][frame, plane, :, j * LANES : (j + 1) * LANES] = total.astype(jnp.bfloat16)
        return carry

    lax.fori_loop(0, frames, one, 0)


def smooth(movie, top, bottom, shifts, place, parts):
    frames, planes, rows, width = movie.shape
    reach = rows + 2 * HALO
    smem = pl.BlockSpec(memory_space=pltpu.SMEM)
    return pl.pallas_call(
        smooth_kernel,
        out_shape=[jax.ShapeDtypeStruct((frames, planes, rows, width // parts), jnp.bfloat16)] * parts,
        in_specs=[smem, smem] + whole_vmem(3),
        out_specs=whole_vmem(parts),
        scratch_shapes=[
            pltpu.VMEM((2 * LANES, 2 * LANES), jnp.bfloat16),
            pltpu.VMEM((planes, width // LANES, reach, LANES), jnp.float32),
        ],
        compiler_params=params(12 * MIB + 8 * movie.size),
        name="smooth",
    )(shifts, place, movie, top, bottom)


def spread_kernel(part_frames, place_ref, kernel_ref, out_ref):
    planes, size, _ = out_ref.shape
    frames = size // GROUP
    me = place_ref[2]
    row = lax.broadcasted_iota(jnp.int32, (size, frames), 0)
    column = lax.broadcasted_iota(jnp.int32, (size, frames), 1)
    tall = (row % frames == column).astype(jnp.bfloat16)
    row = lax.broadcasted_iota(jnp.int32, (frames, size), 0)
    column = lax.broadcasted_iota(jnp.int32, (frames, size), 1) // GROUP
    column = ((column // part_frames) ^ me) * part_frames + column % part_frames
    flat = (column == row).astype(jnp.bfloat16)
    row = lax.broadcasted_iota(jnp.int32, (size, size), 0)
    column = lax.broadcasted_iota(jnp.int32, (size, size), 1)
    same = row // frames == column % GROUP
    for plane in range(planes):
        left = jnp.dot(tall, kernel_ref[plane], preferred_element_type=jnp.float32).astype(jnp.bfloat16)
        full = jnp.dot(left, flat, preferred_element_type=jnp.float32)
        out_ref[plane] = jnp.where(same, full, 0.0).astype(jnp.bfloat16)


def spread(kernel, place, part_frames):
    planes, frames, _ = kernel.shape
    size = frames * GROUP
    return pl.pallas_call(
        functools.partial(spread_kernel, part_frames),
        out_shape=jax.ShapeDtypeStruct((planes, size, size), jnp.bfloat16),
        in_specs=[pl.BlockSpec(memory_space=pltpu.SMEM)] + whole_vmem(1),
        out_specs=whole_vmem(1)[0],
        compiler_params=params(8 * MIB + 16 * size * size),
        name="spread_filters",
    )(place, kernel)


def swap_lanes(pieces):
    count = len(pieces)
    group = LANES // count
    half = count // 2
    lane = lax.broadcasted_iota(jnp.int32, pieces[0].shape, 1) // group
    while half >= 1:
        low = (lane & half) == 0
        result = list(pieces)
        for i in range(count):
            if i & half:
                continue
            a, b = pieces[i], pieces[i + half]
            if 2 * half == count:
                back = pltpu.roll(b, half * group, 1)
                ahead = pltpu.roll(a, half * group, 1)
            else:
                back = pltpu.roll(b, half * group, 1)
                ahead = pltpu.roll(a, LANES - half * group, 1)
            result[i] = jnp.where(low, a, back)
            result[i + half] = jnp.where(low, ahead, b)
        pieces = result
        half //= 2
    return pieces


def contract_kernel(spread_ref, weights_ref, *refs):
    *data_refs, out_ref = refs
    parts = len(data_refs)
    part_frames, planes, rows, width = data_refs[0].shape
    tiles = weights_ref.shape[0]
    frames = parts * part_frames
    octets = rows // OCTET
    slots = (weights_ref.shape[1] - GROUP) // (planes * octets)
    tail = planes * octets * slots
    near = LANES * tiles // width
    owners, owner_rows, _ = out_ref.shape
    owned = owners * owner_rows
    size = frames * GROUP
    eye = lax.broadcasted_iota(jnp.int32, (slots, LANES), 0) == lax.broadcasted_iota(jnp.int32, (slots, LANES), 1)
    total = jnp.zeros((owned, LANES), jnp.float32)
    for q in range(width // LANES):
        lanes = slice(q * LANES, (q + 1) * LANES)
        pooled = jnp.zeros((near * slots, near * frames), jnp.float32)
        for plane in range(planes):
            for first in range(0, rows // GROUP, 2):
                cells = []
                for a in (first, first + 1):
                    pieces = [ref[:, plane, a * GROUP : (a + 1) * GROUP, lanes] for ref in data_refs]
                    cells.append(jnp.concatenate(pieces, axis=0).reshape(size, LANES))
                cells = jnp.concatenate(cells, axis=1)
                spikes = jnp.dot(spread_ref[plane], cells, preferred_element_type=jnp.float32)
                spikes = jnp.maximum(spikes, 0.0)
                for a in (0, 1):
                    sides = []
                    for half in (0, 1):
                        pieces = [
                            spikes[(half * OCTET + r) * frames : (half * OCTET + r + 1) * frames, a * LANES : (a + 1) * LANES]
                            for r in range(OCTET)
                        ]
                        pieces = [piece.astype(jnp.bfloat16) for piece in swap_lanes(pieces)]
                        sides.append(jnp.concatenate(pieces, axis=0))
                    right = jnp.concatenate(sides, axis=1)
                    left = []
                    for half in (0, 1):
                        octet = (first + a) * 2 + half
                        row = (plane * octets + octet) * slots
                        block = weights_ref[q * near : (q + 1) * near, row : row + slots, :]
                        left.append(block.reshape(near * slots, LANES))
                    left = jnp.concatenate(left, axis=1)
                    pooled = pooled + lax.dot_general(
                        left, right, (((1,), (1,)), ((), ())), preferred_element_type=jnp.float32
                    )
        row = lax.broadcasted_iota(jnp.int32, pooled.shape, 0) // slots
        column = lax.broadcasted_iota(jnp.int32, pooled.shape, 1) // frames
        pooled = jnp.where(row == column, pooled, 0.0)
        partial = pooled[:, 0:LANES]
        for at in range(LANES, near * frames, LANES):
            partial = partial + pooled[:, at : at + LANES]
        step = LANES // 2
        while step >= frames:
            partial = partial + pltpu.roll(partial, step, 1)
            step //= 2
        keys, groups = [], []
        for j in range(q * near, (q + 1) * near):
            ids = weights_ref[j, tail : tail + GROUP, :].astype(jnp.float32)
            owner = jnp.sum(jnp.where(eye, ids[0:1, :], 0.0), axis=1, keepdims=True).astype(jnp.int32)
            local = jnp.sum(jnp.where(eye, ids[1:2, :], 0.0), axis=1, keepdims=True).astype(jnp.int32)
            keys.append(owner * owner_rows + local % owner_rows)
            groups.append(local // owner_rows)
        key = jnp.concatenate(keys, axis=0)
        group = jnp.concatenate(groups, axis=0)
        lane_group = lax.broadcasted_iota(jnp.int32, partial.shape, 1) // frames
        partial = jnp.where(lane_group == group, partial, 0.0)
        high = partial.astype(jnp.bfloat16)
        low = (partial - high.astype(jnp.float32)).astype(jnp.bfloat16)
        onehot = (lax.broadcasted_iota(jnp.int32, (near * slots, owned), 1) == key).astype(jnp.bfloat16)
        both = lax.dot_general(
            onehot,
            jnp.concatenate([high, low], axis=1),
            (((0,), (0,)), ((), ())),
            preferred_element_type=jnp.float32,
        )
        total = total + both[:, :LANES] + both[:, LANES:]
    out_ref[...] = total.reshape(owners, owner_rows, LANES)


def contract(spread_filters, weights, data, owners):
    frames = data[0].shape[0] * len(data)
    shape = (owners, COMP_DEV * frames // LANES, LANES)
    return pl.pallas_call(
        contract_kernel,
        out_shape=jax.ShapeDtypeStruct(shape, jnp.float32),
        in_specs=whole_vmem(2 + len(data)),
        out_specs=whole_vmem(1)[0],
        compiler_params=params(12 * MIB + 4 * (spread_filters.size + len(data) * data[0].size + weights.size)),
        name="contract",
    )(spread_filters, weights, *data)


def finish_kernel(parts_ref, out_ref):
    sources, rows, _ = parts_ref.shape
    frames = out_ref.shape[1]
    total = jnp.sum(parts_ref[...], axis=0)
    for group in range(LANES // frames):
        out_ref[group * rows : (group + 1) * rows, :] = total[:, group * frames : (group + 1) * frames]


def finish(parts, frames):
    return pl.pallas_call(
        finish_kernel,
        out_shape=jax.ShapeDtypeStruct((COMP_DEV, frames), jnp.float32),
        in_specs=whole_vmem(1),
        out_specs=whole_vmem(1)[0],
        compiler_params=params(8 * MIB + 8 * parts.size),
        name="finish",
    )(parts)


def body(movie, shifts, filters, weights, slot_owner, slot_local):
    part_frames, planes, rows, width = movie.shape
    tiles = lax.axis_size("tile")
    parts = lax.axis_size("frame")
    frames = part_frames * parts
    slots = weights.shape[0]
    ends = tiles - 1
    top = lax.ppermute(movie[:, :, rows - HALO :, :], "tile", [(i, i + 1) for i in range(ends)])
    bottom = lax.ppermute(movie[:, :, :HALO, :], "tile", [(i + 1, i) for i in range(ends)])
    packed = pack(weights, slot_owner.reshape(1, slots), slot_local.reshape(1, slots), tiles, planes)
    packed = lax.all_to_all(packed, "tile", split_axis=0, concat_axis=0, tiled=True)
    me = lax.axis_index("frame")
    place = jnp.stack([lax.axis_index("tile") * rows, tiles * rows, me]).astype(jnp.int32)
    pieces = smooth(movie, top, bottom, shifts.T, place, parts)
    pieces = [pieces[0]] + [
        lax.ppermute(pieces[k], "frame", [(i, i ^ k) for i in range(parts)]) for k in range(1, parts)
    ]
    deconvolve = spread(build_kernel(filters, frames), place, part_frames)
    traces = contract(deconvolve, packed, pieces, parts * tiles)
    traces = lax.all_to_all(traces, ("frame", "tile"), split_axis=0, concat_axis=0, tiled=True)
    return finish(traces, frames)


def solution(mesh):
    in_specs = (
        P("frame", None, "tile", None),
        P("frame", None),
        P(),
        P(("frame", "tile"), None),
        P(("frame", "tile"), None),
        P(("frame", "tile"), None),
    )
    out_specs = P(("frame", "tile"), None)
    return jax.shard_map(body, mesh=mesh, in_specs=in_specs, out_specs=out_specs, check_vma=False)
```

```python
import functools

import jax
import jax.numpy as jnp
import numpy as np
from jax import lax
from jax.experimental import pallas as pl
from jax.experimental.pallas import tpu as pltpu
from jax.sharding import PartitionSpec as P

COMP_DEV = 32
TAPS = 64
MAXS = 8
RAD = 3
LANES = 128
GROUP = 16
HALO = 16
OCTET = 8
QUAD = 4
MIB = 1 << 20


smooth_sigma = 1.0


def gauss_taps():
    positions = np.arange(-RAD, RAD + 1).astype(np.float32)
    values = np.exp(-positions * positions / np.float32(2.0 * smooth_sigma * smooth_sigma))
    return (values / values.sum(dtype=np.float32)).astype(np.float32)


def build_kernel(filters, count):
    later = jnp.arange(count)[:, None]
    earlier = jnp.arange(count)[None, :]
    offsets = later - earlier
    onehot = (offsets[:, :, None] == jnp.arange(TAPS)[None, None, :]).astype(jnp.float32)
    return jnp.sum(onehot[None] * filters[:, None, None, :], axis=-1).astype(jnp.bfloat16)


def whole_vmem(count):
    return [pl.BlockSpec(memory_space=pltpu.VMEM)] * count


def params(limit):
    return pltpu.CompilerParams(vmem_limit_bytes=limit)


def pack_kernel(tiles, planes, weights_ref, owner_ref, local_ref, out_ref, ids):
    slots, pixels = weights_ref.shape
    octets = pixels // (planes * tiles * LANES)
    for dest in range(tiles):
        for plane in range(planes):
            for octet in range(octets):
                lane = ((plane * tiles + dest) * octets + octet) * LANES
                row = (plane * octets + octet) * slots
                out_ref[dest, row : row + slots, :] = weights_ref[:, lane : lane + LANES]
    ids[...] = jnp.zeros_like(ids)
    ids[0:1, 0:slots] = owner_ref[...].astype(jnp.float32)
    ids[1:2, 0:slots] = local_ref[...].astype(jnp.float32)
    tail = planes * octets * slots
    for dest in range(tiles):
        out_ref[dest, tail : tail + GROUP, :] = ids[...].astype(jnp.bfloat16)


def pack(weights, owner, local, tiles, planes):
    slots, pixels = weights.shape
    rows = pixels // (tiles * LANES) * slots + GROUP
    return pl.pallas_call(
        functools.partial(pack_kernel, tiles, planes),
        out_shape=jax.ShapeDtypeStruct((tiles, rows, LANES), jnp.bfloat16),
        in_specs=whole_vmem(3),
        out_specs=whole_vmem(1)[0],
        scratch_shapes=[pltpu.VMEM((GROUP, LANES), jnp.float32)],
        compiler_params=params(8 * MIB + 5 * weights.size),
        name="pack_weights",
    )(weights, owner, local)


def edges_kernel(movie_ref, down_ref, up_ref):
    frames, planes, rows, _ = movie_ref.shape

    def one(frame, carry):
        tails = [movie_ref[frame, plane, rows - HALO :, :].astype(jnp.float32) for plane in range(planes)]
        heads = [movie_ref[frame, plane, :HALO, :].astype(jnp.float32) for plane in range(planes)]
        tail = [cells[OCTET:] for cells in tails] + [cells[QUAD:OCTET] for cells in tails]
        head = [cells[:OCTET] for cells in heads] + [cells[OCTET : OCTET + QUAD] for cells in heads]
        down_ref[frame] = jnp.concatenate(tail, axis=0).astype(jnp.bfloat16)
        up_ref[frame] = jnp.concatenate(head, axis=0).astype(jnp.bfloat16)
        return carry

    lax.fori_loop(0, frames, one, 0)


def edges(movie):
    frames, planes, _, width = movie.shape
    shape = jax.ShapeDtypeStruct((frames, planes * (OCTET + QUAD), width), jnp.bfloat16)
    return pl.pallas_call(
        edges_kernel,
        out_shape=[shape, shape],
        in_specs=whole_vmem(1),
        out_specs=whole_vmem(2),
        compiler_params=params(8 * MIB + 4 * movie.size),
        name="edges",
    )(movie)


def smooth_kernel(shift_ref, place_ref, movie_ref, top_ref, bottom_ref, *refs):
    *out_refs, band, wide = refs
    frames, planes, rows, width = movie_ref.shape
    blocks = width // LANES
    reach = rows + 2 * HALO
    parts = len(out_refs)
    each = blocks // parts
    taps = gauss_taps()
    high = [float(v) for v in taps.astype(jnp.bfloat16)]
    low = [float(v) for v in taps - taps.astype(jnp.bfloat16).astype(np.float32)]
    lane = lax.broadcasted_iota(jnp.int32, (reach, LANES), 1)
    row = lax.broadcasted_iota(jnp.int32, (reach, LANES), 0)
    first_row, total_rows, me = place_ref[0], place_ref[1], place_ref[2]

    tap = lax.broadcasted_iota(jnp.int32, (2 * LANES, LANES), 0) - lax.broadcasted_iota(jnp.int32, (2 * LANES, LANES), 1)
    tap = tap - (MAXS - RAD)
    for side, values in enumerate((high, low)):
        cells = jnp.zeros((2 * LANES, LANES), jnp.float32)
        for i, value in enumerate(values):
            cells = jnp.where(tap == i, value, cells)
        band[:, side * LANES : (side + 1) * LANES] = cells.astype(jnp.bfloat16)

    def one(frame, carry):
        down = shift_ref[0, frame]
        right = shift_ref[1, frame] + MAXS
        near = lane < right
        zero = jnp.zeros((reach, LANES), jnp.float32)
        place = first_row + row - HALO + down
        inside = (place >= 0) & (place < total_rows)
        start = HALO - RAD - down
        for plane in range(planes):
            moved = []
            for b in range(blocks):
                cells = slice(b * LANES, (b + 1) * LANES)
                top = top_ref[frame, :, cells].astype(jnp.float32)
                bottom = bottom_ref[frame, :, cells].astype(jnp.float32)
                full = slice(plane * OCTET, (plane + 1) * OCTET)
                rest = slice(planes * OCTET + plane * QUAD, planes * OCTET + (plane + 1) * QUAD)
                piece = jnp.concatenate(
                    [
                        top[rest],
                        top[rest],
                        top[full],
                        movie_ref[frame, plane, :, cells].astype(jnp.float32),
                        bottom[full],
                        bottom[rest],
                        bottom[rest],
                    ],
                    axis=0,
                )
                moved.append(pltpu.roll(piece, right, 1))
            shifted = []
            for b in range(blocks + 1):
                before = moved[b - 1] if b > 0 else zero
                own = moved[b] if b < blocks else zero
                cells = jnp.where(near, before, own)
                if b == 0:
                    cells = jnp.where(lane < MAXS, 0.0, cells)
                if b == blocks:
                    cells = jnp.where(lane < MAXS, cells, 0.0)
                shifted.append(cells.astype(jnp.bfloat16))
            cells = jnp.concatenate(
                [jnp.concatenate(shifted[b : b + 2], axis=1) for b in range(blocks)], axis=0
            )
            result = jnp.dot(cells, band[...], preferred_element_type=jnp.float32)
            result = result[:, :LANES] + result[:, LANES:]
            for b in range(blocks):
                wide[plane, b] = jnp.where(inside, result[b * reach : (b + 1) * reach], 0.0)
        for plane in range(planes):
            for k in range(parts):
                for j in range(each):
                    b = (me ^ k) * each + j
                    total = float(taps[RAD]) * wide[plane, b, pl.ds(start + RAD, rows), :]
                    for i in range(RAD):
                        pair = wide[plane, b, pl.ds(start + i, rows), :]
                        pair = pair + wide[plane, b, pl.ds(start + 2 * RAD - i, rows), :]
                        total = total + float(taps[i]) * pair
                    out_refs[k][frame, plane, :, j * LANES : (j + 1) * LANES] = total.astype(jnp.bfloat16)
        return carry

    lax.fori_loop(0, frames, one, 0)


def smooth(movie, top, bottom, shifts, place, parts):
    frames, planes, rows, width = movie.shape
    reach = rows + 2 * HALO
    smem = pl.BlockSpec(memory_space=pltpu.SMEM)
    return pl.pallas_call(
        smooth_kernel,
        out_shape=[jax.ShapeDtypeStruct((frames, planes, rows, width // parts), jnp.bfloat16)] * parts,
        in_specs=[smem, smem] + whole_vmem(3),
        out_specs=whole_vmem(parts),
        scratch_shapes=[
            pltpu.VMEM((2 * LANES, 2 * LANES), jnp.bfloat16),
            pltpu.VMEM((planes, width // LANES, reach, LANES), jnp.float32),
        ],
        compiler_params=params(12 * MIB + 8 * movie.size),
        cost_estimate=pl.CostEstimate(flops=1 << 36, bytes_accessed=8 * movie.size, transcendentals=0),
        name="smooth",
    )(shifts, place, movie, top, bottom)


def spread_kernel(part_frames, place_ref, kernel_ref, out_ref):
    planes, size, _ = out_ref.shape
    frames = size // GROUP
    me = place_ref[2]
    row = lax.broadcasted_iota(jnp.int32, (size, frames), 0)
    column = lax.broadcasted_iota(jnp.int32, (size, frames), 1)
    tall = (row % frames == column).astype(jnp.bfloat16)
    row = lax.broadcasted_iota(jnp.int32, (frames, size), 0)
    column = lax.broadcasted_iota(jnp.int32, (frames, size), 1) // GROUP
    column = ((column // part_frames) ^ me) * part_frames + column % part_frames
    flat = (column == row).astype(jnp.bfloat16)
    row = lax.broadcasted_iota(jnp.int32, (size, size), 0)
    column = lax.broadcasted_iota(jnp.int32, (size, size), 1)
    same = row // frames == column % GROUP
    for plane in range(planes):
        left = jnp.dot(tall, kernel_ref[plane], preferred_element_type=jnp.float32).astype(jnp.bfloat16)
        full = jnp.dot(left, flat, preferred_element_type=jnp.float32)
        out_ref[plane] = jnp.where(same, full, 0.0).astype(jnp.bfloat16)


def spread(kernel, place, part_frames):
    planes, frames, _ = kernel.shape
    size = frames * GROUP
    return pl.pallas_call(
        functools.partial(spread_kernel, part_frames),
        out_shape=jax.ShapeDtypeStruct((planes, size, size), jnp.bfloat16),
        in_specs=[pl.BlockSpec(memory_space=pltpu.SMEM)] + whole_vmem(1),
        out_specs=whole_vmem(1)[0],
        compiler_params=params(8 * MIB + 16 * size * size),
        name="spread_filters",
    )(place, kernel)


def swap_lanes(pieces):
    count = len(pieces)
    group = LANES // count
    half = count // 2
    lane = lax.broadcasted_iota(jnp.int32, pieces[0].shape, 1) // group
    while half >= 1:
        low = (lane & half) == 0
        result = list(pieces)
        for i in range(count):
            if i & half:
                continue
            a, b = pieces[i], pieces[i + half]
            if 2 * half == count:
                back = pltpu.roll(b, half * group, 1)
                ahead = pltpu.roll(a, half * group, 1)
            else:
                back = pltpu.roll(b, half * group, 1)
                ahead = pltpu.roll(a, LANES - half * group, 1)
            result[i] = jnp.where(low, a, back)
            result[i + half] = jnp.where(low, ahead, b)
        pieces = result
        half //= 2
    return pieces


def contract_kernel(spread_ref, weights_ref, *refs):
    *data_refs, out_ref = refs
    parts = len(data_refs)
    part_frames, planes, rows, width = data_refs[0].shape
    tiles = weights_ref.shape[0]
    frames = parts * part_frames
    octets = rows // OCTET
    slots = (weights_ref.shape[1] - GROUP) // (planes * octets)
    tail = planes * octets * slots
    near = LANES * tiles // width
    owners, owner_rows, _ = out_ref.shape
    owned = owners * owner_rows
    size = frames * GROUP
    eye = lax.broadcasted_iota(jnp.int32, (slots, LANES), 0) == lax.broadcasted_iota(jnp.int32, (slots, LANES), 1)
    total = jnp.zeros((owned, LANES), jnp.float32)
    for q in range(width // LANES):
        lanes = slice(q * LANES, (q + 1) * LANES)
        pooled = jnp.zeros((near * slots, near * frames), jnp.float32)
        for plane in range(planes):
            for first in range(0, rows // GROUP, 2):
                cells = []
                for a in (first, first + 1):
                    pieces = [ref[:, plane, a * GROUP : (a + 1) * GROUP, lanes] for ref in data_refs]
                    cells.append(jnp.concatenate(pieces, axis=0).reshape(size, LANES))
                cells = jnp.concatenate(cells, axis=1)
                spikes = jnp.dot(spread_ref[plane], cells, preferred_element_type=jnp.float32)
                spikes = jnp.maximum(spikes, 0.0)
                for a in (0, 1):
                    sides = []
                    for half in (0, 1):
                        pieces = [
                            spikes[(half * OCTET + r) * frames : (half * OCTET + r + 1) * frames, a * LANES : (a + 1) * LANES]
                            for r in range(OCTET)
                        ]
                        pieces = [piece.astype(jnp.bfloat16) for piece in swap_lanes(pieces)]
                        sides.append(jnp.concatenate(pieces, axis=0))
                    right = jnp.concatenate(sides, axis=1)
                    left = []
                    for half in (0, 1):
                        octet = (first + a) * 2 + half
                        row = (plane * octets + octet) * slots
                        block = weights_ref[q * near : (q + 1) * near, row : row + slots, :]
                        left.append(block.reshape(near * slots, LANES))
                    left = jnp.concatenate(left, axis=1)
                    pooled = pooled + lax.dot_general(
                        left, right, (((1,), (1,)), ((), ())), preferred_element_type=jnp.float32
                    )
        row = lax.broadcasted_iota(jnp.int32, pooled.shape, 0) // slots
        column = lax.broadcasted_iota(jnp.int32, pooled.shape, 1) // frames
        pooled = jnp.where(row == column, pooled, 0.0)
        partial = pooled[:, 0:LANES]
        for at in range(LANES, near * frames, LANES):
            partial = partial + pooled[:, at : at + LANES]
        step = LANES // 2
        while step >= frames:
            partial = partial + pltpu.roll(partial, step, 1)
            step //= 2
        keys, groups = [], []
        for j in range(q * near, (q + 1) * near):
            ids = weights_ref[j, tail : tail + GROUP, :].astype(jnp.float32)
            owner = jnp.sum(jnp.where(eye, ids[0:1, :], 0.0), axis=1, keepdims=True).astype(jnp.int32)
            local = jnp.sum(jnp.where(eye, ids[1:2, :], 0.0), axis=1, keepdims=True).astype(jnp.int32)
            keys.append(owner * owner_rows + local % owner_rows)
            groups.append(local // owner_rows)
        key = jnp.concatenate(keys, axis=0)
        group = jnp.concatenate(groups, axis=0)
        lane_group = lax.broadcasted_iota(jnp.int32, partial.shape, 1) // frames
        partial = jnp.where(lane_group == group, partial, 0.0)
        high = partial.astype(jnp.bfloat16)
        low = (partial - high.astype(jnp.float32)).astype(jnp.bfloat16)
        onehot = (lax.broadcasted_iota(jnp.int32, (near * slots, owned), 1) == key).astype(jnp.bfloat16)
        both = lax.dot_general(
            onehot,
            jnp.concatenate([high, low], axis=1),
            (((0,), (0,)), ((), ())),
            preferred_element_type=jnp.float32,
        )
        total = total + both[:, :LANES] + both[:, LANES:]
    out_ref[...] = total.reshape(owners, owner_rows, LANES)


def contract(spread_filters, weights, data, owners):
    frames = data[0].shape[0] * len(data)
    shape = (owners, COMP_DEV * frames // LANES, LANES)
    return pl.pallas_call(
        contract_kernel,
        out_shape=jax.ShapeDtypeStruct(shape, jnp.float32),
        in_specs=whole_vmem(2 + len(data)),
        out_specs=whole_vmem(1)[0],
        compiler_params=params(12 * MIB + 4 * (spread_filters.size + len(data) * data[0].size + weights.size)),
        name="contract",
    )(spread_filters, weights, *data)


def finish_kernel(parts_ref, out_ref):
    sources, rows, _ = parts_ref.shape
    frames = out_ref.shape[1]
    total = jnp.sum(parts_ref[...], axis=0)
    for group in range(LANES // frames):
        out_ref[group * rows : (group + 1) * rows, :] = total[:, group * frames : (group + 1) * frames]


def finish(parts, frames):
    return pl.pallas_call(
        finish_kernel,
        out_shape=jax.ShapeDtypeStruct((COMP_DEV, frames), jnp.float32),
        in_specs=whole_vmem(1),
        out_specs=whole_vmem(1)[0],
        compiler_params=params(8 * MIB + 8 * parts.size),
        name="finish",
    )(parts)


def body(movie, shifts, filters, weights, slot_owner, slot_local):
    part_frames, planes, rows, width = movie.shape
    tiles = lax.axis_size("tile")
    parts = lax.axis_size("frame")
    frames = part_frames * parts
    slots = weights.shape[0]
    ends = tiles - 1
    downward, upward = edges(movie)
    top = lax.ppermute(downward, "tile", [(i, i + 1) for i in range(ends)])
    bottom = lax.ppermute(upward, "tile", [(i + 1, i) for i in range(ends)])
    packed = pack(weights, slot_owner.reshape(1, slots), slot_local.reshape(1, slots), tiles, planes)
    packed = lax.all_to_all(packed, "tile", split_axis=0, concat_axis=0, tiled=True)
    me = lax.axis_index("frame")
    place = jnp.stack([lax.axis_index("tile") * rows, tiles * rows, me]).astype(jnp.int32)
    pieces = smooth(movie, top, bottom, shifts.T, place, parts)
    pieces = [pieces[0]] + [
        lax.ppermute(pieces[k], "frame", [(i, i ^ k) for i in range(parts)]) for k in range(1, parts)
    ]
    deconvolve = spread(build_kernel(filters, frames), place, part_frames)
    traces = contract(deconvolve, packed, pieces, parts * tiles)
    traces = lax.all_to_all(traces, ("frame", "tile"), split_axis=0, concat_axis=0, tiled=True)
    return finish(traces, frames)


def solution(mesh):
    in_specs = (
        P("frame", None, "tile", None),
        P("frame", None),
        P(),
        P(("frame", "tile"), None),
        P(("frame", "tile"), None),
        P(("frame", "tile"), None),
    )
    out_specs = P(("frame", "tile"), None)
    return jax.shard_map(body, mesh=mesh, in_specs=in_specs, out_specs=out_specs, check_vma=False)
```

```python
import functools

import jax
import jax.numpy as jnp
import numpy as np
from jax import lax
from jax.experimental import pallas as pl
from jax.experimental.pallas import tpu as pltpu
from jax.sharding import PartitionSpec as P

COMP_DEV = 32
TAPS = 64
MAXS = 8
RAD = 3
LANES = 128
GROUP = 16
HALO = 16
OCTET = 8
QUAD = 4
MIB = 1 << 20


smooth_sigma = 1.0


def gauss_taps():
    positions = np.arange(-RAD, RAD + 1).astype(np.float32)
    values = np.exp(-positions * positions / np.float32(2.0 * smooth_sigma * smooth_sigma))
    return (values / values.sum(dtype=np.float32)).astype(np.float32)


def build_kernel(filters, count):
    later = jnp.arange(count)[:, None]
    earlier = jnp.arange(count)[None, :]
    offsets = later - earlier
    onehot = (offsets[:, :, None] == jnp.arange(TAPS)[None, None, :]).astype(jnp.float32)
    return jnp.sum(onehot[None] * filters[:, None, None, :], axis=-1).astype(jnp.bfloat16)


def whole_vmem(count):
    return [pl.BlockSpec(memory_space=pltpu.VMEM)] * count


def params(limit):
    return pltpu.CompilerParams(vmem_limit_bytes=limit)


def pack_kernel(tiles, planes, weights_ref, owner_ref, local_ref, gate_ref, out_ref, ids):
    slots, pixels = weights_ref.shape
    octets = pixels // (planes * tiles * LANES)
    for dest in range(tiles):
        for plane in range(planes):
            for octet in range(octets):
                lane = ((plane * tiles + dest) * octets + octet) * LANES
                row = (plane * octets + octet) * slots
                out_ref[dest, row : row + slots, :] = weights_ref[:, lane : lane + LANES]
    ids[...] = jnp.zeros_like(ids)
    ids[0:1, 0:slots] = owner_ref[...].astype(jnp.float32)
    ids[1:2, 0:slots] = local_ref[...].astype(jnp.float32)
    tail = planes * octets * slots
    for dest in range(tiles):
        out_ref[dest, tail : tail + GROUP, :] = ids[...].astype(jnp.bfloat16)


def pack(weights, owner, local, gate, tiles, planes):
    slots, pixels = weights.shape
    rows = pixels // (tiles * LANES) * slots + GROUP
    return pl.pallas_call(
        functools.partial(pack_kernel, tiles, planes),
        out_shape=jax.ShapeDtypeStruct((tiles, rows, LANES), jnp.bfloat16),
        in_specs=whole_vmem(4),
        out_specs=whole_vmem(1)[0],
        scratch_shapes=[pltpu.VMEM((GROUP, LANES), jnp.float32)],
        compiler_params=params(8 * MIB + 5 * weights.size),
        name="pack_weights",
    )(weights, owner, local, gate)


def edges_kernel(movie_ref, down_ref, up_ref):
    frames, planes, rows, _ = movie_ref.shape

    def one(frame, carry):
        tails = [movie_ref[frame, plane, rows - HALO :, :].astype(jnp.float32) for plane in range(planes)]
        heads = [movie_ref[frame, plane, :HALO, :].astype(jnp.float32) for plane in range(planes)]
        tail = [cells[OCTET:] for cells in tails] + [cells[QUAD:OCTET] for cells in tails]
        head = [cells[:OCTET] for cells in heads] + [cells[OCTET : OCTET + QUAD] for cells in heads]
        down_ref[frame] = jnp.concatenate(tail, axis=0).astype(jnp.bfloat16)
        up_ref[frame] = jnp.concatenate(head, axis=0).astype(jnp.bfloat16)
        return carry

    lax.fori_loop(0, frames, one, 0)


def edges(movie):
    frames, planes, _, width = movie.shape
    shape = jax.ShapeDtypeStruct((frames, planes * (OCTET + QUAD), width), jnp.bfloat16)
    return pl.pallas_call(
        edges_kernel,
        out_shape=[shape, shape],
        in_specs=whole_vmem(1),
        out_specs=whole_vmem(2),
        compiler_params=params(8 * MIB + 4 * movie.size),
        name="edges",
    )(movie)


def smooth_kernel(shift_ref, place_ref, movie_ref, top_ref, bottom_ref, *refs):
    *out_refs, band, wide = refs
    frames, planes, rows, width = movie_ref.shape
    blocks = width // LANES
    reach = rows + 2 * HALO
    parts = len(out_refs)
    each = blocks // parts
    taps = gauss_taps()
    high = [float(v) for v in taps.astype(jnp.bfloat16)]
    low = [float(v) for v in taps - taps.astype(jnp.bfloat16).astype(np.float32)]
    lane = lax.broadcasted_iota(jnp.int32, (reach, LANES), 1)
    row = lax.broadcasted_iota(jnp.int32, (reach, LANES), 0)
    first_row, total_rows, me = place_ref[0], place_ref[1], place_ref[2]

    tap = lax.broadcasted_iota(jnp.int32, (2 * LANES, LANES), 0) - lax.broadcasted_iota(jnp.int32, (2 * LANES, LANES), 1)
    tap = tap - (MAXS - RAD)
    for side, values in enumerate((high, low)):
        cells = jnp.zeros((2 * LANES, LANES), jnp.float32)
        for i, value in enumerate(values):
            cells = jnp.where(tap == i, value, cells)
        band[:, side * LANES : (side + 1) * LANES] = cells.astype(jnp.bfloat16)

    def one(frame, carry):
        down = shift_ref[0, frame]
        right = shift_ref[1, frame] + MAXS
        near = lane < right
        zero = jnp.zeros((reach, LANES), jnp.float32)
        place = first_row + row - HALO + down
        inside = (place >= 0) & (place < total_rows)
        start = HALO - RAD - down
        for plane in range(planes):
            moved = []
            for b in range(blocks):
                cells = slice(b * LANES, (b + 1) * LANES)
                top = top_ref[frame, :, cells].astype(jnp.float32)
                bottom = bottom_ref[frame, :, cells].astype(jnp.float32)
                full = slice(plane * OCTET, (plane + 1) * OCTET)
                rest = slice(planes * OCTET + plane * QUAD, planes * OCTET + (plane + 1) * QUAD)
                piece = jnp.concatenate(
                    [
                        top[rest],
                        top[rest],
                        top[full],
                        movie_ref[frame, plane, :, cells].astype(jnp.float32),
                        bottom[full],
                        bottom[rest],
                        bottom[rest],
                    ],
                    axis=0,
                )
                moved.append(pltpu.roll(piece, right, 1))
            shifted = []
            for b in range(blocks + 1):
                before = moved[b - 1] if b > 0 else zero
                own = moved[b] if b < blocks else zero
                cells = jnp.where(near, before, own)
                if b == 0:
                    cells = jnp.where(lane < MAXS, 0.0, cells)
                if b == blocks:
                    cells = jnp.where(lane < MAXS, cells, 0.0)
                shifted.append(cells.astype(jnp.bfloat16))
            cells = jnp.concatenate(
                [jnp.concatenate(shifted[b : b + 2], axis=1) for b in range(blocks)], axis=0
            )
            result = jnp.dot(cells, band[...], preferred_element_type=jnp.float32)
            result = result[:, :LANES] + result[:, LANES:]
            for b in range(blocks):
                wide[plane, b] = jnp.where(inside, result[b * reach : (b + 1) * reach], 0.0)
        for plane in range(planes):
            for k in range(parts):
                for j in range(each):
                    b = (me ^ k) * each + j
                    total = float(taps[RAD]) * wide[plane, b, pl.ds(start + RAD, rows), :]
                    for i in range(RAD):
                        pair = wide[plane, b, pl.ds(start + i, rows), :]
                        pair = pair + wide[plane, b, pl.ds(start + 2 * RAD - i, rows), :]
                        total = total + float(taps[i]) * pair
                    out_refs[k][frame, plane, :, j * LANES : (j + 1) * LANES] = total.astype(jnp.bfloat16)
        return carry

    lax.fori_loop(0, frames, one, 0)


def smooth(movie, top, bottom, shifts, place, parts):
    frames, planes, rows, width = movie.shape
    reach = rows + 2 * HALO
    smem = pl.BlockSpec(memory_space=pltpu.SMEM)
    return pl.pallas_call(
        smooth_kernel,
        out_shape=[jax.ShapeDtypeStruct((frames, planes, rows, width // parts), jnp.bfloat16)] * parts,
        in_specs=[smem, smem] + whole_vmem(3),
        out_specs=whole_vmem(parts),
        scratch_shapes=[
            pltpu.VMEM((2 * LANES, 2 * LANES), jnp.bfloat16),
            pltpu.VMEM((planes, width // LANES, reach, LANES), jnp.float32),
        ],
        compiler_params=params(12 * MIB + 8 * movie.size),
        name="smooth",
    )(shifts, place, movie, top, bottom)


def spread_kernel(part_frames, place_ref, kernel_ref, out_ref):
    planes, size, _ = out_ref.shape
    frames = size // GROUP
    me = place_ref[2]
    row = lax.broadcasted_iota(jnp.int32, (size, frames), 0)
    column = lax.broadcasted_iota(jnp.int32, (size, frames), 1)
    tall = (row % frames == column).astype(jnp.bfloat16)
    row = lax.broadcasted_iota(jnp.int32, (frames, size), 0)
    column = lax.broadcasted_iota(jnp.int32, (frames, size), 1) // GROUP
    column = ((column // part_frames) ^ me) * part_frames + column % part_frames
    flat = (column == row).astype(jnp.bfloat16)
    row = lax.broadcasted_iota(jnp.int32, (size, size), 0)
    column = lax.broadcasted_iota(jnp.int32, (size, size), 1)
    same = row // frames == column % GROUP
    for plane in range(planes):
        left = jnp.dot(tall, kernel_ref[plane], preferred_element_type=jnp.float32).astype(jnp.bfloat16)
        full = jnp.dot(left, flat, preferred_element_type=jnp.float32)
        out_ref[plane] = jnp.where(same, full, 0.0).astype(jnp.bfloat16)


def spread(kernel, place, part_frames):
    planes, frames, _ = kernel.shape
    size = frames * GROUP
    return pl.pallas_call(
        functools.partial(spread_kernel, part_frames),
        out_shape=jax.ShapeDtypeStruct((planes, size, size), jnp.bfloat16),
        in_specs=[pl.BlockSpec(memory_space=pltpu.SMEM)] + whole_vmem(1),
        out_specs=whole_vmem(1)[0],
        compiler_params=params(8 * MIB + 16 * size * size),
        name="spread_filters",
    )(place, kernel)


def swap_lanes(pieces):
    count = len(pieces)
    group = LANES // count
    half = count // 2
    lane = lax.broadcasted_iota(jnp.int32, pieces[0].shape, 1) // group
    while half >= 1:
        low = (lane & half) == 0
        result = list(pieces)
        for i in range(count):
            if i & half:
                continue
            a, b = pieces[i], pieces[i + half]
            if 2 * half == count:
                back = pltpu.roll(b, half * group, 1)
                ahead = pltpu.roll(a, half * group, 1)
            else:
                back = pltpu.roll(b, half * group, 1)
                ahead = pltpu.roll(a, LANES - half * group, 1)
            result[i] = jnp.where(low, a, back)
            result[i + half] = jnp.where(low, ahead, b)
        pieces = result
        half //= 2
    return pieces


def contract_kernel(spread_ref, weights_ref, *refs):
    *data_refs, out_ref = refs
    parts = len(data_refs)
    part_frames, planes, rows, width = data_refs[0].shape
    tiles = weights_ref.shape[0]
    frames = parts * part_frames
    octets = rows // OCTET
    slots = (weights_ref.shape[1] - GROUP) // (planes * octets)
    tail = planes * octets * slots
    near = LANES * tiles // width
    owners, owner_rows, _ = out_ref.shape
    owned = owners * owner_rows
    size = frames * GROUP
    eye = lax.broadcasted_iota(jnp.int32, (slots, LANES), 0) == lax.broadcasted_iota(jnp.int32, (slots, LANES), 1)
    total = jnp.zeros((owned, LANES), jnp.float32)
    for q in range(width // LANES):
        lanes = slice(q * LANES, (q + 1) * LANES)
        pooled = jnp.zeros((near * slots, near * frames), jnp.float32)
        for plane in range(planes):
            for first in range(0, rows // GROUP, 2):
                cells = []
                for a in (first, first + 1):
                    pieces = [ref[:, plane, a * GROUP : (a + 1) * GROUP, lanes] for ref in data_refs]
                    cells.append(jnp.concatenate(pieces, axis=0).reshape(size, LANES))
                cells = jnp.concatenate(cells, axis=1)
                spikes = jnp.dot(spread_ref[plane], cells, preferred_element_type=jnp.float32)
                spikes = jnp.maximum(spikes, 0.0)
                for a in (0, 1):
                    sides = []
                    for half in (0, 1):
                        pieces = [
                            spikes[(half * OCTET + r) * frames : (half * OCTET + r + 1) * frames, a * LANES : (a + 1) * LANES]
                            for r in range(OCTET)
                        ]
                        pieces = [piece.astype(jnp.bfloat16) for piece in swap_lanes(pieces)]
                        sides.append(jnp.concatenate(pieces, axis=0))
                    right = jnp.concatenate(sides, axis=1)
                    left = []
                    for half in (0, 1):
                        octet = (first + a) * 2 + half
                        row = (plane * octets + octet) * slots
                        block = weights_ref[q * near : (q + 1) * near, row : row + slots, :]
                        left.append(block.reshape(near * slots, LANES))
                    left = jnp.concatenate(left, axis=1)
                    pooled = pooled + lax.dot_general(
                        left, right, (((1,), (1,)), ((), ())), preferred_element_type=jnp.float32
                    )
        row = lax.broadcasted_iota(jnp.int32, pooled.shape, 0) // slots
        column = lax.broadcasted_iota(jnp.int32, pooled.shape, 1) // frames
        pooled = jnp.where(row == column, pooled, 0.0)
        partial = pooled[:, 0:LANES]
        for at in range(LANES, near * frames, LANES):
            partial = partial + pooled[:, at : at + LANES]
        step = LANES // 2
        while step >= frames:
            partial = partial + pltpu.roll(partial, step, 1)
            step //= 2
        keys, groups = [], []
        for j in range(q * near, (q + 1) * near):
            ids = weights_ref[j, tail : tail + GROUP, :].astype(jnp.float32)
            owner = jnp.sum(jnp.where(eye, ids[0:1, :], 0.0), axis=1, keepdims=True).astype(jnp.int32)
            local = jnp.sum(jnp.where(eye, ids[1:2, :], 0.0), axis=1, keepdims=True).astype(jnp.int32)
            keys.append(owner * owner_rows + local % owner_rows)
            groups.append(local // owner_rows)
        key = jnp.concatenate(keys, axis=0)
        group = jnp.concatenate(groups, axis=0)
        lane_group = lax.broadcasted_iota(jnp.int32, partial.shape, 1) // frames
        partial = jnp.where(lane_group == group, partial, 0.0)
        high = partial.astype(jnp.bfloat16)
        low = (partial - high.astype(jnp.float32)).astype(jnp.bfloat16)
        onehot = (lax.broadcasted_iota(jnp.int32, (near * slots, owned), 1) == key).astype(jnp.bfloat16)
        both = lax.dot_general(
            onehot,
            jnp.concatenate([high, low], axis=1),
            (((0,), (0,)), ((), ())),
            preferred_element_type=jnp.float32,
        )
        total = total + both[:, :LANES] + both[:, LANES:]
    out_ref[...] = total.reshape(owners, owner_rows, LANES)


def contract(spread_filters, weights, data, owners):
    frames = data[0].shape[0] * len(data)
    shape = (owners, COMP_DEV * frames // LANES, LANES)
    return pl.pallas_call(
        contract_kernel,
        out_shape=jax.ShapeDtypeStruct(shape, jnp.float32),
        in_specs=whole_vmem(2 + len(data)),
        out_specs=whole_vmem(1)[0],
        compiler_params=params(12 * MIB + 4 * (spread_filters.size + len(data) * data[0].size + weights.size)),
        name="contract",
    )(spread_filters, weights, *data)


def finish_kernel(parts_ref, out_ref):
    sources, rows, _ = parts_ref.shape
    frames = out_ref.shape[1]
    total = jnp.sum(parts_ref[...], axis=0)
    for group in range(LANES // frames):
        out_ref[group * rows : (group + 1) * rows, :] = total[:, group * frames : (group + 1) * frames]


def finish(parts, frames):
    return pl.pallas_call(
        finish_kernel,
        out_shape=jax.ShapeDtypeStruct((COMP_DEV, frames), jnp.float32),
        in_specs=whole_vmem(1),
        out_specs=whole_vmem(1)[0],
        compiler_params=params(8 * MIB + 8 * parts.size),
        name="finish",
    )(parts)


def body(movie, shifts, filters, weights, slot_owner, slot_local):
    part_frames, planes, rows, width = movie.shape
    tiles = lax.axis_size("tile")
    parts = lax.axis_size("frame")
    frames = part_frames * parts
    slots = weights.shape[0]
    ends = tiles - 1
    downward, upward = edges(movie)
    top = lax.ppermute(downward, "tile", [(i, i + 1) for i in range(ends)])
    bottom = lax.ppermute(upward, "tile", [(i + 1, i) for i in range(ends)])
    owner, local = slot_owner.reshape(1, slots), slot_local.reshape(1, slots)
    gate = lax.ppermute(local, "frame", [(i, i ^ 1) for i in range(parts)])
    packed = pack(weights, owner, local, gate, tiles, planes)
    packed = lax.all_to_all(packed, "tile", split_axis=0, concat_axis=0, tiled=True)
    me = lax.axis_index("frame")
    place = jnp.stack([lax.axis_index("tile") * rows, tiles * rows, me]).astype(jnp.int32)
    pieces = smooth(movie, top, bottom, shifts.T, place, parts)
    pieces = [pieces[0]] + [
        lax.ppermute(pieces[k], "frame", [(i, i ^ k) for i in range(parts)]) for k in range(1, parts)
    ]
    deconvolve = spread(build_kernel(filters, frames), place, part_frames)
    traces = contract(deconvolve, packed, pieces, parts * tiles)
    traces = lax.all_to_all(traces, ("frame", "tile"), split_axis=0, concat_axis=0, tiled=True)
    return finish(traces, frames)


def solution(mesh):
    in_specs = (
        P("frame", None, "tile", None),
        P("frame", None),
        P(),
        P(("frame", "tile"), None),
        P(("frame", "tile"), None),
        P(("frame", "tile"), None),
    )
    out_specs = P(("frame", "tile"), None)
    return jax.shard_map(body, mesh=mesh, in_specs=in_specs, out_specs=out_specs, check_vma=False)
```

```python
import functools

import jax
import jax.numpy as jnp
import numpy as np
from jax import lax
from jax.experimental import pallas as pl
from jax.experimental.pallas import tpu as pltpu
from jax.sharding import PartitionSpec as P

COMP_DEV = 32
TAPS = 64
MAXS = 8
RAD = 3
LANES = 128
GROUP = 16
HALO = 16
OCTET = 8
QUAD = 4
MIB = 1 << 20


smooth_sigma = 1.0


def gauss_taps():
    positions = np.arange(-RAD, RAD + 1).astype(np.float32)
    values = np.exp(-positions * positions / np.float32(2.0 * smooth_sigma * smooth_sigma))
    return (values / values.sum(dtype=np.float32)).astype(np.float32)


def build_kernel(filters, count):
    later = jnp.arange(count)[:, None]
    earlier = jnp.arange(count)[None, :]
    offsets = later - earlier
    onehot = (offsets[:, :, None] == jnp.arange(TAPS)[None, None, :]).astype(jnp.float32)
    return jnp.sum(onehot[None] * filters[:, None, None, :], axis=-1).astype(jnp.bfloat16)


def whole_vmem(count):
    return [pl.BlockSpec(memory_space=pltpu.VMEM)] * count


def params(limit):
    return pltpu.CompilerParams(vmem_limit_bytes=limit)


def pack(weights, owner, local, place, after, tiles, planes):
    slots, pixels = weights.shape
    octets = pixels // (planes * tiles * LANES)
    tail = planes * octets * slots

    def kernel(place_ref, weights_ref, owner_ref, local_ref, after_ref, *refs):
        *out_refs, ids = refs
        ids[...] = jnp.zeros_like(ids)
        ids[0:1, 0:slots] = owner_ref[...].astype(jnp.float32)
        ids[1:2, 0:slots] = local_ref[...].astype(jnp.float32)
        for k, out_ref in enumerate(out_refs):
            dest = place_ref[3] ^ k
            for plane in range(planes):
                for octet in range(octets):
                    lane = pl.multiple_of(((plane * tiles + dest) * octets + octet) * LANES, LANES)
                    row = (plane * octets + octet) * slots
                    out_ref[row : row + slots, :] = weights_ref[:, pl.ds(lane, LANES)]
            out_ref[tail:, :] = ids[...].astype(jnp.bfloat16)

    return pl.pallas_call(
        kernel,
        out_shape=[jax.ShapeDtypeStruct((tail + GROUP, LANES), jnp.bfloat16)] * tiles,
        in_specs=[pl.BlockSpec(memory_space=pltpu.SMEM)] + whole_vmem(3) + [pl.BlockSpec(memory_space=pl.ANY)],
        out_specs=whole_vmem(tiles),
        scratch_shapes=[pltpu.VMEM((GROUP, LANES), jnp.float32)],
        compiler_params=params(8 * MIB + 5 * weights.size),
        name="pack_weights",
    )(place, weights, owner, local, after)


def edges_kernel(movie_ref, down_ref, up_ref):
    frames, planes, rows, _ = movie_ref.shape

    def one(frame, carry):
        tails = [movie_ref[frame, plane, rows - HALO :, :].astype(jnp.float32) for plane in range(planes)]
        heads = [movie_ref[frame, plane, :HALO, :].astype(jnp.float32) for plane in range(planes)]
        tail = [cells[OCTET:] for cells in tails] + [cells[QUAD:OCTET] for cells in tails]
        head = [cells[:OCTET] for cells in heads] + [cells[OCTET : OCTET + QUAD] for cells in heads]
        down_ref[frame] = jnp.concatenate(tail, axis=0).astype(jnp.bfloat16)
        up_ref[frame] = jnp.concatenate(head, axis=0).astype(jnp.bfloat16)
        return carry

    lax.fori_loop(0, frames, one, 0)


def edges(movie):
    frames, planes, _, width = movie.shape
    shape = jax.ShapeDtypeStruct((frames, planes * (OCTET + QUAD), width), jnp.bfloat16)
    return pl.pallas_call(
        edges_kernel,
        out_shape=[shape, shape],
        in_specs=whole_vmem(1),
        out_specs=whole_vmem(2),
        compiler_params=params(8 * MIB + 4 * movie.size),
        name="edges",
    )(movie)


def smooth_kernel(shift_ref, place_ref, movie_ref, top_ref, bottom_ref, *refs):
    *out_refs, band, wide = refs
    frames, planes, rows, width = movie_ref.shape
    blocks = width // LANES
    reach = rows + 2 * HALO
    parts = len(out_refs)
    each = blocks // parts
    taps = gauss_taps()
    high = [float(v) for v in taps.astype(jnp.bfloat16)]
    low = [float(v) for v in taps - taps.astype(jnp.bfloat16).astype(np.float32)]
    lane = lax.broadcasted_iota(jnp.int32, (reach, LANES), 1)
    row = lax.broadcasted_iota(jnp.int32, (reach, LANES), 0)
    first_row, total_rows, me = place_ref[0], place_ref[1], place_ref[2]

    tap = lax.broadcasted_iota(jnp.int32, (2 * LANES, LANES), 0) - lax.broadcasted_iota(jnp.int32, (2 * LANES, LANES), 1)
    tap = tap - (MAXS - RAD)
    for side, values in enumerate((high, low)):
        cells = jnp.zeros((2 * LANES, LANES), jnp.float32)
        for i, value in enumerate(values):
            cells = jnp.where(tap == i, value, cells)
        band[:, side * LANES : (side + 1) * LANES] = cells.astype(jnp.bfloat16)

    def one(frame, carry):
        down = shift_ref[0, frame]
        right = shift_ref[1, frame] + MAXS
        near = lane < right
        zero = jnp.zeros((reach, LANES), jnp.float32)
        place = first_row + row - HALO + down
        inside = (place >= 0) & (place < total_rows)
        start = HALO - RAD - down
        for plane in range(planes):
            moved = []
            for b in range(blocks):
                cells = slice(b * LANES, (b + 1) * LANES)
                top = top_ref[frame, :, cells].astype(jnp.float32)
                bottom = bottom_ref[frame, :, cells].astype(jnp.float32)
                full = slice(plane * OCTET, (plane + 1) * OCTET)
                rest = slice(planes * OCTET + plane * QUAD, planes * OCTET + (plane + 1) * QUAD)
                piece = jnp.concatenate(
                    [
                        top[rest],
                        top[rest],
                        top[full],
                        movie_ref[frame, plane, :, cells].astype(jnp.float32),
                        bottom[full],
                        bottom[rest],
                        bottom[rest],
                    ],
                    axis=0,
                )
                moved.append(pltpu.roll(piece, right, 1))
            shifted = []
            for b in range(blocks + 1):
                before = moved[b - 1] if b > 0 else zero
                own = moved[b] if b < blocks else zero
                cells = jnp.where(near, before, own)
                if b == 0:
                    cells = jnp.where(lane < MAXS, 0.0, cells)
                if b == blocks:
                    cells = jnp.where(lane < MAXS, cells, 0.0)
                shifted.append(cells.astype(jnp.bfloat16))
            cells = jnp.concatenate(
                [jnp.concatenate(shifted[b : b + 2], axis=1) for b in range(blocks)], axis=0
            )
            result = jnp.dot(cells, band[...], preferred_element_type=jnp.float32)
            result = result[:, :LANES] + result[:, LANES:]
            for b in range(blocks):
                wide[plane, b] = jnp.where(inside, result[b * reach : (b + 1) * reach], 0.0)
        for plane in range(planes):
            for k in range(parts):
                for j in range(each):
                    b = (me ^ k) * each + j
                    total = float(taps[RAD]) * wide[plane, b, pl.ds(start + RAD, rows), :]
                    for i in range(RAD):
                        pair = wide[plane, b, pl.ds(start + i, rows), :]
                        pair = pair + wide[plane, b, pl.ds(start + 2 * RAD - i, rows), :]
                        total = total + float(taps[i]) * pair
                    out_refs[k][frame, plane, :, j * LANES : (j + 1) * LANES] = total.astype(jnp.bfloat16)
        return carry

    lax.fori_loop(0, frames, one, 0)


def smooth(movie, top, bottom, shifts, place, parts):
    frames, planes, rows, width = movie.shape
    reach = rows + 2 * HALO
    smem = pl.BlockSpec(memory_space=pltpu.SMEM)
    return pl.pallas_call(
        smooth_kernel,
        out_shape=[jax.ShapeDtypeStruct((frames, planes, rows, width // parts), jnp.bfloat16)] * parts,
        in_specs=[smem, smem] + whole_vmem(3),
        out_specs=whole_vmem(parts),
        scratch_shapes=[
            pltpu.VMEM((2 * LANES, 2 * LANES), jnp.bfloat16),
            pltpu.VMEM((planes, width // LANES, reach, LANES), jnp.float32),
        ],
        compiler_params=params(12 * MIB + 8 * movie.size),
        name="smooth",
    )(shifts, place, movie, top, bottom)


def spread_kernel(part_frames, place_ref, kernel_ref, out_ref):
    planes, size, _ = out_ref.shape
    frames = size // GROUP
    me = place_ref[2]
    row = lax.broadcasted_iota(jnp.int32, (size, frames), 0)
    column = lax.broadcasted_iota(jnp.int32, (size, frames), 1)
    tall = (row % frames == column).astype(jnp.bfloat16)
    row = lax.broadcasted_iota(jnp.int32, (frames, size), 0)
    column = lax.broadcasted_iota(jnp.int32, (frames, size), 1) // GROUP
    column = ((column // part_frames) ^ me) * part_frames + column % part_frames
    flat = (column == row).astype(jnp.bfloat16)
    row = lax.broadcasted_iota(jnp.int32, (size, size), 0)
    column = lax.broadcasted_iota(jnp.int32, (size, size), 1)
    same = row // frames == column % GROUP
    for plane in range(planes):
        left = jnp.dot(tall, kernel_ref[plane], preferred_element_type=jnp.float32).astype(jnp.bfloat16)
        full = jnp.dot(left, flat, preferred_element_type=jnp.float32)
        out_ref[plane] = jnp.where(same, full, 0.0).astype(jnp.bfloat16)


def spread(kernel, place, part_frames):
    planes, frames, _ = kernel.shape
    size = frames * GROUP
    return pl.pallas_call(
        functools.partial(spread_kernel, part_frames),
        out_shape=jax.ShapeDtypeStruct((planes, size, size), jnp.bfloat16),
        in_specs=[pl.BlockSpec(memory_space=pltpu.SMEM)] + whole_vmem(1),
        out_specs=whole_vmem(1)[0],
        compiler_params=params(8 * MIB + 16 * size * size),
        name="spread_filters",
    )(place, kernel)


def swap_lanes(pieces):
    count = len(pieces)
    group = LANES // count
    half = count // 2
    lane = lax.broadcasted_iota(jnp.int32, pieces[0].shape, 1) // group
    while half >= 1:
        low = (lane & half) == 0
        result = list(pieces)
        for i in range(count):
            if i & half:
                continue
            a, b = pieces[i], pieces[i + half]
            if 2 * half == count:
                back = pltpu.roll(b, half * group, 1)
                ahead = pltpu.roll(a, half * group, 1)
            else:
                back = pltpu.roll(b, half * group, 1)
                ahead = pltpu.roll(a, LANES - half * group, 1)
            result[i] = jnp.where(low, a, back)
            result[i + half] = jnp.where(low, ahead, b)
        pieces = result
        half //= 2
    return pieces


def contract_kernel(parts, place_ref, spread_ref, *refs):
    data_refs, weights_refs, out_ref = refs[:parts], refs[parts:-1], refs[-1]
    part_frames, planes, rows, width = data_refs[0].shape
    tiles = len(weights_refs)
    me = place_ref[3]
    frames = parts * part_frames
    octets = rows // OCTET
    slots = (weights_refs[0].shape[0] - GROUP) // (planes * octets)
    tail = planes * octets * slots
    near = LANES * tiles // width
    owners, owner_rows, _ = out_ref.shape
    owned = owners * owner_rows
    size = frames * GROUP
    eye = lax.broadcasted_iota(jnp.int32, (slots, LANES), 0) == lax.broadcasted_iota(jnp.int32, (slots, LANES), 1)
    keys, groups = [], []
    for ref in weights_refs:
        ids = ref[tail : tail + GROUP, :].astype(jnp.float32)
        owner = jnp.sum(jnp.where(eye, ids[0:1, :], 0.0), axis=1, keepdims=True).astype(jnp.int32)
        local = jnp.sum(jnp.where(eye, ids[1:2, :], 0.0), axis=1, keepdims=True).astype(jnp.int32)
        keys.append(owner * owner_rows + local % owner_rows)
        groups.append(local // owner_rows)
    key = jnp.concatenate(keys, axis=0)
    group = jnp.concatenate(groups, axis=0)
    onehot = (lax.broadcasted_iota(jnp.int32, (tiles * slots, owned), 1) == key).astype(jnp.bfloat16)
    total = jnp.zeros((owned, LANES), jnp.float32)
    for q in range(width // LANES):
        lanes = slice(q * LANES, (q + 1) * LANES)
        pooled = jnp.zeros((tiles * slots, near * frames), jnp.float32)
        for plane in range(planes):
            for first in range(0, rows // GROUP, 2):
                cells = []
                for a in (first, first + 1):
                    pieces = [ref[:, plane, a * GROUP : (a + 1) * GROUP, lanes] for ref in data_refs]
                    cells.append(jnp.concatenate(pieces, axis=0).reshape(size, LANES))
                cells = jnp.concatenate(cells, axis=1)
                spikes = jnp.dot(spread_ref[plane], cells, preferred_element_type=jnp.float32)
                spikes = jnp.maximum(spikes, 0.0)
                for a in (0, 1):
                    sides = []
                    for half in (0, 1):
                        pieces = [
                            spikes[(half * OCTET + r) * frames : (half * OCTET + r + 1) * frames, a * LANES : (a + 1) * LANES]
                            for r in range(OCTET)
                        ]
                        pieces = [piece.astype(jnp.bfloat16) for piece in swap_lanes(pieces)]
                        sides.append(jnp.concatenate(pieces, axis=0))
                    right = jnp.concatenate(sides, axis=1)
                    left = []
                    for half in (0, 1):
                        octet = (first + a) * 2 + half
                        row = (plane * octets + octet) * slots
                        left.append(jnp.concatenate([ref[row : row + slots, :] for ref in weights_refs], axis=0))
                    left = jnp.concatenate(left, axis=1)
                    pooled = pooled + lax.dot_general(
                        left, right, (((1,), (1,)), ((), ())), preferred_element_type=jnp.float32
                    )
        row = (lax.broadcasted_iota(jnp.int32, pooled.shape, 0) // slots) ^ me
        column = lax.broadcasted_iota(jnp.int32, pooled.shape, 1) // frames + q * near
        pooled = jnp.where(row == column, pooled, 0.0)
        partial = pooled[:, 0:LANES]
        for at in range(LANES, near * frames, LANES):
            partial = partial + pooled[:, at : at + LANES]
        step = LANES // 2
        while step >= frames:
            partial = partial + pltpu.roll(partial, step, 1)
            step //= 2
        lane_group = lax.broadcasted_iota(jnp.int32, partial.shape, 1) // frames
        partial = jnp.where(lane_group == group, partial, 0.0)
        high = partial.astype(jnp.bfloat16)
        low = (partial - high.astype(jnp.float32)).astype(jnp.bfloat16)
        both = lax.dot_general(
            onehot,
            jnp.concatenate([high, low], axis=1),
            (((0,), (0,)), ((), ())),
            preferred_element_type=jnp.float32,
        )
        total = total + both[:, :LANES] + both[:, LANES:]
    out_ref[...] = total.reshape(owners, owner_rows, LANES)


def contract(spread_filters, weights, data, place, owners):
    frames = data[0].shape[0] * len(data)
    shape = (owners, COMP_DEV * frames // LANES, LANES)
    inputs = [spread_filters, *data, *weights]
    return pl.pallas_call(
        functools.partial(contract_kernel, len(data)),
        out_shape=jax.ShapeDtypeStruct(shape, jnp.float32),
        in_specs=[pl.BlockSpec(memory_space=pltpu.SMEM)] + whole_vmem(len(inputs)),
        out_specs=whole_vmem(1)[0],
        compiler_params=params(12 * MIB + 4 * sum(cells.size for cells in inputs)),
        name="contract",
    )(place, *inputs)


def finish_kernel(parts_ref, out_ref):
    sources, rows, _ = parts_ref.shape
    frames = out_ref.shape[1]
    total = jnp.sum(parts_ref[...], axis=0)
    for group in range(LANES // frames):
        out_ref[group * rows : (group + 1) * rows, :] = total[:, group * frames : (group + 1) * frames]


def finish(parts, frames):
    return pl.pallas_call(
        finish_kernel,
        out_shape=jax.ShapeDtypeStruct((COMP_DEV, frames), jnp.float32),
        in_specs=whole_vmem(1),
        out_specs=whole_vmem(1)[0],
        compiler_params=params(8 * MIB + 8 * parts.size),
        name="finish",
    )(parts)


def body(movie, shifts, filters, weights, slot_owner, slot_local):
    part_frames, planes, rows, width = movie.shape
    tiles = lax.axis_size("tile")
    parts = lax.axis_size("frame")
    frames = part_frames * parts
    slots = weights.shape[0]
    ends = tiles - 1
    place = jnp.stack([lax.axis_index("tile") * rows, tiles * rows, lax.axis_index("frame"), lax.axis_index("tile")])
    place = place.astype(jnp.int32)
    downward, upward = edges(movie)
    top = lax.ppermute(downward, "tile", [(i, i + 1) for i in range(ends)])
    bottom = lax.ppermute(upward, "tile", [(i + 1, i) for i in range(ends)])
    owner, local = slot_owner.reshape(1, slots), slot_local.reshape(1, slots)
    packed = pack(weights, owner, local, place, upward, tiles, planes)
    landed = [packed[0]] + [None] * ends
    for k in range(ends, 0, -1):
        landed[k] = lax.ppermute(packed[k], "tile", [(i, i ^ k) for i in range(tiles)])
    pieces = smooth(movie, top, bottom, shifts.T, place, parts)
    pieces = [pieces[0]] + [
        lax.ppermute(pieces[k], "frame", [(i, i ^ k) for i in range(parts)]) for k in range(1, parts)
    ]
    deconvolve = spread(build_kernel(filters, frames), place, part_frames)
    traces = contract(deconvolve, landed, pieces, place, parts * tiles)
    traces = lax.all_to_all(traces, ("frame", "tile"), split_axis=0, concat_axis=0, tiled=True)
    return finish(traces, frames)


def solution(mesh):
    in_specs = (
        P("frame", None, "tile", None),
        P("frame", None),
        P(),
        P(("frame", "tile"), None),
        P(("frame", "tile"), None),
        P(("frame", "tile"), None),
    )
    out_specs = P(("frame", "tile"), None)
    return jax.shard_map(body, mesh=mesh, in_specs=in_specs, out_specs=out_specs, check_vma=False)
```

```python
import functools

import jax
import jax.numpy as jnp
import numpy as np
from jax import lax
from jax.experimental import pallas as pl
from jax.experimental.pallas import tpu as pltpu
from jax.sharding import PartitionSpec as P

COMP_DEV = 32
TAPS = 64
MAXS = 8
RAD = 3
LANES = 128
GROUP = 16
HALO = 16
OCTET = 8
QUAD = 4
MIB = 1 << 20


smooth_sigma = 1.0


def gauss_taps():
    positions = np.arange(-RAD, RAD + 1).astype(np.float32)
    values = np.exp(-positions * positions / np.float32(2.0 * smooth_sigma * smooth_sigma))
    return (values / values.sum(dtype=np.float32)).astype(np.float32)


def build_kernel(filters, count):
    later = jnp.arange(count)[:, None]
    earlier = jnp.arange(count)[None, :]
    offsets = later - earlier
    onehot = (offsets[:, :, None] == jnp.arange(TAPS)[None, None, :]).astype(jnp.float32)
    return jnp.sum(onehot[None] * filters[:, None, None, :], axis=-1).astype(jnp.bfloat16)


def whole_vmem(count):
    return [pl.BlockSpec(memory_space=pltpu.VMEM)] * count


def params(limit):
    return pltpu.CompilerParams(vmem_limit_bytes=limit)


def prepare_kernel(order, place_ref, movie_ref, weights_ref, owner_ref, local_ref, *refs):
    down_ref, up_ref, *out_refs, tails, heads, held, ids_held, ids, sems = refs
    frames, planes, rows, _ = movie_ref.shape
    tiles = len(order)
    slots, pixels = weights_ref.shape
    octets = pixels // (planes * tiles * LANES)
    tail = planes * octets * slots
    copies = [
        pltpu.make_async_copy(movie_ref.at[:, :, pl.ds(rows - HALO, HALO), :], tails, sems.at[0]),
        pltpu.make_async_copy(movie_ref.at[:, :, pl.ds(0, HALO), :], heads, sems.at[1]),
        pltpu.make_async_copy(owner_ref, ids_held.at[0], sems.at[2]),
        pltpu.make_async_copy(local_ref, ids_held.at[1], sems.at[3]),
        pltpu.make_async_copy(weights_ref, held, sems.at[4]),
    ]
    for copy in copies:
        copy.start()
    copies[0].wait()
    copies[1].wait()

    def one(frame, carry):
        last = [tails[frame, plane].astype(jnp.float32) for plane in range(planes)]
        first = [heads[frame, plane].astype(jnp.float32) for plane in range(planes)]
        last = [cells[OCTET:] for cells in last] + [cells[QUAD:OCTET] for cells in last]
        first = [cells[:OCTET] for cells in first] + [cells[OCTET : OCTET + QUAD] for cells in first]
        down_ref[frame] = jnp.concatenate(last, axis=0).astype(jnp.bfloat16)
        up_ref[frame] = jnp.concatenate(first, axis=0).astype(jnp.bfloat16)
        return carry

    lax.fori_loop(0, frames, one, 0)
    for copy in copies[2:]:
        copy.wait()
    ids[...] = jnp.zeros_like(ids)
    ids[0:1, 0:slots] = ids_held[0].astype(jnp.float32)
    ids[1:2, 0:slots] = ids_held[1].astype(jnp.float32)
    for k, out_ref in zip(order, out_refs):
        dest = place_ref[2] ^ k
        for plane in range(planes):
            for octet in range(octets):
                lane = pl.multiple_of(((plane * tiles + dest) * octets + octet) * LANES, LANES)
                row = (plane * octets + octet) * slots
                out_ref[row : row + slots, :] = held[:, pl.ds(lane, LANES)]
        out_ref[tail:, :] = ids[...].astype(jnp.bfloat16)


def prepare(movie, weights, owner, local, order, place):
    frames, planes, _, width = movie.shape
    slots, pixels = weights.shape
    tiles = len(order)
    rows = pixels // (tiles * LANES) * slots + GROUP
    edge = jax.ShapeDtypeStruct((frames, planes * (OCTET + QUAD), width), jnp.bfloat16)
    packed = jax.ShapeDtypeStruct((rows, LANES), jnp.bfloat16)
    down, up, *packed = pl.pallas_call(
        functools.partial(prepare_kernel, order),
        out_shape=[edge, edge] + [packed] * tiles,
        in_specs=[pl.BlockSpec(memory_space=pltpu.SMEM)] + [pl.BlockSpec(memory_space=pl.ANY)] * 4,
        out_specs=whole_vmem(2 + tiles),
        scratch_shapes=[
            pltpu.VMEM((frames, planes, HALO, width), jnp.bfloat16),
            pltpu.VMEM((frames, planes, HALO, width), jnp.bfloat16),
            pltpu.VMEM((slots, pixels), jnp.bfloat16),
            pltpu.VMEM((2, 1, slots), jnp.int32),
            pltpu.VMEM((GROUP, LANES), jnp.float32),
            pltpu.SemaphoreType.DMA((5,)),
        ],
        compiler_params=params(8 * MIB + 4 * movie.size + 5 * weights.size),
        name="prepare",
    )(place, movie, weights, owner, local)
    return down, up, packed


def smooth_kernel(shift_ref, place_ref, movie_ref, top_ref, bottom_ref, out_ref, band, wide):
    frames, planes, rows, width = movie_ref.shape
    blocks = width // LANES
    reach = rows + 2 * HALO
    each = blocks // out_ref.shape[0]
    taps = gauss_taps()
    high = [float(v) for v in taps.astype(jnp.bfloat16)]
    low = [float(v) for v in taps - taps.astype(jnp.bfloat16).astype(np.float32)]
    lane = lax.broadcasted_iota(jnp.int32, (reach, LANES), 1)
    row = lax.broadcasted_iota(jnp.int32, (reach, LANES), 0)
    first_row, total_rows = place_ref[0], place_ref[1]

    tap = lax.broadcasted_iota(jnp.int32, (2 * LANES, LANES), 0) - lax.broadcasted_iota(jnp.int32, (2 * LANES, LANES), 1)
    tap = tap - (MAXS - RAD)
    for side, values in enumerate((high, low)):
        cells = jnp.zeros((2 * LANES, LANES), jnp.float32)
        for i, value in enumerate(values):
            cells = jnp.where(tap == i, value, cells)
        band[:, side * LANES : (side + 1) * LANES] = cells.astype(jnp.bfloat16)

    def one(frame, carry):
        down = shift_ref[0, frame]
        right = shift_ref[1, frame] + MAXS
        near = lane < right
        zero = jnp.zeros((reach, LANES), jnp.float32)
        place = first_row + row - HALO + down
        inside = (place >= 0) & (place < total_rows)
        start = HALO - RAD - down
        for plane in range(planes):
            moved = []
            for b in range(blocks):
                cells = slice(b * LANES, (b + 1) * LANES)
                top = top_ref[frame, :, cells].astype(jnp.float32)
                bottom = bottom_ref[frame, :, cells].astype(jnp.float32)
                full = slice(plane * OCTET, (plane + 1) * OCTET)
                rest = slice(planes * OCTET + plane * QUAD, planes * OCTET + (plane + 1) * QUAD)
                piece = jnp.concatenate(
                    [
                        top[rest],
                        top[rest],
                        top[full],
                        movie_ref[frame, plane, :, cells].astype(jnp.float32),
                        bottom[full],
                        bottom[rest],
                        bottom[rest],
                    ],
                    axis=0,
                )
                moved.append(pltpu.roll(piece, right, 1))
            shifted = []
            for b in range(blocks + 1):
                before = moved[b - 1] if b > 0 else zero
                own = moved[b] if b < blocks else zero
                cells = jnp.where(near, before, own)
                if b == 0:
                    cells = jnp.where(lane < MAXS, 0.0, cells)
                if b == blocks:
                    cells = jnp.where(lane < MAXS, cells, 0.0)
                shifted.append(cells.astype(jnp.bfloat16))
            cells = jnp.concatenate(
                [jnp.concatenate(shifted[b : b + 2], axis=1) for b in range(blocks)], axis=0
            )
            result = jnp.dot(cells, band[...], preferred_element_type=jnp.float32)
            result = result[:, :LANES] + result[:, LANES:]
            for b in range(blocks):
                wide[plane, b] = jnp.where(inside, result[b * reach : (b + 1) * reach], 0.0)
        for plane in range(planes):
            for b in range(blocks):
                total = float(taps[RAD]) * wide[plane, b, pl.ds(start + RAD, rows), :]
                for i in range(RAD):
                    pair = wide[plane, b, pl.ds(start + i, rows), :]
                    pair = pair + wide[plane, b, pl.ds(start + 2 * RAD - i, rows), :]
                    total = total + float(taps[i]) * pair
                cells = slice(b % each * LANES, (b % each + 1) * LANES)
                out_ref[b // each, frame, plane, :, cells] = total.astype(jnp.bfloat16)
        return carry

    lax.fori_loop(0, frames, one, 0)


def smooth(movie, top, bottom, shifts, place, parts):
    frames, planes, rows, width = movie.shape
    reach = rows + 2 * HALO
    smem = pl.BlockSpec(memory_space=pltpu.SMEM)
    return pl.pallas_call(
        smooth_kernel,
        out_shape=jax.ShapeDtypeStruct((parts, frames, planes, rows, width // parts), jnp.bfloat16),
        in_specs=[smem, smem] + whole_vmem(3),
        out_specs=whole_vmem(1)[0],
        scratch_shapes=[
            pltpu.VMEM((2 * LANES, 2 * LANES), jnp.bfloat16),
            pltpu.VMEM((planes, width // LANES, reach, LANES), jnp.float32),
        ],
        compiler_params=params(12 * MIB + 8 * movie.size),
        name="smooth",
    )(shifts, place, movie, top, bottom)


def spread_kernel(kernel_ref, out_ref):
    planes, size, _ = out_ref.shape
    frames = size // GROUP
    row = lax.broadcasted_iota(jnp.int32, (size, frames), 0)
    column = lax.broadcasted_iota(jnp.int32, (size, frames), 1)
    tall = (row % frames == column).astype(jnp.bfloat16)
    row = lax.broadcasted_iota(jnp.int32, (frames, size), 0)
    column = lax.broadcasted_iota(jnp.int32, (frames, size), 1)
    flat = (column // GROUP == row).astype(jnp.bfloat16)
    row = lax.broadcasted_iota(jnp.int32, (size, size), 0)
    column = lax.broadcasted_iota(jnp.int32, (size, size), 1)
    same = row // frames == column % GROUP
    for plane in range(planes):
        left = jnp.dot(tall, kernel_ref[plane], preferred_element_type=jnp.float32).astype(jnp.bfloat16)
        full = jnp.dot(left, flat, preferred_element_type=jnp.float32)
        out_ref[plane] = jnp.where(same, full, 0.0).astype(jnp.bfloat16)


def spread(kernel):
    planes, frames, _ = kernel.shape
    size = frames * GROUP
    return pl.pallas_call(
        spread_kernel,
        out_shape=jax.ShapeDtypeStruct((planes, size, size), jnp.bfloat16),
        in_specs=whole_vmem(1),
        out_specs=whole_vmem(1)[0],
        compiler_params=params(8 * MIB + 16 * size * size),
        name="spread_filters",
    )(kernel)


def swap_lanes(pieces):
    count = len(pieces)
    group = LANES // count
    half = count // 2
    lane = lax.broadcasted_iota(jnp.int32, pieces[0].shape, 1) // group
    while half >= 1:
        low = (lane & half) == 0
        result = list(pieces)
        for i in range(count):
            if i & half:
                continue
            a, b = pieces[i], pieces[i + half]
            if 2 * half == count:
                back = pltpu.roll(b, half * group, 1)
                ahead = pltpu.roll(a, half * group, 1)
            else:
                back = pltpu.roll(b, half * group, 1)
                ahead = pltpu.roll(a, LANES - half * group, 1)
            result[i] = jnp.where(low, a, back)
            result[i + half] = jnp.where(low, ahead, b)
        pieces = result
        half //= 2
    return pieces


def contract_kernel(order, place_ref, spread_ref, data_ref, *refs):
    *weights_refs, out_ref = refs
    parts, part_frames, planes, rows, width = data_ref.shape
    tiles = len(weights_refs)
    me = place_ref[2]
    frames = parts * part_frames
    octets = rows // OCTET
    slots = (weights_refs[0].shape[0] - GROUP) // (planes * octets)
    tail = planes * octets * slots
    near = LANES * tiles // width
    owners, owner_rows, _ = out_ref.shape
    owned = owners * owner_rows
    size = frames * GROUP
    eye = lax.broadcasted_iota(jnp.int32, (slots, LANES), 0) == lax.broadcasted_iota(jnp.int32, (slots, LANES), 1)
    keys, groups = [], []
    for ref in weights_refs:
        ids = ref[tail : tail + GROUP, :].astype(jnp.float32)
        owner = jnp.sum(jnp.where(eye, ids[0:1, :], 0.0), axis=1, keepdims=True).astype(jnp.int32)
        local = jnp.sum(jnp.where(eye, ids[1:2, :], 0.0), axis=1, keepdims=True).astype(jnp.int32)
        keys.append(owner * owner_rows + local % owner_rows)
        groups.append(local // owner_rows)
    key = jnp.concatenate(keys, axis=0)
    group = jnp.concatenate(groups, axis=0)
    onehot = (lax.broadcasted_iota(jnp.int32, (tiles * slots, owned), 1) == key).astype(jnp.bfloat16)
    total = jnp.zeros((owned, LANES), jnp.float32)
    for q in range(width // LANES):
        lanes = slice(q * LANES, (q + 1) * LANES)
        pooled = jnp.zeros((tiles * slots, near * frames), jnp.float32)
        for plane in range(planes):
            for first in range(0, rows // GROUP, 2):
                cells = []
                for a in (first, first + 1):
                    cells.append(data_ref[:, :, plane, a * GROUP : (a + 1) * GROUP, lanes].reshape(size, LANES))
                cells = jnp.concatenate(cells, axis=1)
                spikes = jnp.dot(spread_ref[plane], cells, preferred_element_type=jnp.float32)
                spikes = jnp.maximum(spikes, 0.0)
                for a in (0, 1):
                    sides = []
                    for half in (0, 1):
                        pieces = [
                            spikes[(half * OCTET + r) * frames : (half * OCTET + r + 1) * frames, a * LANES : (a + 1) * LANES]
                            for r in range(OCTET)
                        ]
                        pieces = [piece.astype(jnp.bfloat16) for piece in swap_lanes(pieces)]
                        sides.append(jnp.concatenate(pieces, axis=0))
                    right = jnp.concatenate(sides, axis=1)
                    left = []
                    for half in (0, 1):
                        octet = (first + a) * 2 + half
                        row = (plane * octets + octet) * slots
                        left.append(jnp.concatenate([ref[row : row + slots, :] for ref in weights_refs], axis=0))
                    left = jnp.concatenate(left, axis=1)
                    pooled = pooled + lax.dot_general(
                        left, right, (((1,), (1,)), ((), ())), preferred_element_type=jnp.float32
                    )
        column = lax.broadcasted_iota(jnp.int32, (slots, near * frames), 1) // frames + q * near
        pooled = jnp.concatenate(
            [jnp.where(column == me ^ k, pooled[i * slots : (i + 1) * slots], 0.0) for i, k in enumerate(order)], axis=0
        )
        partial = pooled[:, 0:LANES]
        for at in range(LANES, near * frames, LANES):
            partial = partial + pooled[:, at : at + LANES]
        step = LANES // 2
        while step >= frames:
            partial = partial + pltpu.roll(partial, step, 1)
            step //= 2
        lane_group = lax.broadcasted_iota(jnp.int32, partial.shape, 1) // frames
        partial = jnp.where(lane_group == group, partial, 0.0)
        high = partial.astype(jnp.bfloat16)
        low = (partial - high.astype(jnp.float32)).astype(jnp.bfloat16)
        both = lax.dot_general(
            onehot,
            jnp.concatenate([high, low], axis=1),
            (((0,), (0,)), ((), ())),
            preferred_element_type=jnp.float32,
        )
        total = total + both[:, :LANES] + both[:, LANES:]
    out_ref[...] = total.reshape(owners, owner_rows, LANES)


def contract(spread_filters, data, weights, order, place, owners):
    frames = data.shape[0] * data.shape[1]
    shape = (owners, COMP_DEV * frames // LANES, LANES)
    inputs = [spread_filters, data, *weights]
    return pl.pallas_call(
        functools.partial(contract_kernel, order),
        out_shape=jax.ShapeDtypeStruct(shape, jnp.float32),
        in_specs=[pl.BlockSpec(memory_space=pltpu.SMEM)] + whole_vmem(len(inputs)),
        out_specs=whole_vmem(1)[0],
        compiler_params=params(12 * MIB + 4 * sum(cells.size for cells in inputs)),
        name="contract",
    )(place, *inputs)


def finish_kernel(parts_ref, out_ref):
    sources, rows, _ = parts_ref.shape
    frames = out_ref.shape[1]
    total = jnp.sum(parts_ref[...], axis=0)
    for group in range(LANES // frames):
        out_ref[group * rows : (group + 1) * rows, :] = total[:, group * frames : (group + 1) * frames]


def finish(parts, frames):
    return pl.pallas_call(
        finish_kernel,
        out_shape=jax.ShapeDtypeStruct((COMP_DEV, frames), jnp.float32),
        in_specs=whole_vmem(1),
        out_specs=whole_vmem(1)[0],
        compiler_params=params(8 * MIB + 8 * parts.size),
        name="finish",
    )(parts)


def body(movie, shifts, filters, weights, slot_owner, slot_local):
    part_frames, planes, rows, width = movie.shape
    tiles = lax.axis_size("tile")
    parts = lax.axis_size("frame")
    frames = part_frames * parts
    slots = weights.shape[0]
    ends = tiles - 1
    tile = lax.axis_index("tile")
    place = jnp.stack([tile * rows, tiles * rows, tile]).astype(jnp.int32)
    order = list(range(tiles // 2, tiles)) + list(range(tiles // 2 - 1, -1, -1))
    owner, local = slot_owner.reshape(1, slots), slot_local.reshape(1, slots)
    down, up, packed = prepare(movie, weights, owner, local, order, place)
    top = lax.ppermute(down, "tile", [(i, i + 1) for i in range(ends)])
    bottom = lax.ppermute(up, "tile", [(i + 1, i) for i in range(ends)])
    landed = [
        lax.ppermute(cells, "tile", [(i, i ^ k) for i in range(tiles)]) if k else cells
        for k, cells in zip(order, packed)
    ]
    pieces = smooth(movie, top, bottom, shifts.T, place, parts)
    pieces = lax.all_to_all(pieces, "frame", split_axis=0, concat_axis=0, tiled=True)
    deconvolve = spread(build_kernel(filters, frames))
    traces = contract(deconvolve, pieces, landed, order, place, parts * tiles)
    traces = lax.all_to_all(traces, ("frame", "tile"), split_axis=0, concat_axis=0, tiled=True)
    return finish(traces, frames)


def solution(mesh):
    in_specs = (
        P("frame", None, "tile", None),
        P("frame", None),
        P(),
        P(("frame", "tile"), None),
        P(("frame", "tile"), None),
        P(("frame", "tile"), None),
    )
    out_specs = P(("frame", "tile"), None)
    return jax.shard_map(body, mesh=mesh, in_specs=in_specs, out_specs=out_specs, check_vma=False)
```

```python
import functools

import jax
import jax.numpy as jnp
import numpy as np
from jax import lax
from jax.experimental import pallas as pl
from jax.experimental.pallas import tpu as pltpu
from jax.sharding import PartitionSpec as P

COMP_DEV = 32
TAPS = 64
MAXS = 8
RAD = 3
LANES = 128
GROUP = 16
HALO = 16
OCTET = 8
QUAD = 4
MIB = 1 << 20


smooth_sigma = 1.0


def gauss_taps():
    positions = np.arange(-RAD, RAD + 1).astype(np.float32)
    values = np.exp(-positions * positions / np.float32(2.0 * smooth_sigma * smooth_sigma))
    return (values / values.sum(dtype=np.float32)).astype(np.float32)


def build_kernel(filters, count):
    later = jnp.arange(count)[:, None]
    earlier = jnp.arange(count)[None, :]
    offsets = later - earlier
    onehot = (offsets[:, :, None] == jnp.arange(TAPS)[None, None, :]).astype(jnp.float32)
    return jnp.sum(onehot[None] * filters[:, None, None, :], axis=-1).astype(jnp.bfloat16)


def whole_vmem(count):
    return [pl.BlockSpec(memory_space=pltpu.VMEM)] * count


def params(limit):
    return pltpu.CompilerParams(vmem_limit_bytes=limit)


def prepare_kernel(order, place_ref, movie_ref, weights_ref, owner_ref, local_ref, *refs):
    pair_ref, other_ref, *out_refs, tails, heads, held, ids_held, ids, sems = refs
    even = place_ref[3] % 2 == 0
    frames, planes, rows, _ = movie_ref.shape
    tiles = len(order)
    slots, pixels = weights_ref.shape
    octets = pixels // (planes * tiles * LANES)
    tail = planes * octets * slots
    copies = [
        pltpu.make_async_copy(movie_ref.at[:, :, pl.ds(rows - HALO, HALO), :], tails, sems.at[0]),
        pltpu.make_async_copy(movie_ref.at[:, :, pl.ds(0, HALO), :], heads, sems.at[1]),
        pltpu.make_async_copy(owner_ref, ids_held.at[0], sems.at[2]),
        pltpu.make_async_copy(local_ref, ids_held.at[1], sems.at[3]),
        pltpu.make_async_copy(weights_ref, held, sems.at[4]),
    ]
    for copy in copies:
        copy.start()
    copies[0].wait()
    copies[1].wait()

    def one(frame, carry):
        last = [tails[frame, plane].astype(jnp.float32) for plane in range(planes)]
        first = [heads[frame, plane].astype(jnp.float32) for plane in range(planes)]
        last = [cells[OCTET:] for cells in last] + [cells[QUAD:OCTET] for cells in last]
        first = [cells[:OCTET] for cells in first] + [cells[OCTET : OCTET + QUAD] for cells in first]
        last = jnp.concatenate(last, axis=0)
        first = jnp.concatenate(first, axis=0)
        pair_ref[frame] = jnp.where(even, last, first).astype(jnp.bfloat16)
        other_ref[frame] = jnp.where(even, first, last).astype(jnp.bfloat16)
        return carry

    lax.fori_loop(0, frames, one, 0)
    for copy in copies[2:]:
        copy.wait()
    ids[...] = jnp.zeros_like(ids)
    ids[0:1, 0:slots] = ids_held[0].astype(jnp.float32)
    ids[1:2, 0:slots] = ids_held[1].astype(jnp.float32)
    for k, out_ref in zip(order, out_refs):
        dest = place_ref[3] ^ k
        for plane in range(planes):
            for octet in range(octets):
                lane = pl.multiple_of(((plane * tiles + dest) * octets + octet) * LANES, LANES)
                row = (plane * octets + octet) * slots
                out_ref[row : row + slots, :] = held[:, pl.ds(lane, LANES)]
        out_ref[tail:, :] = ids[...].astype(jnp.bfloat16)


def prepare(movie, weights, owner, local, order, place):
    frames, planes, _, width = movie.shape
    slots, pixels = weights.shape
    tiles = len(order)
    rows = pixels // (tiles * LANES) * slots + GROUP
    edge = jax.ShapeDtypeStruct((frames, planes * (OCTET + QUAD), width), jnp.bfloat16)
    packed = jax.ShapeDtypeStruct((rows, LANES), jnp.bfloat16)
    pair, other, *packed = pl.pallas_call(
        functools.partial(prepare_kernel, order),
        out_shape=[edge, edge] + [packed] * tiles,
        in_specs=[pl.BlockSpec(memory_space=pltpu.SMEM)] + [pl.BlockSpec(memory_space=pltpu.HBM)] * 4,
        out_specs=whole_vmem(2 + tiles),
        scratch_shapes=[
            pltpu.VMEM((frames, planes, HALO, width), jnp.bfloat16),
            pltpu.VMEM((frames, planes, HALO, width), jnp.bfloat16),
            pltpu.VMEM((slots, pixels), jnp.bfloat16),
            pltpu.VMEM((2, 1, slots), jnp.int32),
            pltpu.VMEM((GROUP, LANES), jnp.float32),
            pltpu.SemaphoreType.DMA((5,)),
        ],
        compiler_params=params(8 * MIB + 4 * movie.size + 5 * weights.size),
        name="prepare",
    )(place, movie, weights, owner, local)
    return pair, other, packed


def smooth_kernel(shift_ref, place_ref, movie_ref, pair_ref, other_ref, *refs):
    *out_refs, band, wide = refs
    frames, planes, rows, width = movie_ref.shape
    blocks = width // LANES
    reach = rows + 2 * HALO
    parts = len(out_refs)
    each = blocks // parts
    taps = gauss_taps()
    high = [float(v) for v in taps.astype(jnp.bfloat16)]
    low = [float(v) for v in taps - taps.astype(jnp.bfloat16).astype(np.float32)]
    lane = lax.broadcasted_iota(jnp.int32, (reach, LANES), 1)
    row = lax.broadcasted_iota(jnp.int32, (reach, LANES), 0)
    first_row, total_rows, me = place_ref[0], place_ref[1], place_ref[2]
    even = place_ref[3] % 2 == 0

    tap = lax.broadcasted_iota(jnp.int32, (2 * LANES, LANES), 0) - lax.broadcasted_iota(jnp.int32, (2 * LANES, LANES), 1)
    tap = tap - (MAXS - RAD)
    for side, values in enumerate((high, low)):
        cells = jnp.zeros((2 * LANES, LANES), jnp.float32)
        for i, value in enumerate(values):
            cells = jnp.where(tap == i, value, cells)
        band[:, side * LANES : (side + 1) * LANES] = cells.astype(jnp.bfloat16)

    def one(frame, carry):
        down = shift_ref[0, frame]
        right = shift_ref[1, frame] + MAXS
        near = lane < right
        zero = jnp.zeros((reach, LANES), jnp.float32)
        place = first_row + row - HALO + down
        inside = (place >= 0) & (place < total_rows)
        start = HALO - RAD - down
        for plane in range(planes):
            moved = []
            for b in range(blocks):
                cells = slice(b * LANES, (b + 1) * LANES)
                pair = pair_ref[frame, :, cells].astype(jnp.float32)
                other = other_ref[frame, :, cells].astype(jnp.float32)
                top = jnp.where(even, other, pair)
                bottom = jnp.where(even, pair, other)
                full = slice(plane * OCTET, (plane + 1) * OCTET)
                rest = slice(planes * OCTET + plane * QUAD, planes * OCTET + (plane + 1) * QUAD)
                piece = jnp.concatenate(
                    [
                        top[rest],
                        top[rest],
                        top[full],
                        movie_ref[frame, plane, :, cells].astype(jnp.float32),
                        bottom[full],
                        bottom[rest],
                        bottom[rest],
                    ],
                    axis=0,
                )
                moved.append(pltpu.roll(piece, right, 1))
            shifted = []
            for b in range(blocks + 1):
                before = moved[b - 1] if b > 0 else zero
                own = moved[b] if b < blocks else zero
                cells = jnp.where(near, before, own)
                if b == 0:
                    cells = jnp.where(lane < MAXS, 0.0, cells)
                if b == blocks:
                    cells = jnp.where(lane < MAXS, cells, 0.0)
                shifted.append(cells.astype(jnp.bfloat16))
            cells = jnp.concatenate(
                [jnp.concatenate(shifted[b : b + 2], axis=1) for b in range(blocks)], axis=0
            )
            result = jnp.dot(cells, band[...], preferred_element_type=jnp.float32)
            result = result[:, :LANES] + result[:, LANES:]
            for b in range(blocks):
                wide[plane, b] = jnp.where(inside, result[b * reach : (b + 1) * reach], 0.0)
        for plane in range(planes):
            for k in range(parts):
                for j in range(each):
                    b = (me ^ k) * each + j
                    total = float(taps[RAD]) * wide[plane, b, pl.ds(start + RAD, rows), :]
                    for i in range(RAD):
                        pair = wide[plane, b, pl.ds(start + i, rows), :]
                        pair = pair + wide[plane, b, pl.ds(start + 2 * RAD - i, rows), :]
                        total = total + float(taps[i]) * pair
                    out_refs[k][frame, plane, :, j * LANES : (j + 1) * LANES] = total.astype(jnp.bfloat16)
        return carry

    lax.fori_loop(0, frames, one, 0)


def smooth(movie, pair, other, shifts, place, parts):
    frames, planes, rows, width = movie.shape
    reach = rows + 2 * HALO
    smem = pl.BlockSpec(memory_space=pltpu.SMEM)
    return pl.pallas_call(
        smooth_kernel,
        out_shape=[jax.ShapeDtypeStruct((frames, planes, rows, width // parts), jnp.bfloat16)] * parts,
        in_specs=[smem, smem] + whole_vmem(3),
        out_specs=whole_vmem(parts),
        scratch_shapes=[
            pltpu.VMEM((2 * LANES, 2 * LANES), jnp.bfloat16),
            pltpu.VMEM((planes, width // LANES, reach, LANES), jnp.float32),
        ],
        compiler_params=params(12 * MIB + 8 * movie.size),
        name="smooth",
    )(shifts, place, movie, pair, other)


def spread_kernel(part_frames, place_ref, kernel_ref, out_ref):
    planes, size, _ = out_ref.shape
    frames = size // GROUP
    me = place_ref[2]
    row = lax.broadcasted_iota(jnp.int32, (size, frames), 0)
    column = lax.broadcasted_iota(jnp.int32, (size, frames), 1)
    tall = (row % frames == column).astype(jnp.bfloat16)
    row = lax.broadcasted_iota(jnp.int32, (frames, size), 0)
    column = lax.broadcasted_iota(jnp.int32, (frames, size), 1) // GROUP
    last = frames // part_frames - 1
    column = ((last - column // part_frames) ^ me) * part_frames + column % part_frames
    flat = (column == row).astype(jnp.bfloat16)
    row = lax.broadcasted_iota(jnp.int32, (size, size), 0)
    column = lax.broadcasted_iota(jnp.int32, (size, size), 1)
    same = row // frames == column % GROUP
    for plane in range(planes):
        left = jnp.dot(tall, kernel_ref[plane], preferred_element_type=jnp.float32).astype(jnp.bfloat16)
        full = jnp.dot(left, flat, preferred_element_type=jnp.float32)
        out_ref[plane] = jnp.where(same, full, 0.0).astype(jnp.bfloat16)


def spread(kernel, place, part_frames):
    planes, frames, _ = kernel.shape
    size = frames * GROUP
    return pl.pallas_call(
        functools.partial(spread_kernel, part_frames),
        out_shape=jax.ShapeDtypeStruct((planes, size, size), jnp.bfloat16),
        in_specs=[pl.BlockSpec(memory_space=pltpu.SMEM)] + whole_vmem(1),
        out_specs=whole_vmem(1)[0],
        compiler_params=params(8 * MIB + 16 * size * size),
        name="spread_filters",
    )(place, kernel)


def swap_lanes(pieces):
    count = len(pieces)
    group = LANES // count
    half = count // 2
    lane = lax.broadcasted_iota(jnp.int32, pieces[0].shape, 1) // group
    while half >= 1:
        low = (lane & half) == 0
        result = list(pieces)
        for i in range(count):
            if i & half:
                continue
            a, b = pieces[i], pieces[i + half]
            if 2 * half == count:
                back = pltpu.roll(b, half * group, 1)
                ahead = pltpu.roll(a, half * group, 1)
            else:
                back = pltpu.roll(b, half * group, 1)
                ahead = pltpu.roll(a, LANES - half * group, 1)
            result[i] = jnp.where(low, a, back)
            result[i + half] = jnp.where(low, ahead, b)
        pieces = result
        half //= 2
    return pieces


def deconvolve_kernel(parts, spread_ref, *refs):
    data_refs, out_ref = refs[:parts], refs[-1]
    part_frames, planes, rows, width = data_refs[0].shape
    size = spread_ref.shape[1]
    frames = size // GROUP
    octets = rows // OCTET
    for q in range(width // LANES):
        lanes = slice(q * LANES, (q + 1) * LANES)
        for plane in range(planes):
            for first in range(0, rows // GROUP, 2):
                cells = []
                for a in (first, first + 1):
                    pieces = [ref[:, plane, a * GROUP : (a + 1) * GROUP, lanes] for ref in data_refs]
                    cells.append(jnp.concatenate(pieces, axis=0).reshape(size, LANES))
                cells = jnp.concatenate(cells, axis=1)
                spikes = jnp.dot(spread_ref[plane], cells, preferred_element_type=jnp.float32)
                spikes = jnp.maximum(spikes, 0.0)
                for a in (0, 1):
                    for half in (0, 1):
                        pieces = [
                            spikes[(half * OCTET + r) * frames : (half * OCTET + r + 1) * frames, a * LANES : (a + 1) * LANES]
                            for r in range(OCTET)
                        ]
                        octet = plane * octets + (first + a) * 2 + half
                        for j, piece in enumerate(swap_lanes(pieces)):
                            out_ref[q, octet, j * frames : (j + 1) * frames, :] = piece.astype(jnp.bfloat16)


def deconvolve(spread_filters, data, after):
    part_frames, planes, rows, width = data[0].shape
    frames = part_frames * len(data)
    shape = (width // LANES, planes * rows // OCTET, OCTET * frames, LANES)
    return pl.pallas_call(
        functools.partial(deconvolve_kernel, len(data)),
        out_shape=jax.ShapeDtypeStruct(shape, jnp.bfloat16),
        in_specs=whole_vmem(1 + len(data)) + [pl.BlockSpec(memory_space=pl.ANY)] * len(after),
        out_specs=whole_vmem(1)[0],
        compiler_params=params(12 * MIB + 4 * (spread_filters.size + 2 * len(data) * data[0].size)),
        name="deconvolve",
    )(spread_filters, *data, *after)


def pool_kernel(order, place_ref, spikes_ref, *refs):
    *weights_refs, out_ref = refs
    blocks, steps, height, _ = spikes_ref.shape
    tiles = len(weights_refs)
    me = place_ref[3]
    near = tiles // blocks
    frames = height // near
    tail = weights_refs[0].shape[0] - GROUP
    slots = tail // steps
    owners, owner_rows, _ = out_ref.shape
    owned = owners * owner_rows
    eye = lax.broadcasted_iota(jnp.int32, (slots, LANES), 0) == lax.broadcasted_iota(jnp.int32, (slots, LANES), 1)
    keys, groups = [], []
    for ref in weights_refs:
        ids = ref[tail : tail + GROUP, :].astype(jnp.float32)
        owner = jnp.sum(jnp.where(eye, ids[0:1, :], 0.0), axis=1, keepdims=True).astype(jnp.int32)
        local = jnp.sum(jnp.where(eye, ids[1:2, :], 0.0), axis=1, keepdims=True).astype(jnp.int32)
        keys.append(owner * owner_rows + local % owner_rows)
        groups.append(local // owner_rows)
    key = jnp.concatenate(keys, axis=0)
    group = jnp.concatenate(groups, axis=0)
    onehot = (lax.broadcasted_iota(jnp.int32, (tiles * slots, owned), 1) == key).astype(jnp.bfloat16)
    total = jnp.zeros((owned, LANES), jnp.float32)
    for q in range(blocks):
        pooled = jnp.zeros((tiles * slots, height), jnp.float32)
        for step in range(0, steps, 2):
            left = jnp.concatenate(
                [
                    jnp.concatenate([ref[at * slots : (at + 1) * slots, :] for ref in weights_refs], axis=0)
                    for at in (step, step + 1)
                ],
                axis=1,
            )
            right = jnp.concatenate([spikes_ref[q, step], spikes_ref[q, step + 1]], axis=1)
            pooled = pooled + lax.dot_general(
                left, right, (((1,), (1,)), ((), ())), preferred_element_type=jnp.float32
            )
        column = lax.broadcasted_iota(jnp.int32, (slots, height), 1) // frames + q * near
        pooled = jnp.concatenate(
            [jnp.where(column == me ^ k, pooled[i * slots : (i + 1) * slots], 0.0) for i, k in enumerate(order)], axis=0
        )
        partial = pooled[:, 0:LANES]
        for at in range(LANES, height, LANES):
            partial = partial + pooled[:, at : at + LANES]
        step = LANES // 2
        while step >= frames:
            partial = partial + pltpu.roll(partial, step, 1)
            step //= 2
        lane_group = lax.broadcasted_iota(jnp.int32, partial.shape, 1) // frames
        partial = jnp.where(lane_group == group, partial, 0.0)
        high = partial.astype(jnp.bfloat16)
        low = (partial - high.astype(jnp.float32)).astype(jnp.bfloat16)
        both = lax.dot_general(
            onehot,
            jnp.concatenate([high, low], axis=1),
            (((0,), (0,)), ((), ())),
            preferred_element_type=jnp.float32,
        )
        total = total + both[:, :LANES] + both[:, LANES:]
    out_ref[...] = total.reshape(owners, owner_rows, LANES)


def pool(spikes, weights, order, place, frames, owners):
    shape = (owners, COMP_DEV * frames // LANES, LANES)
    inputs = [spikes, *weights]
    return pl.pallas_call(
        functools.partial(pool_kernel, order),
        out_shape=jax.ShapeDtypeStruct(shape, jnp.float32),
        in_specs=[pl.BlockSpec(memory_space=pltpu.SMEM)] + whole_vmem(len(inputs)),
        out_specs=whole_vmem(1)[0],
        compiler_params=params(16 * MIB + 4 * sum(cells.size for cells in inputs)),
        name="pool",
    )(place, *inputs)


def finish_kernel(parts_ref, out_ref):
    sources, rows, _ = parts_ref.shape
    frames = out_ref.shape[1]
    total = jnp.sum(parts_ref[...], axis=0)
    for group in range(LANES // frames):
        out_ref[group * rows : (group + 1) * rows, :] = total[:, group * frames : (group + 1) * frames]


def finish(parts, frames):
    return pl.pallas_call(
        finish_kernel,
        out_shape=jax.ShapeDtypeStruct((COMP_DEV, frames), jnp.float32),
        in_specs=whole_vmem(1),
        out_specs=whole_vmem(1)[0],
        compiler_params=params(8 * MIB + 8 * parts.size),
        name="finish",
    )(parts)


def body(movie, shifts, filters, weights, slot_owner, slot_local):
    part_frames, planes, rows, width = movie.shape
    tiles = lax.axis_size("tile")
    parts = lax.axis_size("frame")
    frames = part_frames * parts
    slots = weights.shape[0]
    ends = tiles - 1
    tile = lax.axis_index("tile")
    place = jnp.stack([tile * rows, tiles * rows, lax.axis_index("frame"), tile]).astype(jnp.int32)
    far, close = list(range(tiles // 2, tiles)), list(range(1, tiles // 2))
    order = far[-2:] + close[:2] + far[-3:-2] + far[:-3] + close[2:] + [0]
    owner, local = slot_owner.reshape(1, slots), slot_local.reshape(1, slots)
    pair, other, packed = prepare(movie, weights, owner, local, order, place)
    pair = lax.ppermute(pair, "tile", [(i, i ^ 1) for i in range(tiles)])
    swaps = [(i, i + 1) for i in range(1, ends, 2)]
    other = lax.ppermute(other, "tile", swaps + [(j, i) for i, j in swaps])
    landed = [
        lax.ppermute(cells, "tile", [(i, i ^ k) for i in range(tiles)]) if k else cells
        for k, cells in zip(order, packed)
    ]
    pieces = smooth(movie, pair, other, shifts.T, place, parts)
    pieces = [
        lax.ppermute(pieces[k], "frame", [(i, i ^ k) for i in range(parts)]) for k in range(parts - 1, 0, -1)
    ] + [pieces[0]]
    spikes = deconvolve(spread(build_kernel(filters, frames), place, part_frames), pieces, landed[: len(far)])
    traces = pool(spikes, landed, order, place, frames, parts * tiles)
    traces = lax.all_to_all(traces, ("frame", "tile"), split_axis=0, concat_axis=0, tiled=True)
    return finish(traces, frames)


def solution(mesh):
    in_specs = (
        P("frame", None, "tile", None),
        P("frame", None),
        P(),
        P(("frame", "tile"), None),
        P(("frame", "tile"), None),
        P(("frame", "tile"), None),
    )
    out_specs = P(("frame", "tile"), None)
    return jax.shard_map(body, mesh=mesh, in_specs=in_specs, out_specs=out_specs, check_vma=False)
```

```python
import functools

import jax
import jax.numpy as jnp
import numpy as np
from jax import lax
from jax.experimental import pallas as pl
from jax.experimental.pallas import tpu as pltpu
from jax.sharding import PartitionSpec as P

COMP_DEV = 32
TAPS = 64
MAXS = 8
RAD = 3
LANES = 128
GROUP = 16
HALO = 16
OCTET = 8
QUAD = 4
MIB = 1 << 20


smooth_sigma = 1.0


def gauss_taps():
    positions = np.arange(-RAD, RAD + 1).astype(np.float32)
    values = np.exp(-positions * positions / np.float32(2.0 * smooth_sigma * smooth_sigma))
    return (values / values.sum(dtype=np.float32)).astype(np.float32)


def build_kernel(filters, count):
    later = jnp.arange(count)[:, None]
    earlier = jnp.arange(count)[None, :]
    offsets = later - earlier
    onehot = (offsets[:, :, None] == jnp.arange(TAPS)[None, None, :]).astype(jnp.float32)
    return jnp.sum(onehot[None] * filters[:, None, None, :], axis=-1).astype(jnp.bfloat16)


def whole_vmem(count):
    return [pl.BlockSpec(memory_space=pltpu.VMEM)] * count


def params(limit):
    return pltpu.CompilerParams(vmem_limit_bytes=limit)


def prepare_kernel(order, place_ref, movie_ref, weights_ref, owner_ref, local_ref, *refs):
    pair_ref, other_ref, *out_refs, tails, heads, held, ids_held, ids, sems = refs
    even = place_ref[3] % 2 == 0
    frames, planes, rows, _ = movie_ref.shape
    tiles = len(order)
    slots, pixels = weights_ref.shape
    octets = pixels // (planes * tiles * LANES)
    tail = planes * octets * slots
    copies = [
        pltpu.make_async_copy(movie_ref.at[:, :, pl.ds(rows - HALO, HALO), :], tails, sems.at[0]),
        pltpu.make_async_copy(movie_ref.at[:, :, pl.ds(0, HALO), :], heads, sems.at[1]),
        pltpu.make_async_copy(owner_ref, ids_held.at[0], sems.at[2]),
        pltpu.make_async_copy(local_ref, ids_held.at[1], sems.at[3]),
        pltpu.make_async_copy(weights_ref, held, sems.at[4]),
    ]
    for copy in copies:
        copy.start()
    copies[0].wait()
    copies[1].wait()

    def one(frame, carry):
        last = [tails[frame, plane].astype(jnp.float32) for plane in range(planes)]
        first = [heads[frame, plane].astype(jnp.float32) for plane in range(planes)]
        last = [cells[OCTET:] for cells in last] + [cells[QUAD:OCTET] for cells in last]
        first = [cells[:OCTET] for cells in first] + [cells[OCTET : OCTET + QUAD] for cells in first]
        last = jnp.concatenate(last, axis=0)
        first = jnp.concatenate(first, axis=0)
        pair_ref[frame] = jnp.where(even, last, first).astype(jnp.bfloat16)
        other_ref[frame] = jnp.where(even, first, last).astype(jnp.bfloat16)
        return carry

    lax.fori_loop(0, frames, one, 0)
    for copy in copies[2:]:
        copy.wait()
    ids[...] = jnp.zeros_like(ids)
    ids[0:1, 0:slots] = ids_held[0].astype(jnp.float32)
    ids[1:2, 0:slots] = ids_held[1].astype(jnp.float32)
    for k, out_ref in zip(order, out_refs):
        dest = place_ref[3] ^ k
        for plane in range(planes):
            for octet in range(octets):
                lane = pl.multiple_of(((plane * tiles + dest) * octets + octet) * LANES, LANES)
                row = (plane * octets + octet) * slots
                out_ref[row : row + slots, :] = held[:, pl.ds(lane, LANES)]
        out_ref[tail:, :] = ids[...].astype(jnp.bfloat16)


def prepare(movie, weights, owner, local, order, place):
    frames, planes, _, width = movie.shape
    slots, pixels = weights.shape
    tiles = len(order)
    rows = pixels // (tiles * LANES) * slots + GROUP
    edge = jax.ShapeDtypeStruct((frames, planes * (OCTET + QUAD), width), jnp.bfloat16)
    packed = jax.ShapeDtypeStruct((rows, LANES), jnp.bfloat16)
    pair, other, *packed = pl.pallas_call(
        functools.partial(prepare_kernel, order),
        out_shape=[edge, edge] + [packed] * tiles,
        in_specs=[pl.BlockSpec(memory_space=pltpu.SMEM)] + [pl.BlockSpec(memory_space=pltpu.HBM)] * 4,
        out_specs=whole_vmem(2 + tiles),
        scratch_shapes=[
            pltpu.VMEM((frames, planes, HALO, width), jnp.bfloat16),
            pltpu.VMEM((frames, planes, HALO, width), jnp.bfloat16),
            pltpu.VMEM((slots, pixels), jnp.bfloat16),
            pltpu.VMEM((2, 1, slots), jnp.int32),
            pltpu.VMEM((GROUP, LANES), jnp.float32),
            pltpu.SemaphoreType.DMA((5,)),
        ],
        compiler_params=params(56 * MIB),
        name="prepare",
    )(place, movie, weights, owner, local)
    return pair, other, packed


def smooth_kernel(shift_ref, place_ref, movie_ref, pair_ref, other_ref, *refs):
    *out_refs, band, wide = refs
    frames, planes, rows, width = movie_ref.shape
    blocks = width // LANES
    reach = rows + 2 * HALO
    parts = len(out_refs)
    each = blocks // parts
    taps = gauss_taps()
    high = [float(v) for v in taps.astype(jnp.bfloat16)]
    low = [float(v) for v in taps - taps.astype(jnp.bfloat16).astype(np.float32)]
    lane = lax.broadcasted_iota(jnp.int32, (reach, LANES), 1)
    row = lax.broadcasted_iota(jnp.int32, (reach, LANES), 0)
    first_row, total_rows, me = place_ref[0], place_ref[1], place_ref[2]
    even = place_ref[3] % 2 == 0

    tap = lax.broadcasted_iota(jnp.int32, (2 * LANES, LANES), 0) - lax.broadcasted_iota(jnp.int32, (2 * LANES, LANES), 1)
    tap = tap - (MAXS - RAD)
    for side, values in enumerate((high, low)):
        cells = jnp.zeros((2 * LANES, LANES), jnp.float32)
        for i, value in enumerate(values):
            cells = jnp.where(tap == i, value, cells)
        band[:, side * LANES : (side + 1) * LANES] = cells.astype(jnp.bfloat16)

    def one(frame, carry):
        down = shift_ref[0, frame]
        right = shift_ref[1, frame] + MAXS
        near = lane < right
        zero = jnp.zeros((reach, LANES), jnp.float32)
        place = first_row + row - HALO + down
        inside = (place >= 0) & (place < total_rows)
        start = HALO - RAD - down
        for plane in range(planes):
            moved = []
            for b in range(blocks):
                cells = slice(b * LANES, (b + 1) * LANES)
                pair = pair_ref[frame, :, cells].astype(jnp.float32)
                other = other_ref[frame, :, cells].astype(jnp.float32)
                top = jnp.where(even, other, pair)
                bottom = jnp.where(even, pair, other)
                full = slice(plane * OCTET, (plane + 1) * OCTET)
                rest = slice(planes * OCTET + plane * QUAD, planes * OCTET + (plane + 1) * QUAD)
                piece = jnp.concatenate(
                    [
                        top[rest],
                        top[rest],
                        top[full],
                        movie_ref[frame, plane, :, cells].astype(jnp.float32),
                        bottom[full],
                        bottom[rest],
                        bottom[rest],
                    ],
                    axis=0,
                )
                moved.append(pltpu.roll(piece, right, 1))
            shifted = []
            for b in range(blocks + 1):
                before = moved[b - 1] if b > 0 else zero
                own = moved[b] if b < blocks else zero
                cells = jnp.where(near, before, own)
                if b == 0:
                    cells = jnp.where(lane < MAXS, 0.0, cells)
                if b == blocks:
                    cells = jnp.where(lane < MAXS, cells, 0.0)
                shifted.append(cells.astype(jnp.bfloat16))
            cells = jnp.concatenate(
                [jnp.concatenate(shifted[b : b + 2], axis=1) for b in range(blocks)], axis=0
            )
            result = jnp.dot(cells, band[...], preferred_element_type=jnp.float32)
            result = result[:, :LANES] + result[:, LANES:]
            for b in range(blocks):
                wide[plane, b] = jnp.where(inside, result[b * reach : (b + 1) * reach], 0.0)
        for plane in range(planes):
            for k in range(parts):
                for j in range(each):
                    b = (me ^ k) * each + j
                    total = float(taps[RAD]) * wide[plane, b, pl.ds(start + RAD, rows), :]
                    for i in range(RAD):
                        pair = wide[plane, b, pl.ds(start + i, rows), :]
                        pair = pair + wide[plane, b, pl.ds(start + 2 * RAD - i, rows), :]
                        total = total + float(taps[i]) * pair
                    out_refs[k][frame, plane, :, j * LANES : (j + 1) * LANES] = total.astype(jnp.bfloat16)
        return carry

    lax.fori_loop(0, frames, one, 0)


def smooth(movie, pair, other, shifts, place, parts):
    frames, planes, rows, width = movie.shape
    reach = rows + 2 * HALO
    smem = pl.BlockSpec(memory_space=pltpu.SMEM)
    return pl.pallas_call(
        smooth_kernel,
        out_shape=[jax.ShapeDtypeStruct((frames, planes, rows, width // parts), jnp.bfloat16)] * parts,
        in_specs=[smem, smem] + whole_vmem(3),
        out_specs=whole_vmem(parts),
        scratch_shapes=[
            pltpu.VMEM((2 * LANES, 2 * LANES), jnp.bfloat16),
            pltpu.VMEM((planes, width // LANES, reach, LANES), jnp.float32),
        ],
        compiler_params=params(12 * MIB + 8 * movie.size),
        name="smooth",
    )(shifts, place, movie, pair, other)


def spread_kernel(part_frames, place_ref, kernel_ref, out_ref):
    planes, size, _ = out_ref.shape
    frames = size // GROUP
    me = place_ref[2]
    row = lax.broadcasted_iota(jnp.int32, (size, frames), 0)
    column = lax.broadcasted_iota(jnp.int32, (size, frames), 1)
    tall = (row % frames == column).astype(jnp.bfloat16)
    row = lax.broadcasted_iota(jnp.int32, (frames, size), 0)
    column = lax.broadcasted_iota(jnp.int32, (frames, size), 1) // GROUP
    last = frames // part_frames - 1
    column = ((last - column // part_frames) ^ me) * part_frames + column % part_frames
    flat = (column == row).astype(jnp.bfloat16)
    row = lax.broadcasted_iota(jnp.int32, (size, size), 0)
    column = lax.broadcasted_iota(jnp.int32, (size, size), 1)
    same = row // frames == column % GROUP
    for plane in range(planes):
        left = jnp.dot(tall, kernel_ref[plane], preferred_element_type=jnp.float32).astype(jnp.bfloat16)
        full = jnp.dot(left, flat, preferred_element_type=jnp.float32)
        out_ref[plane] = jnp.where(same, full, 0.0).astype(jnp.bfloat16)


def spread(kernel, place, part_frames):
    planes, frames, _ = kernel.shape
    size = frames * GROUP
    return pl.pallas_call(
        functools.partial(spread_kernel, part_frames),
        out_shape=jax.ShapeDtypeStruct((planes, size, size), jnp.bfloat16),
        in_specs=[pl.BlockSpec(memory_space=pltpu.SMEM)] + whole_vmem(1),
        out_specs=whole_vmem(1)[0],
        compiler_params=params(8 * MIB + 16 * size * size),
        name="spread_filters",
    )(place, kernel)


def swap_lanes(pieces):
    count = len(pieces)
    group = LANES // count
    half = count // 2
    lane = lax.broadcasted_iota(jnp.int32, pieces[0].shape, 1) // group
    while half >= 1:
        low = (lane & half) == 0
        result = list(pieces)
        for i in range(count):
            if i & half:
                continue
            a, b = pieces[i], pieces[i + half]
            if 2 * half == count:
                back = pltpu.roll(b, half * group, 1)
                ahead = pltpu.roll(a, half * group, 1)
            else:
                back = pltpu.roll(b, half * group, 1)
                ahead = pltpu.roll(a, LANES - half * group, 1)
            result[i] = jnp.where(low, a, back)
            result[i + half] = jnp.where(low, ahead, b)
        pieces = result
        half //= 2
    return pieces


def deconvolve_kernel(parts, spread_ref, *refs):
    data_refs, out_ref = refs[:parts], refs[-1]
    part_frames, planes, rows, width = data_refs[0].shape
    size = spread_ref.shape[1]
    frames = size // GROUP
    octets = rows // OCTET
    for q in range(width // LANES):
        lanes = slice(q * LANES, (q + 1) * LANES)
        for plane in range(planes):
            for first in range(0, rows // GROUP, 2):
                cells = []
                for a in (first, first + 1):
                    pieces = [ref[:, plane, a * GROUP : (a + 1) * GROUP, lanes] for ref in data_refs]
                    cells.append(jnp.concatenate(pieces, axis=0).reshape(size, LANES))
                cells = jnp.concatenate(cells, axis=1)
                spikes = jnp.dot(spread_ref[plane], cells, preferred_element_type=jnp.float32)
                spikes = jnp.maximum(spikes, 0.0)
                for a in (0, 1):
                    for half in (0, 1):
                        pieces = [
                            spikes[(half * OCTET + r) * frames : (half * OCTET + r + 1) * frames, a * LANES : (a + 1) * LANES]
                            for r in range(OCTET)
                        ]
                        octet = plane * octets + (first + a) * 2 + half
                        for j, piece in enumerate(swap_lanes(pieces)):
                            out_ref[q, octet, j * frames : (j + 1) * frames, :] = piece.astype(jnp.bfloat16)


def deconvolve(spread_filters, data, after):
    part_frames, planes, rows, width = data[0].shape
    frames = part_frames * len(data)
    shape = (width // LANES, planes * rows // OCTET, OCTET * frames, LANES)
    return pl.pallas_call(
        functools.partial(deconvolve_kernel, len(data)),
        out_shape=jax.ShapeDtypeStruct(shape, jnp.bfloat16),
        in_specs=whole_vmem(1 + len(data)) + [pl.BlockSpec(memory_space=pl.ANY)] * len(after),
        out_specs=whole_vmem(1)[0],
        compiler_params=params(12 * MIB + 4 * (spread_filters.size + 2 * len(data) * data[0].size)),
        name="deconvolve",
    )(spread_filters, *data, *after)


def pool_kernel(order, place_ref, spikes_ref, *refs):
    *weights_refs, out_ref = refs
    blocks, steps, height, _ = spikes_ref.shape
    tiles = len(weights_refs)
    me = place_ref[3]
    near = tiles // blocks
    frames = height // near
    tail = weights_refs[0].shape[0] - GROUP
    slots = tail // steps
    owners, owner_rows, _ = out_ref.shape
    owned = owners * owner_rows
    eye = lax.broadcasted_iota(jnp.int32, (slots, LANES), 0) == lax.broadcasted_iota(jnp.int32, (slots, LANES), 1)
    keys, groups = [], []
    for ref in weights_refs:
        ids = ref[tail : tail + GROUP, :].astype(jnp.float32)
        owner = jnp.sum(jnp.where(eye, ids[0:1, :], 0.0), axis=1, keepdims=True).astype(jnp.int32)
        local = jnp.sum(jnp.where(eye, ids[1:2, :], 0.0), axis=1, keepdims=True).astype(jnp.int32)
        keys.append(owner * owner_rows + local % owner_rows)
        groups.append(local // owner_rows)
    key = jnp.concatenate(keys, axis=0)
    group = jnp.concatenate(groups, axis=0)
    onehot = (lax.broadcasted_iota(jnp.int32, (tiles * slots, owned), 1) == key).astype(jnp.bfloat16)
    total = jnp.zeros((owned, LANES), jnp.float32)
    for q in range(blocks):
        pooled = jnp.zeros((tiles * slots, height), jnp.float32)
        for step in range(0, steps, 2):
            left = jnp.concatenate(
                [
                    jnp.concatenate([ref[at * slots : (at + 1) * slots, :] for ref in weights_refs], axis=0)
                    for at in (step, step + 1)
                ],
                axis=1,
            )
            right = jnp.concatenate([spikes_ref[q, step], spikes_ref[q, step + 1]], axis=1)
            pooled = pooled + lax.dot_general(
                left, right, (((1,), (1,)), ((), ())), preferred_element_type=jnp.float32
            )
        column = lax.broadcasted_iota(jnp.int32, (slots, height), 1) // frames + q * near
        pooled = jnp.concatenate(
            [jnp.where(column == me ^ k, pooled[i * slots : (i + 1) * slots], 0.0) for i, k in enumerate(order)], axis=0
        )
        partial = pooled[:, 0:LANES]
        for at in range(LANES, height, LANES):
            partial = partial + pooled[:, at : at + LANES]
        step = LANES // 2
        while step >= frames:
            partial = partial + pltpu.roll(partial, step, 1)
            step //= 2
        lane_group = lax.broadcasted_iota(jnp.int32, partial.shape, 1) // frames
        partial = jnp.where(lane_group == group, partial, 0.0)
        high = partial.astype(jnp.bfloat16)
        low = (partial - high.astype(jnp.float32)).astype(jnp.bfloat16)
        both = lax.dot_general(
            onehot,
            jnp.concatenate([high, low], axis=1),
            (((0,), (0,)), ((), ())),
            preferred_element_type=jnp.float32,
        )
        total = total + both[:, :LANES] + both[:, LANES:]
    out_ref[...] = total.reshape(owners, owner_rows, LANES)


def pool(spikes, weights, order, place, frames, owners):
    shape = (owners, COMP_DEV * frames // LANES, LANES)
    inputs = [spikes, *weights]
    return pl.pallas_call(
        functools.partial(pool_kernel, order),
        out_shape=jax.ShapeDtypeStruct(shape, jnp.float32),
        in_specs=[pl.BlockSpec(memory_space=pltpu.SMEM)] + whole_vmem(len(inputs)),
        out_specs=whole_vmem(1)[0],
        compiler_params=params(16 * MIB + 4 * sum(cells.size for cells in inputs)),
        name="pool",
    )(place, *inputs)


def finish_kernel(parts_ref, out_ref):
    sources, rows, _ = parts_ref.shape
    frames = out_ref.shape[1]
    total = jnp.sum(parts_ref[...], axis=0)
    for group in range(LANES // frames):
        out_ref[group * rows : (group + 1) * rows, :] = total[:, group * frames : (group + 1) * frames]


def finish(parts, frames):
    return pl.pallas_call(
        finish_kernel,
        out_shape=jax.ShapeDtypeStruct((COMP_DEV, frames), jnp.float32),
        in_specs=whole_vmem(1),
        out_specs=whole_vmem(1)[0],
        compiler_params=params(8 * MIB + 8 * parts.size),
        name="finish",
    )(parts)


def body(movie, shifts, filters, weights, slot_owner, slot_local):
    part_frames, planes, rows, width = movie.shape
    tiles = lax.axis_size("tile")
    parts = lax.axis_size("frame")
    frames = part_frames * parts
    slots = weights.shape[0]
    ends = tiles - 1
    tile = lax.axis_index("tile")
    place = jnp.stack([tile * rows, tiles * rows, lax.axis_index("frame"), tile]).astype(jnp.int32)
    far, close = list(range(tiles // 2, tiles)), list(range(1, tiles // 2))
    order = far[-2:] + far[-3::-1] + close + [0]
    owner, local = slot_owner.reshape(1, slots), slot_local.reshape(1, slots)
    pair, other, packed = prepare(movie, weights, owner, local, order, place)
    pair = lax.ppermute(pair, "tile", [(i, i ^ 1) for i in range(tiles)])
    swaps = [(i, i + 1) for i in range(1, ends, 2)]
    other = lax.ppermute(other, "tile", swaps + [(j, i) for i, j in swaps])
    landed = [
        lax.ppermute(cells, "tile", [(i, i ^ k) for i in range(tiles)]) if k else cells
        for k, cells in zip(order, packed)
    ]
    pieces = smooth(movie, pair, other, shifts.T, place, parts)
    pieces = [
        lax.ppermute(pieces[k], "frame", [(i, i ^ k) for i in range(parts)]) for k in range(parts - 1, 0, -1)
    ] + [pieces[0]]
    spikes = deconvolve(spread(build_kernel(filters, frames), place, part_frames), pieces, landed[: len(far)])
    traces = pool(spikes, landed, order, place, frames, parts * tiles)
    traces = lax.all_to_all(traces, ("frame", "tile"), split_axis=0, concat_axis=0, tiled=True)
    return finish(traces, frames)


def solution(mesh):
    in_specs = (
        P("frame", None, "tile", None),
        P("frame", None),
        P(),
        P(("frame", "tile"), None),
        P(("frame", "tile"), None),
        P(("frame", "tile"), None),
    )
    out_specs = P(("frame", "tile"), None)
    return jax.shard_map(body, mesh=mesh, in_specs=in_specs, out_specs=out_specs, check_vma=False)
```

```python
import functools

import jax
import jax.numpy as jnp
import numpy as np
from jax import lax
from jax.experimental import pallas as pl
from jax.experimental.pallas import tpu as pltpu
from jax.sharding import PartitionSpec as P

COMP_DEV = 32
TAPS = 64
MAXS = 8
RAD = 3
LANES = 128
GROUP = 16
HALO = 16
OCTET = 8
QUAD = 4
MIB = 1 << 20


smooth_sigma = 1.0


def gauss_taps():
    positions = np.arange(-RAD, RAD + 1).astype(np.float32)
    values = np.exp(-positions * positions / np.float32(2.0 * smooth_sigma * smooth_sigma))
    return (values / values.sum(dtype=np.float32)).astype(np.float32)


def build_kernel(filters, count):
    later = jnp.arange(count)[:, None]
    earlier = jnp.arange(count)[None, :]
    offsets = later - earlier
    onehot = (offsets[:, :, None] == jnp.arange(TAPS)[None, None, :]).astype(jnp.float32)
    return jnp.sum(onehot[None] * filters[:, None, None, :], axis=-1).astype(jnp.bfloat16)


def whole_vmem(count):
    return [pl.BlockSpec(memory_space=pltpu.VMEM)] * count


def params(limit):
    return pltpu.CompilerParams(vmem_limit_bytes=limit)


def edges_kernel(place_ref, movie_ref, pair_ref, other_ref):
    frames, planes, rows, _ = movie_ref.shape
    even = place_ref[3] % 2 == 0

    def one(frame, carry):
        last = [movie_ref[frame, plane, rows - HALO :, :].astype(jnp.float32) for plane in range(planes)]
        first = [movie_ref[frame, plane, :HALO, :].astype(jnp.float32) for plane in range(planes)]
        last = [cells[OCTET:] for cells in last] + [cells[QUAD:OCTET] for cells in last]
        first = [cells[:OCTET] for cells in first] + [cells[OCTET : OCTET + QUAD] for cells in first]
        last = jnp.concatenate(last, axis=0)
        first = jnp.concatenate(first, axis=0)
        pair_ref[frame] = jnp.where(even, last, first).astype(jnp.bfloat16)
        other_ref[frame] = jnp.where(even, first, last).astype(jnp.bfloat16)
        return carry

    lax.fori_loop(0, frames, one, 0)


def edges(movie, place):
    frames, planes, _, width = movie.shape
    shape = jax.ShapeDtypeStruct((frames, planes * (OCTET + QUAD), width), jnp.bfloat16)
    return pl.pallas_call(
        edges_kernel,
        out_shape=[shape, shape],
        in_specs=[pl.BlockSpec(memory_space=pltpu.SMEM)] + whole_vmem(1),
        out_specs=whole_vmem(2),
        compiler_params=params(40 * MIB),
        name="edges",
    )(place, movie)


def pack_kernel(order, planes, place_ref, weights_ref, owner_ref, local_ref, *refs):
    *out_refs, ids = refs
    tiles = len(order)
    slots, pixels = weights_ref.shape
    octets = pixels // (planes * tiles * LANES)
    tail = planes * octets * slots
    ids[...] = jnp.zeros_like(ids)
    ids[0:1, 0:slots] = owner_ref[...].astype(jnp.float32)
    ids[1:2, 0:slots] = local_ref[...].astype(jnp.float32)
    for k, out_ref in zip(order, out_refs):
        dest = place_ref[3] ^ k
        for plane in range(planes):
            for octet in range(octets):
                lane = pl.multiple_of(((plane * tiles + dest) * octets + octet) * LANES, LANES)
                row = (plane * octets + octet) * slots
                out_ref[row : row + slots, :] = weights_ref[:, pl.ds(lane, LANES)]
        out_ref[tail:, :] = ids[...].astype(jnp.bfloat16)


def pack(weights, owner, local, order, planes, place):
    slots, pixels = weights.shape
    tiles = len(order)
    shape = jax.ShapeDtypeStruct((pixels // (tiles * LANES) * slots + GROUP, LANES), jnp.bfloat16)
    return pl.pallas_call(
        functools.partial(pack_kernel, order, planes),
        out_shape=[shape] * tiles,
        in_specs=[pl.BlockSpec(memory_space=pltpu.SMEM)] + whole_vmem(3),
        out_specs=whole_vmem(tiles),
        scratch_shapes=[pltpu.VMEM((GROUP, LANES), jnp.float32)],
        compiler_params=params(8 * MIB + 5 * weights.size),
        name="pack_weights",
    )(place, weights, owner, local)


def smooth_kernel(shift_ref, place_ref, movie_ref, pair_ref, other_ref, *refs):
    *out_refs, band, wide = refs
    frames, planes, rows, width = movie_ref.shape
    blocks = width // LANES
    reach = rows + 2 * HALO
    parts = len(out_refs)
    each = blocks // parts
    taps = gauss_taps()
    high = [float(v) for v in taps.astype(jnp.bfloat16)]
    low = [float(v) for v in taps - taps.astype(jnp.bfloat16).astype(np.float32)]
    lane = lax.broadcasted_iota(jnp.int32, (reach, LANES), 1)
    row = lax.broadcasted_iota(jnp.int32, (reach, LANES), 0)
    first_row, total_rows, me = place_ref[0], place_ref[1], place_ref[2]
    even = place_ref[3] % 2 == 0

    tap = lax.broadcasted_iota(jnp.int32, (2 * LANES, LANES), 0) - lax.broadcasted_iota(jnp.int32, (2 * LANES, LANES), 1)
    tap = tap - (MAXS - RAD)
    for side, values in enumerate((high, low)):
        cells = jnp.zeros((2 * LANES, LANES), jnp.float32)
        for i, value in enumerate(values):
            cells = jnp.where(tap == i, value, cells)
        band[:, side * LANES : (side + 1) * LANES] = cells.astype(jnp.bfloat16)

    def one(frame, carry):
        down = shift_ref[0, frame]
        right = shift_ref[1, frame] + MAXS
        near = lane < right
        zero = jnp.zeros((reach, LANES), jnp.float32)
        place = first_row + row - HALO + down
        inside = (place >= 0) & (place < total_rows)
        start = HALO - RAD - down
        for plane in range(planes):
            moved = []
            for b in range(blocks):
                cells = slice(b * LANES, (b + 1) * LANES)
                pair = pair_ref[frame, :, cells].astype(jnp.float32)
                other = other_ref[frame, :, cells].astype(jnp.float32)
                top = jnp.where(even, other, pair)
                bottom = jnp.where(even, pair, other)
                full = slice(plane * OCTET, (plane + 1) * OCTET)
                rest = slice(planes * OCTET + plane * QUAD, planes * OCTET + (plane + 1) * QUAD)
                piece = jnp.concatenate(
                    [
                        top[rest],
                        top[rest],
                        top[full],
                        movie_ref[frame, plane, :, cells].astype(jnp.float32),
                        bottom[full],
                        bottom[rest],
                        bottom[rest],
                    ],
                    axis=0,
                )
                moved.append(pltpu.roll(piece, right, 1))
            shifted = []
            for b in range(blocks + 1):
                before = moved[b - 1] if b > 0 else zero
                own = moved[b] if b < blocks else zero
                cells = jnp.where(near, before, own)
                if b == 0:
                    cells = jnp.where(lane < MAXS, 0.0, cells)
                if b == blocks:
                    cells = jnp.where(lane < MAXS, cells, 0.0)
                shifted.append(cells.astype(jnp.bfloat16))
            cells = jnp.concatenate(
                [jnp.concatenate(shifted[b : b + 2], axis=1) for b in range(blocks)], axis=0
            )
            result = jnp.dot(cells, band[...], preferred_element_type=jnp.float32)
            result = result[:, :LANES] + result[:, LANES:]
            for b in range(blocks):
                wide[plane, b] = jnp.where(inside, result[b * reach : (b + 1) * reach], 0.0)
        for plane in range(planes):
            for k in range(parts):
                for j in range(each):
                    b = (me ^ k) * each + j
                    total = float(taps[RAD]) * wide[plane, b, pl.ds(start + RAD, rows), :]
                    for i in range(RAD):
                        pair = wide[plane, b, pl.ds(start + i, rows), :]
                        pair = pair + wide[plane, b, pl.ds(start + 2 * RAD - i, rows), :]
                        total = total + float(taps[i]) * pair
                    out_refs[k][frame, plane, :, j * LANES : (j + 1) * LANES] = total.astype(jnp.bfloat16)
        return carry

    lax.fori_loop(0, frames, one, 0)


def smooth(movie, pair, other, shifts, place, parts):
    frames, planes, rows, width = movie.shape
    reach = rows + 2 * HALO
    smem = pl.BlockSpec(memory_space=pltpu.SMEM)
    return pl.pallas_call(
        smooth_kernel,
        out_shape=[jax.ShapeDtypeStruct((frames, planes, rows, width // parts), jnp.bfloat16)] * parts,
        in_specs=[smem, smem] + whole_vmem(3),
        out_specs=whole_vmem(parts),
        scratch_shapes=[
            pltpu.VMEM((2 * LANES, 2 * LANES), jnp.bfloat16),
            pltpu.VMEM((planes, width // LANES, reach, LANES), jnp.float32),
        ],
        compiler_params=params(12 * MIB + 8 * movie.size),
        name="smooth",
    )(shifts, place, movie, pair, other)


def spread_kernel(part_frames, place_ref, kernel_ref, out_ref):
    planes, size, _ = out_ref.shape
    frames = size // GROUP
    me = place_ref[2]
    row = lax.broadcasted_iota(jnp.int32, (size, frames), 0)
    column = lax.broadcasted_iota(jnp.int32, (size, frames), 1)
    tall = (row % frames == column).astype(jnp.bfloat16)
    row = lax.broadcasted_iota(jnp.int32, (frames, size), 0)
    column = lax.broadcasted_iota(jnp.int32, (frames, size), 1) // GROUP
    last = frames // part_frames - 1
    column = ((last - column // part_frames) ^ me) * part_frames + column % part_frames
    flat = (column == row).astype(jnp.bfloat16)
    row = lax.broadcasted_iota(jnp.int32, (size, size), 0)
    column = lax.broadcasted_iota(jnp.int32, (size, size), 1)
    same = row // frames == column % GROUP
    for plane in range(planes):
        left = jnp.dot(tall, kernel_ref[plane], preferred_element_type=jnp.float32).astype(jnp.bfloat16)
        full = jnp.dot(left, flat, preferred_element_type=jnp.float32)
        out_ref[plane] = jnp.where(same, full, 0.0).astype(jnp.bfloat16)


def spread(kernel, place, part_frames):
    planes, frames, _ = kernel.shape
    size = frames * GROUP
    return pl.pallas_call(
        functools.partial(spread_kernel, part_frames),
        out_shape=jax.ShapeDtypeStruct((planes, size, size), jnp.bfloat16),
        in_specs=[pl.BlockSpec(memory_space=pltpu.SMEM)] + whole_vmem(1),
        out_specs=whole_vmem(1)[0],
        compiler_params=params(8 * MIB + 16 * size * size),
        name="spread_filters",
    )(place, kernel)


def swap_lanes(pieces):
    count = len(pieces)
    group = LANES // count
    half = count // 2
    lane = lax.broadcasted_iota(jnp.int32, pieces[0].shape, 1) // group
    while half >= 1:
        low = (lane & half) == 0
        result = list(pieces)
        for i in range(count):
            if i & half:
                continue
            a, b = pieces[i], pieces[i + half]
            if 2 * half == count:
                back = pltpu.roll(b, half * group, 1)
                ahead = pltpu.roll(a, half * group, 1)
            else:
                back = pltpu.roll(b, half * group, 1)
                ahead = pltpu.roll(a, LANES - half * group, 1)
            result[i] = jnp.where(low, a, back)
            result[i + half] = jnp.where(low, ahead, b)
        pieces = result
        half //= 2
    return pieces


def deconvolve_kernel(parts, spread_ref, *refs):
    data_refs, out_ref = refs[:parts], refs[-1]
    part_frames, planes, rows, width = data_refs[0].shape
    size = spread_ref.shape[1]
    frames = size // GROUP
    octets = rows // OCTET
    for q in range(width // LANES):
        lanes = slice(q * LANES, (q + 1) * LANES)
        for plane in range(planes):
            for first in range(0, rows // GROUP, 2):
                cells = []
                for a in (first, first + 1):
                    pieces = [ref[:, plane, a * GROUP : (a + 1) * GROUP, lanes] for ref in data_refs]
                    cells.append(jnp.concatenate(pieces, axis=0).reshape(size, LANES))
                cells = jnp.concatenate(cells, axis=1)
                spikes = jnp.dot(spread_ref[plane], cells, preferred_element_type=jnp.float32)
                spikes = jnp.maximum(spikes, 0.0)
                for a in (0, 1):
                    for half in (0, 1):
                        pieces = [
                            spikes[(half * OCTET + r) * frames : (half * OCTET + r + 1) * frames, a * LANES : (a + 1) * LANES]
                            for r in range(OCTET)
                        ]
                        octet = plane * octets + (first + a) * 2 + half
                        for j, piece in enumerate(swap_lanes(pieces)):
                            out_ref[q, octet, j * frames : (j + 1) * frames, :] = piece.astype(jnp.bfloat16)


def deconvolve(spread_filters, data, after):
    part_frames, planes, rows, width = data[0].shape
    frames = part_frames * len(data)
    shape = (width // LANES, planes * rows // OCTET, OCTET * frames, LANES)
    return pl.pallas_call(
        functools.partial(deconvolve_kernel, len(data)),
        out_shape=jax.ShapeDtypeStruct(shape, jnp.bfloat16),
        in_specs=whole_vmem(1 + len(data)) + [pl.BlockSpec(memory_space=pl.ANY)] * len(after),
        out_specs=whole_vmem(1)[0],
        compiler_params=params(12 * MIB + 4 * (spread_filters.size + 2 * len(data) * data[0].size)),
        name="deconvolve",
    )(spread_filters, *data, *after)


def pool_kernel(order, place_ref, spikes_ref, *refs):
    *weights_refs, out_ref = refs
    blocks, steps, height, _ = spikes_ref.shape
    tiles = len(weights_refs)
    me = place_ref[3]
    near = tiles // blocks
    frames = height // near
    tail = weights_refs[0].shape[0] - GROUP
    slots = tail // steps
    owners, owner_rows, _ = out_ref.shape
    owned = owners * owner_rows
    eye = lax.broadcasted_iota(jnp.int32, (slots, LANES), 0) == lax.broadcasted_iota(jnp.int32, (slots, LANES), 1)
    keys, groups = [], []
    for ref in weights_refs:
        ids = ref[tail : tail + GROUP, :].astype(jnp.float32)
        owner = jnp.sum(jnp.where(eye, ids[0:1, :], 0.0), axis=1, keepdims=True).astype(jnp.int32)
        local = jnp.sum(jnp.where(eye, ids[1:2, :], 0.0), axis=1, keepdims=True).astype(jnp.int32)
        keys.append(owner * owner_rows + local % owner_rows)
        groups.append(local // owner_rows)
    key = jnp.concatenate(keys, axis=0)
    group = jnp.concatenate(groups, axis=0)
    onehot = (lax.broadcasted_iota(jnp.int32, (tiles * slots, owned), 1) == key).astype(jnp.bfloat16)
    total = jnp.zeros((owned, LANES), jnp.float32)
    for q in range(blocks):
        pooled = jnp.zeros((tiles * slots, height), jnp.float32)
        for step in range(0, steps, 2):
            left = jnp.concatenate(
                [
                    jnp.concatenate([ref[at * slots : (at + 1) * slots, :] for ref in weights_refs], axis=0)
                    for at in (step, step + 1)
                ],
                axis=1,
            )
            right = jnp.concatenate([spikes_ref[q, step], spikes_ref[q, step + 1]], axis=1)
            pooled = pooled + lax.dot_general(
                left, right, (((1,), (1,)), ((), ())), preferred_element_type=jnp.float32
            )
        column = lax.broadcasted_iota(jnp.int32, (slots, height), 1) // frames + q * near
        pooled = jnp.concatenate(
            [jnp.where(column == me ^ k, pooled[i * slots : (i + 1) * slots], 0.0) for i, k in enumerate(order)], axis=0
        )
        partial = pooled[:, 0:LANES]
        for at in range(LANES, height, LANES):
            partial = partial + pooled[:, at : at + LANES]
        step = LANES // 2
        while step >= frames:
            partial = partial + pltpu.roll(partial, step, 1)
            step //= 2
        lane_group = lax.broadcasted_iota(jnp.int32, partial.shape, 1) // frames
        partial = jnp.where(lane_group == group, partial, 0.0)
        high = partial.astype(jnp.bfloat16)
        low = (partial - high.astype(jnp.float32)).astype(jnp.bfloat16)
        both = lax.dot_general(
            onehot,
            jnp.concatenate([high, low], axis=1),
            (((0,), (0,)), ((), ())),
            preferred_element_type=jnp.float32,
        )
        total = total + both[:, :LANES] + both[:, LANES:]
    out_ref[...] = total.reshape(owners, owner_rows, LANES)


def pool(spikes, weights, order, place, frames, owners):
    shape = (owners, COMP_DEV * frames // LANES, LANES)
    inputs = [spikes, *weights]
    return pl.pallas_call(
        functools.partial(pool_kernel, order),
        out_shape=jax.ShapeDtypeStruct(shape, jnp.float32),
        in_specs=[pl.BlockSpec(memory_space=pltpu.SMEM)] + whole_vmem(len(inputs)),
        out_specs=whole_vmem(1)[0],
        compiler_params=params(16 * MIB + 4 * sum(cells.size for cells in inputs)),
        name="pool",
    )(place, *inputs)


def finish_kernel(parts_ref, out_ref):
    sources, rows, _ = parts_ref.shape
    frames = out_ref.shape[1]
    total = jnp.sum(parts_ref[...], axis=0)
    for group in range(LANES // frames):
        out_ref[group * rows : (group + 1) * rows, :] = total[:, group * frames : (group + 1) * frames]


def finish(parts, frames):
    return pl.pallas_call(
        finish_kernel,
        out_shape=jax.ShapeDtypeStruct((COMP_DEV, frames), jnp.float32),
        in_specs=whole_vmem(1),
        out_specs=whole_vmem(1)[0],
        compiler_params=params(8 * MIB + 8 * parts.size),
        name="finish",
    )(parts)


def body(movie, shifts, filters, weights, slot_owner, slot_local):
    part_frames, planes, rows, width = movie.shape
    tiles = lax.axis_size("tile")
    parts = lax.axis_size("frame")
    frames = part_frames * parts
    slots = weights.shape[0]
    ends = tiles - 1
    tile = lax.axis_index("tile")
    place = jnp.stack([tile * rows, tiles * rows, lax.axis_index("frame"), tile]).astype(jnp.int32)
    far, close = list(range(tiles // 2, tiles)), list(range(1, tiles // 2))
    order = far[-2:] + close[:1] + far[-3:-2] + close[1:2] + far[:-3] + close[2:] + [0]
    owner, local = slot_owner.reshape(1, slots), slot_local.reshape(1, slots)
    pair, other = edges(movie, place)
    packed = pack(weights, owner, local, order, planes, place)
    pair = lax.ppermute(pair, "tile", [(i, i ^ 1) for i in range(tiles)])
    swaps = [(i, i + 1) for i in range(1, ends, 2)]
    other = lax.ppermute(other, "tile", swaps + [(j, i) for i, j in swaps])
    landed = [
        lax.ppermute(cells, "tile", [(i, i ^ k) for i in range(tiles)]) if k else cells
        for k, cells in zip(order, packed)
    ]
    pieces = smooth(movie, pair, other, shifts.T, place, parts)
    pieces = [
        lax.ppermute(pieces[k], "frame", [(i, i ^ k) for i in range(parts)]) for k in range(parts - 1, 0, -1)
    ] + [pieces[0]]
    spikes = deconvolve(spread(build_kernel(filters, frames), place, part_frames), pieces, landed[: len(far) + 1])
    traces = pool(spikes, landed, order, place, frames, parts * tiles)
    traces = lax.all_to_all(traces, ("frame", "tile"), split_axis=0, concat_axis=0, tiled=True)
    return finish(traces, frames)


def solution(mesh):
    in_specs = (
        P("frame", None, "tile", None),
        P("frame", None),
        P(),
        P(("frame", "tile"), None),
        P(("frame", "tile"), None),
        P(("frame", "tile"), None),
    )
    out_specs = P(("frame", "tile"), None)
    return jax.shard_map(body, mesh=mesh, in_specs=in_specs, out_specs=out_specs, check_vma=False)
```

```python
import functools

import jax
import jax.numpy as jnp
import numpy as np
from jax import lax
from jax.experimental import pallas as pl
from jax.experimental.pallas import tpu as pltpu
from jax.sharding import PartitionSpec as P

COMP_DEV = 32
TAPS = 64
MAXS = 8
RAD = 3
LANES = 128
GROUP = 16
HALO = 16
OCTET = 8
QUAD = 4
MIB = 1 << 20


smooth_sigma = 1.0


def gauss_taps():
    positions = np.arange(-RAD, RAD + 1).astype(np.float32)
    values = np.exp(-positions * positions / np.float32(2.0 * smooth_sigma * smooth_sigma))
    return (values / values.sum(dtype=np.float32)).astype(np.float32)


def build_kernel(filters, count):
    later = jnp.arange(count)[:, None]
    earlier = jnp.arange(count)[None, :]
    offsets = later - earlier
    onehot = (offsets[:, :, None] == jnp.arange(TAPS)[None, None, :]).astype(jnp.float32)
    return jnp.sum(onehot[None] * filters[:, None, None, :], axis=-1).astype(jnp.bfloat16)


def whole_vmem(count):
    return [pl.BlockSpec(memory_space=pltpu.VMEM)] * count


def params(limit):
    return pltpu.CompilerParams(vmem_limit_bytes=limit)


def edges_kernel(place_ref, movie_ref, pair_ref, other_ref):
    frames, planes, rows, _ = movie_ref.shape
    even = place_ref[3] % 2 == 0

    def one(frame, carry):
        last = [movie_ref[frame, plane, rows - HALO :, :].astype(jnp.float32) for plane in range(planes)]
        first = [movie_ref[frame, plane, :HALO, :].astype(jnp.float32) for plane in range(planes)]
        last = [cells[OCTET:] for cells in last] + [cells[QUAD:OCTET] for cells in last]
        first = [cells[:OCTET] for cells in first] + [cells[OCTET : OCTET + QUAD] for cells in first]
        last = jnp.concatenate(last, axis=0)
        first = jnp.concatenate(first, axis=0)
        pair_ref[frame] = jnp.where(even, last, first).astype(jnp.bfloat16)
        other_ref[frame] = jnp.where(even, first, last).astype(jnp.bfloat16)
        return carry

    lax.fori_loop(0, frames, one, 0)


def edges(movie, place):
    frames, planes, _, width = movie.shape
    shape = jax.ShapeDtypeStruct((frames, planes * (OCTET + QUAD), width), jnp.bfloat16)
    return pl.pallas_call(
        edges_kernel,
        out_shape=[shape, shape],
        in_specs=[pl.BlockSpec(memory_space=pltpu.SMEM)] + whole_vmem(1),
        out_specs=whole_vmem(2),
        compiler_params=params(40 * MIB),
        name="edges",
    )(place, movie)


def pack_kernel(order, planes, place_ref, weights_ref, owner_ref, local_ref, *refs):
    *out_refs, ids = refs
    tiles = len(order)
    slots, pixels = weights_ref.shape
    octets = pixels // (planes * tiles * LANES)
    tail = planes * octets * slots
    ids[...] = jnp.zeros_like(ids)
    ids[0:1, 0:slots] = owner_ref[...].astype(jnp.float32)
    ids[1:2, 0:slots] = local_ref[...].astype(jnp.float32)
    for k, out_ref in zip(order, out_refs):
        dest = place_ref[3] ^ k
        for plane in range(planes):
            for octet in range(octets):
                lane = pl.multiple_of(((plane * tiles + dest) * octets + octet) * LANES, LANES)
                row = (plane * octets + octet) * slots
                out_ref[row : row + slots, :] = weights_ref[:, pl.ds(lane, LANES)]
        out_ref[tail:, :] = ids[...].astype(jnp.bfloat16)


def pack(weights, owner, local, order, planes, place):
    slots, pixels = weights.shape
    tiles = len(order)
    shape = jax.ShapeDtypeStruct((pixels // (tiles * LANES) * slots + GROUP, LANES), jnp.bfloat16)
    return pl.pallas_call(
        functools.partial(pack_kernel, order, planes),
        out_shape=[shape] * tiles,
        in_specs=[pl.BlockSpec(memory_space=pltpu.SMEM)] + whole_vmem(3),
        out_specs=whole_vmem(tiles),
        scratch_shapes=[pltpu.VMEM((GROUP, LANES), jnp.float32)],
        compiler_params=params(8 * MIB + 5 * weights.size),
        name="pack_weights",
    )(place, weights, owner, local)


def smooth_kernel(shift_ref, place_ref, movie_ref, pair_ref, other_ref, *refs):
    *out_refs, band, wide = refs
    frames, planes, rows, width = movie_ref.shape
    blocks = width // LANES
    reach = rows + 2 * HALO
    parts = len(out_refs)
    each = blocks // parts
    taps = gauss_taps()
    high = [float(v) for v in taps.astype(jnp.bfloat16)]
    low = [float(v) for v in taps - taps.astype(jnp.bfloat16).astype(np.float32)]
    lane = lax.broadcasted_iota(jnp.int32, (reach, LANES), 1)
    row = lax.broadcasted_iota(jnp.int32, (reach, LANES), 0)
    first_row, total_rows, me = place_ref[0], place_ref[1], place_ref[2]
    even = place_ref[3] % 2 == 0

    tap = lax.broadcasted_iota(jnp.int32, (2 * LANES, LANES), 0) - lax.broadcasted_iota(jnp.int32, (2 * LANES, LANES), 1)
    tap = tap - (MAXS - RAD)
    for side, values in enumerate((high, low)):
        cells = jnp.zeros((2 * LANES, LANES), jnp.float32)
        for i, value in enumerate(values):
            cells = jnp.where(tap == i, value, cells)
        band[:, side * LANES : (side + 1) * LANES] = cells.astype(jnp.bfloat16)

    def one(frame, carry):
        down = shift_ref[0, frame]
        right = shift_ref[1, frame] + MAXS
        near = lane < right
        zero = jnp.zeros((reach, LANES), jnp.float32)
        place = first_row + row - HALO + down
        inside = (place >= 0) & (place < total_rows)
        start = HALO - RAD - down
        for plane in range(planes):
            moved = []
            for b in range(blocks):
                cells = slice(b * LANES, (b + 1) * LANES)
                pair = pair_ref[frame, :, cells].astype(jnp.float32)
                other = other_ref[frame, :, cells].astype(jnp.float32)
                top = jnp.where(even, other, pair)
                bottom = jnp.where(even, pair, other)
                full = slice(plane * OCTET, (plane + 1) * OCTET)
                rest = slice(planes * OCTET + plane * QUAD, planes * OCTET + (plane + 1) * QUAD)
                piece = jnp.concatenate(
                    [
                        top[rest],
                        top[rest],
                        top[full],
                        movie_ref[frame, plane, :, cells].astype(jnp.float32),
                        bottom[full],
                        bottom[rest],
                        bottom[rest],
                    ],
                    axis=0,
                )
                moved.append(pltpu.roll(piece, right, 1))
            shifted = []
            for b in range(blocks + 1):
                before = moved[b - 1] if b > 0 else zero
                own = moved[b] if b < blocks else zero
                cells = jnp.where(near, before, own)
                if b == 0:
                    cells = jnp.where(lane < MAXS, 0.0, cells)
                if b == blocks:
                    cells = jnp.where(lane < MAXS, cells, 0.0)
                shifted.append(cells.astype(jnp.bfloat16))
            cells = jnp.concatenate(
                [jnp.concatenate(shifted[b : b + 2], axis=1) for b in range(blocks)], axis=0
            )
            result = jnp.dot(cells, band[...], preferred_element_type=jnp.float32)
            result = result[:, :LANES] + result[:, LANES:]
            for b in range(blocks):
                wide[plane, b] = jnp.where(inside, result[b * reach : (b + 1) * reach], 0.0)
        for plane in range(planes):
            for k in range(parts):
                for j in range(each):
                    b = (me ^ k) * each + j
                    total = float(taps[RAD]) * wide[plane, b, pl.ds(start + RAD, rows), :]
                    for i in range(RAD):
                        pair = wide[plane, b, pl.ds(start + i, rows), :]
                        pair = pair + wide[plane, b, pl.ds(start + 2 * RAD - i, rows), :]
                        total = total + float(taps[i]) * pair
                    out_refs[k][frame, plane, :, j * LANES : (j + 1) * LANES] = total.astype(jnp.bfloat16)
        return carry

    lax.fori_loop(0, frames, one, 0)


def smooth(movie, pair, other, shifts, place, parts):
    frames, planes, rows, width = movie.shape
    reach = rows + 2 * HALO
    smem = pl.BlockSpec(memory_space=pltpu.SMEM)
    return pl.pallas_call(
        smooth_kernel,
        out_shape=[jax.ShapeDtypeStruct((frames, planes, rows, width // parts), jnp.bfloat16)] * parts,
        in_specs=[smem, smem] + whole_vmem(3),
        out_specs=whole_vmem(parts),
        scratch_shapes=[
            pltpu.VMEM((2 * LANES, 2 * LANES), jnp.bfloat16),
            pltpu.VMEM((planes, width // LANES, reach, LANES), jnp.float32),
        ],
        compiler_params=params(12 * MIB + 8 * movie.size),
        name="smooth",
    )(shifts, place, movie, pair, other)


def spread_kernel(part_frames, place_ref, kernel_ref, out_ref):
    planes, size, _ = out_ref.shape
    frames = size // GROUP
    me = place_ref[2]
    row = lax.broadcasted_iota(jnp.int32, (size, frames), 0)
    column = lax.broadcasted_iota(jnp.int32, (size, frames), 1)
    tall = (row % frames == column).astype(jnp.bfloat16)
    row = lax.broadcasted_iota(jnp.int32, (frames, size), 0)
    column = lax.broadcasted_iota(jnp.int32, (frames, size), 1) // GROUP
    last = frames // part_frames - 1
    column = ((last - column // part_frames) ^ me) * part_frames + column % part_frames
    flat = (column == row).astype(jnp.bfloat16)
    row = lax.broadcasted_iota(jnp.int32, (size, size), 0)
    column = lax.broadcasted_iota(jnp.int32, (size, size), 1)
    same = row // frames == column % GROUP
    for plane in range(planes):
        left = jnp.dot(tall, kernel_ref[plane], preferred_element_type=jnp.float32).astype(jnp.bfloat16)
        full = jnp.dot(left, flat, preferred_element_type=jnp.float32)
        out_ref[plane] = jnp.where(same, full, 0.0).astype(jnp.bfloat16)


def spread(kernel, place, part_frames):
    planes, frames, _ = kernel.shape
    size = frames * GROUP
    return pl.pallas_call(
        functools.partial(spread_kernel, part_frames),
        out_shape=jax.ShapeDtypeStruct((planes, size, size), jnp.bfloat16),
        in_specs=[pl.BlockSpec(memory_space=pltpu.SMEM)] + whole_vmem(1),
        out_specs=whole_vmem(1)[0],
        compiler_params=params(8 * MIB + 16 * size * size),
        name="spread_filters",
    )(place, kernel)


def swap_lanes(pieces):
    count = len(pieces)
    group = LANES // count
    half = count // 2
    lane = lax.broadcasted_iota(jnp.int32, pieces[0].shape, 1) // group
    while half >= 1:
        low = (lane & half) == 0
        result = list(pieces)
        for i in range(count):
            if i & half:
                continue
            a, b = pieces[i], pieces[i + half]
            if 2 * half == count:
                back = pltpu.roll(b, half * group, 1)
                ahead = pltpu.roll(a, half * group, 1)
            else:
                back = pltpu.roll(b, half * group, 1)
                ahead = pltpu.roll(a, LANES - half * group, 1)
            result[i] = jnp.where(low, a, back)
            result[i + half] = jnp.where(low, ahead, b)
        pieces = result
        half //= 2
    return pieces


def deconvolve_kernel(parts, spread_ref, *refs):
    data_refs, out_ref = refs[:parts], refs[-1]
    part_frames, planes, rows, width = data_refs[0].shape
    size = spread_ref.shape[1]
    frames = size // GROUP
    octets = rows // OCTET
    for q in range(width // LANES):
        lanes = slice(q * LANES, (q + 1) * LANES)
        for plane in range(planes):
            for first in range(0, rows // GROUP, 2):
                cells = []
                for a in (first, first + 1):
                    pieces = [ref[:, plane, a * GROUP : (a + 1) * GROUP, lanes] for ref in data_refs]
                    cells.append(jnp.concatenate(pieces, axis=0).reshape(size, LANES))
                cells = jnp.concatenate(cells, axis=1)
                spikes = jnp.dot(spread_ref[plane], cells, preferred_element_type=jnp.float32)
                spikes = jnp.maximum(spikes, 0.0)
                for a in (0, 1):
                    for half in (0, 1):
                        pieces = [
                            spikes[(half * OCTET + r) * frames : (half * OCTET + r + 1) * frames, a * LANES : (a + 1) * LANES]
                            for r in range(OCTET)
                        ]
                        octet = plane * octets + (first + a) * 2 + half
                        for j, piece in enumerate(swap_lanes(pieces)):
                            out_ref[q, octet, j * frames : (j + 1) * frames, :] = piece.astype(jnp.bfloat16)


def deconvolve(spread_filters, data, after):
    part_frames, planes, rows, width = data[0].shape
    frames = part_frames * len(data)
    shape = (width // LANES, planes * rows // OCTET, OCTET * frames, LANES)
    return pl.pallas_call(
        functools.partial(deconvolve_kernel, len(data)),
        out_shape=jax.ShapeDtypeStruct(shape, jnp.bfloat16),
        in_specs=whole_vmem(1 + len(data)) + [pl.BlockSpec(memory_space=pl.ANY)] * len(after),
        out_specs=whole_vmem(1)[0],
        compiler_params=params(12 * MIB + 4 * (spread_filters.size + 2 * len(data) * data[0].size)),
        name="deconvolve",
    )(spread_filters, *data, *after)


def pool_kernel(order, place_ref, spikes_ref, *refs):
    *weights_refs, out_ref = refs
    blocks, steps, height, _ = spikes_ref.shape
    tiles = len(weights_refs)
    me = place_ref[3]
    near = tiles // blocks
    frames = height // near
    tail = weights_refs[0].shape[0] - GROUP
    slots = tail // steps
    owners, owner_rows, _ = out_ref.shape
    owned = owners * owner_rows
    eye = lax.broadcasted_iota(jnp.int32, (slots, LANES), 0) == lax.broadcasted_iota(jnp.int32, (slots, LANES), 1)
    keys, groups = [], []
    for ref in weights_refs:
        ids = ref[tail : tail + GROUP, :].astype(jnp.float32)
        owner = jnp.sum(jnp.where(eye, ids[0:1, :], 0.0), axis=1, keepdims=True).astype(jnp.int32)
        local = jnp.sum(jnp.where(eye, ids[1:2, :], 0.0), axis=1, keepdims=True).astype(jnp.int32)
        keys.append(owner * owner_rows + local % owner_rows)
        groups.append(local // owner_rows)
    key = jnp.concatenate(keys, axis=0)
    group = jnp.concatenate(groups, axis=0)
    onehot = (lax.broadcasted_iota(jnp.int32, (tiles * slots, owned), 1) == key).astype(jnp.bfloat16)
    total = jnp.zeros((owned, LANES), jnp.float32)
    for q in range(blocks):
        pooled = jnp.zeros((tiles * slots, height), jnp.float32)
        for step in range(0, steps, 2):
            left = jnp.concatenate(
                [
                    jnp.concatenate([ref[at * slots : (at + 1) * slots, :] for ref in weights_refs], axis=0)
                    for at in (step, step + 1)
                ],
                axis=1,
            )
            right = jnp.concatenate([spikes_ref[q, step], spikes_ref[q, step + 1]], axis=1)
            pooled = pooled + lax.dot_general(
                left, right, (((1,), (1,)), ((), ())), preferred_element_type=jnp.float32
            )
        column = lax.broadcasted_iota(jnp.int32, (slots, height), 1) // frames + q * near
        pooled = jnp.concatenate(
            [jnp.where(column == me ^ k, pooled[i * slots : (i + 1) * slots], 0.0) for i, k in enumerate(order)], axis=0
        )
        partial = pooled[:, 0:LANES]
        for at in range(LANES, height, LANES):
            partial = partial + pooled[:, at : at + LANES]
        step = LANES // 2
        while step >= frames:
            partial = partial + pltpu.roll(partial, step, 1)
            step //= 2
        lane_group = lax.broadcasted_iota(jnp.int32, partial.shape, 1) // frames
        partial = jnp.where(lane_group == group, partial, 0.0)
        high = partial.astype(jnp.bfloat16)
        low = (partial - high.astype(jnp.float32)).astype(jnp.bfloat16)
        both = lax.dot_general(
            onehot,
            jnp.concatenate([high, low], axis=1),
            (((0,), (0,)), ((), ())),
            preferred_element_type=jnp.float32,
        )
        total = total + both[:, :LANES] + both[:, LANES:]
    out_ref[...] = total.reshape(owners, owner_rows, LANES)


def pool(spikes, weights, order, place, frames, owners):
    shape = (owners, COMP_DEV * frames // LANES, LANES)
    inputs = [spikes, *weights]
    return pl.pallas_call(
        functools.partial(pool_kernel, order),
        out_shape=jax.ShapeDtypeStruct(shape, jnp.float32),
        in_specs=[pl.BlockSpec(memory_space=pltpu.SMEM)] + whole_vmem(len(inputs)),
        out_specs=whole_vmem(1)[0],
        compiler_params=params(16 * MIB + 4 * sum(cells.size for cells in inputs)),
        name="pool",
    )(place, *inputs)


def finish_kernel(parts_ref, out_ref):
    sources, rows, _ = parts_ref.shape
    frames = out_ref.shape[1]
    total = jnp.sum(parts_ref[...], axis=0)
    for group in range(LANES // frames):
        out_ref[group * rows : (group + 1) * rows, :] = total[:, group * frames : (group + 1) * frames]


def finish(parts, frames):
    return pl.pallas_call(
        finish_kernel,
        out_shape=jax.ShapeDtypeStruct((COMP_DEV, frames), jnp.float32),
        in_specs=whole_vmem(1),
        out_specs=whole_vmem(1)[0],
        compiler_params=params(8 * MIB + 8 * parts.size),
        name="finish",
    )(parts)


def body(movie, shifts, filters, weights, slot_owner, slot_local):
    part_frames, planes, rows, width = movie.shape
    tiles = lax.axis_size("tile")
    parts = lax.axis_size("frame")
    frames = part_frames * parts
    slots = weights.shape[0]
    ends = tiles - 1
    tile = lax.axis_index("tile")
    place = jnp.stack([tile * rows, tiles * rows, lax.axis_index("frame"), tile]).astype(jnp.int32)
    far, close = list(range(tiles // 2, tiles)), list(range(1, tiles // 2))
    order = close[:1] + far[-2:] + far[-3::-1] + close[1:] + [0]
    owner, local = slot_owner.reshape(1, slots), slot_local.reshape(1, slots)
    pair, other = edges(movie, place)
    packed = pack(weights, owner, local, order, planes, place)
    pair = lax.ppermute(pair, "tile", [(i, i ^ 1) for i in range(tiles)])
    swaps = [(i, i + 1) for i in range(1, ends, 2)]
    other = lax.ppermute(other, "tile", swaps + [(j, i) for i, j in swaps])
    landed = [
        lax.ppermute(cells, "tile", [(i, i ^ k) for i in range(tiles)]) if k else cells
        for k, cells in zip(order, packed)
    ]
    pieces = smooth(movie, pair, other, shifts.T, place, parts)
    pieces = [
        lax.ppermute(pieces[k], "frame", [(i, i ^ k) for i in range(parts)]) for k in range(parts - 1, 0, -1)
    ] + [pieces[0]]
    spikes = deconvolve(spread(build_kernel(filters, frames), place, part_frames), pieces, landed[: len(far) + 1])
    traces = pool(spikes, landed, order, place, frames, parts * tiles)
    traces = lax.all_to_all(traces, ("frame", "tile"), split_axis=0, concat_axis=0, tiled=True)
    return finish(traces, frames)


def solution(mesh):
    in_specs = (
        P("frame", None, "tile", None),
        P("frame", None),
        P(),
        P(("frame", "tile"), None),
        P(("frame", "tile"), None),
        P(("frame", "tile"), None),
    )
    out_specs = P(("frame", "tile"), None)
    return jax.shard_map(body, mesh=mesh, in_specs=in_specs, out_specs=out_specs, check_vma=False)
```

```python
import functools

import jax
import jax.numpy as jnp
import numpy as np
from jax import lax
from jax.experimental import pallas as pl
from jax.experimental.pallas import tpu as pltpu
from jax.sharding import PartitionSpec as P

COMP_DEV = 32
TAPS = 64
MAXS = 8
RAD = 3
LANES = 128
GROUP = 16
HALO = 16
OCTET = 8
QUAD = 4
MIB = 1 << 20


smooth_sigma = 1.0


def gauss_taps():
    positions = np.arange(-RAD, RAD + 1).astype(np.float32)
    values = np.exp(-positions * positions / np.float32(2.0 * smooth_sigma * smooth_sigma))
    return (values / values.sum(dtype=np.float32)).astype(np.float32)


def build_kernel(filters, count):
    later = jnp.arange(count)[:, None]
    earlier = jnp.arange(count)[None, :]
    offsets = later - earlier
    onehot = (offsets[:, :, None] == jnp.arange(TAPS)[None, None, :]).astype(jnp.float32)
    return jnp.sum(onehot[None] * filters[:, None, None, :], axis=-1).astype(jnp.bfloat16)


def whole_vmem(count):
    return [pl.BlockSpec(memory_space=pltpu.VMEM)] * count


def params(limit):
    return pltpu.CompilerParams(vmem_limit_bytes=limit)


def edges_kernel(place_ref, movie_ref, pair_ref, other_ref):
    frames, planes, rows, _ = movie_ref.shape
    even = place_ref[3] % 2 == 0

    def one(frame, carry):
        last = [movie_ref[frame, plane, rows - HALO :, :].astype(jnp.float32) for plane in range(planes)]
        first = [movie_ref[frame, plane, :HALO, :].astype(jnp.float32) for plane in range(planes)]
        last = [cells[OCTET:] for cells in last] + [cells[QUAD:OCTET] for cells in last]
        first = [cells[:OCTET] for cells in first] + [cells[OCTET : OCTET + QUAD] for cells in first]
        last = jnp.concatenate(last, axis=0)
        first = jnp.concatenate(first, axis=0)
        pair_ref[frame] = jnp.where(even, last, first).astype(jnp.bfloat16)
        other_ref[frame] = jnp.where(even, first, last).astype(jnp.bfloat16)
        return carry

    lax.fori_loop(0, frames, one, 0)


def edges(movie, place):
    frames, planes, _, width = movie.shape
    shape = jax.ShapeDtypeStruct((frames, planes * (OCTET + QUAD), width), jnp.bfloat16)
    return pl.pallas_call(
        edges_kernel,
        out_shape=[shape, shape],
        in_specs=[pl.BlockSpec(memory_space=pltpu.SMEM)] + whole_vmem(1),
        out_specs=whole_vmem(2),
        compiler_params=params(40 * MIB),
        name="edges",
    )(place, movie)


def pack_kernel(order, planes, place_ref, weights_ref, owner_ref, local_ref, *refs):
    *out_refs, ids = refs
    tiles = len(order)
    slots, pixels = weights_ref.shape
    octets = pixels // (planes * tiles * LANES)
    tail = planes * octets * slots
    ids[...] = jnp.zeros_like(ids)
    ids[0:1, 0:slots] = owner_ref[...].astype(jnp.float32)
    ids[1:2, 0:slots] = local_ref[...].astype(jnp.float32)
    for k, out_ref in zip(order, out_refs):
        dest = place_ref[3] ^ k
        for plane in range(planes):
            for octet in range(octets):
                lane = pl.multiple_of(((plane * tiles + dest) * octets + octet) * LANES, LANES)
                row = (plane * octets + octet) * slots
                out_ref[row : row + slots, :] = weights_ref[:, pl.ds(lane, LANES)]
        out_ref[tail:, :] = ids[...].astype(jnp.bfloat16)


def pack(weights, owner, local, order, planes, place):
    slots, pixels = weights.shape
    tiles = len(order)
    shape = jax.ShapeDtypeStruct((pixels // (tiles * LANES) * slots + GROUP, LANES), jnp.bfloat16)
    return pl.pallas_call(
        functools.partial(pack_kernel, order, planes),
        out_shape=[shape] * tiles,
        in_specs=[pl.BlockSpec(memory_space=pltpu.SMEM)] + whole_vmem(3),
        out_specs=whole_vmem(tiles),
        scratch_shapes=[pltpu.VMEM((GROUP, LANES), jnp.float32)],
        compiler_params=params(8 * MIB + 5 * weights.size),
        name="pack_weights",
    )(place, weights, owner, local)


def smooth_kernel(shift_ref, place_ref, movie_ref, other_ref, pair_ref, *refs):
    *out_refs, band, wide = refs
    frames, planes, rows, width = movie_ref.shape
    blocks = width // LANES
    reach = rows + 2 * HALO
    parts = len(out_refs)
    each = blocks // parts
    taps = gauss_taps()
    high = [float(v) for v in taps.astype(jnp.bfloat16)]
    low = [float(v) for v in taps - taps.astype(jnp.bfloat16).astype(np.float32)]
    lane = lax.broadcasted_iota(jnp.int32, (reach, LANES), 1)
    row = lax.broadcasted_iota(jnp.int32, (reach, LANES), 0)
    first_row, total_rows, me = place_ref[0], place_ref[1], place_ref[2]
    even = place_ref[3] % 2 == 0

    tap = lax.broadcasted_iota(jnp.int32, (2 * LANES, LANES), 0) - lax.broadcasted_iota(jnp.int32, (2 * LANES, LANES), 1)
    tap = tap - (MAXS - RAD)
    for side, values in enumerate((high, low)):
        cells = jnp.zeros((2 * LANES, LANES), jnp.float32)
        for i, value in enumerate(values):
            cells = jnp.where(tap == i, value, cells)
        band[:, side * LANES : (side + 1) * LANES] = cells.astype(jnp.bfloat16)

    def one(frame, carry):
        down = shift_ref[0, frame]
        right = shift_ref[1, frame] + MAXS
        near = lane < right
        zero = jnp.zeros((reach, LANES), jnp.float32)
        place = first_row + row - HALO + down
        inside = (place >= 0) & (place < total_rows)
        start = HALO - RAD - down
        for plane in range(planes):
            moved = []
            for b in range(blocks):
                cells = slice(b * LANES, (b + 1) * LANES)
                pair = pair_ref[frame, :, cells].astype(jnp.float32)
                other = other_ref[frame, :, cells].astype(jnp.float32)
                top = jnp.where(even, other, pair)
                bottom = jnp.where(even, pair, other)
                full = slice(plane * OCTET, (plane + 1) * OCTET)
                rest = slice(planes * OCTET + plane * QUAD, planes * OCTET + (plane + 1) * QUAD)
                piece = jnp.concatenate(
                    [
                        top[rest],
                        top[rest],
                        top[full],
                        movie_ref[frame, plane, :, cells].astype(jnp.float32),
                        bottom[full],
                        bottom[rest],
                        bottom[rest],
                    ],
                    axis=0,
                )
                moved.append(pltpu.roll(piece, right, 1))
            shifted = []
            for b in range(blocks + 1):
                before = moved[b - 1] if b > 0 else zero
                own = moved[b] if b < blocks else zero
                cells = jnp.where(near, before, own)
                if b == 0:
                    cells = jnp.where(lane < MAXS, 0.0, cells)
                if b == blocks:
                    cells = jnp.where(lane < MAXS, cells, 0.0)
                shifted.append(cells.astype(jnp.bfloat16))
            cells = jnp.concatenate(
                [jnp.concatenate(shifted[b : b + 2], axis=1) for b in range(blocks)], axis=0
            )
            result = jnp.dot(cells, band[...], preferred_element_type=jnp.float32)
            result = result[:, :LANES] + result[:, LANES:]
            for b in range(blocks):
                wide[plane, b] = jnp.where(inside, result[b * reach : (b + 1) * reach], 0.0)
        for plane in range(planes):
            for k in range(parts):
                for j in range(each):
                    b = (me ^ k) * each + j
                    total = float(taps[RAD]) * wide[plane, b, pl.ds(start + RAD, rows), :]
                    for i in range(RAD):
                        pair = wide[plane, b, pl.ds(start + i, rows), :]
                        pair = pair + wide[plane, b, pl.ds(start + 2 * RAD - i, rows), :]
                        total = total + float(taps[i]) * pair
                    out_refs[k][frame, plane, :, j * LANES : (j + 1) * LANES] = total.astype(jnp.bfloat16)
        return carry

    lax.fori_loop(0, frames, one, 0)


def smooth(movie, pair, other, shifts, place, parts):
    frames, planes, rows, width = movie.shape
    reach = rows + 2 * HALO
    smem = pl.BlockSpec(memory_space=pltpu.SMEM)
    return pl.pallas_call(
        smooth_kernel,
        out_shape=[jax.ShapeDtypeStruct((frames, planes, rows, width // parts), jnp.bfloat16)] * parts,
        in_specs=[smem, smem] + whole_vmem(3),
        out_specs=whole_vmem(parts),
        scratch_shapes=[
            pltpu.VMEM((2 * LANES, 2 * LANES), jnp.bfloat16),
            pltpu.VMEM((planes, width // LANES, reach, LANES), jnp.float32),
        ],
        compiler_params=params(12 * MIB + 8 * movie.size),
        name="smooth",
    )(shifts, place, movie, other, pair)


def spread_kernel(part_frames, place_ref, kernel_ref, out_ref):
    planes, size, _ = out_ref.shape
    frames = size // GROUP
    me = place_ref[2]
    row = lax.broadcasted_iota(jnp.int32, (size, frames), 0)
    column = lax.broadcasted_iota(jnp.int32, (size, frames), 1)
    tall = (row % frames == column).astype(jnp.bfloat16)
    row = lax.broadcasted_iota(jnp.int32, (frames, size), 0)
    column = lax.broadcasted_iota(jnp.int32, (frames, size), 1) // GROUP
    last = frames // part_frames - 1
    column = ((last - column // part_frames) ^ me) * part_frames + column % part_frames
    flat = (column == row).astype(jnp.bfloat16)
    row = lax.broadcasted_iota(jnp.int32, (size, size), 0)
    column = lax.broadcasted_iota(jnp.int32, (size, size), 1)
    same = row // frames == column % GROUP
    for plane in range(planes):
        left = jnp.dot(tall, kernel_ref[plane], preferred_element_type=jnp.float32).astype(jnp.bfloat16)
        full = jnp.dot(left, flat, preferred_element_type=jnp.float32)
        out_ref[plane] = jnp.where(same, full, 0.0).astype(jnp.bfloat16)


def spread(kernel, place, part_frames):
    planes, frames, _ = kernel.shape
    size = frames * GROUP
    return pl.pallas_call(
        functools.partial(spread_kernel, part_frames),
        out_shape=jax.ShapeDtypeStruct((planes, size, size), jnp.bfloat16),
        in_specs=[pl.BlockSpec(memory_space=pltpu.SMEM)] + whole_vmem(1),
        out_specs=whole_vmem(1)[0],
        compiler_params=params(8 * MIB + 16 * size * size),
        name="spread_filters",
    )(place, kernel)


def swap_lanes(pieces):
    count = len(pieces)
    group = LANES // count
    half = count // 2
    lane = lax.broadcasted_iota(jnp.int32, pieces[0].shape, 1) // group
    while half >= 1:
        low = (lane & half) == 0
        result = list(pieces)
        for i in range(count):
            if i & half:
                continue
            a, b = pieces[i], pieces[i + half]
            if 2 * half == count:
                back = pltpu.roll(b, half * group, 1)
                ahead = pltpu.roll(a, half * group, 1)
            else:
                back = pltpu.roll(b, half * group, 1)
                ahead = pltpu.roll(a, LANES - half * group, 1)
            result[i] = jnp.where(low, a, back)
            result[i + half] = jnp.where(low, ahead, b)
        pieces = result
        half //= 2
    return pieces


def deconvolve_kernel(parts, spread_ref, *refs):
    data_refs, out_ref = refs[:parts], refs[-1]
    part_frames, planes, rows, width = data_refs[0].shape
    size = spread_ref.shape[1]
    frames = size // GROUP
    octets = rows // OCTET
    for q in range(width // LANES):
        lanes = slice(q * LANES, (q + 1) * LANES)
        for plane in range(planes):
            for first in range(0, rows // GROUP, 2):
                cells = []
                for a in (first, first + 1):
                    pieces = [ref[:, plane, a * GROUP : (a + 1) * GROUP, lanes] for ref in data_refs]
                    cells.append(jnp.concatenate(pieces, axis=0).reshape(size, LANES))
                cells = jnp.concatenate(cells, axis=1)
                spikes = jnp.dot(spread_ref[plane], cells, preferred_element_type=jnp.float32)
                spikes = jnp.maximum(spikes, 0.0)
                for a in (0, 1):
                    for half in (0, 1):
                        pieces = [
                            spikes[(half * OCTET + r) * frames : (half * OCTET + r + 1) * frames, a * LANES : (a + 1) * LANES]
                            for r in range(OCTET)
                        ]
                        octet = plane * octets + (first + a) * 2 + half
                        for j, piece in enumerate(swap_lanes(pieces)):
                            out_ref[q, octet, j * frames : (j + 1) * frames, :] = piece.astype(jnp.bfloat16)


def deconvolve(spread_filters, data, after):
    part_frames, planes, rows, width = data[0].shape
    frames = part_frames * len(data)
    shape = (width // LANES, planes * rows // OCTET, OCTET * frames, LANES)
    return pl.pallas_call(
        functools.partial(deconvolve_kernel, len(data)),
        out_shape=jax.ShapeDtypeStruct(shape, jnp.bfloat16),
        in_specs=whole_vmem(1 + len(data)) + [pl.BlockSpec(memory_space=pl.ANY)] * len(after),
        out_specs=whole_vmem(1)[0],
        compiler_params=params(12 * MIB + 4 * (spread_filters.size + 2 * len(data) * data[0].size)),
        name="deconvolve",
    )(spread_filters, *data, *after)


def pool_kernel(order, place_ref, spikes_ref, *refs):
    *weights_refs, out_ref = refs
    blocks, steps, height, _ = spikes_ref.shape
    tiles = len(weights_refs)
    me = place_ref[3]
    near = tiles // blocks
    frames = height // near
    tail = weights_refs[0].shape[0] - GROUP
    slots = tail // steps
    owners, owner_rows, _ = out_ref.shape
    owned = owners * owner_rows
    eye = lax.broadcasted_iota(jnp.int32, (slots, LANES), 0) == lax.broadcasted_iota(jnp.int32, (slots, LANES), 1)
    keys, groups = [], []
    for ref in weights_refs:
        ids = ref[tail : tail + GROUP, :].astype(jnp.float32)
        owner = jnp.sum(jnp.where(eye, ids[0:1, :], 0.0), axis=1, keepdims=True).astype(jnp.int32)
        local = jnp.sum(jnp.where(eye, ids[1:2, :], 0.0), axis=1, keepdims=True).astype(jnp.int32)
        keys.append(owner * owner_rows + local % owner_rows)
        groups.append(local // owner_rows)
    key = jnp.concatenate(keys, axis=0)
    group = jnp.concatenate(groups, axis=0)
    onehot = (lax.broadcasted_iota(jnp.int32, (tiles * slots, owned), 1) == key).astype(jnp.bfloat16)
    total = jnp.zeros((owned, LANES), jnp.float32)
    for q in range(blocks):
        pooled = jnp.zeros((tiles * slots, height), jnp.float32)
        for step in range(0, steps, 2):
            left = jnp.concatenate(
                [
                    jnp.concatenate([ref[at * slots : (at + 1) * slots, :] for ref in weights_refs], axis=0)
                    for at in (step, step + 1)
                ],
                axis=1,
            )
            right = jnp.concatenate([spikes_ref[q, step], spikes_ref[q, step + 1]], axis=1)
            pooled = pooled + lax.dot_general(
                left, right, (((1,), (1,)), ((), ())), preferred_element_type=jnp.float32
            )
        column = lax.broadcasted_iota(jnp.int32, (slots, height), 1) // frames + q * near
        pooled = jnp.concatenate(
            [jnp.where(column == me ^ k, pooled[i * slots : (i + 1) * slots], 0.0) for i, k in enumerate(order)], axis=0
        )
        partial = pooled[:, 0:LANES]
        for at in range(LANES, height, LANES):
            partial = partial + pooled[:, at : at + LANES]
        step = LANES // 2
        while step >= frames:
            partial = partial + pltpu.roll(partial, step, 1)
            step //= 2
        lane_group = lax.broadcasted_iota(jnp.int32, partial.shape, 1) // frames
        partial = jnp.where(lane_group == group, partial, 0.0)
        high = partial.astype(jnp.bfloat16)
        low = (partial - high.astype(jnp.float32)).astype(jnp.bfloat16)
        both = lax.dot_general(
            onehot,
            jnp.concatenate([high, low], axis=1),
            (((0,), (0,)), ((), ())),
            preferred_element_type=jnp.float32,
        )
        total = total + both[:, :LANES] + both[:, LANES:]
    out_ref[...] = total.reshape(owners, owner_rows, LANES)


def pool(spikes, weights, order, place, frames, owners):
    shape = (owners, COMP_DEV * frames // LANES, LANES)
    inputs = [spikes, *weights]
    return pl.pallas_call(
        functools.partial(pool_kernel, order),
        out_shape=jax.ShapeDtypeStruct(shape, jnp.float32),
        in_specs=[pl.BlockSpec(memory_space=pltpu.SMEM)] + whole_vmem(len(inputs)),
        out_specs=whole_vmem(1)[0],
        compiler_params=params(16 * MIB + 4 * sum(cells.size for cells in inputs)),
        name="pool",
    )(place, *inputs)


def finish_kernel(parts_ref, out_ref):
    sources, rows, _ = parts_ref.shape
    frames = out_ref.shape[1]
    total = jnp.sum(parts_ref[...], axis=0)
    for group in range(LANES // frames):
        out_ref[group * rows : (group + 1) * rows, :] = total[:, group * frames : (group + 1) * frames]


def finish(parts, frames):
    return pl.pallas_call(
        finish_kernel,
        out_shape=jax.ShapeDtypeStruct((COMP_DEV, frames), jnp.float32),
        in_specs=whole_vmem(1),
        out_specs=whole_vmem(1)[0],
        compiler_params=params(8 * MIB + 8 * parts.size),
        name="finish",
    )(parts)


def body(movie, shifts, filters, weights, slot_owner, slot_local):
    part_frames, planes, rows, width = movie.shape
    tiles = lax.axis_size("tile")
    parts = lax.axis_size("frame")
    frames = part_frames * parts
    slots = weights.shape[0]
    ends = tiles - 1
    tile = lax.axis_index("tile")
    place = jnp.stack([tile * rows, tiles * rows, lax.axis_index("frame"), tile]).astype(jnp.int32)
    far, close = list(range(tiles // 2, tiles)), list(range(1, tiles // 2))
    order = close + far[-2:] + far[-3::-1] + [0]
    owner, local = slot_owner.reshape(1, slots), slot_local.reshape(1, slots)
    pair, other = edges(movie, place)
    packed = pack(weights, owner, local, order, planes, place)
    swaps = [(i, i + 1) for i in range(1, ends, 2)]
    other = lax.ppermute(other, "tile", swaps + [(j, i) for i, j in swaps])
    pair = lax.ppermute(pair, "tile", [(i, i ^ 1) for i in range(tiles)])
    landed = [
        lax.ppermute(cells, "tile", [(i, i ^ k) for i in range(tiles)]) if k else cells
        for k, cells in zip(order, packed)
    ]
    pieces = smooth(movie, pair, other, shifts.T, place, parts)
    pieces = [
        lax.ppermute(pieces[k], "frame", [(i, i ^ k) for i in range(parts)]) for k in range(parts - 1, 0, -1)
    ] + [pieces[0]]
    spikes = deconvolve(spread(build_kernel(filters, frames), place, part_frames), pieces, landed[: len(far) + 1])
    traces = pool(spikes, landed, order, place, frames, parts * tiles)
    traces = lax.all_to_all(traces, ("frame", "tile"), split_axis=0, concat_axis=0, tiled=True)
    return finish(traces, frames)


def solution(mesh):
    in_specs = (
        P("frame", None, "tile", None),
        P("frame", None),
        P(),
        P(("frame", "tile"), None),
        P(("frame", "tile"), None),
        P(("frame", "tile"), None),
    )
    out_specs = P(("frame", "tile"), None)
    return jax.shard_map(body, mesh=mesh, in_specs=in_specs, out_specs=out_specs, check_vma=False)
```

```python
import functools

import jax
import jax.numpy as jnp
import numpy as np
from jax import lax
from jax.experimental import pallas as pl
from jax.experimental.pallas import tpu as pltpu
from jax.sharding import PartitionSpec as P

COMP_DEV = 32
TAPS = 64
MAXS = 8
RAD = 3
LANES = 128
GROUP = 16
HALO = 16
OCTET = 8
QUAD = 4
MIB = 1 << 20


smooth_sigma = 1.0


def gauss_taps():
    positions = np.arange(-RAD, RAD + 1).astype(np.float32)
    values = np.exp(-positions * positions / np.float32(2.0 * smooth_sigma * smooth_sigma))
    return (values / values.sum(dtype=np.float32)).astype(np.float32)


def build_kernel(filters, count):
    later = jnp.arange(count)[:, None]
    earlier = jnp.arange(count)[None, :]
    offsets = later - earlier
    onehot = (offsets[:, :, None] == jnp.arange(TAPS)[None, None, :]).astype(jnp.float32)
    return jnp.sum(onehot[None] * filters[:, None, None, :], axis=-1).astype(jnp.bfloat16)


def whole_vmem(count):
    return [pl.BlockSpec(memory_space=pltpu.VMEM)] * count


def params(limit):
    return pltpu.CompilerParams(vmem_limit_bytes=limit)


def edges_kernel(place_ref, movie_ref, pair_ref, other_ref):
    frames, planes, rows, _ = movie_ref.shape
    even = place_ref[3] % 2 == 0

    def one(frame, carry):
        last = [movie_ref[frame, plane, rows - HALO :, :].astype(jnp.float32) for plane in range(planes)]
        first = [movie_ref[frame, plane, :HALO, :].astype(jnp.float32) for plane in range(planes)]
        last = [cells[OCTET:] for cells in last] + [cells[QUAD:OCTET] for cells in last]
        first = [cells[:OCTET] for cells in first] + [cells[OCTET : OCTET + QUAD] for cells in first]
        last = jnp.concatenate(last, axis=0)
        first = jnp.concatenate(first, axis=0)
        pair_ref[frame] = jnp.where(even, last, first).astype(jnp.bfloat16)
        other_ref[frame] = jnp.where(even, first, last).astype(jnp.bfloat16)
        return carry

    lax.fori_loop(0, frames, one, 0)


def edges(movie, place):
    frames, planes, _, width = movie.shape
    shape = jax.ShapeDtypeStruct((frames, planes * (OCTET + QUAD), width), jnp.bfloat16)
    return pl.pallas_call(
        edges_kernel,
        out_shape=[shape, shape],
        in_specs=[pl.BlockSpec(memory_space=pltpu.SMEM)] + whole_vmem(1),
        out_specs=whole_vmem(2),
        compiler_params=params(40 * MIB),
        name="edges",
    )(place, movie)


def pack_kernel(order, tiles, planes, place_ref, weights_ref, owner_ref, local_ref, *refs):
    *out_refs, ids = refs[-1 - len(order) :]
    slots, pixels = weights_ref.shape
    octets = pixels // (planes * tiles * LANES)
    tail = planes * octets * slots
    ids[...] = jnp.zeros_like(ids)
    ids[0:1, 0:slots] = owner_ref[...].astype(jnp.float32)
    ids[1:2, 0:slots] = local_ref[...].astype(jnp.float32)
    for k, out_ref in zip(order, out_refs):
        dest = place_ref[3] ^ k
        for plane in range(planes):
            for octet in range(octets):
                lane = pl.multiple_of(((plane * tiles + dest) * octets + octet) * LANES, LANES)
                row = (plane * octets + octet) * slots
                out_ref[row : row + slots, :] = weights_ref[:, pl.ds(lane, LANES)]
        out_ref[tail:, :] = ids[...].astype(jnp.bfloat16)


def pack(weights, owner, local, order, tiles, planes, place, *after):
    slots, pixels = weights.shape
    shape = jax.ShapeDtypeStruct((pixels // (tiles * LANES) * slots + GROUP, LANES), jnp.bfloat16)
    return pl.pallas_call(
        functools.partial(pack_kernel, order, tiles, planes),
        out_shape=[shape] * len(order),
        in_specs=[pl.BlockSpec(memory_space=pltpu.SMEM)] + whole_vmem(3) + [pl.BlockSpec(memory_space=pl.ANY)] * len(after),
        out_specs=whole_vmem(len(order)),
        scratch_shapes=[pltpu.VMEM((GROUP, LANES), jnp.float32)],
        compiler_params=params(8 * MIB + 5 * weights.size),
        name="pack_weights",
    )(place, weights, owner, local, *after)


def smooth_kernel(shift_ref, place_ref, movie_ref, other_ref, pair_ref, *refs):
    *out_refs, band, wide = refs
    frames, planes, rows, width = movie_ref.shape
    blocks = width // LANES
    reach = rows + 2 * HALO
    parts = len(out_refs)
    each = blocks // parts
    taps = gauss_taps()
    high = [float(v) for v in taps.astype(jnp.bfloat16)]
    low = [float(v) for v in taps - taps.astype(jnp.bfloat16).astype(np.float32)]
    lane = lax.broadcasted_iota(jnp.int32, (reach, LANES), 1)
    row = lax.broadcasted_iota(jnp.int32, (reach, LANES), 0)
    first_row, total_rows, me = place_ref[0], place_ref[1], place_ref[2]
    even = place_ref[3] % 2 == 0

    tap = lax.broadcasted_iota(jnp.int32, (2 * LANES, LANES), 0) - lax.broadcasted_iota(jnp.int32, (2 * LANES, LANES), 1)
    tap = tap - (MAXS - RAD)
    for side, values in enumerate((high, low)):
        cells = jnp.zeros((2 * LANES, LANES), jnp.float32)
        for i, value in enumerate(values):
            cells = jnp.where(tap == i, value, cells)
        band[:, side * LANES : (side + 1) * LANES] = cells.astype(jnp.bfloat16)

    def one(frame, carry):
        down = shift_ref[0, frame]
        right = shift_ref[1, frame] + MAXS
        near = lane < right
        zero = jnp.zeros((reach, LANES), jnp.float32)
        place = first_row + row - HALO + down
        inside = (place >= 0) & (place < total_rows)
        start = HALO - RAD - down
        for plane in range(planes):
            moved = []
            for b in range(blocks):
                cells = slice(b * LANES, (b + 1) * LANES)
                pair = pair_ref[frame, :, cells].astype(jnp.float32)
                other = other_ref[frame, :, cells].astype(jnp.float32)
                top = jnp.where(even, other, pair)
                bottom = jnp.where(even, pair, other)
                full = slice(plane * OCTET, (plane + 1) * OCTET)
                rest = slice(planes * OCTET + plane * QUAD, planes * OCTET + (plane + 1) * QUAD)
                piece = jnp.concatenate(
                    [
                        top[rest],
                        top[rest],
                        top[full],
                        movie_ref[frame, plane, :, cells].astype(jnp.float32),
                        bottom[full],
                        bottom[rest],
                        bottom[rest],
                    ],
                    axis=0,
                )
                moved.append(pltpu.roll(piece, right, 1))
            shifted = []
            for b in range(blocks + 1):
                before = moved[b - 1] if b > 0 else zero
                own = moved[b] if b < blocks else zero
                cells = jnp.where(near, before, own)
                if b == 0:
                    cells = jnp.where(lane < MAXS, 0.0, cells)
                if b == blocks:
                    cells = jnp.where(lane < MAXS, cells, 0.0)
                shifted.append(cells.astype(jnp.bfloat16))
            cells = jnp.concatenate(
                [jnp.concatenate(shifted[b : b + 2], axis=1) for b in range(blocks)], axis=0
            )
            result = jnp.dot(cells, band[...], preferred_element_type=jnp.float32)
            result = result[:, :LANES] + result[:, LANES:]
            for b in range(blocks):
                wide[plane, b] = jnp.where(inside, result[b * reach : (b + 1) * reach], 0.0)
        for plane in range(planes):
            for k in range(parts):
                for j in range(each):
                    b = (me ^ k) * each + j
                    total = float(taps[RAD]) * wide[plane, b, pl.ds(start + RAD, rows), :]
                    for i in range(RAD):
                        pair = wide[plane, b, pl.ds(start + i, rows), :]
                        pair = pair + wide[plane, b, pl.ds(start + 2 * RAD - i, rows), :]
                        total = total + float(taps[i]) * pair
                    out_refs[k][frame, plane, :, j * LANES : (j + 1) * LANES] = total.astype(jnp.bfloat16)
        return carry

    lax.fori_loop(0, frames, one, 0)


def smooth(movie, pair, other, shifts, place, parts):
    frames, planes, rows, width = movie.shape
    reach = rows + 2 * HALO
    smem = pl.BlockSpec(memory_space=pltpu.SMEM)
    return pl.pallas_call(
        smooth_kernel,
        out_shape=[jax.ShapeDtypeStruct((frames, planes, rows, width // parts), jnp.bfloat16)] * parts,
        in_specs=[smem, smem] + whole_vmem(3),
        out_specs=whole_vmem(parts),
        scratch_shapes=[
            pltpu.VMEM((2 * LANES, 2 * LANES), jnp.bfloat16),
            pltpu.VMEM((planes, width // LANES, reach, LANES), jnp.float32),
        ],
        compiler_params=params(12 * MIB + 8 * movie.size),
        name="smooth",
    )(shifts, place, movie, other, pair)


def spread_kernel(part_frames, place_ref, kernel_ref, out_ref):
    planes, size, _ = out_ref.shape
    frames = size // GROUP
    me = place_ref[2]
    row = lax.broadcasted_iota(jnp.int32, (size, frames), 0)
    column = lax.broadcasted_iota(jnp.int32, (size, frames), 1)
    tall = (row % frames == column).astype(jnp.bfloat16)
    row = lax.broadcasted_iota(jnp.int32, (frames, size), 0)
    column = lax.broadcasted_iota(jnp.int32, (frames, size), 1) // GROUP
    last = frames // part_frames - 1
    column = ((last - column // part_frames) ^ me) * part_frames + column % part_frames
    flat = (column == row).astype(jnp.bfloat16)
    row = lax.broadcasted_iota(jnp.int32, (size, size), 0)
    column = lax.broadcasted_iota(jnp.int32, (size, size), 1)
    same = row // frames == column % GROUP
    for plane in range(planes):
        left = jnp.dot(tall, kernel_ref[plane], preferred_element_type=jnp.float32).astype(jnp.bfloat16)
        full = jnp.dot(left, flat, preferred_element_type=jnp.float32)
        out_ref[plane] = jnp.where(same, full, 0.0).astype(jnp.bfloat16)


def spread(kernel, place, part_frames):
    planes, frames, _ = kernel.shape
    size = frames * GROUP
    return pl.pallas_call(
        functools.partial(spread_kernel, part_frames),
        out_shape=jax.ShapeDtypeStruct((planes, size, size), jnp.bfloat16),
        in_specs=[pl.BlockSpec(memory_space=pltpu.SMEM)] + whole_vmem(1),
        out_specs=whole_vmem(1)[0],
        compiler_params=params(8 * MIB + 16 * size * size),
        name="spread_filters",
    )(place, kernel)


def swap_lanes(pieces):
    count = len(pieces)
    group = LANES // count
    half = count // 2
    lane = lax.broadcasted_iota(jnp.int32, pieces[0].shape, 1) // group
    while half >= 1:
        low = (lane & half) == 0
        result = list(pieces)
        for i in range(count):
            if i & half:
                continue
            a, b = pieces[i], pieces[i + half]
            if 2 * half == count:
                back = pltpu.roll(b, half * group, 1)
                ahead = pltpu.roll(a, half * group, 1)
            else:
                back = pltpu.roll(b, half * group, 1)
                ahead = pltpu.roll(a, LANES - half * group, 1)
            result[i] = jnp.where(low, a, back)
            result[i + half] = jnp.where(low, ahead, b)
        pieces = result
        half //= 2
    return pieces


def deconvolve_kernel(parts, spread_ref, *refs):
    data_refs, out_ref = refs[:parts], refs[-1]
    part_frames, planes, rows, width = data_refs[0].shape
    size = spread_ref.shape[1]
    frames = size // GROUP
    octets = rows // OCTET
    for q in range(width // LANES):
        lanes = slice(q * LANES, (q + 1) * LANES)
        for plane in range(planes):
            for first in range(0, rows // GROUP, 2):
                cells = []
                for a in (first, first + 1):
                    pieces = [ref[:, plane, a * GROUP : (a + 1) * GROUP, lanes] for ref in data_refs]
                    cells.append(jnp.concatenate(pieces, axis=0).reshape(size, LANES))
                cells = jnp.concatenate(cells, axis=1)
                spikes = jnp.dot(spread_ref[plane], cells, preferred_element_type=jnp.float32)
                spikes = jnp.maximum(spikes, 0.0)
                for a in (0, 1):
                    for half in (0, 1):
                        pieces = [
                            spikes[(half * OCTET + r) * frames : (half * OCTET + r + 1) * frames, a * LANES : (a + 1) * LANES]
                            for r in range(OCTET)
                        ]
                        octet = plane * octets + (first + a) * 2 + half
                        for j, piece in enumerate(swap_lanes(pieces)):
                            out_ref[q, octet, j * frames : (j + 1) * frames, :] = piece.astype(jnp.bfloat16)


def deconvolve(spread_filters, data, after):
    part_frames, planes, rows, width = data[0].shape
    frames = part_frames * len(data)
    shape = (width // LANES, planes * rows // OCTET, OCTET * frames, LANES)
    return pl.pallas_call(
        functools.partial(deconvolve_kernel, len(data)),
        out_shape=jax.ShapeDtypeStruct(shape, jnp.bfloat16),
        in_specs=whole_vmem(1 + len(data)) + [pl.BlockSpec(memory_space=pl.ANY)] * len(after),
        out_specs=whole_vmem(1)[0],
        compiler_params=params(12 * MIB + 4 * (spread_filters.size + 2 * len(data) * data[0].size)),
        name="deconvolve",
    )(spread_filters, *data, *after)


def pool_kernel(order, place_ref, spikes_ref, *refs):
    *weights_refs, out_ref = refs
    blocks, steps, height, _ = spikes_ref.shape
    tiles = len(weights_refs)
    me = place_ref[3]
    near = tiles // blocks
    frames = height // near
    tail = weights_refs[0].shape[0] - GROUP
    slots = tail // steps
    owners, owner_rows, _ = out_ref.shape
    owned = owners * owner_rows
    eye = lax.broadcasted_iota(jnp.int32, (slots, LANES), 0) == lax.broadcasted_iota(jnp.int32, (slots, LANES), 1)
    keys, groups = [], []
    for ref in weights_refs:
        ids = ref[tail : tail + GROUP, :].astype(jnp.float32)
        owner = jnp.sum(jnp.where(eye, ids[0:1, :], 0.0), axis=1, keepdims=True).astype(jnp.int32)
        local = jnp.sum(jnp.where(eye, ids[1:2, :], 0.0), axis=1, keepdims=True).astype(jnp.int32)
        keys.append(owner * owner_rows + local % owner_rows)
        groups.append(local // owner_rows)
    key = jnp.concatenate(keys, axis=0)
    group = jnp.concatenate(groups, axis=0)
    onehot = (lax.broadcasted_iota(jnp.int32, (tiles * slots, owned), 1) == key).astype(jnp.bfloat16)
    total = jnp.zeros((owned, LANES), jnp.float32)
    for q in range(blocks):
        pooled = jnp.zeros((tiles * slots, height), jnp.float32)
        for step in range(0, steps, 2):
            left = jnp.concatenate(
                [
                    jnp.concatenate([ref[at * slots : (at + 1) * slots, :] for ref in weights_refs], axis=0)
                    for at in (step, step + 1)
                ],
                axis=1,
            )
            right = jnp.concatenate([spikes_ref[q, step], spikes_ref[q, step + 1]], axis=1)
            pooled = pooled + lax.dot_general(
                left, right, (((1,), (1,)), ((), ())), preferred_element_type=jnp.float32
            )
        column = lax.broadcasted_iota(jnp.int32, (slots, height), 1) // frames + q * near
        pooled = jnp.concatenate(
            [jnp.where(column == me ^ k, pooled[i * slots : (i + 1) * slots], 0.0) for i, k in enumerate(order)], axis=0
        )
        partial = pooled[:, 0:LANES]
        for at in range(LANES, height, LANES):
            partial = partial + pooled[:, at : at + LANES]
        step = LANES // 2
        while step >= frames:
            partial = partial + pltpu.roll(partial, step, 1)
            step //= 2
        lane_group = lax.broadcasted_iota(jnp.int32, partial.shape, 1) // frames
        partial = jnp.where(lane_group == group, partial, 0.0)
        high = partial.astype(jnp.bfloat16)
        low = (partial - high.astype(jnp.float32)).astype(jnp.bfloat16)
        both = lax.dot_general(
            onehot,
            jnp.concatenate([high, low], axis=1),
            (((0,), (0,)), ((), ())),
            preferred_element_type=jnp.float32,
        )
        total = total + both[:, :LANES] + both[:, LANES:]
    out_ref[...] = total.reshape(owners, owner_rows, LANES)


def pool(spikes, weights, order, place, frames, owners):
    shape = (owners, COMP_DEV * frames // LANES, LANES)
    inputs = [spikes, *weights]
    return pl.pallas_call(
        functools.partial(pool_kernel, order),
        out_shape=jax.ShapeDtypeStruct(shape, jnp.float32),
        in_specs=[pl.BlockSpec(memory_space=pltpu.SMEM)] + whole_vmem(len(inputs)),
        out_specs=whole_vmem(1)[0],
        compiler_params=params(16 * MIB + 4 * sum(cells.size for cells in inputs)),
        name="pool",
    )(place, *inputs)


def finish_kernel(parts_ref, out_ref):
    sources, rows, _ = parts_ref.shape
    frames = out_ref.shape[1]
    total = jnp.sum(parts_ref[...], axis=0)
    for group in range(LANES // frames):
        out_ref[group * rows : (group + 1) * rows, :] = total[:, group * frames : (group + 1) * frames]


def finish(parts, frames):
    return pl.pallas_call(
        finish_kernel,
        out_shape=jax.ShapeDtypeStruct((COMP_DEV, frames), jnp.float32),
        in_specs=whole_vmem(1),
        out_specs=whole_vmem(1)[0],
        compiler_params=params(8 * MIB + 8 * parts.size),
        name="finish",
    )(parts)


def body(movie, shifts, filters, weights, slot_owner, slot_local):
    part_frames, planes, rows, width = movie.shape
    tiles = lax.axis_size("tile")
    parts = lax.axis_size("frame")
    frames = part_frames * parts
    slots = weights.shape[0]
    ends = tiles - 1
    tile = lax.axis_index("tile")
    place = jnp.stack([tile * rows, tiles * rows, lax.axis_index("frame"), tile]).astype(jnp.int32)
    far, close = list(range(tiles // 2, tiles)), list(range(1, tiles // 2))
    order = close[1:2] + close[:1] + close[2:] + far[-2:] + far[-3::-1] + [0]
    owner, local = slot_owner.reshape(1, slots), slot_local.reshape(1, slots)
    pair, other = edges(movie, place)
    swaps = [(i, i + 1) for i in range(1, ends, 2)]
    other = lax.ppermute(other, "tile", swaps + [(j, i) for i, j in swaps])
    pair = lax.ppermute(pair, "tile", [(i, i ^ 1) for i in range(tiles)])
    packed = pack(weights, owner, local, order[:1], tiles, planes, place)
    packed += pack(weights, owner, local, order[1:], tiles, planes, place, other)
    landed = [
        lax.ppermute(cells, "tile", [(i, i ^ k) for i in range(tiles)]) if k else cells
        for k, cells in zip(order, packed)
    ]
    pieces = smooth(movie, pair, other, shifts.T, place, parts)
    pieces = [
        lax.ppermute(pieces[k], "frame", [(i, i ^ k) for i in range(parts)]) for k in range(parts - 1, 0, -1)
    ] + [pieces[0]]
    spikes = deconvolve(spread(build_kernel(filters, frames), place, part_frames), pieces, landed[: len(far) + 1])
    traces = pool(spikes, landed, order, place, frames, parts * tiles)
    traces = lax.all_to_all(traces, ("frame", "tile"), split_axis=0, concat_axis=0, tiled=True)
    return finish(traces, frames)


def solution(mesh):
    in_specs = (
        P("frame", None, "tile", None),
        P("frame", None),
        P(),
        P(("frame", "tile"), None),
        P(("frame", "tile"), None),
        P(("frame", "tile"), None),
    )
    out_specs = P(("frame", "tile"), None)
    return jax.shard_map(body, mesh=mesh, in_specs=in_specs, out_specs=out_specs, check_vma=False)
```

```python
import functools

import jax
import jax.numpy as jnp
import numpy as np
from jax import lax
from jax.experimental import pallas as pl
from jax.experimental.pallas import tpu as pltpu
from jax.sharding import PartitionSpec as P

COMP_DEV = 32
TAPS = 64
MAXS = 8
RAD = 3
LANES = 128
GROUP = 16
HALO = 16
OCTET = 8
QUAD = 4
MIB = 1 << 20


smooth_sigma = 1.0


def gauss_taps():
    positions = np.arange(-RAD, RAD + 1).astype(np.float32)
    values = np.exp(-positions * positions / np.float32(2.0 * smooth_sigma * smooth_sigma))
    return (values / values.sum(dtype=np.float32)).astype(np.float32)


def build_kernel(filters, count):
    later = jnp.arange(count)[:, None]
    earlier = jnp.arange(count)[None, :]
    offsets = later - earlier
    onehot = (offsets[:, :, None] == jnp.arange(TAPS)[None, None, :]).astype(jnp.float32)
    return jnp.sum(onehot[None] * filters[:, None, None, :], axis=-1).astype(jnp.bfloat16)


def whole_vmem(count):
    return [pl.BlockSpec(memory_space=pltpu.VMEM)] * count


def params(limit):
    return pltpu.CompilerParams(vmem_limit_bytes=limit)


def edges_kernel(place_ref, movie_ref, pair_ref, other_ref):
    frames, planes, rows, _ = movie_ref.shape
    even = place_ref[3] % 2 == 0

    def one(frame, carry):
        last = [movie_ref[frame, plane, rows - HALO :, :].astype(jnp.float32) for plane in range(planes)]
        first = [movie_ref[frame, plane, :HALO, :].astype(jnp.float32) for plane in range(planes)]
        last = [cells[OCTET:] for cells in last] + [cells[QUAD:OCTET] for cells in last]
        first = [cells[:OCTET] for cells in first] + [cells[OCTET : OCTET + QUAD] for cells in first]
        last = jnp.concatenate(last, axis=0)
        first = jnp.concatenate(first, axis=0)
        pair_ref[frame] = jnp.where(even, last, first).astype(jnp.bfloat16)
        other_ref[frame] = jnp.where(even, first, last).astype(jnp.bfloat16)
        return carry

    lax.fori_loop(0, frames, one, 0)


def edges(movie, place):
    frames, planes, _, width = movie.shape
    shape = jax.ShapeDtypeStruct((frames, planes * (OCTET + QUAD), width), jnp.bfloat16)
    return pl.pallas_call(
        edges_kernel,
        out_shape=[shape, shape],
        in_specs=[pl.BlockSpec(memory_space=pltpu.SMEM)] + whole_vmem(1),
        out_specs=whole_vmem(2),
        compiler_params=params(40 * MIB),
        name="edges",
    )(place, movie)


def pack_kernel(order, tiles, planes, place_ref, weights_ref, owner_ref, local_ref, *refs):
    *out_refs, ids = refs[-1 - len(order) :]
    slots, pixels = weights_ref.shape
    octets = pixels // (planes * tiles * LANES)
    tail = planes * octets * slots
    ids[...] = jnp.zeros_like(ids)
    ids[0:1, 0:slots] = owner_ref[...].astype(jnp.float32)
    ids[1:2, 0:slots] = local_ref[...].astype(jnp.float32)
    for k, out_ref in zip(order, out_refs):
        dest = place_ref[3] ^ k
        for plane in range(planes):
            for octet in range(octets):
                lane = pl.multiple_of(((plane * tiles + dest) * octets + octet) * LANES, LANES)
                row = (plane * octets + octet) * slots
                out_ref[row : row + slots, :] = weights_ref[:, pl.ds(lane, LANES)]
        out_ref[tail:, :] = ids[...].astype(jnp.bfloat16)


def pack(weights, owner, local, order, tiles, planes, place, *after):
    slots, pixels = weights.shape
    shape = jax.ShapeDtypeStruct((pixels // (tiles * LANES) * slots + GROUP, LANES), jnp.bfloat16)
    return pl.pallas_call(
        functools.partial(pack_kernel, order, tiles, planes),
        out_shape=[shape] * len(order),
        in_specs=[pl.BlockSpec(memory_space=pltpu.SMEM)] + whole_vmem(3) + [pl.BlockSpec(memory_space=pl.ANY)] * len(after),
        out_specs=whole_vmem(len(order)),
        scratch_shapes=[pltpu.VMEM((GROUP, LANES), jnp.float32)],
        compiler_params=params(8 * MIB + 5 * weights.size),
        name="pack_weights",
    )(place, weights, owner, local, *after)


def smooth_kernel(shift_ref, place_ref, movie_ref, other_ref, pair_ref, *refs):
    *out_refs, band, wide = refs
    frames, planes, rows, width = movie_ref.shape
    blocks = width // LANES
    reach = rows + 2 * HALO
    parts = len(out_refs)
    each = blocks // parts
    taps = gauss_taps()
    high = [float(v) for v in taps.astype(jnp.bfloat16)]
    low = [float(v) for v in taps - taps.astype(jnp.bfloat16).astype(np.float32)]
    lane = lax.broadcasted_iota(jnp.int32, (reach, LANES), 1)
    row = lax.broadcasted_iota(jnp.int32, (reach, LANES), 0)
    first_row, total_rows, me = place_ref[0], place_ref[1], place_ref[2]
    even = place_ref[3] % 2 == 0

    tap = lax.broadcasted_iota(jnp.int32, (2 * LANES, LANES), 0) - lax.broadcasted_iota(jnp.int32, (2 * LANES, LANES), 1)
    tap = tap - (MAXS - RAD)
    for side, values in enumerate((high, low)):
        cells = jnp.zeros((2 * LANES, LANES), jnp.float32)
        for i, value in enumerate(values):
            cells = jnp.where(tap == i, value, cells)
        band[:, side * LANES : (side + 1) * LANES] = cells.astype(jnp.bfloat16)

    def one(frame, carry):
        down = shift_ref[0, frame]
        right = shift_ref[1, frame] + MAXS
        near = lane < right
        zero = jnp.zeros((reach, LANES), jnp.float32)
        place = first_row + row - HALO + down
        inside = (place >= 0) & (place < total_rows)
        start = HALO - RAD - down
        for plane in range(planes):
            moved = []
            for b in range(blocks):
                cells = slice(b * LANES, (b + 1) * LANES)
                pair = pair_ref[frame, :, cells].astype(jnp.float32)
                other = other_ref[frame, :, cells].astype(jnp.float32)
                top = jnp.where(even, other, pair)
                bottom = jnp.where(even, pair, other)
                full = slice(plane * OCTET, (plane + 1) * OCTET)
                rest = slice(planes * OCTET + plane * QUAD, planes * OCTET + (plane + 1) * QUAD)
                piece = jnp.concatenate(
                    [
                        top[rest],
                        top[rest],
                        top[full],
                        movie_ref[frame, plane, :, cells].astype(jnp.float32),
                        bottom[full],
                        bottom[rest],
                        bottom[rest],
                    ],
                    axis=0,
                )
                moved.append(pltpu.roll(piece, right, 1))
            shifted = []
            for b in range(blocks + 1):
                before = moved[b - 1] if b > 0 else zero
                own = moved[b] if b < blocks else zero
                cells = jnp.where(near, before, own)
                if b == 0:
                    cells = jnp.where(lane < MAXS, 0.0, cells)
                if b == blocks:
                    cells = jnp.where(lane < MAXS, cells, 0.0)
                shifted.append(cells.astype(jnp.bfloat16))
            cells = jnp.concatenate(
                [jnp.concatenate(shifted[b : b + 2], axis=1) for b in range(blocks)], axis=0
            )
            result = jnp.dot(cells, band[...], preferred_element_type=jnp.float32)
            result = result[:, :LANES] + result[:, LANES:]
            for b in range(blocks):
                wide[plane, b] = jnp.where(inside, result[b * reach : (b + 1) * reach], 0.0)
        for plane in range(planes):
            for k in range(parts):
                for j in range(each):
                    b = (me ^ k) * each + j
                    total = float(taps[RAD]) * wide[plane, b, pl.ds(start + RAD, rows), :]
                    for i in range(RAD):
                        pair = wide[plane, b, pl.ds(start + i, rows), :]
                        pair = pair + wide[plane, b, pl.ds(start + 2 * RAD - i, rows), :]
                        total = total + float(taps[i]) * pair
                    out_refs[k][frame, plane, :, j * LANES : (j + 1) * LANES] = total.astype(jnp.bfloat16)
        return carry

    lax.fori_loop(0, frames, one, 0)


def smooth(movie, pair, other, shifts, place, parts):
    frames, planes, rows, width = movie.shape
    reach = rows + 2 * HALO
    smem = pl.BlockSpec(memory_space=pltpu.SMEM)
    return pl.pallas_call(
        smooth_kernel,
        out_shape=[jax.ShapeDtypeStruct((frames, planes, rows, width // parts), jnp.bfloat16)] * parts,
        in_specs=[smem, smem] + whole_vmem(3),
        out_specs=whole_vmem(parts),
        scratch_shapes=[
            pltpu.VMEM((2 * LANES, 2 * LANES), jnp.bfloat16),
            pltpu.VMEM((planes, width // LANES, reach, LANES), jnp.float32),
        ],
        compiler_params=params(12 * MIB + 8 * movie.size),
        name="smooth",
    )(shifts, place, movie, other, pair)


def spread_kernel(part_frames, place_ref, kernel_ref, out_ref):
    planes, size, _ = out_ref.shape
    frames = size // GROUP
    me = place_ref[2]
    row = lax.broadcasted_iota(jnp.int32, (size, frames), 0)
    column = lax.broadcasted_iota(jnp.int32, (size, frames), 1)
    tall = (row % frames == column).astype(jnp.bfloat16)
    row = lax.broadcasted_iota(jnp.int32, (frames, size), 0)
    column = lax.broadcasted_iota(jnp.int32, (frames, size), 1) // GROUP
    last = frames // part_frames - 1
    column = ((last - column // part_frames) ^ me) * part_frames + column % part_frames
    flat = (column == row).astype(jnp.bfloat16)
    row = lax.broadcasted_iota(jnp.int32, (size, size), 0)
    column = lax.broadcasted_iota(jnp.int32, (size, size), 1)
    same = row // frames == column % GROUP
    for plane in range(planes):
        left = jnp.dot(tall, kernel_ref[plane], preferred_element_type=jnp.float32).astype(jnp.bfloat16)
        full = jnp.dot(left, flat, preferred_element_type=jnp.float32)
        out_ref[plane] = jnp.where(same, full, 0.0).astype(jnp.bfloat16)


def spread(kernel, place, part_frames):
    planes, frames, _ = kernel.shape
    size = frames * GROUP
    return pl.pallas_call(
        functools.partial(spread_kernel, part_frames),
        out_shape=jax.ShapeDtypeStruct((planes, size, size), jnp.bfloat16),
        in_specs=[pl.BlockSpec(memory_space=pltpu.SMEM)] + whole_vmem(1),
        out_specs=whole_vmem(1)[0],
        compiler_params=params(8 * MIB + 16 * size * size),
        name="spread_filters",
    )(place, kernel)


def swap_lanes(pieces):
    count = len(pieces)
    group = LANES // count
    half = count // 2
    lane = lax.broadcasted_iota(jnp.int32, pieces[0].shape, 1) // group
    while half >= 1:
        low = (lane & half) == 0
        result = list(pieces)
        for i in range(count):
            if i & half:
                continue
            a, b = pieces[i], pieces[i + half]
            if 2 * half == count:
                back = pltpu.roll(b, half * group, 1)
                ahead = pltpu.roll(a, half * group, 1)
            else:
                back = pltpu.roll(b, half * group, 1)
                ahead = pltpu.roll(a, LANES - half * group, 1)
            result[i] = jnp.where(low, a, back)
            result[i + half] = jnp.where(low, ahead, b)
        pieces = result
        half //= 2
    return pieces


def deconvolve_kernel(parts, spread_ref, *refs):
    data_refs, out_ref = refs[:parts], refs[-1]
    part_frames, planes, rows, width = data_refs[0].shape
    size = spread_ref.shape[1]
    frames = size // GROUP
    octets = rows // OCTET
    for q in range(width // LANES):
        lanes = slice(q * LANES, (q + 1) * LANES)
        for plane in range(planes):
            for first in range(0, rows // GROUP, 2):
                cells = []
                for a in (first, first + 1):
                    pieces = [ref[:, plane, a * GROUP : (a + 1) * GROUP, lanes] for ref in data_refs]
                    cells.append(jnp.concatenate(pieces, axis=0).reshape(size, LANES))
                cells = jnp.concatenate(cells, axis=1)
                spikes = jnp.dot(spread_ref[plane], cells, preferred_element_type=jnp.float32)
                spikes = jnp.maximum(spikes, 0.0)
                for a in (0, 1):
                    for half in (0, 1):
                        pieces = [
                            spikes[(half * OCTET + r) * frames : (half * OCTET + r + 1) * frames, a * LANES : (a + 1) * LANES]
                            for r in range(OCTET)
                        ]
                        octet = plane * octets + (first + a) * 2 + half
                        for j, piece in enumerate(swap_lanes(pieces)):
                            out_ref[q, octet, j * frames : (j + 1) * frames, :] = piece.astype(jnp.bfloat16)


def deconvolve(spread_filters, data, after):
    part_frames, planes, rows, width = data[0].shape
    frames = part_frames * len(data)
    shape = (width // LANES, planes * rows // OCTET, OCTET * frames, LANES)
    return pl.pallas_call(
        functools.partial(deconvolve_kernel, len(data)),
        out_shape=jax.ShapeDtypeStruct(shape, jnp.bfloat16),
        in_specs=whole_vmem(1 + len(data)) + [pl.BlockSpec(memory_space=pl.ANY)] * len(after),
        out_specs=whole_vmem(1)[0],
        compiler_params=params(12 * MIB + 4 * (spread_filters.size + 2 * len(data) * data[0].size)),
        name="deconvolve",
    )(spread_filters, *data, *after)


def pool_kernel(order, place_ref, spikes_ref, *refs):
    *weights_refs, out_ref = refs
    blocks, steps, height, _ = spikes_ref.shape
    tiles = len(weights_refs)
    me = place_ref[3]
    near = tiles // blocks
    frames = height // near
    tail = weights_refs[0].shape[0] - GROUP
    slots = tail // steps
    owners, owner_rows, _ = out_ref.shape
    owned = owners * owner_rows
    eye = lax.broadcasted_iota(jnp.int32, (slots, LANES), 0) == lax.broadcasted_iota(jnp.int32, (slots, LANES), 1)
    keys, groups = [], []
    for ref in weights_refs:
        ids = ref[tail : tail + GROUP, :].astype(jnp.float32)
        owner = jnp.sum(jnp.where(eye, ids[0:1, :], 0.0), axis=1, keepdims=True).astype(jnp.int32)
        local = jnp.sum(jnp.where(eye, ids[1:2, :], 0.0), axis=1, keepdims=True).astype(jnp.int32)
        keys.append(owner * owner_rows + local % owner_rows)
        groups.append(local // owner_rows)
    key = jnp.concatenate(keys, axis=0)
    group = jnp.concatenate(groups, axis=0)
    onehot = (lax.broadcasted_iota(jnp.int32, (tiles * slots, owned), 1) == key).astype(jnp.bfloat16)
    total = jnp.zeros((owned, LANES), jnp.float32)
    for q in range(blocks):
        pooled = jnp.zeros((tiles * slots, height), jnp.float32)
        for step in range(0, steps, 2):
            left = jnp.concatenate(
                [
                    jnp.concatenate([ref[at * slots : (at + 1) * slots, :] for ref in weights_refs], axis=0)
                    for at in (step, step + 1)
                ],
                axis=1,
            )
            right = jnp.concatenate([spikes_ref[q, step], spikes_ref[q, step + 1]], axis=1)
            pooled = pooled + lax.dot_general(
                left, right, (((1,), (1,)), ((), ())), preferred_element_type=jnp.float32
            )
        column = lax.broadcasted_iota(jnp.int32, (slots, height), 1) // frames + q * near
        pooled = jnp.concatenate(
            [jnp.where(column == me ^ k, pooled[i * slots : (i + 1) * slots], 0.0) for i, k in enumerate(order)], axis=0
        )
        partial = pooled[:, 0:LANES]
        for at in range(LANES, height, LANES):
            partial = partial + pooled[:, at : at + LANES]
        step = LANES // 2
        while step >= frames:
            partial = partial + pltpu.roll(partial, step, 1)
            step //= 2
        lane_group = lax.broadcasted_iota(jnp.int32, partial.shape, 1) // frames
        partial = jnp.where(lane_group == group, partial, 0.0)
        high = partial.astype(jnp.bfloat16)
        low = (partial - high.astype(jnp.float32)).astype(jnp.bfloat16)
        both = lax.dot_general(
            onehot,
            jnp.concatenate([high, low], axis=1),
            (((0,), (0,)), ((), ())),
            preferred_element_type=jnp.float32,
        )
        total = total + both[:, :LANES] + both[:, LANES:]
    out_ref[...] = total.reshape(owners, owner_rows, LANES)


def pool(spikes, weights, order, place, frames, owners):
    shape = (owners, COMP_DEV * frames // LANES, LANES)
    inputs = [spikes, *weights]
    return pl.pallas_call(
        functools.partial(pool_kernel, order),
        out_shape=jax.ShapeDtypeStruct(shape, jnp.float32),
        in_specs=[pl.BlockSpec(memory_space=pltpu.SMEM)] + whole_vmem(len(inputs)),
        out_specs=whole_vmem(1)[0],
        compiler_params=params(16 * MIB + 4 * sum(cells.size for cells in inputs)),
        name="pool",
    )(place, *inputs)


def finish_kernel(parts_ref, out_ref):
    sources, rows, _ = parts_ref.shape
    frames = out_ref.shape[1]
    total = jnp.sum(parts_ref[...], axis=0)
    for group in range(LANES // frames):
        out_ref[group * rows : (group + 1) * rows, :] = total[:, group * frames : (group + 1) * frames]


def finish(parts, frames):
    return pl.pallas_call(
        finish_kernel,
        out_shape=jax.ShapeDtypeStruct((COMP_DEV, frames), jnp.float32),
        in_specs=whole_vmem(1),
        out_specs=whole_vmem(1)[0],
        compiler_params=params(8 * MIB + 8 * parts.size),
        name="finish",
    )(parts)


def body(movie, shifts, filters, weights, slot_owner, slot_local):
    part_frames, planes, rows, width = movie.shape
    tiles = lax.axis_size("tile")
    parts = lax.axis_size("frame")
    frames = part_frames * parts
    slots = weights.shape[0]
    ends = tiles - 1
    tile = lax.axis_index("tile")
    place = jnp.stack([tile * rows, tiles * rows, lax.axis_index("frame"), tile]).astype(jnp.int32)
    far, close = list(range(tiles // 2, tiles)), list(range(1, tiles // 2))
    order = close[1:2] + far[-2:] + close[:1] + far[-3::-1] + close[2:] + [0]
    owner, local = slot_owner.reshape(1, slots), slot_local.reshape(1, slots)
    pair, other = edges(movie, place)
    swaps = [(i, i + 1) for i in range(1, ends, 2)]
    other = lax.ppermute(other, "tile", swaps + [(j, i) for i, j in swaps])
    pair = lax.ppermute(pair, "tile", [(i, i ^ 1) for i in range(tiles)])
    packed = pack(weights, owner, local, order[:1], tiles, planes, place)
    packed += pack(weights, owner, local, order[1:], tiles, planes, place, other)
    landed = [
        lax.ppermute(cells, "tile", [(i, i ^ k) for i in range(tiles)]) if k else cells
        for k, cells in zip(order, packed)
    ]
    pieces = smooth(movie, pair, other, shifts.T, place, parts)
    pieces = [
        lax.ppermute(pieces[k], "frame", [(i, i ^ k) for i in range(parts)]) for k in range(parts - 1, 0, -1)
    ] + [pieces[0]]
    spikes = deconvolve(spread(build_kernel(filters, frames), place, part_frames), pieces, landed[: len(far) + 1])
    traces = pool(spikes, landed, order, place, frames, parts * tiles)
    traces = lax.all_to_all(traces, ("frame", "tile"), split_axis=0, concat_axis=0, tiled=True)
    return finish(traces, frames)


def solution(mesh):
    in_specs = (
        P("frame", None, "tile", None),
        P("frame", None),
        P(),
        P(("frame", "tile"), None),
        P(("frame", "tile"), None),
        P(("frame", "tile"), None),
    )
    out_specs = P(("frame", "tile"), None)
    return jax.shard_map(body, mesh=mesh, in_specs=in_specs, out_specs=out_specs, check_vma=False)
```

```python
import functools

import jax
import jax.numpy as jnp
import numpy as np
from jax import lax
from jax.experimental import pallas as pl
from jax.experimental.pallas import tpu as pltpu
from jax.sharding import PartitionSpec as P

COMP_DEV = 32
TAPS = 64
MAXS = 8
RAD = 3
LANES = 128
GROUP = 16
HALO = 16
OCTET = 8
QUAD = 4
MIB = 1 << 20


smooth_sigma = 1.0


def gauss_taps():
    positions = np.arange(-RAD, RAD + 1).astype(np.float32)
    values = np.exp(-positions * positions / np.float32(2.0 * smooth_sigma * smooth_sigma))
    return (values / values.sum(dtype=np.float32)).astype(np.float32)


def build_kernel(filters, count):
    later = jnp.arange(count)[:, None]
    earlier = jnp.arange(count)[None, :]
    offsets = later - earlier
    onehot = (offsets[:, :, None] == jnp.arange(TAPS)[None, None, :]).astype(jnp.float32)
    return jnp.sum(onehot[None] * filters[:, None, None, :], axis=-1).astype(jnp.bfloat16)


def whole_vmem(count):
    return [pl.BlockSpec(memory_space=pltpu.VMEM)] * count


def params(limit):
    return pltpu.CompilerParams(vmem_limit_bytes=limit)


def edges_kernel(place_ref, movie_ref, pair_ref, other_ref):
    frames, planes, rows, _ = movie_ref.shape
    even = place_ref[3] % 2 == 0

    def one(frame, carry):
        last = [movie_ref[frame, plane, rows - HALO :, :].astype(jnp.float32) for plane in range(planes)]
        first = [movie_ref[frame, plane, :HALO, :].astype(jnp.float32) for plane in range(planes)]
        last = [cells[OCTET:] for cells in last] + [cells[QUAD:OCTET] for cells in last]
        first = [cells[:OCTET] for cells in first] + [cells[OCTET : OCTET + QUAD] for cells in first]
        last = jnp.concatenate(last, axis=0)
        first = jnp.concatenate(first, axis=0)
        pair_ref[frame] = jnp.where(even, last, first).astype(jnp.bfloat16)
        other_ref[frame] = jnp.where(even, first, last).astype(jnp.bfloat16)
        return carry

    lax.fori_loop(0, frames, one, 0)


def edges(movie, place):
    frames, planes, _, width = movie.shape
    shape = jax.ShapeDtypeStruct((frames, planes * (OCTET + QUAD), width), jnp.bfloat16)
    return pl.pallas_call(
        edges_kernel,
        out_shape=[shape, shape],
        in_specs=[pl.BlockSpec(memory_space=pltpu.SMEM)] + whole_vmem(1),
        out_specs=whole_vmem(2),
        compiler_params=params(40 * MIB),
        name="edges",
    )(place, movie)


def pack_kernel(order, planes, place_ref, weights_ref, owner_ref, local_ref, *refs):
    *out_refs, ids = refs
    tiles = len(order)
    slots, pixels = weights_ref.shape
    octets = pixels // (planes * tiles * LANES)
    tail = planes * octets * slots
    ids[...] = jnp.zeros_like(ids)
    ids[0:1, 0:slots] = owner_ref[...].astype(jnp.float32)
    ids[1:2, 0:slots] = local_ref[...].astype(jnp.float32)
    for k, out_ref in zip(order, out_refs):
        dest = place_ref[3] ^ k
        for plane in range(planes):
            for octet in range(octets):
                lane = pl.multiple_of(((plane * tiles + dest) * octets + octet) * LANES, LANES)
                row = (plane * octets + octet) * slots
                out_ref[row : row + slots, :] = weights_ref[:, pl.ds(lane, LANES)]
        out_ref[tail:, :] = ids[...].astype(jnp.bfloat16)


def pack(weights, owner, local, order, planes, place):
    slots, pixels = weights.shape
    tiles = len(order)
    shape = jax.ShapeDtypeStruct((pixels // (tiles * LANES) * slots + GROUP, LANES), jnp.bfloat16)
    return pl.pallas_call(
        functools.partial(pack_kernel, order, planes),
        out_shape=[shape] * tiles,
        in_specs=[pl.BlockSpec(memory_space=pltpu.SMEM)] + whole_vmem(3),
        out_specs=whole_vmem(tiles),
        scratch_shapes=[pltpu.VMEM((GROUP, LANES), jnp.float32)],
        compiler_params=params(8 * MIB + 5 * weights.size),
        name="pack_weights",
    )(place, weights, owner, local)


def smooth_kernel(shift_ref, place_ref, movie_ref, other_ref, pair_ref, *refs):
    *out_refs, band, wide = refs
    frames, planes, rows, width = movie_ref.shape
    blocks = width // LANES
    reach = rows + 2 * HALO
    parts = len(out_refs)
    each = blocks // parts
    taps = gauss_taps()
    high = [float(v) for v in taps.astype(jnp.bfloat16)]
    low = [float(v) for v in taps - taps.astype(jnp.bfloat16).astype(np.float32)]
    lane = lax.broadcasted_iota(jnp.int32, (reach, LANES), 1)
    row = lax.broadcasted_iota(jnp.int32, (reach, LANES), 0)
    first_row, total_rows, me = place_ref[0], place_ref[1], place_ref[2]
    even = place_ref[3] % 2 == 0

    tap = lax.broadcasted_iota(jnp.int32, (2 * LANES, LANES), 0) - lax.broadcasted_iota(jnp.int32, (2 * LANES, LANES), 1)
    tap = tap - (MAXS - RAD)
    for side, values in enumerate((high, low)):
        cells = jnp.zeros((2 * LANES, LANES), jnp.float32)
        for i, value in enumerate(values):
            cells = jnp.where(tap == i, value, cells)
        band[:, side * LANES : (side + 1) * LANES] = cells.astype(jnp.bfloat16)

    def one(frame, carry):
        down = shift_ref[0, frame]
        right = shift_ref[1, frame] + MAXS
        near = lane < right
        zero = jnp.zeros((reach, LANES), jnp.float32)
        place = first_row + row - HALO + down
        inside = (place >= 0) & (place < total_rows)
        start = HALO - RAD - down
        for plane in range(planes):
            moved = []
            for b in range(blocks):
                cells = slice(b * LANES, (b + 1) * LANES)
                pair = pair_ref[frame, :, cells].astype(jnp.float32)
                other = other_ref[frame, :, cells].astype(jnp.float32)
                top = jnp.where(even, other, pair)
                bottom = jnp.where(even, pair, other)
                full = slice(plane * OCTET, (plane + 1) * OCTET)
                rest = slice(planes * OCTET + plane * QUAD, planes * OCTET + (plane + 1) * QUAD)
                piece = jnp.concatenate(
                    [
                        top[rest],
                        top[rest],
                        top[full],
                        movie_ref[frame, plane, :, cells].astype(jnp.float32),
                        bottom[full],
                        bottom[rest],
                        bottom[rest],
                    ],
                    axis=0,
                )
                moved.append(pltpu.roll(piece, right, 1))
            shifted = []
            for b in range(blocks + 1):
                before = moved[b - 1] if b > 0 else zero
                own = moved[b] if b < blocks else zero
                cells = jnp.where(near, before, own)
                if b == 0:
                    cells = jnp.where(lane < MAXS, 0.0, cells)
                if b == blocks:
                    cells = jnp.where(lane < MAXS, cells, 0.0)
                shifted.append(cells.astype(jnp.bfloat16))
            cells = jnp.concatenate(
                [jnp.concatenate(shifted[b : b + 2], axis=1) for b in range(blocks)], axis=0
            )
            result = jnp.dot(cells, band[...], preferred_element_type=jnp.float32)
            result = result[:, :LANES] + result[:, LANES:]
            for b in range(blocks):
                wide[plane, b] = jnp.where(inside, result[b * reach : (b + 1) * reach], 0.0)
        for plane in range(planes):
            for k in range(parts):
                for j in range(each):
                    b = (me ^ k) * each + j
                    total = float(taps[RAD]) * wide[plane, b, pl.ds(start + RAD, rows), :]
                    for i in range(RAD):
                        pair = wide[plane, b, pl.ds(start + i, rows), :]
                        pair = pair + wide[plane, b, pl.ds(start + 2 * RAD - i, rows), :]
                        total = total + float(taps[i]) * pair
                    out_refs[k][frame, plane, :, j * LANES : (j + 1) * LANES] = total.astype(jnp.bfloat16)
        return carry

    lax.fori_loop(0, frames, one, 0)


def smooth(movie, pair, other, shifts, place, parts):
    frames, planes, rows, width = movie.shape
    reach = rows + 2 * HALO
    smem = pl.BlockSpec(memory_space=pltpu.SMEM)
    return pl.pallas_call(
        smooth_kernel,
        out_shape=[jax.ShapeDtypeStruct((frames, planes, rows, width // parts), jnp.bfloat16)] * parts,
        in_specs=[smem, smem] + whole_vmem(3),
        out_specs=whole_vmem(parts),
        scratch_shapes=[
            pltpu.VMEM((2 * LANES, 2 * LANES), jnp.bfloat16),
            pltpu.VMEM((planes, width // LANES, reach, LANES), jnp.float32),
        ],
        compiler_params=params(12 * MIB + 8 * movie.size),
        name="smooth",
    )(shifts, place, movie, other, pair)


def spread_kernel(part_frames, place_ref, kernel_ref, out_ref):
    planes, size, _ = out_ref.shape
    frames = size // GROUP
    me = place_ref[2]
    row = lax.broadcasted_iota(jnp.int32, (size, frames), 0)
    column = lax.broadcasted_iota(jnp.int32, (size, frames), 1)
    tall = (row % frames == column).astype(jnp.bfloat16)
    row = lax.broadcasted_iota(jnp.int32, (frames, size), 0)
    column = lax.broadcasted_iota(jnp.int32, (frames, size), 1) // GROUP
    last = frames // part_frames - 1
    column = ((last - column // part_frames) ^ me) * part_frames + column % part_frames
    flat = (column == row).astype(jnp.bfloat16)
    row = lax.broadcasted_iota(jnp.int32, (size, size), 0)
    column = lax.broadcasted_iota(jnp.int32, (size, size), 1)
    same = row // frames == column % GROUP
    for plane in range(planes):
        left = jnp.dot(tall, kernel_ref[plane], preferred_element_type=jnp.float32).astype(jnp.bfloat16)
        full = jnp.dot(left, flat, preferred_element_type=jnp.float32)
        out_ref[plane] = jnp.where(same, full, 0.0).astype(jnp.bfloat16)


def spread(kernel, place, part_frames):
    planes, frames, _ = kernel.shape
    size = frames * GROUP
    return pl.pallas_call(
        functools.partial(spread_kernel, part_frames),
        out_shape=jax.ShapeDtypeStruct((planes, size, size), jnp.bfloat16),
        in_specs=[pl.BlockSpec(memory_space=pltpu.SMEM)] + whole_vmem(1),
        out_specs=whole_vmem(1)[0],
        compiler_params=params(8 * MIB + 16 * size * size),
        name="spread_filters",
    )(place, kernel)


def swap_lanes(pieces):
    count = len(pieces)
    group = LANES // count
    half = count // 2
    lane = lax.broadcasted_iota(jnp.int32, pieces[0].shape, 1) // group
    while half >= 1:
        low = (lane & half) == 0
        result = list(pieces)
        for i in range(count):
            if i & half:
                continue
            a, b = pieces[i], pieces[i + half]
            if 2 * half == count:
                back = pltpu.roll(b, half * group, 1)
                ahead = pltpu.roll(a, half * group, 1)
            else:
                back = pltpu.roll(b, half * group, 1)
                ahead = pltpu.roll(a, LANES - half * group, 1)
            result[i] = jnp.where(low, a, back)
            result[i + half] = jnp.where(low, ahead, b)
        pieces = result
        half //= 2
    return pieces


def deconvolve_kernel(parts, spread_ref, *refs):
    data_refs, out_ref = refs[:parts], refs[-1]
    part_frames, planes, rows, width = data_refs[0].shape
    size = spread_ref.shape[1]
    frames = size // GROUP
    octets = rows // OCTET
    for q in range(width // LANES):
        lanes = slice(q * LANES, (q + 1) * LANES)
        for plane in range(planes):
            for first in range(0, rows // GROUP, 2):
                cells = []
                for a in (first, first + 1):
                    pieces = [ref[:, plane, a * GROUP : (a + 1) * GROUP, lanes] for ref in data_refs]
                    cells.append(jnp.concatenate(pieces, axis=0).reshape(size, LANES))
                cells = jnp.concatenate(cells, axis=1)
                spikes = jnp.dot(spread_ref[plane], cells, preferred_element_type=jnp.float32)
                spikes = jnp.maximum(spikes, 0.0)
                for a in (0, 1):
                    for half in (0, 1):
                        pieces = [
                            spikes[(half * OCTET + r) * frames : (half * OCTET + r + 1) * frames, a * LANES : (a + 1) * LANES]
                            for r in range(OCTET)
                        ]
                        octet = plane * octets + (first + a) * 2 + half
                        for j, piece in enumerate(swap_lanes(pieces)):
                            out_ref[q, octet, j * frames : (j + 1) * frames, :] = piece.astype(jnp.bfloat16)


def deconvolve(spread_filters, data, after):
    part_frames, planes, rows, width = data[0].shape
    frames = part_frames * len(data)
    shape = (width // LANES, planes * rows // OCTET, OCTET * frames, LANES)
    return pl.pallas_call(
        functools.partial(deconvolve_kernel, len(data)),
        out_shape=jax.ShapeDtypeStruct(shape, jnp.bfloat16),
        in_specs=whole_vmem(1 + len(data)) + [pl.BlockSpec(memory_space=pl.ANY)] * len(after),
        out_specs=whole_vmem(1)[0],
        compiler_params=params(12 * MIB + 4 * (spread_filters.size + 2 * len(data) * data[0].size)),
        name="deconvolve",
    )(spread_filters, *data, *after)


def pool_kernel(order, place_ref, spikes_ref, *refs):
    *weights_refs, out_ref = refs
    blocks, steps, height, _ = spikes_ref.shape
    tiles = len(weights_refs)
    me = place_ref[3]
    near = tiles // blocks
    frames = height // near
    tail = weights_refs[0].shape[0] - GROUP
    slots = tail // steps
    owners, owner_rows, _ = out_ref.shape
    owned = owners * owner_rows
    eye = lax.broadcasted_iota(jnp.int32, (slots, LANES), 0) == lax.broadcasted_iota(jnp.int32, (slots, LANES), 1)
    keys, groups = [], []
    for ref in weights_refs:
        ids = ref[tail : tail + GROUP, :].astype(jnp.float32)
        owner = jnp.sum(jnp.where(eye, ids[0:1, :], 0.0), axis=1, keepdims=True).astype(jnp.int32)
        local = jnp.sum(jnp.where(eye, ids[1:2, :], 0.0), axis=1, keepdims=True).astype(jnp.int32)
        keys.append(owner * owner_rows + local % owner_rows)
        groups.append(local // owner_rows)
    key = jnp.concatenate(keys, axis=0)
    group = jnp.concatenate(groups, axis=0)
    onehot = (lax.broadcasted_iota(jnp.int32, (tiles * slots, owned), 1) == key).astype(jnp.bfloat16)
    total = jnp.zeros((owned, LANES), jnp.float32)
    for q in range(blocks):
        pooled = jnp.zeros((tiles * slots, height), jnp.float32)
        for step in range(0, steps, 2):
            left = jnp.concatenate(
                [
                    jnp.concatenate([ref[at * slots : (at + 1) * slots, :] for ref in weights_refs], axis=0)
                    for at in (step, step + 1)
                ],
                axis=1,
            )
            right = jnp.concatenate([spikes_ref[q, step], spikes_ref[q, step + 1]], axis=1)
            pooled = pooled + lax.dot_general(
                left, right, (((1,), (1,)), ((), ())), preferred_element_type=jnp.float32
            )
        column = lax.broadcasted_iota(jnp.int32, (slots, height), 1) // frames + q * near
        pooled = jnp.concatenate(
            [jnp.where(column == me ^ k, pooled[i * slots : (i + 1) * slots], 0.0) for i, k in enumerate(order)], axis=0
        )
        partial = pooled[:, 0:LANES]
        for at in range(LANES, height, LANES):
            partial = partial + pooled[:, at : at + LANES]
        step = LANES // 2
        while step >= frames:
            partial = partial + pltpu.roll(partial, step, 1)
            step //= 2
        lane_group = lax.broadcasted_iota(jnp.int32, partial.shape, 1) // frames
        partial = jnp.where(lane_group == group, partial, 0.0)
        high = partial.astype(jnp.bfloat16)
        low = (partial - high.astype(jnp.float32)).astype(jnp.bfloat16)
        both = lax.dot_general(
            onehot,
            jnp.concatenate([high, low], axis=1),
            (((0,), (0,)), ((), ())),
            preferred_element_type=jnp.float32,
        )
        total = total + both[:, :LANES] + both[:, LANES:]
    out_ref[...] = total.reshape(owners, owner_rows, LANES)


def pool(spikes, weights, order, place, frames, owners):
    shape = (owners, COMP_DEV * frames // LANES, LANES)
    inputs = [spikes, *weights]
    return pl.pallas_call(
        functools.partial(pool_kernel, order),
        out_shape=jax.ShapeDtypeStruct(shape, jnp.float32),
        in_specs=[pl.BlockSpec(memory_space=pltpu.SMEM)] + whole_vmem(len(inputs)),
        out_specs=whole_vmem(1)[0],
        compiler_params=params(16 * MIB + 4 * sum(cells.size for cells in inputs)),
        name="pool",
    )(place, *inputs)


def finish_kernel(parts_ref, out_ref):
    sources, rows, _ = parts_ref.shape
    frames = out_ref.shape[1]
    total = jnp.sum(parts_ref[...], axis=0)
    for group in range(LANES // frames):
        out_ref[group * rows : (group + 1) * rows, :] = total[:, group * frames : (group + 1) * frames]


def finish(parts, frames):
    return pl.pallas_call(
        finish_kernel,
        out_shape=jax.ShapeDtypeStruct((COMP_DEV, frames), jnp.float32),
        in_specs=whole_vmem(1),
        out_specs=whole_vmem(1)[0],
        compiler_params=params(8 * MIB + 8 * parts.size),
        name="finish",
    )(parts)


def body(movie, shifts, filters, weights, slot_owner, slot_local):
    part_frames, planes, rows, width = movie.shape
    tiles = lax.axis_size("tile")
    parts = lax.axis_size("frame")
    frames = part_frames * parts
    slots = weights.shape[0]
    ends = tiles - 1
    tile = lax.axis_index("tile")
    place = jnp.stack([tile * rows, tiles * rows, lax.axis_index("frame"), tile]).astype(jnp.int32)
    far, close = list(range(tiles // 2, tiles)), list(range(1, tiles // 2))
    order = close[1:2] + far[-2:] + far[:1] + close[:1] + far[-3:0:-1] + close[2:] + [0]
    owner, local = slot_owner.reshape(1, slots), slot_local.reshape(1, slots)
    pair, other = edges(movie, place)
    packed = pack(weights, owner, local, order, planes, place)
    swaps = [(i, i + 1) for i in range(1, ends, 2)]
    other = lax.ppermute(other, "tile", swaps + [(j, i) for i, j in swaps])
    pair = lax.ppermute(pair, "tile", [(i, i ^ 1) for i in range(tiles)])
    landed = [
        lax.ppermute(cells, "tile", [(i, i ^ k) for i in range(tiles)]) if k else cells
        for k, cells in zip(order, packed)
    ]
    pieces = smooth(movie, pair, other, shifts.T, place, parts)
    pieces = [
        lax.ppermute(pieces[k], "frame", [(i, i ^ k) for i in range(parts)]) for k in range(parts - 1, 0, -1)
    ] + [pieces[0]]
    spikes = deconvolve(spread(build_kernel(filters, frames), place, part_frames), pieces, landed[: len(far) + 1])
    traces = pool(spikes, landed, order, place, frames, parts * tiles)
    traces = lax.all_to_all(traces, ("frame", "tile"), split_axis=0, concat_axis=0, tiled=True)
    return finish(traces, frames)


def solution(mesh):
    in_specs = (
        P("frame", None, "tile", None),
        P("frame", None),
        P(),
        P(("frame", "tile"), None),
        P(("frame", "tile"), None),
        P(("frame", "tile"), None),
    )
    out_specs = P(("frame", "tile"), None)
    return jax.shard_map(body, mesh=mesh, in_specs=in_specs, out_specs=out_specs, check_vma=False)
```

```python
import functools

import jax
import jax.numpy as jnp
import numpy as np
from jax import lax
from jax.experimental import pallas as pl
from jax.experimental.pallas import tpu as pltpu
from jax.sharding import PartitionSpec as P

COMP_DEV = 32
TAPS = 64
MAXS = 8
RAD = 3
LANES = 128
GROUP = 16
HALO = 16
OCTET = 8
QUAD = 4
MIB = 1 << 20


smooth_sigma = 1.0


def gauss_taps():
    positions = np.arange(-RAD, RAD + 1).astype(np.float32)
    values = np.exp(-positions * positions / np.float32(2.0 * smooth_sigma * smooth_sigma))
    return (values / values.sum(dtype=np.float32)).astype(np.float32)


def build_kernel(filters, count):
    later = jnp.arange(count)[:, None]
    earlier = jnp.arange(count)[None, :]
    offsets = later - earlier
    onehot = (offsets[:, :, None] == jnp.arange(TAPS)[None, None, :]).astype(jnp.float32)
    return jnp.sum(onehot[None] * filters[:, None, None, :], axis=-1).astype(jnp.bfloat16)


def whole_vmem(count):
    return [pl.BlockSpec(memory_space=pltpu.VMEM)] * count


def params(limit):
    return pltpu.CompilerParams(vmem_limit_bytes=limit)


def edges_kernel(place_ref, movie_ref, pair_ref, other_ref):
    frames, planes, rows, _ = movie_ref.shape
    even = place_ref[3] % 2 == 0

    def one(frame, carry):
        last = [movie_ref[frame, plane, rows - HALO :, :].astype(jnp.float32) for plane in range(planes)]
        first = [movie_ref[frame, plane, :HALO, :].astype(jnp.float32) for plane in range(planes)]
        last = [cells[OCTET:] for cells in last] + [cells[QUAD:OCTET] for cells in last]
        first = [cells[:OCTET] for cells in first] + [cells[OCTET : OCTET + QUAD] for cells in first]
        last = jnp.concatenate(last, axis=0)
        first = jnp.concatenate(first, axis=0)
        pair_ref[frame] = jnp.where(even, last, first).astype(jnp.bfloat16)
        other_ref[frame] = jnp.where(even, first, last).astype(jnp.bfloat16)
        return carry

    lax.fori_loop(0, frames, one, 0)


def edges(movie, place):
    frames, planes, _, width = movie.shape
    shape = jax.ShapeDtypeStruct((frames, planes * (OCTET + QUAD), width), jnp.bfloat16)
    return pl.pallas_call(
        edges_kernel,
        out_shape=[shape, shape],
        in_specs=[pl.BlockSpec(memory_space=pltpu.SMEM)] + whole_vmem(1),
        out_specs=whole_vmem(2),
        compiler_params=params(40 * MIB),
        name="edges",
    )(place, movie)


def pack_kernel(order, planes, place_ref, weights_ref, owner_ref, local_ref, *refs):
    *out_refs, ids = refs
    tiles = len(order)
    slots, pixels = weights_ref.shape
    octets = pixels // (planes * tiles * LANES)
    tail = planes * octets * slots
    ids[...] = jnp.zeros_like(ids)
    ids[0:1, 0:slots] = owner_ref[...].astype(jnp.float32)
    ids[1:2, 0:slots] = local_ref[...].astype(jnp.float32)
    for k, out_ref in zip(order, out_refs):
        dest = place_ref[3] ^ k
        for plane in range(planes):
            for octet in range(octets):
                lane = pl.multiple_of(((plane * tiles + dest) * octets + octet) * LANES, LANES)
                row = (plane * octets + octet) * slots
                out_ref[row : row + slots, :] = weights_ref[:, pl.ds(lane, LANES)]
        out_ref[tail:, :] = ids[...].astype(jnp.bfloat16)


def pack(weights, owner, local, order, planes, place):
    slots, pixels = weights.shape
    tiles = len(order)
    shape = jax.ShapeDtypeStruct((pixels // (tiles * LANES) * slots + GROUP, LANES), jnp.bfloat16)
    return pl.pallas_call(
        functools.partial(pack_kernel, order, planes),
        out_shape=[shape] * tiles,
        in_specs=[pl.BlockSpec(memory_space=pltpu.SMEM)] + whole_vmem(3),
        out_specs=whole_vmem(tiles),
        scratch_shapes=[pltpu.VMEM((GROUP, LANES), jnp.float32)],
        compiler_params=params(8 * MIB + 5 * weights.size),
        name="pack_weights",
    )(place, weights, owner, local)


def smooth_kernel(shift_ref, place_ref, movie_ref, other_ref, pair_ref, *refs):
    *out_refs, band, wide = refs
    frames, planes, rows, width = movie_ref.shape
    blocks = width // LANES
    reach = rows + 2 * HALO
    parts = len(out_refs)
    each = blocks // parts
    together = wide.shape[0]
    taps = gauss_taps()
    high = [float(v) for v in taps.astype(jnp.bfloat16)]
    low = [float(v) for v in taps - taps.astype(jnp.bfloat16).astype(np.float32)]
    lane = lax.broadcasted_iota(jnp.int32, (reach, LANES), 1)
    row = lax.broadcasted_iota(jnp.int32, (reach, LANES), 0)
    first_row, total_rows, me = place_ref[0], place_ref[1], place_ref[2]
    even = place_ref[3] % 2 == 0

    tap = lax.broadcasted_iota(jnp.int32, (2 * LANES, LANES), 0) - lax.broadcasted_iota(jnp.int32, (2 * LANES, LANES), 1)
    tap = tap - (MAXS - RAD)
    for side, values in enumerate((high, low)):
        cells = jnp.zeros((2 * LANES, LANES), jnp.float32)
        for i, value in enumerate(values):
            cells = jnp.where(tap == i, value, cells)
        band[:, side * LANES : (side + 1) * LANES] = cells.astype(jnp.bfloat16)

    def some(step, carry):
        chosen = [step * together + u for u in range(together)]
        stacked = []
        for frame in chosen:
            right = shift_ref[1, frame] + MAXS
            near = lane < right
            zero = jnp.zeros((reach, LANES), jnp.float32)
            for plane in range(planes):
                moved = []
                for b in range(blocks):
                    cells = slice(b * LANES, (b + 1) * LANES)
                    pair = pair_ref[frame, :, cells].astype(jnp.float32)
                    other = other_ref[frame, :, cells].astype(jnp.float32)
                    top = jnp.where(even, other, pair)
                    bottom = jnp.where(even, pair, other)
                    full = slice(plane * OCTET, (plane + 1) * OCTET)
                    rest = slice(planes * OCTET + plane * QUAD, planes * OCTET + (plane + 1) * QUAD)
                    piece = jnp.concatenate(
                        [
                            top[rest],
                            top[rest],
                            top[full],
                            movie_ref[frame, plane, :, cells].astype(jnp.float32),
                            bottom[full],
                            bottom[rest],
                            bottom[rest],
                        ],
                        axis=0,
                    )
                    moved.append(pltpu.roll(piece, right, 1))
                shifted = []
                for b in range(blocks + 1):
                    before = moved[b - 1] if b > 0 else zero
                    own = moved[b] if b < blocks else zero
                    cells = jnp.where(near, before, own)
                    if b == 0:
                        cells = jnp.where(lane < MAXS, 0.0, cells)
                    if b == blocks:
                        cells = jnp.where(lane < MAXS, cells, 0.0)
                    shifted.append(cells.astype(jnp.bfloat16))
                stacked += [jnp.concatenate(shifted[b : b + 2], axis=1) for b in range(blocks)]
        result = jnp.dot(jnp.concatenate(stacked, axis=0), band[...], preferred_element_type=jnp.float32)
        result = result[:, :LANES] + result[:, LANES:]
        for u, frame in enumerate(chosen):
            place = first_row + row - HALO + shift_ref[0, frame]
            inside = (place >= 0) & (place < total_rows)
            for plane in range(planes):
                for b in range(blocks):
                    at = ((u * planes + plane) * blocks + b) * reach
                    wide[u, plane, b] = jnp.where(inside, result[at : at + reach], 0.0)
        for u, frame in enumerate(chosen):
            start = HALO - RAD - shift_ref[0, frame]
            for plane in range(planes):
                for k in range(parts):
                    for j in range(each):
                        b = (me ^ k) * each + j
                        total = float(taps[RAD]) * wide[u, plane, b, pl.ds(start + RAD, rows), :]
                        for i in range(RAD):
                            pair = wide[u, plane, b, pl.ds(start + i, rows), :]
                            pair = pair + wide[u, plane, b, pl.ds(start + 2 * RAD - i, rows), :]
                            total = total + float(taps[i]) * pair
                        out_refs[k][frame, plane, :, j * LANES : (j + 1) * LANES] = total.astype(jnp.bfloat16)
        return carry

    lax.fori_loop(0, frames // together, some, 0)


def smooth(movie, pair, other, shifts, place, parts):
    frames, planes, rows, width = movie.shape
    reach = rows + 2 * HALO
    smem = pl.BlockSpec(memory_space=pltpu.SMEM)
    return pl.pallas_call(
        smooth_kernel,
        out_shape=[jax.ShapeDtypeStruct((frames, planes, rows, width // parts), jnp.bfloat16)] * parts,
        in_specs=[smem, smem] + whole_vmem(3),
        out_specs=whole_vmem(parts),
        scratch_shapes=[
            pltpu.VMEM((2 * LANES, 2 * LANES), jnp.bfloat16),
            pltpu.VMEM((2 - frames % 2, planes, width // LANES, reach, LANES), jnp.float32),
        ],
        compiler_params=params(20 * MIB + 8 * movie.size),
        name="smooth",
    )(shifts, place, movie, other, pair)


def spread_kernel(part_frames, place_ref, kernel_ref, out_ref):
    planes, size, _ = out_ref.shape
    frames = size // GROUP
    me = place_ref[2]
    row = lax.broadcasted_iota(jnp.int32, (size, frames), 0)
    column = lax.broadcasted_iota(jnp.int32, (size, frames), 1)
    tall = (row % frames == column).astype(jnp.bfloat16)
    row = lax.broadcasted_iota(jnp.int32, (frames, size), 0)
    column = lax.broadcasted_iota(jnp.int32, (frames, size), 1) // GROUP
    last = frames // part_frames - 1
    column = ((last - column // part_frames) ^ me) * part_frames + column % part_frames
    flat = (column == row).astype(jnp.bfloat16)
    row = lax.broadcasted_iota(jnp.int32, (size, size), 0)
    column = lax.broadcasted_iota(jnp.int32, (size, size), 1)
    same = row // frames == column % GROUP
    for plane in range(planes):
        left = jnp.dot(tall, kernel_ref[plane], preferred_element_type=jnp.float32).astype(jnp.bfloat16)
        full = jnp.dot(left, flat, preferred_element_type=jnp.float32)
        out_ref[plane] = jnp.where(same, full, 0.0).astype(jnp.bfloat16)


def spread(kernel, place, part_frames):
    planes, frames, _ = kernel.shape
    size = frames * GROUP
    return pl.pallas_call(
        functools.partial(spread_kernel, part_frames),
        out_shape=jax.ShapeDtypeStruct((planes, size, size), jnp.bfloat16),
        in_specs=[pl.BlockSpec(memory_space=pltpu.SMEM)] + whole_vmem(1),
        out_specs=whole_vmem(1)[0],
        compiler_params=params(8 * MIB + 16 * size * size),
        name="spread_filters",
    )(place, kernel)


def swap_lanes(pieces):
    count = len(pieces)
    group = LANES // count
    half = count // 2
    lane = lax.broadcasted_iota(jnp.int32, pieces[0].shape, 1) // group
    while half >= 1:
        low = (lane & half) == 0
        result = list(pieces)
        for i in range(count):
            if i & half:
                continue
            a, b = pieces[i], pieces[i + half]
            if 2 * half == count:
                back = pltpu.roll(b, half * group, 1)
                ahead = pltpu.roll(a, half * group, 1)
            else:
                back = pltpu.roll(b, half * group, 1)
                ahead = pltpu.roll(a, LANES - half * group, 1)
            result[i] = jnp.where(low, a, back)
            result[i + half] = jnp.where(low, ahead, b)
        pieces = result
        half //= 2
    return pieces


def deconvolve_kernel(parts, spread_ref, *refs):
    data_refs, out_ref = refs[:parts], refs[-1]
    part_frames, planes, rows, width = data_refs[0].shape
    size = spread_ref.shape[1]
    frames = size // GROUP
    octets = rows // OCTET
    for q in range(width // LANES):
        lanes = slice(q * LANES, (q + 1) * LANES)
        for plane in range(planes):
            for first in range(0, rows // GROUP, 2):
                cells = []
                for a in (first, first + 1):
                    pieces = [ref[:, plane, a * GROUP : (a + 1) * GROUP, lanes] for ref in data_refs]
                    cells.append(jnp.concatenate(pieces, axis=0).reshape(size, LANES))
                cells = jnp.concatenate(cells, axis=1)
                spikes = jnp.dot(spread_ref[plane], cells, preferred_element_type=jnp.float32)
                spikes = jnp.maximum(spikes, 0.0)
                for a in (0, 1):
                    for half in (0, 1):
                        pieces = [
                            spikes[(half * OCTET + r) * frames : (half * OCTET + r + 1) * frames, a * LANES : (a + 1) * LANES]
                            for r in range(OCTET)
                        ]
                        octet = plane * octets + (first + a) * 2 + half
                        for j, piece in enumerate(swap_lanes(pieces)):
                            out_ref[q, octet, j * frames : (j + 1) * frames, :] = piece.astype(jnp.bfloat16)


def deconvolve(spread_filters, data, after):
    part_frames, planes, rows, width = data[0].shape
    frames = part_frames * len(data)
    shape = (width // LANES, planes * rows // OCTET, OCTET * frames, LANES)
    return pl.pallas_call(
        functools.partial(deconvolve_kernel, len(data)),
        out_shape=jax.ShapeDtypeStruct(shape, jnp.bfloat16),
        in_specs=whole_vmem(1 + len(data)) + [pl.BlockSpec(memory_space=pl.ANY)] * len(after),
        out_specs=whole_vmem(1)[0],
        compiler_params=params(12 * MIB + 4 * (spread_filters.size + 2 * len(data) * data[0].size)),
        name="deconvolve",
    )(spread_filters, *data, *after)


def pool_kernel(order, place_ref, spikes_ref, *refs):
    *weights_refs, out_ref = refs
    blocks, steps, height, _ = spikes_ref.shape
    tiles = len(weights_refs)
    me = place_ref[3]
    near = tiles // blocks
    frames = height // near
    tail = weights_refs[0].shape[0] - GROUP
    slots = tail // steps
    owners, owner_rows, _ = out_ref.shape
    owned = owners * owner_rows
    eye = lax.broadcasted_iota(jnp.int32, (slots, LANES), 0) == lax.broadcasted_iota(jnp.int32, (slots, LANES), 1)
    keys, groups = [], []
    for ref in weights_refs:
        ids = ref[tail : tail + GROUP, :].astype(jnp.float32)
        owner = jnp.sum(jnp.where(eye, ids[0:1, :], 0.0), axis=1, keepdims=True).astype(jnp.int32)
        local = jnp.sum(jnp.where(eye, ids[1:2, :], 0.0), axis=1, keepdims=True).astype(jnp.int32)
        keys.append(owner * owner_rows + local % owner_rows)
        groups.append(local // owner_rows)
    key = jnp.concatenate(keys, axis=0)
    group = jnp.concatenate(groups, axis=0)
    onehot = (lax.broadcasted_iota(jnp.int32, (tiles * slots, owned), 1) == key).astype(jnp.bfloat16)
    total = jnp.zeros((owned, LANES), jnp.float32)
    for q in range(blocks):
        pooled = jnp.zeros((tiles * slots, height), jnp.float32)
        for step in range(0, steps, 2):
            left = jnp.concatenate(
                [
                    jnp.concatenate([ref[at * slots : (at + 1) * slots, :] for ref in weights_refs], axis=0)
                    for at in (step, step + 1)
                ],
                axis=1,
            )
            right = jnp.concatenate([spikes_ref[q, step], spikes_ref[q, step + 1]], axis=1)
            pooled = pooled + lax.dot_general(
                left, right, (((1,), (1,)), ((), ())), preferred_element_type=jnp.float32
            )
        column = lax.broadcasted_iota(jnp.int32, (slots, height), 1) // frames + q * near
        pooled = jnp.concatenate(
            [jnp.where(column == me ^ k, pooled[i * slots : (i + 1) * slots], 0.0) for i, k in enumerate(order)], axis=0
        )
        partial = pooled[:, 0:LANES]
        for at in range(LANES, height, LANES):
            partial = partial + pooled[:, at : at + LANES]
        step = LANES // 2
        while step >= frames:
            partial = partial + pltpu.roll(partial, step, 1)
            step //= 2
        lane_group = lax.broadcasted_iota(jnp.int32, partial.shape, 1) // frames
        partial = jnp.where(lane_group == group, partial, 0.0)
        high = partial.astype(jnp.bfloat16)
        low = (partial - high.astype(jnp.float32)).astype(jnp.bfloat16)
        both = lax.dot_general(
            onehot,
            jnp.concatenate([high, low], axis=1),
            (((0,), (0,)), ((), ())),
            preferred_element_type=jnp.float32,
        )
        total = total + both[:, :LANES] + both[:, LANES:]
    out_ref[...] = total.reshape(owners, owner_rows, LANES)


def pool(spikes, weights, order, place, frames, owners):
    shape = (owners, COMP_DEV * frames // LANES, LANES)
    inputs = [spikes, *weights]
    return pl.pallas_call(
        functools.partial(pool_kernel, order),
        out_shape=jax.ShapeDtypeStruct(shape, jnp.float32),
        in_specs=[pl.BlockSpec(memory_space=pltpu.SMEM)] + whole_vmem(len(inputs)),
        out_specs=whole_vmem(1)[0],
        compiler_params=params(16 * MIB + 4 * sum(cells.size for cells in inputs)),
        name="pool",
    )(place, *inputs)


def finish_kernel(parts_ref, out_ref):
    sources, rows, _ = parts_ref.shape
    frames = out_ref.shape[1]
    total = jnp.sum(parts_ref[...], axis=0)
    for group in range(LANES // frames):
        out_ref[group * rows : (group + 1) * rows, :] = total[:, group * frames : (group + 1) * frames]


def finish(parts, frames):
    return pl.pallas_call(
        finish_kernel,
        out_shape=jax.ShapeDtypeStruct((COMP_DEV, frames), jnp.float32),
        in_specs=whole_vmem(1),
        out_specs=whole_vmem(1)[0],
        compiler_params=params(8 * MIB + 8 * parts.size),
        name="finish",
    )(parts)


def body(movie, shifts, filters, weights, slot_owner, slot_local):
    part_frames, planes, rows, width = movie.shape
    tiles = lax.axis_size("tile")
    parts = lax.axis_size("frame")
    frames = part_frames * parts
    slots = weights.shape[0]
    ends = tiles - 1
    tile = lax.axis_index("tile")
    place = jnp.stack([tile * rows, tiles * rows, lax.axis_index("frame"), tile]).astype(jnp.int32)
    far, close = list(range(tiles // 2, tiles)), list(range(1, tiles // 2))
    order = close[1:2] + far[-2:] + far[:1] + far[-3:0:-1] + close[:1] + close[2:] + [0]
    owner, local = slot_owner.reshape(1, slots), slot_local.reshape(1, slots)
    pair, other = edges(movie, place)
    packed = pack(weights, owner, local, order, planes, place)
    swaps = [(i, i + 1) for i in range(1, ends, 2)]
    other = lax.ppermute(other, "tile", swaps + [(j, i) for i, j in swaps])
    pair = lax.ppermute(pair, "tile", [(i, i ^ 1) for i in range(tiles)])
    landed = [
        lax.ppermute(cells, "tile", [(i, i ^ k) for i in range(tiles)]) if k else cells
        for k, cells in zip(order, packed)
    ]
    pieces = smooth(movie, pair, other, shifts.T, place, parts)
    pieces = [
        lax.ppermute(pieces[k], "frame", [(i, i ^ k) for i in range(parts)]) for k in range(parts - 1, 0, -1)
    ] + [pieces[0]]
    spikes = deconvolve(spread(build_kernel(filters, frames), place, part_frames), pieces, landed[: len(far)])
    traces = pool(spikes, landed, order, place, frames, parts * tiles)
    traces = lax.all_to_all(traces, ("frame", "tile"), split_axis=0, concat_axis=0, tiled=True)
    return finish(traces, frames)


def solution(mesh):
    in_specs = (
        P("frame", None, "tile", None),
        P("frame", None),
        P(),
        P(("frame", "tile"), None),
        P(("frame", "tile"), None),
        P(("frame", "tile"), None),
    )
    out_specs = P(("frame", "tile"), None)
    return jax.shard_map(body, mesh=mesh, in_specs=in_specs, out_specs=out_specs, check_vma=False)
```

```python
import functools

import jax
import jax.numpy as jnp
import numpy as np
from jax import lax
from jax.experimental import pallas as pl
from jax.experimental.pallas import tpu as pltpu
from jax.sharding import PartitionSpec as P

COMP_DEV = 32
TAPS = 64
MAXS = 8
RAD = 3
LANES = 128
GROUP = 16
HALO = 16
OCTET = 8
QUAD = 4
MIB = 1 << 20


smooth_sigma = 1.0


def gauss_taps():
    positions = np.arange(-RAD, RAD + 1).astype(np.float32)
    values = np.exp(-positions * positions / np.float32(2.0 * smooth_sigma * smooth_sigma))
    return (values / values.sum(dtype=np.float32)).astype(np.float32)


def build_kernel(filters, count):
    later = jnp.arange(count)[:, None]
    earlier = jnp.arange(count)[None, :]
    offsets = later - earlier
    onehot = (offsets[:, :, None] == jnp.arange(TAPS)[None, None, :]).astype(jnp.float32)
    return jnp.sum(onehot[None] * filters[:, None, None, :], axis=-1).astype(jnp.bfloat16)


def whole_vmem(count):
    return [pl.BlockSpec(memory_space=pltpu.VMEM)] * count


def params(limit):
    return pltpu.CompilerParams(vmem_limit_bytes=limit)


def edges_kernel(place_ref, movie_ref, pair_ref, other_ref):
    frames, planes, rows, _ = movie_ref.shape
    even = place_ref[3] % 2 == 0

    def one(frame, carry):
        last = [movie_ref[frame, plane, rows - HALO :, :].astype(jnp.float32) for plane in range(planes)]
        first = [movie_ref[frame, plane, :HALO, :].astype(jnp.float32) for plane in range(planes)]
        last = [cells[OCTET:] for cells in last] + [cells[QUAD:OCTET] for cells in last]
        first = [cells[:OCTET] for cells in first] + [cells[OCTET : OCTET + QUAD] for cells in first]
        last = jnp.concatenate(last, axis=0)
        first = jnp.concatenate(first, axis=0)
        pair_ref[frame] = jnp.where(even, last, first).astype(jnp.bfloat16)
        other_ref[frame] = jnp.where(even, first, last).astype(jnp.bfloat16)
        return carry

    lax.fori_loop(0, frames, one, 0)


def edges(movie, place):
    frames, planes, _, width = movie.shape
    shape = jax.ShapeDtypeStruct((frames, planes * (OCTET + QUAD), width), jnp.bfloat16)
    return pl.pallas_call(
        edges_kernel,
        out_shape=[shape, shape],
        in_specs=[pl.BlockSpec(memory_space=pltpu.SMEM)] + whole_vmem(1),
        out_specs=whole_vmem(2),
        compiler_params=params(40 * MIB),
        name="edges",
    )(place, movie)


def pack_kernel(order, planes, place_ref, weights_ref, owner_ref, local_ref, *refs):
    *out_refs, ids = refs
    tiles = len(order)
    slots, pixels = weights_ref.shape
    octets = pixels // (planes * tiles * LANES)
    tail = planes * octets * slots
    ids[...] = jnp.zeros_like(ids)
    ids[0:1, 0:slots] = owner_ref[...].astype(jnp.float32)
    ids[1:2, 0:slots] = local_ref[...].astype(jnp.float32)
    for k, out_ref in zip(order, out_refs):
        dest = place_ref[3] ^ k
        for plane in range(planes):
            for octet in range(octets):
                lane = pl.multiple_of(((plane * tiles + dest) * octets + octet) * LANES, LANES)
                row = (plane * octets + octet) * slots
                out_ref[row : row + slots, :] = weights_ref[:, pl.ds(lane, LANES)]
        out_ref[tail:, :] = ids[...].astype(jnp.bfloat16)


def pack(weights, owner, local, order, planes, place):
    slots, pixels = weights.shape
    tiles = len(order)
    shape = jax.ShapeDtypeStruct((pixels // (tiles * LANES) * slots + GROUP, LANES), jnp.bfloat16)
    return pl.pallas_call(
        functools.partial(pack_kernel, order, planes),
        out_shape=[shape] * tiles,
        in_specs=[pl.BlockSpec(memory_space=pltpu.SMEM)] + whole_vmem(3),
        out_specs=whole_vmem(tiles),
        scratch_shapes=[pltpu.VMEM((GROUP, LANES), jnp.float32)],
        compiler_params=params(8 * MIB + 5 * weights.size),
        name="pack_weights",
    )(place, weights, owner, local)


def smooth_kernel(shift_ref, place_ref, movie_ref, other_ref, pair_ref, *refs):
    *out_refs, band, wide = refs
    frames, planes, rows, width = movie_ref.shape
    blocks = width // LANES
    reach = rows + 2 * HALO
    parts = len(out_refs)
    each = blocks // parts
    together = wide.shape[0]
    taps = gauss_taps()
    high = [float(v) for v in taps.astype(jnp.bfloat16)]
    low = [float(v) for v in taps - taps.astype(jnp.bfloat16).astype(np.float32)]
    lane = lax.broadcasted_iota(jnp.int32, (reach, LANES), 1)
    row = lax.broadcasted_iota(jnp.int32, (reach, LANES), 0)
    first_row, total_rows, me = place_ref[0], place_ref[1], place_ref[2]
    even = place_ref[3] % 2 == 0

    tap = lax.broadcasted_iota(jnp.int32, (2 * LANES, LANES), 0) - lax.broadcasted_iota(jnp.int32, (2 * LANES, LANES), 1)
    tap = tap - (MAXS - RAD)
    for side, values in enumerate((high, low)):
        cells = jnp.zeros((2 * LANES, LANES), jnp.float32)
        for i, value in enumerate(values):
            cells = jnp.where(tap == i, value, cells)
        band[:, side * LANES : (side + 1) * LANES] = cells.astype(jnp.bfloat16)

    def some(step, carry):
        chosen = [step * together + u for u in range(together)]
        stacked = []
        for frame in chosen:
            right = shift_ref[1, frame] + MAXS
            near = lane < right
            zero = jnp.zeros((reach, LANES), jnp.float32)
            for plane in range(planes):
                moved = []
                for b in range(blocks):
                    cells = slice(b * LANES, (b + 1) * LANES)
                    pair = pair_ref[frame, :, cells].astype(jnp.float32)
                    other = other_ref[frame, :, cells].astype(jnp.float32)
                    top = jnp.where(even, other, pair)
                    bottom = jnp.where(even, pair, other)
                    full = slice(plane * OCTET, (plane + 1) * OCTET)
                    rest = slice(planes * OCTET + plane * QUAD, planes * OCTET + (plane + 1) * QUAD)
                    piece = jnp.concatenate(
                        [
                            top[rest],
                            top[rest],
                            top[full],
                            movie_ref[frame, plane, :, cells].astype(jnp.float32),
                            bottom[full],
                            bottom[rest],
                            bottom[rest],
                        ],
                        axis=0,
                    )
                    moved.append(pltpu.roll(piece, right, 1))
                shifted = []
                for b in range(blocks + 1):
                    before = moved[b - 1] if b > 0 else zero
                    own = moved[b] if b < blocks else zero
                    cells = jnp.where(near, before, own)
                    if b == 0:
                        cells = jnp.where(lane < MAXS, 0.0, cells)
                    if b == blocks:
                        cells = jnp.where(lane < MAXS, cells, 0.0)
                    shifted.append(cells.astype(jnp.bfloat16))
                stacked += [jnp.concatenate(shifted[b : b + 2], axis=1) for b in range(blocks)]
        result = jnp.dot(jnp.concatenate(stacked, axis=0), band[...], preferred_element_type=jnp.float32)
        result = result[:, :LANES] + result[:, LANES:]
        for u, frame in enumerate(chosen):
            place = first_row + row - HALO + shift_ref[0, frame]
            inside = (place >= 0) & (place < total_rows)
            for plane in range(planes):
                for b in range(blocks):
                    at = ((u * planes + plane) * blocks + b) * reach
                    wide[u, plane, b] = jnp.where(inside, result[at : at + reach], 0.0)
        for u, frame in enumerate(chosen):
            start = HALO - RAD - shift_ref[0, frame]
            for plane in range(planes):
                for k in range(parts):
                    for j in range(each):
                        b = (me ^ k) * each + j
                        total = float(taps[RAD]) * wide[u, plane, b, pl.ds(start + RAD, rows), :]
                        for i in range(RAD):
                            pair = wide[u, plane, b, pl.ds(start + i, rows), :]
                            pair = pair + wide[u, plane, b, pl.ds(start + 2 * RAD - i, rows), :]
                            total = total + float(taps[i]) * pair
                        out_refs[k][frame, plane, :, j * LANES : (j + 1) * LANES] = total.astype(jnp.bfloat16)
        return carry

    lax.fori_loop(0, frames // together, some, 0)


def smooth(movie, pair, other, shifts, place, parts):
    frames, planes, rows, width = movie.shape
    reach = rows + 2 * HALO
    smem = pl.BlockSpec(memory_space=pltpu.SMEM)
    return pl.pallas_call(
        smooth_kernel,
        out_shape=[jax.ShapeDtypeStruct((frames, planes, rows, width // parts), jnp.bfloat16)] * parts,
        in_specs=[smem, smem] + whole_vmem(3),
        out_specs=whole_vmem(parts),
        scratch_shapes=[
            pltpu.VMEM((2 * LANES, 2 * LANES), jnp.bfloat16),
            pltpu.VMEM((2 - frames % 2, planes, width // LANES, reach, LANES), jnp.float32),
        ],
        compiler_params=params(20 * MIB + 8 * movie.size),
        name="smooth",
    )(shifts, place, movie, other, pair)


def spread_kernel(part_frames, place_ref, kernel_ref, out_ref):
    planes, size, _ = out_ref.shape
    frames = size // GROUP
    me = place_ref[2]
    row = lax.broadcasted_iota(jnp.int32, (size, frames), 0)
    column = lax.broadcasted_iota(jnp.int32, (size, frames), 1)
    tall = (row % frames == column).astype(jnp.bfloat16)
    row = lax.broadcasted_iota(jnp.int32, (frames, size), 0)
    column = lax.broadcasted_iota(jnp.int32, (frames, size), 1) // GROUP
    last = frames // part_frames - 1
    column = ((last - column // part_frames) ^ me) * part_frames + column % part_frames
    flat = (column == row).astype(jnp.bfloat16)
    row = lax.broadcasted_iota(jnp.int32, (size, size), 0)
    column = lax.broadcasted_iota(jnp.int32, (size, size), 1)
    same = row // frames == column % GROUP
    for plane in range(planes):
        left = jnp.dot(tall, kernel_ref[plane], preferred_element_type=jnp.float32).astype(jnp.bfloat16)
        full = jnp.dot(left, flat, preferred_element_type=jnp.float32)
        out_ref[plane] = jnp.where(same, full, 0.0).astype(jnp.bfloat16)


def spread(kernel, place, part_frames):
    planes, frames, _ = kernel.shape
    size = frames * GROUP
    return pl.pallas_call(
        functools.partial(spread_kernel, part_frames),
        out_shape=jax.ShapeDtypeStruct((planes, size, size), jnp.bfloat16),
        in_specs=[pl.BlockSpec(memory_space=pltpu.SMEM)] + whole_vmem(1),
        out_specs=whole_vmem(1)[0],
        compiler_params=params(8 * MIB + 16 * size * size),
        name="spread_filters",
    )(place, kernel)


def swap_lanes(pieces):
    count = len(pieces)
    group = LANES // count
    half = count // 2
    lane = lax.broadcasted_iota(jnp.int32, pieces[0].shape, 1) // group
    while half >= 1:
        low = (lane & half) == 0
        result = list(pieces)
        for i in range(count):
            if i & half:
                continue
            a, b = pieces[i], pieces[i + half]
            if 2 * half == count:
                back = pltpu.roll(b, half * group, 1)
                ahead = pltpu.roll(a, half * group, 1)
            else:
                back = pltpu.roll(b, half * group, 1)
                ahead = pltpu.roll(a, LANES - half * group, 1)
            result[i] = jnp.where(low, a, back)
            result[i + half] = jnp.where(low, ahead, b)
        pieces = result
        half //= 2
    return pieces


def deconvolve_kernel(parts, spread_ref, *refs):
    data_refs, out_ref = refs[:parts], refs[-1]
    part_frames, planes, rows, width = data_refs[0].shape
    size = spread_ref.shape[1]
    frames = size // GROUP
    octets = rows // OCTET
    for q in range(width // LANES):
        lanes = slice(q * LANES, (q + 1) * LANES)
        for plane in range(planes):
            for first in range(0, rows // GROUP, 2):
                cells = []
                for a in (first, first + 1):
                    pieces = [ref[:, plane, a * GROUP : (a + 1) * GROUP, lanes] for ref in data_refs]
                    cells.append(jnp.concatenate(pieces, axis=0).reshape(size, LANES))
                cells = jnp.concatenate(cells, axis=1)
                spikes = jnp.dot(spread_ref[plane], cells, preferred_element_type=jnp.float32)
                spikes = jnp.maximum(spikes, 0.0)
                for a in (0, 1):
                    for half in (0, 1):
                        pieces = [
                            spikes[(half * OCTET + r) * frames : (half * OCTET + r + 1) * frames, a * LANES : (a + 1) * LANES]
                            for r in range(OCTET)
                        ]
                        octet = plane * octets + (first + a) * 2 + half
                        for j, piece in enumerate(swap_lanes(pieces)):
                            out_ref[q, octet, j * frames : (j + 1) * frames, :] = piece.astype(jnp.bfloat16)


def deconvolve(spread_filters, data, after):
    part_frames, planes, rows, width = data[0].shape
    frames = part_frames * len(data)
    shape = (width // LANES, planes * rows // OCTET, OCTET * frames, LANES)
    return pl.pallas_call(
        functools.partial(deconvolve_kernel, len(data)),
        out_shape=jax.ShapeDtypeStruct(shape, jnp.bfloat16),
        in_specs=whole_vmem(1 + len(data)) + [pl.BlockSpec(memory_space=pl.ANY)] * len(after),
        out_specs=whole_vmem(1)[0],
        compiler_params=params(12 * MIB + 4 * (spread_filters.size + 2 * len(data) * data[0].size)),
        name="deconvolve",
    )(spread_filters, *data, *after)


def pool_kernel(order, place_ref, spikes_ref, *refs):
    *weights_refs, out_ref = refs
    blocks, steps, height, _ = spikes_ref.shape
    tiles = len(weights_refs)
    me = place_ref[3]
    near = tiles // blocks
    frames = height // near
    tail = weights_refs[0].shape[0] - GROUP
    slots = tail // steps
    owners, owner_rows, _ = out_ref.shape
    owned = owners * owner_rows
    eye = lax.broadcasted_iota(jnp.int32, (slots, LANES), 0) == lax.broadcasted_iota(jnp.int32, (slots, LANES), 1)
    keys, groups = [], []
    for ref in weights_refs:
        ids = ref[tail : tail + GROUP, :].astype(jnp.float32)
        owner = jnp.sum(jnp.where(eye, ids[0:1, :], 0.0), axis=1, keepdims=True).astype(jnp.int32)
        local = jnp.sum(jnp.where(eye, ids[1:2, :], 0.0), axis=1, keepdims=True).astype(jnp.int32)
        keys.append(owner * owner_rows + local % owner_rows)
        groups.append(local // owner_rows)
    key = jnp.concatenate(keys, axis=0)
    group = jnp.concatenate(groups, axis=0)
    onehot = (lax.broadcasted_iota(jnp.int32, (tiles * slots, owned), 1) == key).astype(jnp.bfloat16)
    total = jnp.zeros((owned, LANES), jnp.float32)
    for q in range(blocks):
        pooled = jnp.zeros((tiles * slots, height), jnp.float32)
        for step in range(0, steps, 2):
            left = jnp.concatenate(
                [
                    jnp.concatenate([ref[at * slots : (at + 1) * slots, :] for ref in weights_refs], axis=0)
                    for at in (step, step + 1)
                ],
                axis=1,
            )
            right = jnp.concatenate([spikes_ref[q, step], spikes_ref[q, step + 1]], axis=1)
            pooled = pooled + lax.dot_general(
                left, right, (((1,), (1,)), ((), ())), preferred_element_type=jnp.float32
            )
        column = lax.broadcasted_iota(jnp.int32, (slots, height), 1) // frames + q * near
        pooled = jnp.concatenate(
            [jnp.where(column == me ^ k, pooled[i * slots : (i + 1) * slots], 0.0) for i, k in enumerate(order)], axis=0
        )
        partial = pooled[:, 0:LANES]
        for at in range(LANES, height, LANES):
            partial = partial + pooled[:, at : at + LANES]
        step = LANES // 2
        while step >= frames:
            partial = partial + pltpu.roll(partial, step, 1)
            step //= 2
        lane_group = lax.broadcasted_iota(jnp.int32, partial.shape, 1) // frames
        partial = jnp.where(lane_group == group, partial, 0.0)
        high = partial.astype(jnp.bfloat16)
        low = (partial - high.astype(jnp.float32)).astype(jnp.bfloat16)
        both = lax.dot_general(
            onehot,
            jnp.concatenate([high, low], axis=1),
            (((0,), (0,)), ((), ())),
            preferred_element_type=jnp.float32,
        )
        total = total + both[:, :LANES] + both[:, LANES:]
    out_ref[...] = total.reshape(owners, owner_rows, LANES)


def pool(spikes, weights, order, place, frames, owners):
    shape = (owners, COMP_DEV * frames // LANES, LANES)
    inputs = [spikes, *weights]
    return pl.pallas_call(
        functools.partial(pool_kernel, order),
        out_shape=jax.ShapeDtypeStruct(shape, jnp.float32),
        in_specs=[pl.BlockSpec(memory_space=pltpu.SMEM)] + whole_vmem(len(inputs)),
        out_specs=whole_vmem(1)[0],
        compiler_params=params(16 * MIB + 4 * sum(cells.size for cells in inputs)),
        name="pool",
    )(place, *inputs)


def finish_kernel(parts_ref, out_ref):
    sources, rows, _ = parts_ref.shape
    frames = out_ref.shape[1]
    total = jnp.sum(parts_ref[...], axis=0)
    for group in range(LANES // frames):
        out_ref[group * rows : (group + 1) * rows, :] = total[:, group * frames : (group + 1) * frames]


def finish(parts, frames):
    return pl.pallas_call(
        finish_kernel,
        out_shape=jax.ShapeDtypeStruct((COMP_DEV, frames), jnp.float32),
        in_specs=whole_vmem(1),
        out_specs=whole_vmem(1)[0],
        compiler_params=params(8 * MIB + 8 * parts.size),
        name="finish",
    )(parts)


def body(movie, shifts, filters, weights, slot_owner, slot_local):
    part_frames, planes, rows, width = movie.shape
    tiles = lax.axis_size("tile")
    parts = lax.axis_size("frame")
    frames = part_frames * parts
    slots = weights.shape[0]
    ends = tiles - 1
    tile = lax.axis_index("tile")
    place = jnp.stack([tile * rows, tiles * rows, lax.axis_index("frame"), tile]).astype(jnp.int32)
    far, close = list(range(tiles // 2, tiles)), list(range(1, tiles // 2))
    order = close[1:2] + far[-2:] + close[:1] + far[:1] + far[-3:0:-1] + close[2:] + [0]
    owner, local = slot_owner.reshape(1, slots), slot_local.reshape(1, slots)
    pair, other = edges(movie, place)
    packed = pack(weights, owner, local, order, planes, place)
    swaps = [(i, i + 1) for i in range(1, ends, 2)]
    other = lax.ppermute(other, "tile", swaps + [(j, i) for i, j in swaps])
    pair = lax.ppermute(pair, "tile", [(i, i ^ 1) for i in range(tiles)])
    landed = [
        lax.ppermute(cells, "tile", [(i, i ^ k) for i in range(tiles)]) if k else cells
        for k, cells in zip(order, packed)
    ]
    pieces = smooth(movie, pair, other, shifts.T, place, parts)
    pieces = [
        lax.ppermute(pieces[k], "frame", [(i, i ^ k) for i in range(parts)]) for k in range(parts - 1, 0, -1)
    ] + [pieces[0]]
    spikes = deconvolve(spread(build_kernel(filters, frames), place, part_frames), pieces, landed[: len(far) + 1])
    traces = pool(spikes, landed, order, place, frames, parts * tiles)
    traces = lax.all_to_all(traces, ("frame", "tile"), split_axis=0, concat_axis=0, tiled=True)
    return finish(traces, frames)


def solution(mesh):
    in_specs = (
        P("frame", None, "tile", None),
        P("frame", None),
        P(),
        P(("frame", "tile"), None),
        P(("frame", "tile"), None),
        P(("frame", "tile"), None),
    )
    out_specs = P(("frame", "tile"), None)
    return jax.shard_map(body, mesh=mesh, in_specs=in_specs, out_specs=out_specs, check_vma=False)
```

```python
import functools

import jax
import jax.numpy as jnp
import numpy as np
from jax import lax
from jax.experimental import pallas as pl
from jax.experimental.pallas import tpu as pltpu
from jax.sharding import PartitionSpec as P

COMP_DEV = 32
TAPS = 64
MAXS = 8
RAD = 3
LANES = 128
GROUP = 16
HALO = 16
OCTET = 8
QUAD = 4
MIB = 1 << 20


smooth_sigma = 1.0


def gauss_taps():
    positions = np.arange(-RAD, RAD + 1).astype(np.float32)
    values = np.exp(-positions * positions / np.float32(2.0 * smooth_sigma * smooth_sigma))
    return (values / values.sum(dtype=np.float32)).astype(np.float32)


def build_kernel(filters, count):
    later = jnp.arange(count)[:, None]
    earlier = jnp.arange(count)[None, :]
    offsets = later - earlier
    onehot = (offsets[:, :, None] == jnp.arange(TAPS)[None, None, :]).astype(jnp.float32)
    return jnp.sum(onehot[None] * filters[:, None, None, :], axis=-1).astype(jnp.bfloat16)


def whole_vmem(count):
    return [pl.BlockSpec(memory_space=pltpu.VMEM)] * count


def params(limit):
    return pltpu.CompilerParams(vmem_limit_bytes=limit)


def edges_kernel(place_ref, movie_ref, pair_ref, other_ref):
    frames, planes, rows, _ = movie_ref.shape
    even = place_ref[3] % 2 == 0

    def one(frame, carry):
        last = [movie_ref[frame, plane, rows - HALO :, :].astype(jnp.float32) for plane in range(planes)]
        first = [movie_ref[frame, plane, :HALO, :].astype(jnp.float32) for plane in range(planes)]
        last = [cells[OCTET:] for cells in last] + [cells[QUAD:OCTET] for cells in last]
        first = [cells[:OCTET] for cells in first] + [cells[OCTET : OCTET + QUAD] for cells in first]
        last = jnp.concatenate(last, axis=0)
        first = jnp.concatenate(first, axis=0)
        pair_ref[frame] = jnp.where(even, last, first).astype(jnp.bfloat16)
        other_ref[frame] = jnp.where(even, first, last).astype(jnp.bfloat16)
        return carry

    lax.fori_loop(0, frames, one, 0)


def edges(movie, place):
    frames, planes, _, width = movie.shape
    shape = jax.ShapeDtypeStruct((frames, planes * (OCTET + QUAD), width), jnp.bfloat16)
    return pl.pallas_call(
        edges_kernel,
        out_shape=[shape, shape],
        in_specs=[pl.BlockSpec(memory_space=pltpu.SMEM)] + whole_vmem(1),
        out_specs=whole_vmem(2),
        compiler_params=params(40 * MIB),
        name="edges",
    )(place, movie)


def pack_kernel(order, planes, place_ref, weights_ref, owner_ref, local_ref, *refs):
    *out_refs, ids = refs
    tiles = len(order)
    slots, pixels = weights_ref.shape
    octets = pixels // (planes * tiles * LANES)
    tail = planes * octets * slots
    ids[...] = jnp.zeros_like(ids)
    ids[0:1, 0:slots] = owner_ref[...].astype(jnp.float32)
    ids[1:2, 0:slots] = local_ref[...].astype(jnp.float32)
    for k, out_ref in zip(order, out_refs):
        dest = place_ref[3] ^ k
        for plane in range(planes):
            for octet in range(octets):
                lane = pl.multiple_of(((plane * tiles + dest) * octets + octet) * LANES, LANES)
                row = (plane * octets + octet) * slots
                out_ref[row : row + slots, :] = weights_ref[:, pl.ds(lane, LANES)]
        out_ref[tail:, :] = ids[...].astype(jnp.bfloat16)


def pack(weights, owner, local, order, planes, place):
    slots, pixels = weights.shape
    tiles = len(order)
    shape = jax.ShapeDtypeStruct((pixels // (tiles * LANES) * slots + GROUP, LANES), jnp.bfloat16)
    return pl.pallas_call(
        functools.partial(pack_kernel, order, planes),
        out_shape=[shape] * tiles,
        in_specs=[pl.BlockSpec(memory_space=pltpu.SMEM)] + whole_vmem(3),
        out_specs=whole_vmem(tiles),
        scratch_shapes=[pltpu.VMEM((GROUP, LANES), jnp.float32)],
        compiler_params=params(8 * MIB + 5 * weights.size),
        name="pack_weights",
    )(place, weights, owner, local)


def smooth_kernel(shift_ref, place_ref, movie_ref, other_ref, pair_ref, *refs):
    *out_refs, band, wide = refs
    frames, planes, rows, width = movie_ref.shape
    blocks = width // LANES
    reach = rows + 2 * HALO
    parts = len(out_refs)
    each = blocks // parts
    together = wide.shape[0]
    taps = gauss_taps()
    high = [float(v) for v in taps.astype(jnp.bfloat16)]
    low = [float(v) for v in taps - taps.astype(jnp.bfloat16).astype(np.float32)]
    lane = lax.broadcasted_iota(jnp.int32, (reach, LANES), 1)
    row = lax.broadcasted_iota(jnp.int32, (reach, LANES), 0)
    first_row, total_rows, me = place_ref[0], place_ref[1], place_ref[2]
    even = place_ref[3] % 2 == 0

    tap = lax.broadcasted_iota(jnp.int32, (2 * LANES, LANES), 0) - lax.broadcasted_iota(jnp.int32, (2 * LANES, LANES), 1)
    tap = tap - (MAXS - RAD)
    for side, values in enumerate((high, low)):
        cells = jnp.zeros((2 * LANES, LANES), jnp.float32)
        for i, value in enumerate(values):
            cells = jnp.where(tap == i, value, cells)
        band[:, side * LANES : (side + 1) * LANES] = cells.astype(jnp.bfloat16)

    def some(step, carry):
        chosen = [step * together + u for u in range(together)]
        stacked = []
        for frame in chosen:
            right = shift_ref[1, frame] + MAXS
            near = lane < right
            zero = jnp.zeros((reach, LANES), jnp.float32)
            for plane in range(planes):
                moved = []
                for b in range(blocks):
                    cells = slice(b * LANES, (b + 1) * LANES)
                    pair = pair_ref[frame, :, cells].astype(jnp.float32)
                    other = other_ref[frame, :, cells].astype(jnp.float32)
                    top = jnp.where(even, other, pair)
                    bottom = jnp.where(even, pair, other)
                    full = slice(plane * OCTET, (plane + 1) * OCTET)
                    rest = slice(planes * OCTET + plane * QUAD, planes * OCTET + (plane + 1) * QUAD)
                    piece = jnp.concatenate(
                        [
                            top[rest],
                            top[rest],
                            top[full],
                            movie_ref[frame, plane, :, cells].astype(jnp.float32),
                            bottom[full],
                            bottom[rest],
                            bottom[rest],
                        ],
                        axis=0,
                    )
                    moved.append(pltpu.roll(piece, right, 1))
                shifted = []
                for b in range(blocks + 1):
                    before = moved[b - 1] if b > 0 else zero
                    own = moved[b] if b < blocks else zero
                    cells = jnp.where(near, before, own)
                    if b == 0:
                        cells = jnp.where(lane < MAXS, 0.0, cells)
                    if b == blocks:
                        cells = jnp.where(lane < MAXS, cells, 0.0)
                    shifted.append(cells.astype(jnp.bfloat16))
                stacked += [jnp.concatenate(shifted[b : b + 2], axis=1) for b in range(blocks)]
        result = jnp.dot(jnp.concatenate(stacked, axis=0), band[...], preferred_element_type=jnp.float32)
        result = result[:, :LANES] + result[:, LANES:]
        for u, frame in enumerate(chosen):
            place = first_row + row - HALO + shift_ref[0, frame]
            inside = (place >= 0) & (place < total_rows)
            for plane in range(planes):
                for b in range(blocks):
                    at = ((u * planes + plane) * blocks + b) * reach
                    wide[u, plane, b] = jnp.where(inside, result[at : at + reach], 0.0)
        for u, frame in enumerate(chosen):
            start = HALO - RAD - shift_ref[0, frame]
            for plane in range(planes):
                for k in range(parts):
                    for j in range(each):
                        b = (me ^ k) * each + j
                        total = float(taps[RAD]) * wide[u, plane, b, pl.ds(start + RAD, rows), :]
                        for i in range(RAD):
                            pair = wide[u, plane, b, pl.ds(start + i, rows), :]
                            pair = pair + wide[u, plane, b, pl.ds(start + 2 * RAD - i, rows), :]
                            total = total + float(taps[i]) * pair
                        out_refs[k][frame, plane, :, j * LANES : (j + 1) * LANES] = total.astype(jnp.bfloat16)
        return carry

    lax.fori_loop(0, frames // together, some, 0)


def smooth(movie, pair, other, shifts, place, parts):
    frames, planes, rows, width = movie.shape
    reach = rows + 2 * HALO
    smem = pl.BlockSpec(memory_space=pltpu.SMEM)
    return pl.pallas_call(
        smooth_kernel,
        out_shape=[jax.ShapeDtypeStruct((frames, planes, rows, width // parts), jnp.bfloat16)] * parts,
        in_specs=[smem, smem] + whole_vmem(3),
        out_specs=whole_vmem(parts),
        scratch_shapes=[
            pltpu.VMEM((2 * LANES, 2 * LANES), jnp.bfloat16),
            pltpu.VMEM((2 - frames % 2, planes, width // LANES, reach, LANES), jnp.float32),
        ],
        compiler_params=params(20 * MIB + 8 * movie.size),
        name="smooth",
    )(shifts, place, movie, other, pair)


def spread_kernel(part_frames, place_ref, kernel_ref, out_ref):
    planes, size, _ = out_ref.shape
    frames = size // GROUP
    me = place_ref[2]
    row = lax.broadcasted_iota(jnp.int32, (size, frames), 0)
    column = lax.broadcasted_iota(jnp.int32, (size, frames), 1)
    tall = (row % frames == column).astype(jnp.bfloat16)
    row = lax.broadcasted_iota(jnp.int32, (frames, size), 0)
    column = lax.broadcasted_iota(jnp.int32, (frames, size), 1) // GROUP
    last = frames // part_frames - 1
    column = ((last - column // part_frames) ^ me) * part_frames + column % part_frames
    flat = (column == row).astype(jnp.bfloat16)
    row = lax.broadcasted_iota(jnp.int32, (size, size), 0)
    column = lax.broadcasted_iota(jnp.int32, (size, size), 1)
    same = row // frames == column % GROUP
    for plane in range(planes):
        left = jnp.dot(tall, kernel_ref[plane], preferred_element_type=jnp.float32).astype(jnp.bfloat16)
        full = jnp.dot(left, flat, preferred_element_type=jnp.float32)
        out_ref[plane] = jnp.where(same, full, 0.0).astype(jnp.bfloat16)


def spread(kernel, place, part_frames):
    planes, frames, _ = kernel.shape
    size = frames * GROUP
    return pl.pallas_call(
        functools.partial(spread_kernel, part_frames),
        out_shape=jax.ShapeDtypeStruct((planes, size, size), jnp.bfloat16),
        in_specs=[pl.BlockSpec(memory_space=pltpu.SMEM)] + whole_vmem(1),
        out_specs=whole_vmem(1)[0],
        compiler_params=params(8 * MIB + 16 * size * size),
        name="spread_filters",
    )(place, kernel)


def swap_lanes(pieces):
    count = len(pieces)
    group = LANES // count
    half = count // 2
    lane = lax.broadcasted_iota(jnp.int32, pieces[0].shape, 1) // group
    while half >= 1:
        low = (lane & half) == 0
        result = list(pieces)
        for i in range(count):
            if i & half:
                continue
            a, b = pieces[i], pieces[i + half]
            if 2 * half == count:
                back = pltpu.roll(b, half * group, 1)
                ahead = pltpu.roll(a, half * group, 1)
            else:
                back = pltpu.roll(b, half * group, 1)
                ahead = pltpu.roll(a, LANES - half * group, 1)
            result[i] = jnp.where(low, a, back)
            result[i + half] = jnp.where(low, ahead, b)
        pieces = result
        half //= 2
    return pieces


def deconvolve_kernel(parts, spread_ref, *refs):
    data_refs, out_ref = refs[:parts], refs[-1]
    part_frames, planes, rows, width = data_refs[0].shape
    size = spread_ref.shape[1]
    frames = size // GROUP
    octets = rows // OCTET
    for q in range(width // LANES):
        lanes = slice(q * LANES, (q + 1) * LANES)
        for plane in range(planes):
            for first in range(0, rows // GROUP, 2):
                cells = []
                for a in (first, first + 1):
                    pieces = [ref[:, plane, a * GROUP : (a + 1) * GROUP, lanes] for ref in data_refs]
                    cells.append(jnp.concatenate(pieces, axis=0).reshape(size, LANES))
                cells = jnp.concatenate(cells, axis=1)
                spikes = jnp.dot(spread_ref[plane], cells, preferred_element_type=jnp.float32)
                spikes = jnp.maximum(spikes, 0.0)
                for a in (0, 1):
                    for half in (0, 1):
                        pieces = [
                            spikes[(half * OCTET + r) * frames : (half * OCTET + r + 1) * frames, a * LANES : (a + 1) * LANES]
                            for r in range(OCTET)
                        ]
                        octet = plane * octets + (first + a) * 2 + half
                        for j, piece in enumerate(swap_lanes(pieces)):
                            out_ref[q, octet, j * frames : (j + 1) * frames, :] = piece.astype(jnp.bfloat16)


def deconvolve(spread_filters, data, after):
    part_frames, planes, rows, width = data[0].shape
    frames = part_frames * len(data)
    shape = (width // LANES, planes * rows // OCTET, OCTET * frames, LANES)
    return pl.pallas_call(
        functools.partial(deconvolve_kernel, len(data)),
        out_shape=jax.ShapeDtypeStruct(shape, jnp.bfloat16),
        in_specs=whole_vmem(1 + len(data)) + [pl.BlockSpec(memory_space=pl.ANY)] * len(after),
        out_specs=whole_vmem(1)[0],
        compiler_params=params(12 * MIB + 4 * (spread_filters.size + 2 * len(data) * data[0].size)),
        name="deconvolve",
    )(spread_filters, *data, *after)


def pool_kernel(order, place_ref, spikes_ref, *refs):
    *weights_refs, out_ref = refs
    blocks, steps, height, _ = spikes_ref.shape
    tiles = len(weights_refs)
    me = place_ref[3]
    near = tiles // blocks
    frames = height // near
    tail = weights_refs[0].shape[0] - GROUP
    slots = tail // steps
    owners, owner_rows, _ = out_ref.shape
    owned = owners * owner_rows
    eye = lax.broadcasted_iota(jnp.int32, (slots, LANES), 0) == lax.broadcasted_iota(jnp.int32, (slots, LANES), 1)
    keys, groups = [], []
    for ref in weights_refs:
        ids = ref[tail : tail + GROUP, :].astype(jnp.float32)
        owner = jnp.sum(jnp.where(eye, ids[0:1, :], 0.0), axis=1, keepdims=True).astype(jnp.int32)
        local = jnp.sum(jnp.where(eye, ids[1:2, :], 0.0), axis=1, keepdims=True).astype(jnp.int32)
        keys.append(owner * owner_rows + local % owner_rows)
        groups.append(local // owner_rows)
    key = jnp.concatenate(keys, axis=0)
    group = jnp.concatenate(groups, axis=0)
    onehot = (lax.broadcasted_iota(jnp.int32, (tiles * slots, owned), 1) == key).astype(jnp.bfloat16)
    total = jnp.zeros((owned, LANES), jnp.float32)
    for q in range(blocks):
        pooled = jnp.zeros((tiles * slots, height), jnp.float32)
        for step in range(0, steps, 2):
            left = jnp.concatenate(
                [
                    jnp.concatenate([ref[at * slots : (at + 1) * slots, :] for ref in weights_refs], axis=0)
                    for at in (step, step + 1)
                ],
                axis=1,
            )
            right = jnp.concatenate([spikes_ref[q, step], spikes_ref[q, step + 1]], axis=1)
            pooled = pooled + lax.dot_general(
                left, right, (((1,), (1,)), ((), ())), preferred_element_type=jnp.float32
            )
        column = lax.broadcasted_iota(jnp.int32, (slots, height), 1) // frames + q * near
        pooled = jnp.concatenate(
            [jnp.where(column == me ^ k, pooled[i * slots : (i + 1) * slots], 0.0) for i, k in enumerate(order)], axis=0
        )
        partial = pooled[:, 0:LANES]
        for at in range(LANES, height, LANES):
            partial = partial + pooled[:, at : at + LANES]
        step = LANES // 2
        while step >= frames:
            partial = partial + pltpu.roll(partial, step, 1)
            step //= 2
        lane_group = lax.broadcasted_iota(jnp.int32, partial.shape, 1) // frames
        partial = jnp.where(lane_group == group, partial, 0.0)
        high = partial.astype(jnp.bfloat16)
        low = (partial - high.astype(jnp.float32)).astype(jnp.bfloat16)
        both = lax.dot_general(
            onehot,
            jnp.concatenate([high, low], axis=1),
            (((0,), (0,)), ((), ())),
            preferred_element_type=jnp.float32,
        )
        total = total + both[:, :LANES] + both[:, LANES:]
    out_ref[...] = total.reshape(owners, owner_rows, LANES)


def pool(spikes, weights, order, place, frames, owners):
    shape = (owners, COMP_DEV * frames // LANES, LANES)
    inputs = [spikes, *weights]
    return pl.pallas_call(
        functools.partial(pool_kernel, order),
        out_shape=jax.ShapeDtypeStruct(shape, jnp.float32),
        in_specs=[pl.BlockSpec(memory_space=pltpu.SMEM)] + whole_vmem(len(inputs)),
        out_specs=whole_vmem(1)[0],
        compiler_params=params(16 * MIB + 4 * sum(cells.size for cells in inputs)),
        name="pool",
    )(place, *inputs)


def finish_kernel(parts_ref, out_ref):
    sources, rows, _ = parts_ref.shape
    frames = out_ref.shape[1]
    total = jnp.sum(parts_ref[...], axis=0)
    for group in range(LANES // frames):
        out_ref[group * rows : (group + 1) * rows, :] = total[:, group * frames : (group + 1) * frames]


def finish(parts, frames):
    return pl.pallas_call(
        finish_kernel,
        out_shape=jax.ShapeDtypeStruct((COMP_DEV, frames), jnp.float32),
        in_specs=whole_vmem(1),
        out_specs=whole_vmem(1)[0],
        compiler_params=params(8 * MIB + 8 * parts.size),
        name="finish",
    )(parts)


def body(movie, shifts, filters, weights, slot_owner, slot_local):
    part_frames, planes, rows, width = movie.shape
    tiles = lax.axis_size("tile")
    parts = lax.axis_size("frame")
    frames = part_frames * parts
    slots = weights.shape[0]
    ends = tiles - 1
    tile = lax.axis_index("tile")
    place = jnp.stack([tile * rows, tiles * rows, lax.axis_index("frame"), tile]).astype(jnp.int32)
    far, close = list(range(tiles // 2, tiles)), list(range(1, tiles // 2))
    order = close[1:2] + far[-2:] + close[:1] + far[:1] + far[-3:0:-1] + close[2:] + [0]
    owner, local = slot_owner.reshape(1, slots), slot_local.reshape(1, slots)
    pair, other = edges(movie, place)
    packed = pack(weights, owner, local, order, planes, place)
    swaps = [(i, i + 1) for i in range(1, ends, 2)]
    other = lax.ppermute(other, "tile", swaps + [(j, i) for i, j in swaps])
    pair = lax.ppermute(pair, "tile", [(i, i ^ 1) for i in range(tiles)])
    landed = [
        lax.ppermute(cells, "tile", [(i, i ^ k) for i in range(tiles)]) if k else cells
        for k, cells in zip(order, packed)
    ]
    pieces = smooth(movie, pair, other, shifts.T, place, parts)
    pieces = [
        lax.ppermute(pieces[k], "frame", [(i, i ^ k) for i in range(parts)]) for k in range(parts - 1, 0, -1)
    ] + [pieces[0]]
    spikes = deconvolve(spread(build_kernel(filters, frames), place, part_frames), pieces, landed[: len(far)])
    traces = pool(spikes, landed, order, place, frames, parts * tiles)
    traces = lax.all_to_all(traces, ("frame", "tile"), split_axis=0, concat_axis=0, tiled=True)
    return finish(traces, frames)


def solution(mesh):
    in_specs = (
        P("frame", None, "tile", None),
        P("frame", None),
        P(),
        P(("frame", "tile"), None),
        P(("frame", "tile"), None),
        P(("frame", "tile"), None),
    )
    out_specs = P(("frame", "tile"), None)
    return jax.shard_map(body, mesh=mesh, in_specs=in_specs, out_specs=out_specs, check_vma=False)
```

```python
import functools

import jax
import jax.numpy as jnp
import numpy as np
from jax import lax
from jax.experimental import pallas as pl
from jax.experimental.pallas import tpu as pltpu
from jax.sharding import PartitionSpec as P

COMP_DEV = 32
TAPS = 64
MAXS = 8
RAD = 3
LANES = 128
GROUP = 16
HALO = 16
OCTET = 8
QUAD = 4
MIB = 1 << 20


smooth_sigma = 1.0


def gauss_taps():
    positions = np.arange(-RAD, RAD + 1).astype(np.float32)
    values = np.exp(-positions * positions / np.float32(2.0 * smooth_sigma * smooth_sigma))
    return (values / values.sum(dtype=np.float32)).astype(np.float32)


def build_kernel(filters, count):
    later = jnp.arange(count)[:, None]
    earlier = jnp.arange(count)[None, :]
    offsets = later - earlier
    onehot = (offsets[:, :, None] == jnp.arange(TAPS)[None, None, :]).astype(jnp.float32)
    return jnp.sum(onehot[None] * filters[:, None, None, :], axis=-1).astype(jnp.bfloat16)


def whole_vmem(count):
    return [pl.BlockSpec(memory_space=pltpu.VMEM)] * count


def params(limit):
    return pltpu.CompilerParams(vmem_limit_bytes=limit)


def edges_kernel(place_ref, movie_ref, pair_ref, other_ref):
    frames, planes, rows, _ = movie_ref.shape
    even = place_ref[3] % 2 == 0

    def one(frame, carry):
        last = [movie_ref[frame, plane, rows - HALO :, :].astype(jnp.float32) for plane in range(planes)]
        first = [movie_ref[frame, plane, :HALO, :].astype(jnp.float32) for plane in range(planes)]
        last = [cells[OCTET:] for cells in last] + [cells[QUAD:OCTET] for cells in last]
        first = [cells[:OCTET] for cells in first] + [cells[OCTET : OCTET + QUAD] for cells in first]
        last = jnp.concatenate(last, axis=0)
        first = jnp.concatenate(first, axis=0)
        pair_ref[frame] = jnp.where(even, last, first).astype(jnp.bfloat16)
        other_ref[frame] = jnp.where(even, first, last).astype(jnp.bfloat16)
        return carry

    lax.fori_loop(0, frames, one, 0)


def edges(movie, place):
    frames, planes, _, width = movie.shape
    shape = jax.ShapeDtypeStruct((frames, planes * (OCTET + QUAD), width), jnp.bfloat16)
    return pl.pallas_call(
        edges_kernel,
        out_shape=[shape, shape],
        in_specs=[pl.BlockSpec(memory_space=pltpu.SMEM)] + whole_vmem(1),
        out_specs=whole_vmem(2),
        compiler_params=params(40 * MIB),
        name="edges",
    )(place, movie)


def pack_kernel(order, planes, place_ref, weights_ref, owner_ref, local_ref, *refs):
    *out_refs, ids = refs
    tiles = len(order)
    slots, pixels = weights_ref.shape
    octets = pixels // (planes * tiles * LANES)
    tail = planes * octets * slots
    ids[...] = jnp.zeros_like(ids)
    ids[0:1, 0:slots] = owner_ref[...].astype(jnp.float32)
    ids[1:2, 0:slots] = local_ref[...].astype(jnp.float32)
    for k, out_ref in zip(order, out_refs):
        dest = place_ref[3] ^ k
        for plane in range(planes):
            for octet in range(octets):
                lane = pl.multiple_of(((plane * tiles + dest) * octets + octet) * LANES, LANES)
                row = (plane * octets + octet) * slots
                out_ref[row : row + slots, :] = weights_ref[:, pl.ds(lane, LANES)]
        out_ref[tail:, :] = ids[...].astype(jnp.bfloat16)


def pack(weights, owner, local, order, planes, place):
    slots, pixels = weights.shape
    tiles = len(order)
    shape = jax.ShapeDtypeStruct((pixels // (tiles * LANES) * slots + GROUP, LANES), jnp.bfloat16)
    return pl.pallas_call(
        functools.partial(pack_kernel, order, planes),
        out_shape=[shape] * tiles,
        in_specs=[pl.BlockSpec(memory_space=pltpu.SMEM)] + whole_vmem(3),
        out_specs=whole_vmem(tiles),
        scratch_shapes=[pltpu.VMEM((GROUP, LANES), jnp.float32)],
        compiler_params=params(8 * MIB + 5 * weights.size),
        name="pack_weights",
    )(place, weights, owner, local)


def smooth_kernel(shift_ref, place_ref, movie_ref, other_ref, pair_ref, *refs):
    *out_refs, band, wide = refs
    frames, planes, rows, width = movie_ref.shape
    blocks = width // LANES
    reach = rows + 2 * HALO
    parts = len(out_refs)
    each = blocks // parts
    together = wide.shape[0]
    taps = gauss_taps()
    high = [float(v) for v in taps.astype(jnp.bfloat16)]
    low = [float(v) for v in taps - taps.astype(jnp.bfloat16).astype(np.float32)]
    lane = lax.broadcasted_iota(jnp.int32, (reach, LANES), 1)
    row = lax.broadcasted_iota(jnp.int32, (reach, LANES), 0)
    first_row, total_rows, me = place_ref[0], place_ref[1], place_ref[2]
    even = place_ref[3] % 2 == 0

    tap = lax.broadcasted_iota(jnp.int32, (2 * LANES, LANES), 0) - lax.broadcasted_iota(jnp.int32, (2 * LANES, LANES), 1)
    tap = tap - (MAXS - RAD)
    for side, values in enumerate((high, low)):
        cells = jnp.zeros((2 * LANES, LANES), jnp.float32)
        for i, value in enumerate(values):
            cells = jnp.where(tap == i, value, cells)
        band[:, side * LANES : (side + 1) * LANES] = cells.astype(jnp.bfloat16)

    def some(step, carry):
        chosen = [step * together + u for u in range(together)]
        stacked = []
        for frame in chosen:
            right = shift_ref[1, frame] + MAXS
            near = lane < right
            zero = jnp.zeros((reach, LANES), jnp.float32)
            for plane in range(planes):
                moved = []
                for b in range(blocks):
                    cells = slice(b * LANES, (b + 1) * LANES)
                    pair = pair_ref[frame, :, cells].astype(jnp.float32)
                    other = other_ref[frame, :, cells].astype(jnp.float32)
                    top = jnp.where(even, other, pair)
                    bottom = jnp.where(even, pair, other)
                    full = slice(plane * OCTET, (plane + 1) * OCTET)
                    rest = slice(planes * OCTET + plane * QUAD, planes * OCTET + (plane + 1) * QUAD)
                    piece = jnp.concatenate(
                        [
                            top[rest],
                            top[rest],
                            top[full],
                            movie_ref[frame, plane, :, cells].astype(jnp.float32),
                            bottom[full],
                            bottom[rest],
                            bottom[rest],
                        ],
                        axis=0,
                    )
                    moved.append(pltpu.roll(piece, right, 1))
                shifted = []
                for b in range(blocks + 1):
                    before = moved[b - 1] if b > 0 else zero
                    own = moved[b] if b < blocks else zero
                    cells = jnp.where(near, before, own)
                    if b == 0:
                        cells = jnp.where(lane < MAXS, 0.0, cells)
                    if b == blocks:
                        cells = jnp.where(lane < MAXS, cells, 0.0)
                    shifted.append(cells.astype(jnp.bfloat16))
                stacked += [jnp.concatenate(shifted[b : b + 2], axis=1) for b in range(blocks)]
        result = jnp.dot(jnp.concatenate(stacked, axis=0), band[...], preferred_element_type=jnp.float32)
        result = result[:, :LANES] + result[:, LANES:]
        for u, frame in enumerate(chosen):
            place = first_row + row - HALO + shift_ref[0, frame]
            inside = (place >= 0) & (place < total_rows)
            for plane in range(planes):
                for b in range(blocks):
                    at = ((u * planes + plane) * blocks + b) * reach
                    wide[u, plane, b] = jnp.where(inside, result[at : at + reach], 0.0)
        for u, frame in enumerate(chosen):
            start = HALO - RAD - shift_ref[0, frame]
            for plane in range(planes):
                for k in range(parts):
                    for j in range(each):
                        b = (me ^ k) * each + j
                        total = float(taps[RAD]) * wide[u, plane, b, pl.ds(start + RAD, rows), :]
                        for i in range(RAD):
                            pair = wide[u, plane, b, pl.ds(start + i, rows), :]
                            pair = pair + wide[u, plane, b, pl.ds(start + 2 * RAD - i, rows), :]
                            total = total + float(taps[i]) * pair
                        out_refs[k][frame, plane, :, j * LANES : (j + 1) * LANES] = total.astype(jnp.bfloat16)
        return carry

    lax.fori_loop(0, frames // together, some, 0)


def smooth(movie, pair, other, shifts, place, parts):
    frames, planes, rows, width = movie.shape
    reach = rows + 2 * HALO
    smem = pl.BlockSpec(memory_space=pltpu.SMEM)
    return pl.pallas_call(
        smooth_kernel,
        out_shape=[jax.ShapeDtypeStruct((frames, planes, rows, width // parts), jnp.bfloat16)] * parts,
        in_specs=[smem, smem] + whole_vmem(3),
        out_specs=whole_vmem(parts),
        scratch_shapes=[
            pltpu.VMEM((2 * LANES, 2 * LANES), jnp.bfloat16),
            pltpu.VMEM((2 - frames % 2, planes, width // LANES, reach, LANES), jnp.float32),
        ],
        compiler_params=params(20 * MIB + 8 * movie.size),
        name="smooth",
    )(shifts, place, movie, other, pair)


def spread_kernel(part_frames, place_ref, kernel_ref, out_ref):
    planes, size, _ = out_ref.shape
    frames = size // GROUP
    me = place_ref[2]
    row = lax.broadcasted_iota(jnp.int32, (size, frames), 0)
    column = lax.broadcasted_iota(jnp.int32, (size, frames), 1)
    tall = (row % frames == column).astype(jnp.bfloat16)
    row = lax.broadcasted_iota(jnp.int32, (frames, size), 0)
    column = lax.broadcasted_iota(jnp.int32, (frames, size), 1) // GROUP
    last = frames // part_frames - 1
    column = ((last - column // part_frames) ^ me) * part_frames + column % part_frames
    flat = (column == row).astype(jnp.bfloat16)
    row = lax.broadcasted_iota(jnp.int32, (size, size), 0)
    column = lax.broadcasted_iota(jnp.int32, (size, size), 1)
    same = row // frames == column % GROUP
    for plane in range(planes):
        left = jnp.dot(tall, kernel_ref[plane], preferred_element_type=jnp.float32).astype(jnp.bfloat16)
        full = jnp.dot(left, flat, preferred_element_type=jnp.float32)
        out_ref[plane] = jnp.where(same, full, 0.0).astype(jnp.bfloat16)


def spread(kernel, place, part_frames):
    planes, frames, _ = kernel.shape
    size = frames * GROUP
    return pl.pallas_call(
        functools.partial(spread_kernel, part_frames),
        out_shape=jax.ShapeDtypeStruct((planes, size, size), jnp.bfloat16),
        in_specs=[pl.BlockSpec(memory_space=pltpu.SMEM)] + whole_vmem(1),
        out_specs=whole_vmem(1)[0],
        compiler_params=params(8 * MIB + 16 * size * size),
        name="spread_filters",
    )(place, kernel)


def swap_lanes(pieces):
    count = len(pieces)
    group = LANES // count
    half = count // 2
    lane = lax.broadcasted_iota(jnp.int32, pieces[0].shape, 1) // group
    while half >= 1:
        low = (lane & half) == 0
        result = list(pieces)
        for i in range(count):
            if i & half:
                continue
            a, b = pieces[i], pieces[i + half]
            if 2 * half == count:
                back = pltpu.roll(b, half * group, 1)
                ahead = pltpu.roll(a, half * group, 1)
            else:
                back = pltpu.roll(b, half * group, 1)
                ahead = pltpu.roll(a, LANES - half * group, 1)
            result[i] = jnp.where(low, a, back)
            result[i + half] = jnp.where(low, ahead, b)
        pieces = result
        half //= 2
    return pieces


def deconvolve_kernel(parts, spread_ref, *refs):
    data_refs, out_ref = refs[:parts], refs[-1]
    part_frames, planes, rows, width = data_refs[0].shape
    size = spread_ref.shape[1]
    frames = size // GROUP
    octets = rows // OCTET
    for q in range(width // LANES):
        lanes = slice(q * LANES, (q + 1) * LANES)
        for plane in range(planes):
            for first in range(0, rows // GROUP, 2):
                cells = []
                for a in (first, first + 1):
                    pieces = [ref[:, plane, a * GROUP : (a + 1) * GROUP, lanes] for ref in data_refs]
                    cells.append(jnp.concatenate(pieces, axis=0).reshape(size, LANES))
                cells = jnp.concatenate(cells, axis=1)
                spikes = jnp.dot(spread_ref[plane], cells, preferred_element_type=jnp.float32)
                spikes = jnp.maximum(spikes, 0.0)
                for a in (0, 1):
                    for half in (0, 1):
                        pieces = [
                            spikes[(half * OCTET + r) * frames : (half * OCTET + r + 1) * frames, a * LANES : (a + 1) * LANES]
                            for r in range(OCTET)
                        ]
                        octet = plane * octets + (first + a) * 2 + half
                        for j, piece in enumerate(swap_lanes(pieces)):
                            out_ref[q, octet, j * frames : (j + 1) * frames, :] = piece.astype(jnp.bfloat16)


def deconvolve(spread_filters, data, after):
    part_frames, planes, rows, width = data[0].shape
    frames = part_frames * len(data)
    shape = (width // LANES, planes * rows // OCTET, OCTET * frames, LANES)
    return pl.pallas_call(
        functools.partial(deconvolve_kernel, len(data)),
        out_shape=jax.ShapeDtypeStruct(shape, jnp.bfloat16),
        in_specs=whole_vmem(1 + len(data)) + [pl.BlockSpec(memory_space=pl.ANY)] * len(after),
        out_specs=whole_vmem(1)[0],
        compiler_params=params(12 * MIB + 4 * (spread_filters.size + 2 * len(data) * data[0].size)),
        name="deconvolve",
    )(spread_filters, *data, *after)


def pool_kernel(order, place_ref, spikes_ref, *refs):
    *weights_refs, out_ref = refs
    blocks, steps, height, _ = spikes_ref.shape
    tiles = len(weights_refs)
    me = place_ref[3]
    near = tiles // blocks
    frames = height // near
    tail = weights_refs[0].shape[0] - GROUP
    slots = tail // steps
    owners, owner_rows, _ = out_ref.shape
    owned = owners * owner_rows
    eye = lax.broadcasted_iota(jnp.int32, (slots, LANES), 0) == lax.broadcasted_iota(jnp.int32, (slots, LANES), 1)
    keys, groups = [], []
    for ref in weights_refs:
        ids = ref[tail : tail + GROUP, :].astype(jnp.float32)
        owner = jnp.sum(jnp.where(eye, ids[0:1, :], 0.0), axis=1, keepdims=True).astype(jnp.int32)
        local = jnp.sum(jnp.where(eye, ids[1:2, :], 0.0), axis=1, keepdims=True).astype(jnp.int32)
        keys.append(owner * owner_rows + local % owner_rows)
        groups.append(local // owner_rows)
    key = jnp.concatenate(keys, axis=0)
    group = jnp.concatenate(groups, axis=0)
    onehot = (lax.broadcasted_iota(jnp.int32, (tiles * slots, owned), 1) == key).astype(jnp.bfloat16)
    total = jnp.zeros((owned, LANES), jnp.float32)
    for q in range(blocks):
        pooled = jnp.zeros((tiles * slots, height), jnp.float32)
        for step in range(0, steps, 2):
            left = jnp.concatenate(
                [
                    jnp.concatenate([ref[at * slots : (at + 1) * slots, :] for ref in weights_refs], axis=0)
                    for at in (step, step + 1)
                ],
                axis=1,
            )
            right = jnp.concatenate([spikes_ref[q, step], spikes_ref[q, step + 1]], axis=1)
            pooled = pooled + lax.dot_general(
                left, right, (((1,), (1,)), ((), ())), preferred_element_type=jnp.float32
            )
        column = lax.broadcasted_iota(jnp.int32, (slots, height), 1) // frames + q * near
        pooled = jnp.concatenate(
            [jnp.where(column == me ^ k, pooled[i * slots : (i + 1) * slots], 0.0) for i, k in enumerate(order)], axis=0
        )
        partial = pooled[:, 0:LANES]
        for at in range(LANES, height, LANES):
            partial = partial + pooled[:, at : at + LANES]
        step = LANES // 2
        while step >= frames:
            partial = partial + pltpu.roll(partial, step, 1)
            step //= 2
        lane_group = lax.broadcasted_iota(jnp.int32, partial.shape, 1) // frames
        partial = jnp.where(lane_group == group, partial, 0.0)
        high = partial.astype(jnp.bfloat16)
        low = (partial - high.astype(jnp.float32)).astype(jnp.bfloat16)
        both = lax.dot_general(
            onehot,
            jnp.concatenate([high, low], axis=1),
            (((0,), (0,)), ((), ())),
            preferred_element_type=jnp.float32,
        )
        total = total + both[:, :LANES] + both[:, LANES:]
    out_ref[...] = total.reshape(owners, owner_rows, LANES)


def pool(spikes, weights, order, place, frames, owners):
    shape = (owners, COMP_DEV * frames // LANES, LANES)
    inputs = [spikes, *weights]
    return pl.pallas_call(
        functools.partial(pool_kernel, order),
        out_shape=jax.ShapeDtypeStruct(shape, jnp.float32),
        in_specs=[pl.BlockSpec(memory_space=pltpu.SMEM)] + whole_vmem(len(inputs)),
        out_specs=whole_vmem(1)[0],
        compiler_params=params(16 * MIB + 4 * sum(cells.size for cells in inputs)),
        name="pool",
    )(place, *inputs)


def finish_kernel(parts_ref, out_ref):
    sources, rows, _ = parts_ref.shape
    frames = out_ref.shape[1]
    total = jnp.sum(parts_ref[...], axis=0)
    for group in range(LANES // frames):
        out_ref[group * rows : (group + 1) * rows, :] = total[:, group * frames : (group + 1) * frames]


def finish(parts, frames):
    return pl.pallas_call(
        finish_kernel,
        out_shape=jax.ShapeDtypeStruct((COMP_DEV, frames), jnp.float32),
        in_specs=whole_vmem(1),
        out_specs=whole_vmem(1)[0],
        compiler_params=params(8 * MIB + 8 * parts.size),
        name="finish",
    )(parts)


def body(movie, shifts, filters, weights, slot_owner, slot_local):
    part_frames, planes, rows, width = movie.shape
    tiles = lax.axis_size("tile")
    parts = lax.axis_size("frame")
    frames = part_frames * parts
    slots = weights.shape[0]
    ends = tiles - 1
    tile = lax.axis_index("tile")
    place = jnp.stack([tile * rows, tiles * rows, lax.axis_index("frame"), tile]).astype(jnp.int32)
    far, close = list(range(tiles // 2, tiles)), list(range(1, tiles // 2))
    order = close[1:2] + far[-2:] + far[:1] + close[:1] + far[-3:0:-1] + close[2:] + [0]
    owner, local = slot_owner.reshape(1, slots), slot_local.reshape(1, slots)
    pair, other = edges(movie, place)
    packed = pack(weights, owner, local, order, planes, place)
    swaps = [(i, i + 1) for i in range(1, ends, 2)]
    other = lax.ppermute(other, "tile", swaps + [(j, i) for i, j in swaps])
    pair = lax.ppermute(pair, "tile", [(i, i ^ 1) for i in range(tiles)])
    landed = [
        lax.ppermute(cells, "tile", [(i, i ^ k) for i in range(tiles)]) if k else cells
        for k, cells in zip(order, packed)
    ]
    pieces = smooth(movie, pair, other, shifts.T, place, parts)
    pieces = [
        lax.ppermute(pieces[k], "frame", [(i, i ^ k) for i in range(parts)]) for k in range(parts - 1, 0, -1)
    ] + [pieces[0]]
    spikes = deconvolve(spread(build_kernel(filters, frames), place, part_frames), pieces, landed[: len(far) + 1])
    traces = pool(spikes, landed, order, place, frames, parts * tiles)
    traces = lax.all_to_all(traces, ("frame", "tile"), split_axis=0, concat_axis=0, tiled=True)
    return finish(traces, frames)


def solution(mesh):
    in_specs = (
        P("frame", None, "tile", None),
        P("frame", None),
        P(),
        P(("frame", "tile"), None),
        P(("frame", "tile"), None),
        P(("frame", "tile"), None),
    )
    out_specs = P(("frame", "tile"), None)
    return jax.shard_map(body, mesh=mesh, in_specs=in_specs, out_specs=out_specs, check_vma=False)
```

```python
import functools

import jax
import jax.numpy as jnp
import numpy as np
from jax import lax
from jax.experimental import pallas as pl
from jax.experimental.pallas import tpu as pltpu
from jax.sharding import PartitionSpec as P

COMP_DEV = 32
TAPS = 64
MAXS = 8
RAD = 3
LANES = 128
GROUP = 16
HALO = 16
OCTET = 8
QUAD = 4
MIB = 1 << 20


smooth_sigma = 1.0


def gauss_taps():
    positions = np.arange(-RAD, RAD + 1).astype(np.float32)
    values = np.exp(-positions * positions / np.float32(2.0 * smooth_sigma * smooth_sigma))
    return (values / values.sum(dtype=np.float32)).astype(np.float32)


def build_kernel(filters, count):
    later = jnp.arange(count)[:, None]
    earlier = jnp.arange(count)[None, :]
    offsets = later - earlier
    onehot = (offsets[:, :, None] == jnp.arange(TAPS)[None, None, :]).astype(jnp.float32)
    return jnp.sum(onehot[None] * filters[:, None, None, :], axis=-1).astype(jnp.bfloat16)


def whole_vmem(count):
    return [pl.BlockSpec(memory_space=pltpu.VMEM)] * count


def params(limit):
    return pltpu.CompilerParams(vmem_limit_bytes=limit)


def edges_kernel(place_ref, movie_ref, pair_ref, other_ref):
    frames, planes, rows, _ = movie_ref.shape
    even = place_ref[3] % 2 == 0

    def one(frame, carry):
        last = [movie_ref[frame, plane, rows - HALO :, :].astype(jnp.float32) for plane in range(planes)]
        first = [movie_ref[frame, plane, :HALO, :].astype(jnp.float32) for plane in range(planes)]
        last = [cells[OCTET:] for cells in last] + [cells[QUAD:OCTET] for cells in last]
        first = [cells[:OCTET] for cells in first] + [cells[OCTET : OCTET + QUAD] for cells in first]
        last = jnp.concatenate(last, axis=0)
        first = jnp.concatenate(first, axis=0)
        pair_ref[frame] = jnp.where(even, last, first).astype(jnp.bfloat16)
        other_ref[frame] = jnp.where(even, first, last).astype(jnp.bfloat16)
        return carry

    lax.fori_loop(0, frames, one, 0)


def edges(movie, place):
    frames, planes, _, width = movie.shape
    shape = jax.ShapeDtypeStruct((frames, planes * (OCTET + QUAD), width), jnp.bfloat16)
    return pl.pallas_call(
        edges_kernel,
        out_shape=[shape, shape],
        in_specs=[pl.BlockSpec(memory_space=pltpu.SMEM)] + whole_vmem(1),
        out_specs=whole_vmem(2),
        compiler_params=params(40 * MIB),
        name="edges",
    )(place, movie)


def pack_kernel(order, planes, place_ref, weights_ref, owner_ref, local_ref, *refs):
    *out_refs, ids = refs
    tiles = len(order)
    slots, pixels = weights_ref.shape
    octets = pixels // (planes * tiles * LANES)
    tail = planes * octets * slots
    ids[...] = jnp.zeros_like(ids)
    ids[0:1, 0:slots] = owner_ref[...].astype(jnp.float32)
    ids[1:2, 0:slots] = local_ref[...].astype(jnp.float32)
    for k, out_ref in zip(order, out_refs):
        dest = place_ref[3] ^ k
        for plane in range(planes):
            for octet in range(octets):
                lane = pl.multiple_of(((plane * tiles + dest) * octets + octet) * LANES, LANES)
                row = (plane * octets + octet) * slots
                out_ref[row : row + slots, :] = weights_ref[:, pl.ds(lane, LANES)]
        out_ref[tail:, :] = ids[...].astype(jnp.bfloat16)


def pack(weights, owner, local, order, planes, place):
    slots, pixels = weights.shape
    tiles = len(order)
    shape = jax.ShapeDtypeStruct((pixels // (tiles * LANES) * slots + GROUP, LANES), jnp.bfloat16)
    return pl.pallas_call(
        functools.partial(pack_kernel, order, planes),
        out_shape=[shape] * tiles,
        in_specs=[pl.BlockSpec(memory_space=pltpu.SMEM)] + whole_vmem(3),
        out_specs=whole_vmem(tiles),
        scratch_shapes=[pltpu.VMEM((GROUP, LANES), jnp.float32)],
        compiler_params=params(8 * MIB + 5 * weights.size),
        name="pack_weights",
    )(place, weights, owner, local)


def smooth_kernel(shift_ref, place_ref, movie_ref, other_ref, pair_ref, *refs):
    *out_refs, band, wide = refs
    frames, planes, rows, width = movie_ref.shape
    blocks = width // LANES
    reach = rows + 2 * HALO
    parts = len(out_refs)
    each = blocks // parts
    together = wide.shape[0]
    taps = gauss_taps()
    high = [float(v) for v in taps.astype(jnp.bfloat16)]
    low = [float(v) for v in taps - taps.astype(jnp.bfloat16).astype(np.float32)]
    lane = lax.broadcasted_iota(jnp.int32, (reach, LANES), 1)
    row = lax.broadcasted_iota(jnp.int32, (reach, LANES), 0)
    first_row, total_rows, me = place_ref[0], place_ref[1], place_ref[2]
    even = place_ref[3] % 2 == 0

    tap = lax.broadcasted_iota(jnp.int32, (2 * LANES, LANES), 0) - lax.broadcasted_iota(jnp.int32, (2 * LANES, LANES), 1)
    tap = tap - (MAXS - RAD)
    for side, values in enumerate((high, low)):
        cells = jnp.zeros((2 * LANES, LANES), jnp.float32)
        for i, value in enumerate(values):
            cells = jnp.where(tap == i, value, cells)
        band[:, side * LANES : (side + 1) * LANES] = cells.astype(jnp.bfloat16)

    def some(step, carry):
        chosen = [step * together + u for u in range(together)]
        stacked = []
        for frame in chosen:
            right = shift_ref[1, frame] + MAXS
            near = lane < right
            zero = jnp.zeros((reach, LANES), jnp.float32)
            for plane in range(planes):
                moved = []
                for b in range(blocks):
                    cells = slice(b * LANES, (b + 1) * LANES)
                    pair = pair_ref[frame, :, cells].astype(jnp.float32)
                    other = other_ref[frame, :, cells].astype(jnp.float32)
                    top = jnp.where(even, other, pair)
                    bottom = jnp.where(even, pair, other)
                    full = slice(plane * OCTET, (plane + 1) * OCTET)
                    rest = slice(planes * OCTET + plane * QUAD, planes * OCTET + (plane + 1) * QUAD)
                    piece = jnp.concatenate(
                        [
                            top[rest],
                            top[rest],
                            top[full],
                            movie_ref[frame, plane, :, cells].astype(jnp.float32),
                            bottom[full],
                            bottom[rest],
                            bottom[rest],
                        ],
                        axis=0,
                    )
                    moved.append(pltpu.roll(piece, right, 1))
                shifted = []
                for b in range(blocks + 1):
                    before = moved[b - 1] if b > 0 else zero
                    own = moved[b] if b < blocks else zero
                    cells = jnp.where(near, before, own)
                    if b == 0:
                        cells = jnp.where(lane < MAXS, 0.0, cells)
                    if b == blocks:
                        cells = jnp.where(lane < MAXS, cells, 0.0)
                    shifted.append(cells.astype(jnp.bfloat16))
                stacked += [jnp.concatenate(shifted[b : b + 2], axis=1) for b in range(blocks)]
        result = jnp.dot(jnp.concatenate(stacked, axis=0), band[...], preferred_element_type=jnp.float32)
        result = result[:, :LANES] + result[:, LANES:]
        for u, frame in enumerate(chosen):
            place = first_row + row - HALO + shift_ref[0, frame]
            inside = (place >= 0) & (place < total_rows)
            for plane in range(planes):
                for b in range(blocks):
                    at = ((u * planes + plane) * blocks + b) * reach
                    wide[u, plane, b] = jnp.where(inside, result[at : at + reach], 0.0)
        for u, frame in enumerate(chosen):
            start = HALO - RAD - shift_ref[0, frame]
            for plane in range(planes):
                for k in range(parts):
                    for j in range(each):
                        b = (me ^ k) * each + j
                        total = float(taps[RAD]) * wide[u, plane, b, pl.ds(start + RAD, rows), :]
                        for i in range(RAD):
                            pair = wide[u, plane, b, pl.ds(start + i, rows), :]
                            pair = pair + wide[u, plane, b, pl.ds(start + 2 * RAD - i, rows), :]
                            total = total + float(taps[i]) * pair
                        out_refs[k][frame, plane, :, j * LANES : (j + 1) * LANES] = total.astype(jnp.bfloat16)
        return carry

    lax.fori_loop(0, frames // together, some, 0)


def smooth(movie, pair, other, shifts, place, parts):
    frames, planes, rows, width = movie.shape
    reach = rows + 2 * HALO
    smem = pl.BlockSpec(memory_space=pltpu.SMEM)
    return pl.pallas_call(
        smooth_kernel,
        out_shape=[jax.ShapeDtypeStruct((frames, planes, rows, width // parts), jnp.bfloat16)] * parts,
        in_specs=[smem, smem] + whole_vmem(3),
        out_specs=whole_vmem(parts),
        scratch_shapes=[
            pltpu.VMEM((2 * LANES, 2 * LANES), jnp.bfloat16),
            pltpu.VMEM((2 - frames % 2, planes, width // LANES, reach, LANES), jnp.float32),
        ],
        compiler_params=params(20 * MIB + 8 * movie.size),
        name="smooth",
    )(shifts, place, movie, other, pair)


def spread_kernel(part_frames, place_ref, kernel_ref, out_ref):
    planes, size, _ = out_ref.shape
    frames = size // GROUP
    me = place_ref[2]
    row = lax.broadcasted_iota(jnp.int32, (size, frames), 0)
    column = lax.broadcasted_iota(jnp.int32, (size, frames), 1)
    tall = (row % frames == column).astype(jnp.bfloat16)
    row = lax.broadcasted_iota(jnp.int32, (frames, size), 0)
    column = lax.broadcasted_iota(jnp.int32, (frames, size), 1) // GROUP
    last = frames // part_frames - 1
    column = ((last - column // part_frames) ^ me) * part_frames + column % part_frames
    flat = (column == row).astype(jnp.bfloat16)
    row = lax.broadcasted_iota(jnp.int32, (size, size), 0)
    column = lax.broadcasted_iota(jnp.int32, (size, size), 1)
    same = row // frames == column % GROUP
    for plane in range(planes):
        left = jnp.dot(tall, kernel_ref[plane], preferred_element_type=jnp.float32).astype(jnp.bfloat16)
        full = jnp.dot(left, flat, preferred_element_type=jnp.float32)
        out_ref[plane] = jnp.where(same, full, 0.0).astype(jnp.bfloat16)


def spread(kernel, place, part_frames):
    planes, frames, _ = kernel.shape
    size = frames * GROUP
    return pl.pallas_call(
        functools.partial(spread_kernel, part_frames),
        out_shape=jax.ShapeDtypeStruct((planes, size, size), jnp.bfloat16),
        in_specs=[pl.BlockSpec(memory_space=pltpu.SMEM)] + whole_vmem(1),
        out_specs=whole_vmem(1)[0],
        compiler_params=params(8 * MIB + 16 * size * size),
        name="spread_filters",
    )(place, kernel)


def swap_lanes(pieces):
    count = len(pieces)
    group = LANES // count
    half = count // 2
    lane = lax.broadcasted_iota(jnp.int32, pieces[0].shape, 1) // group
    while half >= 1:
        low = (lane & half) == 0
        result = list(pieces)
        for i in range(count):
            if i & half:
                continue
            a, b = pieces[i], pieces[i + half]
            if 2 * half == count:
                back = pltpu.roll(b, half * group, 1)
                ahead = pltpu.roll(a, half * group, 1)
            else:
                back = pltpu.roll(b, half * group, 1)
                ahead = pltpu.roll(a, LANES - half * group, 1)
            result[i] = jnp.where(low, a, back)
            result[i + half] = jnp.where(low, ahead, b)
        pieces = result
        half //= 2
    return pieces


def deconvolve_kernel(parts, spread_ref, *refs):
    data_refs, out_ref = refs[:parts], refs[-1]
    part_frames, planes, rows, width = data_refs[0].shape
    size = spread_ref.shape[1]
    frames = size // GROUP
    octets = rows // OCTET
    for q in range(width // LANES):
        lanes = slice(q * LANES, (q + 1) * LANES)
        for plane in range(planes):
            for first in range(0, rows // GROUP, 2):
                cells = []
                for a in (first, first + 1):
                    pieces = [ref[:, plane, a * GROUP : (a + 1) * GROUP, lanes] for ref in data_refs]
                    cells.append(jnp.concatenate(pieces, axis=0).reshape(size, LANES))
                cells = jnp.concatenate(cells, axis=1)
                spikes = jnp.dot(spread_ref[plane], cells, preferred_element_type=jnp.float32)
                spikes = jnp.maximum(spikes, 0.0)
                for a in (0, 1):
                    for half in (0, 1):
                        pieces = [
                            spikes[(half * OCTET + r) * frames : (half * OCTET + r + 1) * frames, a * LANES : (a + 1) * LANES]
                            for r in range(OCTET)
                        ]
                        octet = plane * octets + (first + a) * 2 + half
                        for j, piece in enumerate(swap_lanes(pieces)):
                            out_ref[q, octet, j * frames : (j + 1) * frames, :] = piece.astype(jnp.bfloat16)


def deconvolve(spread_filters, data, after):
    part_frames, planes, rows, width = data[0].shape
    frames = part_frames * len(data)
    shape = (width // LANES, planes * rows // OCTET, OCTET * frames, LANES)
    return pl.pallas_call(
        functools.partial(deconvolve_kernel, len(data)),
        out_shape=jax.ShapeDtypeStruct(shape, jnp.bfloat16),
        in_specs=whole_vmem(1 + len(data)) + [pl.BlockSpec(memory_space=pl.ANY)] * len(after),
        out_specs=whole_vmem(1)[0],
        compiler_params=params(12 * MIB + 4 * (spread_filters.size + 2 * len(data) * data[0].size)),
        name="deconvolve",
    )(spread_filters, *data, *after)


def pool_kernel(order, place_ref, spikes_ref, *refs):
    *weights_refs, out_ref = refs
    blocks, steps, height, _ = spikes_ref.shape
    tiles = len(weights_refs)
    me = place_ref[3]
    near = tiles // blocks
    frames = height // near
    tail = weights_refs[0].shape[0] - GROUP
    slots = tail // steps
    owners, owner_rows, _ = out_ref.shape
    owned = owners * owner_rows
    eye = lax.broadcasted_iota(jnp.int32, (slots, LANES), 0) == lax.broadcasted_iota(jnp.int32, (slots, LANES), 1)
    keys, groups = [], []
    for ref in weights_refs:
        ids = ref[tail : tail + GROUP, :].astype(jnp.float32)
        owner = jnp.sum(jnp.where(eye, ids[0:1, :], 0.0), axis=1, keepdims=True).astype(jnp.int32)
        local = jnp.sum(jnp.where(eye, ids[1:2, :], 0.0), axis=1, keepdims=True).astype(jnp.int32)
        keys.append(owner * owner_rows + local % owner_rows)
        groups.append(local // owner_rows)
    key = jnp.concatenate(keys, axis=0)
    group = jnp.concatenate(groups, axis=0)
    onehot = (lax.broadcasted_iota(jnp.int32, (tiles * slots, owned), 1) == key).astype(jnp.bfloat16)
    total = jnp.zeros((owned, LANES), jnp.float32)
    for q in range(blocks):
        pooled = jnp.zeros((tiles * slots, height), jnp.float32)
        for step in range(0, steps, 2):
            left = jnp.concatenate(
                [
                    jnp.concatenate([ref[at * slots : (at + 1) * slots, :] for ref in weights_refs], axis=0)
                    for at in (step, step + 1)
                ],
                axis=1,
            )
            right = jnp.concatenate([spikes_ref[q, step], spikes_ref[q, step + 1]], axis=1)
            pooled = pooled + lax.dot_general(
                left, right, (((1,), (1,)), ((), ())), preferred_element_type=jnp.float32
            )
        column = lax.broadcasted_iota(jnp.int32, (slots, height), 1) // frames + q * near
        pooled = jnp.concatenate(
            [jnp.where(column == me ^ k, pooled[i * slots : (i + 1) * slots], 0.0) for i, k in enumerate(order)], axis=0
        )
        partial = pooled[:, 0:LANES]
        for at in range(LANES, height, LANES):
            partial = partial + pooled[:, at : at + LANES]
        step = LANES // 2
        while step >= frames:
            partial = partial + pltpu.roll(partial, step, 1)
            step //= 2
        lane_group = lax.broadcasted_iota(jnp.int32, partial.shape, 1) // frames
        partial = jnp.where(lane_group == group, partial, 0.0)
        high = partial.astype(jnp.bfloat16)
        low = (partial - high.astype(jnp.float32)).astype(jnp.bfloat16)
        both = lax.dot_general(
            onehot,
            jnp.concatenate([high, low], axis=1),
            (((0,), (0,)), ((), ())),
            preferred_element_type=jnp.float32,
        )
        total = total + both[:, :LANES] + both[:, LANES:]
    out_ref[...] = total.reshape(owners, owner_rows, LANES)


def pool(spikes, weights, order, place, frames, owners):
    shape = (owners, COMP_DEV * frames // LANES, LANES)
    inputs = [spikes, *weights]
    return pl.pallas_call(
        functools.partial(pool_kernel, order),
        out_shape=jax.ShapeDtypeStruct(shape, jnp.float32),
        in_specs=[pl.BlockSpec(memory_space=pltpu.SMEM)] + whole_vmem(len(inputs)),
        out_specs=whole_vmem(1)[0],
        compiler_params=params(16 * MIB + 4 * sum(cells.size for cells in inputs)),
        name="pool",
    )(place, *inputs)


def finish_kernel(parts_ref, out_ref):
    sources, rows, _ = parts_ref.shape
    frames = out_ref.shape[1]
    total = jnp.sum(parts_ref[...], axis=0)
    for group in range(LANES // frames):
        out_ref[group * rows : (group + 1) * rows, :] = total[:, group * frames : (group + 1) * frames]


def finish(parts, frames):
    return pl.pallas_call(
        finish_kernel,
        out_shape=jax.ShapeDtypeStruct((COMP_DEV, frames), jnp.float32),
        in_specs=whole_vmem(1),
        out_specs=whole_vmem(1)[0],
        compiler_params=params(8 * MIB + 8 * parts.size),
        name="finish",
    )(parts)


def body(movie, shifts, filters, weights, slot_owner, slot_local):
    part_frames, planes, rows, width = movie.shape
    tiles = lax.axis_size("tile")
    parts = lax.axis_size("frame")
    frames = part_frames * parts
    slots = weights.shape[0]
    ends = tiles - 1
    tile = lax.axis_index("tile")
    place = jnp.stack([tile * rows, tiles * rows, lax.axis_index("frame"), tile]).astype(jnp.int32)
    far, close = list(range(tiles // 2, tiles)), list(range(1, tiles // 2))
    order = close[1:2] + far[-2:-1] + far[:1] + close[:1] + far[-1:] + far[-3:0:-1] + close[2:] + [0]
    owner, local = slot_owner.reshape(1, slots), slot_local.reshape(1, slots)
    pair, other = edges(movie, place)
    packed = pack(weights, owner, local, order, planes, place)
    swaps = [(i, i + 1) for i in range(1, ends, 2)]
    other = lax.ppermute(other, "tile", swaps + [(j, i) for i, j in swaps])
    pair = lax.ppermute(pair, "tile", [(i, i ^ 1) for i in range(tiles)])
    landed = [
        lax.ppermute(cells, "tile", [(i, i ^ k) for i in range(tiles)]) if k else cells
        for k, cells in zip(order, packed)
    ]
    pieces = smooth(movie, pair, other, shifts.T, place, parts)
    pieces = [
        lax.ppermute(pieces[k], "frame", [(i, i ^ k) for i in range(parts)]) for k in range(parts - 1, 0, -1)
    ] + [pieces[0]]
    spikes = deconvolve(spread(build_kernel(filters, frames), place, part_frames), pieces, landed[: len(far) + 1])
    traces = pool(spikes, landed, order, place, frames, parts * tiles)
    traces = lax.all_to_all(traces, ("frame", "tile"), split_axis=0, concat_axis=0, tiled=True)
    return finish(traces, frames)


def solution(mesh):
    in_specs = (
        P("frame", None, "tile", None),
        P("frame", None),
        P(),
        P(("frame", "tile"), None),
        P(("frame", "tile"), None),
        P(("frame", "tile"), None),
    )
    out_specs = P(("frame", "tile"), None)
    return jax.shard_map(body, mesh=mesh, in_specs=in_specs, out_specs=out_specs, check_vma=False)
```

```python
import functools

import jax
import jax.numpy as jnp
import numpy as np
from jax import lax
from jax.experimental import pallas as pl
from jax.experimental.pallas import tpu as pltpu
from jax.sharding import PartitionSpec as P

COMP_DEV = 32
TAPS = 64
MAXS = 8
RAD = 3
LANES = 128
GROUP = 16
HALO = 16
OCTET = 8
QUAD = 4
MIB = 1 << 20


smooth_sigma = 1.0


def gauss_taps():
    positions = np.arange(-RAD, RAD + 1).astype(np.float32)
    values = np.exp(-positions * positions / np.float32(2.0 * smooth_sigma * smooth_sigma))
    return (values / values.sum(dtype=np.float32)).astype(np.float32)


def build_kernel(filters, count):
    later = jnp.arange(count)[:, None]
    earlier = jnp.arange(count)[None, :]
    offsets = later - earlier
    onehot = (offsets[:, :, None] == jnp.arange(TAPS)[None, None, :]).astype(jnp.float32)
    return jnp.sum(onehot[None] * filters[:, None, None, :], axis=-1).astype(jnp.bfloat16)


def whole_vmem(count):
    return [pl.BlockSpec(memory_space=pltpu.VMEM)] * count


def params(limit):
    return pltpu.CompilerParams(vmem_limit_bytes=limit)


def edges_kernel(place_ref, movie_ref, pair_ref, other_ref):
    frames, planes, rows, _ = movie_ref.shape
    even = place_ref[3] % 2 == 0

    def one(frame, carry):
        last = [movie_ref[frame, plane, rows - HALO :, :].astype(jnp.float32) for plane in range(planes)]
        first = [movie_ref[frame, plane, :HALO, :].astype(jnp.float32) for plane in range(planes)]
        last = [cells[OCTET:] for cells in last] + [cells[QUAD:OCTET] for cells in last]
        first = [cells[:OCTET] for cells in first] + [cells[OCTET : OCTET + QUAD] for cells in first]
        last = jnp.concatenate(last, axis=0)
        first = jnp.concatenate(first, axis=0)
        pair_ref[frame] = jnp.where(even, last, first).astype(jnp.bfloat16)
        other_ref[frame] = jnp.where(even, first, last).astype(jnp.bfloat16)
        return carry

    lax.fori_loop(0, frames, one, 0)


def edges(movie, place):
    frames, planes, _, width = movie.shape
    shape = jax.ShapeDtypeStruct((frames, planes * (OCTET + QUAD), width), jnp.bfloat16)
    return pl.pallas_call(
        edges_kernel,
        out_shape=[shape, shape],
        in_specs=[pl.BlockSpec(memory_space=pltpu.SMEM)] + whole_vmem(1),
        out_specs=whole_vmem(2),
        compiler_params=params(40 * MIB),
        name="edges",
    )(place, movie)


def pack_kernel(order, planes, place_ref, weights_ref, owner_ref, local_ref, *refs):
    *out_refs, ids = refs
    tiles = len(order)
    slots, pixels = weights_ref.shape
    octets = pixels // (planes * tiles * LANES)
    tail = planes * octets * slots
    ids[...] = jnp.zeros_like(ids)
    ids[0:1, 0:slots] = owner_ref[...].astype(jnp.float32)
    ids[1:2, 0:slots] = local_ref[...].astype(jnp.float32)
    for k, out_ref in zip(order, out_refs):
        dest = place_ref[3] ^ k
        for plane in range(planes):
            for octet in range(octets):
                lane = pl.multiple_of(((plane * tiles + dest) * octets + octet) * LANES, LANES)
                row = (plane * octets + octet) * slots
                out_ref[row : row + slots, :] = weights_ref[:, pl.ds(lane, LANES)]
        out_ref[tail:, :] = ids[...].astype(jnp.bfloat16)


def pack(weights, owner, local, order, planes, place):
    slots, pixels = weights.shape
    tiles = len(order)
    shape = jax.ShapeDtypeStruct((pixels // (tiles * LANES) * slots + GROUP, LANES), jnp.bfloat16)
    return pl.pallas_call(
        functools.partial(pack_kernel, order, planes),
        out_shape=[shape] * tiles,
        in_specs=[pl.BlockSpec(memory_space=pltpu.SMEM)] + whole_vmem(3),
        out_specs=whole_vmem(tiles),
        scratch_shapes=[pltpu.VMEM((GROUP, LANES), jnp.float32)],
        compiler_params=params(8 * MIB + 5 * weights.size),
        name="pack_weights",
    )(place, weights, owner, local)


def smooth_kernel(shift_ref, place_ref, movie_ref, other_ref, pair_ref, *refs):
    *out_refs, band, wide = refs
    frames, planes, rows, width = movie_ref.shape
    blocks = width // LANES
    reach = rows + 2 * HALO
    parts = len(out_refs)
    each = blocks // parts
    together = wide.shape[0]
    taps = gauss_taps()
    high = [float(v) for v in taps.astype(jnp.bfloat16)]
    low = [float(v) for v in taps - taps.astype(jnp.bfloat16).astype(np.float32)]
    lane = lax.broadcasted_iota(jnp.int32, (reach, LANES), 1)
    row = lax.broadcasted_iota(jnp.int32, (reach, LANES), 0)
    first_row, total_rows, me = place_ref[0], place_ref[1], place_ref[2]
    even = place_ref[3] % 2 == 0

    tap = lax.broadcasted_iota(jnp.int32, (2 * LANES, LANES), 0) - lax.broadcasted_iota(jnp.int32, (2 * LANES, LANES), 1)
    tap = tap - (MAXS - RAD)
    for side, values in enumerate((high, low)):
        cells = jnp.zeros((2 * LANES, LANES), jnp.float32)
        for i, value in enumerate(values):
            cells = jnp.where(tap == i, value, cells)
        band[:, side * LANES : (side + 1) * LANES] = cells.astype(jnp.bfloat16)

    def some(step, carry):
        chosen = [step * together + u for u in range(together)]
        stacked = []
        for frame in chosen:
            right = shift_ref[1, frame] + MAXS
            near = lane < right
            zero = jnp.zeros((reach, LANES), jnp.float32)
            for plane in range(planes):
                moved = []
                for b in range(blocks):
                    cells = slice(b * LANES, (b + 1) * LANES)
                    pair = pair_ref[frame, :, cells].astype(jnp.float32)
                    other = other_ref[frame, :, cells].astype(jnp.float32)
                    top = jnp.where(even, other, pair)
                    bottom = jnp.where(even, pair, other)
                    full = slice(plane * OCTET, (plane + 1) * OCTET)
                    rest = slice(planes * OCTET + plane * QUAD, planes * OCTET + (plane + 1) * QUAD)
                    piece = jnp.concatenate(
                        [
                            top[rest],
                            top[rest],
                            top[full],
                            movie_ref[frame, plane, :, cells].astype(jnp.float32),
                            bottom[full],
                            bottom[rest],
                            bottom[rest],
                        ],
                        axis=0,
                    )
                    moved.append(pltpu.roll(piece, right, 1))
                shifted = []
                for b in range(blocks + 1):
                    before = moved[b - 1] if b > 0 else zero
                    own = moved[b] if b < blocks else zero
                    cells = jnp.where(near, before, own)
                    if b == 0:
                        cells = jnp.where(lane < MAXS, 0.0, cells)
                    if b == blocks:
                        cells = jnp.where(lane < MAXS, cells, 0.0)
                    shifted.append(cells.astype(jnp.bfloat16))
                stacked += [jnp.concatenate(shifted[b : b + 2], axis=1) for b in range(blocks)]
        result = jnp.dot(jnp.concatenate(stacked, axis=0), band[...], preferred_element_type=jnp.float32)
        result = result[:, :LANES] + result[:, LANES:]
        for u, frame in enumerate(chosen):
            place = first_row + row - HALO + shift_ref[0, frame]
            inside = (place >= 0) & (place < total_rows)
            for plane in range(planes):
                for b in range(blocks):
                    at = ((u * planes + plane) * blocks + b) * reach
                    wide[u, plane, b] = jnp.where(inside, result[at : at + reach], 0.0)
        for u, frame in enumerate(chosen):
            start = HALO - RAD - shift_ref[0, frame]
            for plane in range(planes):
                for k in range(parts):
                    for j in range(each):
                        b = (me ^ k) * each + j
                        total = float(taps[RAD]) * wide[u, plane, b, pl.ds(start + RAD, rows), :]
                        for i in range(RAD):
                            pair = wide[u, plane, b, pl.ds(start + i, rows), :]
                            pair = pair + wide[u, plane, b, pl.ds(start + 2 * RAD - i, rows), :]
                            total = total + float(taps[i]) * pair
                        out_refs[k][frame, plane, :, j * LANES : (j + 1) * LANES] = total.astype(jnp.bfloat16)
        return carry

    lax.fori_loop(0, frames // together, some, 0)


def smooth(movie, pair, other, shifts, place, parts):
    frames, planes, rows, width = movie.shape
    reach = rows + 2 * HALO
    smem = pl.BlockSpec(memory_space=pltpu.SMEM)
    return pl.pallas_call(
        smooth_kernel,
        out_shape=[jax.ShapeDtypeStruct((frames, planes, rows, width // parts), jnp.bfloat16)] * parts,
        in_specs=[smem, smem] + whole_vmem(3),
        out_specs=whole_vmem(parts),
        scratch_shapes=[
            pltpu.VMEM((2 * LANES, 2 * LANES), jnp.bfloat16),
            pltpu.VMEM((2 - frames % 2, planes, width // LANES, reach, LANES), jnp.float32),
        ],
        compiler_params=params(20 * MIB + 8 * movie.size),
        name="smooth",
    )(shifts, place, movie, other, pair)


def spread_kernel(part_frames, place_ref, kernel_ref, out_ref):
    planes, size, _ = out_ref.shape
    frames = size // GROUP
    me = place_ref[2]
    row = lax.broadcasted_iota(jnp.int32, (size, frames), 0)
    column = lax.broadcasted_iota(jnp.int32, (size, frames), 1)
    tall = (row % frames == column).astype(jnp.bfloat16)
    row = lax.broadcasted_iota(jnp.int32, (frames, size), 0)
    column = lax.broadcasted_iota(jnp.int32, (frames, size), 1) // GROUP
    last = frames // part_frames - 1
    column = ((last - column // part_frames) ^ me) * part_frames + column % part_frames
    flat = (column == row).astype(jnp.bfloat16)
    row = lax.broadcasted_iota(jnp.int32, (size, size), 0)
    column = lax.broadcasted_iota(jnp.int32, (size, size), 1)
    same = row // frames == column % GROUP
    for plane in range(planes):
        left = jnp.dot(tall, kernel_ref[plane], preferred_element_type=jnp.float32).astype(jnp.bfloat16)
        full = jnp.dot(left, flat, preferred_element_type=jnp.float32)
        out_ref[plane] = jnp.where(same, full, 0.0).astype(jnp.bfloat16)


def spread(kernel, place, part_frames):
    planes, frames, _ = kernel.shape
    size = frames * GROUP
    return pl.pallas_call(
        functools.partial(spread_kernel, part_frames),
        out_shape=jax.ShapeDtypeStruct((planes, size, size), jnp.bfloat16),
        in_specs=[pl.BlockSpec(memory_space=pltpu.SMEM)] + whole_vmem(1),
        out_specs=whole_vmem(1)[0],
        compiler_params=params(8 * MIB + 16 * size * size),
        name="spread_filters",
    )(place, kernel)


def swap_lanes(pieces):
    count = len(pieces)
    group = LANES // count
    half = count // 2
    lane = lax.broadcasted_iota(jnp.int32, pieces[0].shape, 1) // group
    while half >= 1:
        low = (lane & half) == 0
        result = list(pieces)
        for i in range(count):
            if i & half:
                continue
            a, b = pieces[i], pieces[i + half]
            if 2 * half == count:
                back = pltpu.roll(b, half * group, 1)
                ahead = pltpu.roll(a, half * group, 1)
            else:
                back = pltpu.roll(b, half * group, 1)
                ahead = pltpu.roll(a, LANES - half * group, 1)
            result[i] = jnp.where(low, a, back)
            result[i + half] = jnp.where(low, ahead, b)
        pieces = result
        half //= 2
    return pieces


def deconvolve_kernel(parts, spread_ref, *refs):
    data_refs, out_ref = refs[:parts], refs[-1]
    part_frames, planes, rows, width = data_refs[0].shape
    size = spread_ref.shape[1]
    frames = size // GROUP
    octets = rows // OCTET
    for q in range(width // LANES):
        lanes = slice(q * LANES, (q + 1) * LANES)
        for plane in range(planes):
            for first in range(0, rows // GROUP, 2):
                cells = []
                for a in (first, first + 1):
                    pieces = [ref[:, plane, a * GROUP : (a + 1) * GROUP, lanes] for ref in data_refs]
                    cells.append(jnp.concatenate(pieces, axis=0).reshape(size, LANES))
                cells = jnp.concatenate(cells, axis=1)
                spikes = jnp.dot(spread_ref[plane], cells, preferred_element_type=jnp.float32)
                spikes = jnp.maximum(spikes, 0.0)
                for a in (0, 1):
                    for half in (0, 1):
                        pieces = [
                            spikes[(half * OCTET + r) * frames : (half * OCTET + r + 1) * frames, a * LANES : (a + 1) * LANES]
                            for r in range(OCTET)
                        ]
                        octet = plane * octets + (first + a) * 2 + half
                        for j, piece in enumerate(swap_lanes(pieces)):
                            out_ref[q, octet, j * frames : (j + 1) * frames, :] = piece.astype(jnp.bfloat16)


def deconvolve(spread_filters, data, after):
    part_frames, planes, rows, width = data[0].shape
    frames = part_frames * len(data)
    shape = (width // LANES, planes * rows // OCTET, OCTET * frames, LANES)
    return pl.pallas_call(
        functools.partial(deconvolve_kernel, len(data)),
        out_shape=jax.ShapeDtypeStruct(shape, jnp.bfloat16),
        in_specs=whole_vmem(1 + len(data)) + [pl.BlockSpec(memory_space=pl.ANY)] * len(after),
        out_specs=whole_vmem(1)[0],
        compiler_params=params(12 * MIB + 4 * (spread_filters.size + 2 * len(data) * data[0].size)),
        name="deconvolve",
    )(spread_filters, *data, *after)


def pool_kernel(order, place_ref, spikes_ref, *refs):
    *weights_refs, out_ref = refs
    blocks, steps, height, _ = spikes_ref.shape
    tiles = len(weights_refs)
    me = place_ref[3]
    near = tiles // blocks
    frames = height // near
    tail = weights_refs[0].shape[0] - GROUP
    slots = tail // steps
    owners, owner_rows, _ = out_ref.shape
    owned = owners * owner_rows
    eye = lax.broadcasted_iota(jnp.int32, (slots, LANES), 0) == lax.broadcasted_iota(jnp.int32, (slots, LANES), 1)
    keys, groups = [], []
    for ref in weights_refs:
        ids = ref[tail : tail + GROUP, :].astype(jnp.float32)
        owner = jnp.sum(jnp.where(eye, ids[0:1, :], 0.0), axis=1, keepdims=True).astype(jnp.int32)
        local = jnp.sum(jnp.where(eye, ids[1:2, :], 0.0), axis=1, keepdims=True).astype(jnp.int32)
        keys.append(owner * owner_rows + local % owner_rows)
        groups.append(local // owner_rows)
    key = jnp.concatenate(keys, axis=0)
    group = jnp.concatenate(groups, axis=0)
    onehot = (lax.broadcasted_iota(jnp.int32, (tiles * slots, owned), 1) == key).astype(jnp.bfloat16)
    total = jnp.zeros((owned, LANES), jnp.float32)
    for q in range(blocks):
        pooled = jnp.zeros((tiles * slots, height), jnp.float32)
        for step in range(0, steps, 2):
            left = jnp.concatenate(
                [
                    jnp.concatenate([ref[at * slots : (at + 1) * slots, :] for ref in weights_refs], axis=0)
                    for at in (step, step + 1)
                ],
                axis=1,
            )
            right = jnp.concatenate([spikes_ref[q, step], spikes_ref[q, step + 1]], axis=1)
            pooled = pooled + lax.dot_general(
                left, right, (((1,), (1,)), ((), ())), preferred_element_type=jnp.float32
            )
        column = lax.broadcasted_iota(jnp.int32, (slots, height), 1) // frames + q * near
        pooled = jnp.concatenate(
            [jnp.where(column == me ^ k, pooled[i * slots : (i + 1) * slots], 0.0) for i, k in enumerate(order)], axis=0
        )
        partial = pooled[:, 0:LANES]
        for at in range(LANES, height, LANES):
            partial = partial + pooled[:, at : at + LANES]
        step = LANES // 2
        while step >= frames:
            partial = partial + pltpu.roll(partial, step, 1)
            step //= 2
        lane_group = lax.broadcasted_iota(jnp.int32, partial.shape, 1) // frames
        partial = jnp.where(lane_group == group, partial, 0.0)
        high = partial.astype(jnp.bfloat16)
        low = (partial - high.astype(jnp.float32)).astype(jnp.bfloat16)
        both = lax.dot_general(
            onehot,
            jnp.concatenate([high, low], axis=1),
            (((0,), (0,)), ((), ())),
            preferred_element_type=jnp.float32,
        )
        total = total + both[:, :LANES] + both[:, LANES:]
    out_ref[...] = total.reshape(owners, owner_rows, LANES)


def pool(spikes, weights, order, place, frames, owners):
    shape = (owners, COMP_DEV * frames // LANES, LANES)
    inputs = [spikes, *weights]
    return pl.pallas_call(
        functools.partial(pool_kernel, order),
        out_shape=jax.ShapeDtypeStruct(shape, jnp.float32),
        in_specs=[pl.BlockSpec(memory_space=pltpu.SMEM)] + whole_vmem(len(inputs)),
        out_specs=whole_vmem(1)[0],
        compiler_params=params(16 * MIB + 4 * sum(cells.size for cells in inputs)),
        name="pool",
    )(place, *inputs)


def finish_kernel(parts_ref, out_ref):
    sources, rows, _ = parts_ref.shape
    frames = out_ref.shape[1]
    total = jnp.sum(parts_ref[...], axis=0)
    for group in range(LANES // frames):
        out_ref[group * rows : (group + 1) * rows, :] = total[:, group * frames : (group + 1) * frames]


def finish(parts, frames):
    return pl.pallas_call(
        finish_kernel,
        out_shape=jax.ShapeDtypeStruct((COMP_DEV, frames), jnp.float32),
        in_specs=whole_vmem(1),
        out_specs=whole_vmem(1)[0],
        compiler_params=params(8 * MIB + 8 * parts.size),
        name="finish",
    )(parts)


def body(movie, shifts, filters, weights, slot_owner, slot_local):
    part_frames, planes, rows, width = movie.shape
    tiles = lax.axis_size("tile")
    parts = lax.axis_size("frame")
    frames = part_frames * parts
    slots = weights.shape[0]
    ends = tiles - 1
    tile = lax.axis_index("tile")
    place = jnp.stack([tile * rows, tiles * rows, lax.axis_index("frame"), tile]).astype(jnp.int32)
    far, close = list(range(tiles // 2, tiles)), list(range(1, tiles // 2))
    order = far[-2:-1] + close[1:2] + far[:1] + close[:1] + far[-1:] + far[-3:0:-1] + close[2:] + [0]
    owner, local = slot_owner.reshape(1, slots), slot_local.reshape(1, slots)
    pair, other = edges(movie, place)
    packed = pack(weights, owner, local, order, planes, place)
    swaps = [(i, i + 1) for i in range(1, ends, 2)]
    other = lax.ppermute(other, "tile", swaps + [(j, i) for i, j in swaps])
    pair = lax.ppermute(pair, "tile", [(i, i ^ 1) for i in range(tiles)])
    landed = [
        lax.ppermute(cells, "tile", [(i, i ^ k) for i in range(tiles)]) if k else cells
        for k, cells in zip(order, packed)
    ]
    pieces = smooth(movie, pair, other, shifts.T, place, parts)
    pieces = [
        lax.ppermute(pieces[k], "frame", [(i, i ^ k) for i in range(parts)]) for k in range(parts - 1, 0, -1)
    ] + [pieces[0]]
    spikes = deconvolve(spread(build_kernel(filters, frames), place, part_frames), pieces, landed[: len(far) + 1])
    traces = pool(spikes, landed, order, place, frames, parts * tiles)
    traces = lax.all_to_all(traces, ("frame", "tile"), split_axis=0, concat_axis=0, tiled=True)
    return finish(traces, frames)


def solution(mesh):
    in_specs = (
        P("frame", None, "tile", None),
        P("frame", None),
        P(),
        P(("frame", "tile"), None),
        P(("frame", "tile"), None),
        P(("frame", "tile"), None),
    )
    out_specs = P(("frame", "tile"), None)
    return jax.shard_map(body, mesh=mesh, in_specs=in_specs, out_specs=out_specs, check_vma=False)
```

```python
import functools

import jax
import jax.numpy as jnp
import numpy as np
from jax import lax
from jax.experimental import pallas as pl
from jax.experimental.pallas import tpu as pltpu
from jax.sharding import PartitionSpec as P

COMP_DEV = 32
TAPS = 64
MAXS = 8
RAD = 3
LANES = 128
GROUP = 16
HALO = 16
OCTET = 8
QUAD = 4
MIB = 1 << 20


smooth_sigma = 1.0


def gauss_taps():
    positions = np.arange(-RAD, RAD + 1).astype(np.float32)
    values = np.exp(-positions * positions / np.float32(2.0 * smooth_sigma * smooth_sigma))
    return (values / values.sum(dtype=np.float32)).astype(np.float32)


def build_kernel(filters, count):
    later = jnp.arange(count)[:, None]
    earlier = jnp.arange(count)[None, :]
    offsets = later - earlier
    onehot = (offsets[:, :, None] == jnp.arange(TAPS)[None, None, :]).astype(jnp.float32)
    return jnp.sum(onehot[None] * filters[:, None, None, :], axis=-1).astype(jnp.bfloat16)


def whole_vmem(count):
    return [pl.BlockSpec(memory_space=pltpu.VMEM)] * count


def params(limit):
    return pltpu.CompilerParams(vmem_limit_bytes=limit)


def edges_kernel(place_ref, movie_ref, pair_ref, other_ref):
    frames, planes, rows, _ = movie_ref.shape
    even = place_ref[3] % 2 == 0

    def one(frame, carry):
        last = [movie_ref[frame, plane, rows - HALO :, :].astype(jnp.float32) for plane in range(planes)]
        first = [movie_ref[frame, plane, :HALO, :].astype(jnp.float32) for plane in range(planes)]
        last = [cells[OCTET:] for cells in last] + [cells[QUAD:OCTET] for cells in last]
        first = [cells[:OCTET] for cells in first] + [cells[OCTET : OCTET + QUAD] for cells in first]
        last = jnp.concatenate(last, axis=0)
        first = jnp.concatenate(first, axis=0)
        pair_ref[frame] = jnp.where(even, last, first).astype(jnp.bfloat16)
        other_ref[frame] = jnp.where(even, first, last).astype(jnp.bfloat16)
        return carry

    lax.fori_loop(0, frames, one, 0)


def edges(movie, place):
    frames, planes, _, width = movie.shape
    shape = jax.ShapeDtypeStruct((frames, planes * (OCTET + QUAD), width), jnp.bfloat16)
    return pl.pallas_call(
        edges_kernel,
        out_shape=[shape, shape],
        in_specs=[pl.BlockSpec(memory_space=pltpu.SMEM)] + whole_vmem(1),
        out_specs=whole_vmem(2),
        compiler_params=params(40 * MIB),
        name="edges",
    )(place, movie)


def pack_kernel(order, tiles, planes, place_ref, weights_ref, owner_ref, local_ref, *refs):
    *out_refs, ids = refs[-1 - len(order) :]
    slots, pixels = weights_ref.shape
    octets = pixels // (planes * tiles * LANES)
    tail = planes * octets * slots
    ids[...] = jnp.zeros_like(ids)
    ids[0:1, 0:slots] = owner_ref[...].astype(jnp.float32)
    ids[1:2, 0:slots] = local_ref[...].astype(jnp.float32)
    for k, out_ref in zip(order, out_refs):
        dest = place_ref[3] ^ k
        for plane in range(planes):
            for octet in range(octets):
                lane = pl.multiple_of(((plane * tiles + dest) * octets + octet) * LANES, LANES)
                row = (plane * octets + octet) * slots
                out_ref[row : row + slots, :] = weights_ref[:, pl.ds(lane, LANES)]
        out_ref[tail:, :] = ids[...].astype(jnp.bfloat16)


def pack(weights, owner, local, order, tiles, planes, place, *after):
    slots, pixels = weights.shape
    shape = jax.ShapeDtypeStruct((pixels // (tiles * LANES) * slots + GROUP, LANES), jnp.bfloat16)
    return pl.pallas_call(
        functools.partial(pack_kernel, order, tiles, planes),
        out_shape=[shape] * len(order),
        in_specs=[pl.BlockSpec(memory_space=pltpu.SMEM)] + whole_vmem(3) + [pl.BlockSpec(memory_space=pl.ANY)] * len(after),
        out_specs=whole_vmem(len(order)),
        scratch_shapes=[pltpu.VMEM((GROUP, LANES), jnp.float32)],
        compiler_params=params(8 * MIB + 5 * weights.size),
        name="pack_weights",
    )(place, weights, owner, local, *after)


def smooth_kernel(shift_ref, place_ref, movie_ref, other_ref, pair_ref, *refs):
    *out_refs, band, wide = refs
    frames, planes, rows, width = movie_ref.shape
    blocks = width // LANES
    reach = rows + 2 * HALO
    parts = len(out_refs)
    each = blocks // parts
    together = wide.shape[0]
    taps = gauss_taps()
    high = [float(v) for v in taps.astype(jnp.bfloat16)]
    low = [float(v) for v in taps - taps.astype(jnp.bfloat16).astype(np.float32)]
    lane = lax.broadcasted_iota(jnp.int32, (reach, LANES), 1)
    row = lax.broadcasted_iota(jnp.int32, (reach, LANES), 0)
    first_row, total_rows, me = place_ref[0], place_ref[1], place_ref[2]
    even = place_ref[3] % 2 == 0

    tap = lax.broadcasted_iota(jnp.int32, (2 * LANES, LANES), 0) - lax.broadcasted_iota(jnp.int32, (2 * LANES, LANES), 1)
    tap = tap - (MAXS - RAD)
    for side, values in enumerate((high, low)):
        cells = jnp.zeros((2 * LANES, LANES), jnp.float32)
        for i, value in enumerate(values):
            cells = jnp.where(tap == i, value, cells)
        band[:, side * LANES : (side + 1) * LANES] = cells.astype(jnp.bfloat16)

    def some(step, carry):
        chosen = [step * together + u for u in range(together)]
        stacked = []
        for frame in chosen:
            right = shift_ref[1, frame] + MAXS
            near = lane < right
            zero = jnp.zeros((reach, LANES), jnp.float32)
            for plane in range(planes):
                moved = []
                for b in range(blocks):
                    cells = slice(b * LANES, (b + 1) * LANES)
                    pair = pair_ref[frame, :, cells].astype(jnp.float32)
                    other = other_ref[frame, :, cells].astype(jnp.float32)
                    top = jnp.where(even, other, pair)
                    bottom = jnp.where(even, pair, other)
                    full = slice(plane * OCTET, (plane + 1) * OCTET)
                    rest = slice(planes * OCTET + plane * QUAD, planes * OCTET + (plane + 1) * QUAD)
                    piece = jnp.concatenate(
                        [
                            top[rest],
                            top[rest],
                            top[full],
                            movie_ref[frame, plane, :, cells].astype(jnp.float32),
                            bottom[full],
                            bottom[rest],
                            bottom[rest],
                        ],
                        axis=0,
                    )
                    moved.append(pltpu.roll(piece, right, 1))
                shifted = []
                for b in range(blocks + 1):
                    before = moved[b - 1] if b > 0 else zero
                    own = moved[b] if b < blocks else zero
                    cells = jnp.where(near, before, own)
                    if b == 0:
                        cells = jnp.where(lane < MAXS, 0.0, cells)
                    if b == blocks:
                        cells = jnp.where(lane < MAXS, cells, 0.0)
                    shifted.append(cells.astype(jnp.bfloat16))
                stacked += [jnp.concatenate(shifted[b : b + 2], axis=1) for b in range(blocks)]
        result = jnp.dot(jnp.concatenate(stacked, axis=0), band[...], preferred_element_type=jnp.float32)
        result = result[:, :LANES] + result[:, LANES:]
        for u, frame in enumerate(chosen):
            place = first_row + row - HALO + shift_ref[0, frame]
            inside = (place >= 0) & (place < total_rows)
            for plane in range(planes):
                for b in range(blocks):
                    at = ((u * planes + plane) * blocks + b) * reach
                    wide[u, plane, b] = jnp.where(inside, result[at : at + reach], 0.0)
        for u, frame in enumerate(chosen):
            start = HALO - RAD - shift_ref[0, frame]
            for plane in range(planes):
                for k in range(parts):
                    for j in range(each):
                        b = (me ^ k) * each + j
                        total = float(taps[RAD]) * wide[u, plane, b, pl.ds(start + RAD, rows), :]
                        for i in range(RAD):
                            pair = wide[u, plane, b, pl.ds(start + i, rows), :]
                            pair = pair + wide[u, plane, b, pl.ds(start + 2 * RAD - i, rows), :]
                            total = total + float(taps[i]) * pair
                        out_refs[k][frame, plane, :, j * LANES : (j + 1) * LANES] = total.astype(jnp.bfloat16)
        return carry

    lax.fori_loop(0, frames // together, some, 0)


def smooth(movie, pair, other, shifts, place, parts):
    frames, planes, rows, width = movie.shape
    reach = rows + 2 * HALO
    smem = pl.BlockSpec(memory_space=pltpu.SMEM)
    return pl.pallas_call(
        smooth_kernel,
        out_shape=[jax.ShapeDtypeStruct((frames, planes, rows, width // parts), jnp.bfloat16)] * parts,
        in_specs=[smem, smem] + whole_vmem(3),
        out_specs=whole_vmem(parts),
        scratch_shapes=[
            pltpu.VMEM((2 * LANES, 2 * LANES), jnp.bfloat16),
            pltpu.VMEM((2 - frames % 2, planes, width // LANES, reach, LANES), jnp.float32),
        ],
        compiler_params=params(20 * MIB + 8 * movie.size),
        name="smooth",
    )(shifts, place, movie, other, pair)


def spread_kernel(part_frames, place_ref, kernel_ref, out_ref):
    planes, size, _ = out_ref.shape
    frames = size // GROUP
    me = place_ref[2]
    row = lax.broadcasted_iota(jnp.int32, (size, frames), 0)
    column = lax.broadcasted_iota(jnp.int32, (size, frames), 1)
    tall = (row % frames == column).astype(jnp.bfloat16)
    row = lax.broadcasted_iota(jnp.int32, (frames, size), 0)
    column = lax.broadcasted_iota(jnp.int32, (frames, size), 1) // GROUP
    last = frames // part_frames - 1
    column = ((last - column // part_frames) ^ me) * part_frames + column % part_frames
    flat = (column == row).astype(jnp.bfloat16)
    row = lax.broadcasted_iota(jnp.int32, (size, size), 0)
    column = lax.broadcasted_iota(jnp.int32, (size, size), 1)
    same = row // frames == column % GROUP
    for plane in range(planes):
        left = jnp.dot(tall, kernel_ref[plane], preferred_element_type=jnp.float32).astype(jnp.bfloat16)
        full = jnp.dot(left, flat, preferred_element_type=jnp.float32)
        out_ref[plane] = jnp.where(same, full, 0.0).astype(jnp.bfloat16)


def spread(kernel, place, part_frames):
    planes, frames, _ = kernel.shape
    size = frames * GROUP
    return pl.pallas_call(
        functools.partial(spread_kernel, part_frames),
        out_shape=jax.ShapeDtypeStruct((planes, size, size), jnp.bfloat16),
        in_specs=[pl.BlockSpec(memory_space=pltpu.SMEM)] + whole_vmem(1),
        out_specs=whole_vmem(1)[0],
        compiler_params=params(8 * MIB + 16 * size * size),
        name="spread_filters",
    )(place, kernel)


def swap_lanes(pieces):
    count = len(pieces)
    group = LANES // count
    half = count // 2
    lane = lax.broadcasted_iota(jnp.int32, pieces[0].shape, 1) // group
    while half >= 1:
        low = (lane & half) == 0
        result = list(pieces)
        for i in range(count):
            if i & half:
                continue
            a, b = pieces[i], pieces[i + half]
            if 2 * half == count:
                back = pltpu.roll(b, half * group, 1)
                ahead = pltpu.roll(a, half * group, 1)
            else:
                back = pltpu.roll(b, half * group, 1)
                ahead = pltpu.roll(a, LANES - half * group, 1)
            result[i] = jnp.where(low, a, back)
            result[i + half] = jnp.where(low, ahead, b)
        pieces = result
        half //= 2
    return pieces


def deconvolve_kernel(parts, spread_ref, *refs):
    data_refs, out_ref = refs[:parts], refs[-1]
    part_frames, planes, rows, width = data_refs[0].shape
    size = spread_ref.shape[1]
    frames = size // GROUP
    octets = rows // OCTET
    for q in range(width // LANES):
        lanes = slice(q * LANES, (q + 1) * LANES)
        for plane in range(planes):
            for first in range(0, rows // GROUP, 2):
                cells = []
                for a in (first, first + 1):
                    pieces = [ref[:, plane, a * GROUP : (a + 1) * GROUP, lanes] for ref in data_refs]
                    cells.append(jnp.concatenate(pieces, axis=0).reshape(size, LANES))
                cells = jnp.concatenate(cells, axis=1)
                spikes = jnp.dot(spread_ref[plane], cells, preferred_element_type=jnp.float32)
                spikes = jnp.maximum(spikes, 0.0)
                for a in (0, 1):
                    for half in (0, 1):
                        pieces = [
                            spikes[(half * OCTET + r) * frames : (half * OCTET + r + 1) * frames, a * LANES : (a + 1) * LANES]
                            for r in range(OCTET)
                        ]
                        octet = plane * octets + (first + a) * 2 + half
                        for j, piece in enumerate(swap_lanes(pieces)):
                            out_ref[q, octet, j * frames : (j + 1) * frames, :] = piece.astype(jnp.bfloat16)


def deconvolve(spread_filters, data, after):
    part_frames, planes, rows, width = data[0].shape
    frames = part_frames * len(data)
    shape = (width // LANES, planes * rows // OCTET, OCTET * frames, LANES)
    return pl.pallas_call(
        functools.partial(deconvolve_kernel, len(data)),
        out_shape=jax.ShapeDtypeStruct(shape, jnp.bfloat16),
        in_specs=whole_vmem(1 + len(data)) + [pl.BlockSpec(memory_space=pl.ANY)] * len(after),
        out_specs=whole_vmem(1)[0],
        compiler_params=params(12 * MIB + 4 * (spread_filters.size + 2 * len(data) * data[0].size)),
        name="deconvolve",
    )(spread_filters, *data, *after)


def pool_kernel(order, place_ref, spikes_ref, *refs):
    *weights_refs, out_ref = refs
    blocks, steps, height, _ = spikes_ref.shape
    tiles = len(weights_refs)
    me = place_ref[3]
    near = tiles // blocks
    frames = height // near
    tail = weights_refs[0].shape[0] - GROUP
    slots = tail // steps
    owners, owner_rows, _ = out_ref.shape
    owned = owners * owner_rows
    eye = lax.broadcasted_iota(jnp.int32, (slots, LANES), 0) == lax.broadcasted_iota(jnp.int32, (slots, LANES), 1)
    keys, groups = [], []
    for ref in weights_refs:
        ids = ref[tail : tail + GROUP, :].astype(jnp.float32)
        owner = jnp.sum(jnp.where(eye, ids[0:1, :], 0.0), axis=1, keepdims=True).astype(jnp.int32)
        local = jnp.sum(jnp.where(eye, ids[1:2, :], 0.0), axis=1, keepdims=True).astype(jnp.int32)
        keys.append(owner * owner_rows + local % owner_rows)
        groups.append(local // owner_rows)
    key = jnp.concatenate(keys, axis=0)
    group = jnp.concatenate(groups, axis=0)
    onehot = (lax.broadcasted_iota(jnp.int32, (tiles * slots, owned), 1) == key).astype(jnp.bfloat16)
    total = jnp.zeros((owned, LANES), jnp.float32)
    for q in range(blocks):
        pooled = jnp.zeros((tiles * slots, height), jnp.float32)
        for step in range(0, steps, 2):
            left = jnp.concatenate(
                [
                    jnp.concatenate([ref[at * slots : (at + 1) * slots, :] for ref in weights_refs], axis=0)
                    for at in (step, step + 1)
                ],
                axis=1,
            )
            right = jnp.concatenate([spikes_ref[q, step], spikes_ref[q, step + 1]], axis=1)
            pooled = pooled + lax.dot_general(
                left, right, (((1,), (1,)), ((), ())), preferred_element_type=jnp.float32
            )
        column = lax.broadcasted_iota(jnp.int32, (slots, height), 1) // frames + q * near
        pooled = jnp.concatenate(
            [jnp.where(column == me ^ k, pooled[i * slots : (i + 1) * slots], 0.0) for i, k in enumerate(order)], axis=0
        )
        partial = pooled[:, 0:LANES]
        for at in range(LANES, height, LANES):
            partial = partial + pooled[:, at : at + LANES]
        step = LANES // 2
        while step >= frames:
            partial = partial + pltpu.roll(partial, step, 1)
            step //= 2
        lane_group = lax.broadcasted_iota(jnp.int32, partial.shape, 1) // frames
        partial = jnp.where(lane_group == group, partial, 0.0)
        high = partial.astype(jnp.bfloat16)
        low = (partial - high.astype(jnp.float32)).astype(jnp.bfloat16)
        both = lax.dot_general(
            onehot,
            jnp.concatenate([high, low], axis=1),
            (((0,), (0,)), ((), ())),
            preferred_element_type=jnp.float32,
        )
        total = total + both[:, :LANES] + both[:, LANES:]
    out_ref[...] = total.reshape(owners, owner_rows, LANES)


def pool(spikes, weights, order, place, frames, owners):
    shape = (owners, COMP_DEV * frames // LANES, LANES)
    inputs = [spikes, *weights]
    return pl.pallas_call(
        functools.partial(pool_kernel, order),
        out_shape=jax.ShapeDtypeStruct(shape, jnp.float32),
        in_specs=[pl.BlockSpec(memory_space=pltpu.SMEM)] + whole_vmem(len(inputs)),
        out_specs=whole_vmem(1)[0],
        compiler_params=params(16 * MIB + 4 * sum(cells.size for cells in inputs)),
        name="pool",
    )(place, *inputs)


def finish_kernel(parts_ref, out_ref):
    sources, rows, _ = parts_ref.shape
    frames = out_ref.shape[1]
    total = jnp.sum(parts_ref[...], axis=0)
    for group in range(LANES // frames):
        out_ref[group * rows : (group + 1) * rows, :] = total[:, group * frames : (group + 1) * frames]


def finish(parts, frames):
    return pl.pallas_call(
        finish_kernel,
        out_shape=jax.ShapeDtypeStruct((COMP_DEV, frames), jnp.float32),
        in_specs=whole_vmem(1),
        out_specs=whole_vmem(1)[0],
        compiler_params=params(8 * MIB + 8 * parts.size),
        name="finish",
    )(parts)


def body(movie, shifts, filters, weights, slot_owner, slot_local):
    part_frames, planes, rows, width = movie.shape
    tiles = lax.axis_size("tile")
    parts = lax.axis_size("frame")
    frames = part_frames * parts
    slots = weights.shape[0]
    ends = tiles - 1
    tile = lax.axis_index("tile")
    place = jnp.stack([tile * rows, tiles * rows, lax.axis_index("frame"), tile]).astype(jnp.int32)
    far, close = list(range(tiles // 2, tiles)), list(range(1, tiles // 2))
    order = close[1:2] + far[-2:-1] + far[:1] + close[:1] + far[-1:] + far[-3:0:-1] + close[2:] + [0]
    owner, local = slot_owner.reshape(1, slots), slot_local.reshape(1, slots)
    pair, other = edges(movie, place)
    swaps = [(i, i + 1) for i in range(1, ends, 2)]
    other = lax.ppermute(other, "tile", swaps + [(j, i) for i, j in swaps])
    pair = lax.ppermute(pair, "tile", [(i, i ^ 1) for i in range(tiles)])
    packed = pack(weights, owner, local, order[:3], tiles, planes, place)
    packed += pack(weights, owner, local, order[3:], tiles, planes, place, other)
    landed = [
        lax.ppermute(cells, "tile", [(i, i ^ k) for i in range(tiles)]) if k else cells
        for k, cells in zip(order, packed)
    ]
    pieces = smooth(movie, pair, other, shifts.T, place, parts)
    pieces = [
        lax.ppermute(pieces[k], "frame", [(i, i ^ k) for i in range(parts)]) for k in range(parts - 1, 0, -1)
    ] + [pieces[0]]
    spikes = deconvolve(spread(build_kernel(filters, frames), place, part_frames), pieces, landed[: len(far) + 1])
    traces = pool(spikes, landed, order, place, frames, parts * tiles)
    traces = lax.all_to_all(traces, ("frame", "tile"), split_axis=0, concat_axis=0, tiled=True)
    return finish(traces, frames)


def solution(mesh):
    in_specs = (
        P("frame", None, "tile", None),
        P("frame", None),
        P(),
        P(("frame", "tile"), None),
        P(("frame", "tile"), None),
        P(("frame", "tile"), None),
    )
    out_specs = P(("frame", "tile"), None)
    return jax.shard_map(body, mesh=mesh, in_specs=in_specs, out_specs=out_specs, check_vma=False)
```

```python
import functools

import jax
import jax.numpy as jnp
import numpy as np
from jax import lax
from jax.experimental import pallas as pl
from jax.experimental.pallas import tpu as pltpu
from jax.sharding import PartitionSpec as P

COMP_DEV = 32
TAPS = 64
MAXS = 8
RAD = 3
LANES = 128
GROUP = 16
HALO = 16
OCTET = 8
QUAD = 4
MIB = 1 << 20


smooth_sigma = 1.0


def gauss_taps():
    positions = np.arange(-RAD, RAD + 1).astype(np.float32)
    values = np.exp(-positions * positions / np.float32(2.0 * smooth_sigma * smooth_sigma))
    return (values / values.sum(dtype=np.float32)).astype(np.float32)


def build_kernel(filters, count):
    later = jnp.arange(count)[:, None]
    earlier = jnp.arange(count)[None, :]
    offsets = later - earlier
    onehot = (offsets[:, :, None] == jnp.arange(TAPS)[None, None, :]).astype(jnp.float32)
    return jnp.sum(onehot[None] * filters[:, None, None, :], axis=-1).astype(jnp.bfloat16)


def whole_vmem(count):
    return [pl.BlockSpec(memory_space=pltpu.VMEM)] * count


def params(limit):
    return pltpu.CompilerParams(vmem_limit_bytes=limit)


def edges_kernel(place_ref, movie_ref, pair_ref, other_ref):
    frames, planes, rows, _ = movie_ref.shape
    even = place_ref[3] % 2 == 0

    def one(frame, carry):
        last = [movie_ref[frame, plane, rows - HALO :, :].astype(jnp.float32) for plane in range(planes)]
        first = [movie_ref[frame, plane, :HALO, :].astype(jnp.float32) for plane in range(planes)]
        last = [cells[OCTET:] for cells in last] + [cells[QUAD:OCTET] for cells in last]
        first = [cells[:OCTET] for cells in first] + [cells[OCTET : OCTET + QUAD] for cells in first]
        last = jnp.concatenate(last, axis=0)
        first = jnp.concatenate(first, axis=0)
        pair_ref[frame] = jnp.where(even, last, first).astype(jnp.bfloat16)
        other_ref[frame] = jnp.where(even, first, last).astype(jnp.bfloat16)
        return carry

    lax.fori_loop(0, frames, one, 0)


def edges(movie, place):
    frames, planes, _, width = movie.shape
    shape = jax.ShapeDtypeStruct((frames, planes * (OCTET + QUAD), width), jnp.bfloat16)
    return pl.pallas_call(
        edges_kernel,
        out_shape=[shape, shape],
        in_specs=[pl.BlockSpec(memory_space=pltpu.SMEM)] + whole_vmem(1),
        out_specs=whole_vmem(2),
        compiler_params=params(40 * MIB),
        name="edges",
    )(place, movie)


def pack_kernel(order, tiles, planes, place_ref, weights_ref, owner_ref, local_ref, *refs):
    *out_refs, ids = refs[-1 - len(order) :]
    slots, pixels = weights_ref.shape
    octets = pixels // (planes * tiles * LANES)
    tail = planes * octets * slots
    ids[...] = jnp.zeros_like(ids)
    ids[0:1, 0:slots] = owner_ref[...].astype(jnp.float32)
    ids[1:2, 0:slots] = local_ref[...].astype(jnp.float32)
    for k, out_ref in zip(order, out_refs):
        dest = place_ref[3] ^ k
        for plane in range(planes):
            for octet in range(octets):
                lane = pl.multiple_of(((plane * tiles + dest) * octets + octet) * LANES, LANES)
                row = (plane * octets + octet) * slots
                out_ref[row : row + slots, :] = weights_ref[:, pl.ds(lane, LANES)]
        out_ref[tail:, :] = ids[...].astype(jnp.bfloat16)


def pack(weights, owner, local, order, tiles, planes, place, *after):
    slots, pixels = weights.shape
    shape = jax.ShapeDtypeStruct((pixels // (tiles * LANES) * slots + GROUP, LANES), jnp.bfloat16)
    return pl.pallas_call(
        functools.partial(pack_kernel, order, tiles, planes),
        out_shape=[shape] * len(order),
        in_specs=[pl.BlockSpec(memory_space=pltpu.SMEM)] + whole_vmem(3) + [pl.BlockSpec(memory_space=pl.ANY)] * len(after),
        out_specs=whole_vmem(len(order)),
        scratch_shapes=[pltpu.VMEM((GROUP, LANES), jnp.float32)],
        compiler_params=params(8 * MIB + 5 * weights.size),
        name="pack_weights",
    )(place, weights, owner, local, *after)


def smooth_kernel(shift_ref, place_ref, movie_ref, other_ref, pair_ref, *refs):
    *out_refs, band, wide = refs
    frames, planes, rows, width = movie_ref.shape
    blocks = width // LANES
    reach = rows + 2 * HALO
    parts = len(out_refs)
    each = blocks // parts
    together = wide.shape[0]
    taps = gauss_taps()
    high = [float(v) for v in taps.astype(jnp.bfloat16)]
    low = [float(v) for v in taps - taps.astype(jnp.bfloat16).astype(np.float32)]
    lane = lax.broadcasted_iota(jnp.int32, (reach, LANES), 1)
    row = lax.broadcasted_iota(jnp.int32, (reach, LANES), 0)
    first_row, total_rows, me = place_ref[0], place_ref[1], place_ref[2]
    even = place_ref[3] % 2 == 0

    tap = lax.broadcasted_iota(jnp.int32, (2 * LANES, LANES), 0) - lax.broadcasted_iota(jnp.int32, (2 * LANES, LANES), 1)
    tap = tap - (MAXS - RAD)
    for side, values in enumerate((high, low)):
        cells = jnp.zeros((2 * LANES, LANES), jnp.float32)
        for i, value in enumerate(values):
            cells = jnp.where(tap == i, value, cells)
        band[:, side * LANES : (side + 1) * LANES] = cells.astype(jnp.bfloat16)

    def some(step, carry):
        chosen = [step * together + u for u in range(together)]
        stacked = []
        for frame in chosen:
            right = shift_ref[1, frame] + MAXS
            near = lane < right
            zero = jnp.zeros((reach, LANES), jnp.float32)
            for plane in range(planes):
                moved = []
                for b in range(blocks):
                    cells = slice(b * LANES, (b + 1) * LANES)
                    pair = pair_ref[frame, :, cells].astype(jnp.float32)
                    other = other_ref[frame, :, cells].astype(jnp.float32)
                    top = jnp.where(even, other, pair)
                    bottom = jnp.where(even, pair, other)
                    full = slice(plane * OCTET, (plane + 1) * OCTET)
                    rest = slice(planes * OCTET + plane * QUAD, planes * OCTET + (plane + 1) * QUAD)
                    piece = jnp.concatenate(
                        [
                            top[rest],
                            top[rest],
                            top[full],
                            movie_ref[frame, plane, :, cells].astype(jnp.float32),
                            bottom[full],
                            bottom[rest],
                            bottom[rest],
                        ],
                        axis=0,
                    )
                    moved.append(pltpu.roll(piece, right, 1))
                shifted = []
                for b in range(blocks + 1):
                    before = moved[b - 1] if b > 0 else zero
                    own = moved[b] if b < blocks else zero
                    cells = jnp.where(near, before, own)
                    if b == 0:
                        cells = jnp.where(lane < MAXS, 0.0, cells)
                    if b == blocks:
                        cells = jnp.where(lane < MAXS, cells, 0.0)
                    shifted.append(cells.astype(jnp.bfloat16))
                stacked += [jnp.concatenate(shifted[b : b + 2], axis=1) for b in range(blocks)]
        result = jnp.dot(jnp.concatenate(stacked, axis=0), band[...], preferred_element_type=jnp.float32)
        result = result[:, :LANES] + result[:, LANES:]
        for u, frame in enumerate(chosen):
            place = first_row + row - HALO + shift_ref[0, frame]
            inside = (place >= 0) & (place < total_rows)
            for plane in range(planes):
                for b in range(blocks):
                    at = ((u * planes + plane) * blocks + b) * reach
                    wide[u, plane, b] = jnp.where(inside, result[at : at + reach], 0.0)
        for u, frame in enumerate(chosen):
            start = HALO - RAD - shift_ref[0, frame]
            for plane in range(planes):
                for k in range(parts):
                    for j in range(each):
                        b = (me ^ k) * each + j
                        total = float(taps[RAD]) * wide[u, plane, b, pl.ds(start + RAD, rows), :]
                        for i in range(RAD):
                            pair = wide[u, plane, b, pl.ds(start + i, rows), :]
                            pair = pair + wide[u, plane, b, pl.ds(start + 2 * RAD - i, rows), :]
                            total = total + float(taps[i]) * pair
                        out_refs[k][frame, plane, :, j * LANES : (j + 1) * LANES] = total.astype(jnp.bfloat16)
        return carry

    lax.fori_loop(0, frames // together, some, 0)


def smooth(movie, pair, other, shifts, place, parts):
    frames, planes, rows, width = movie.shape
    reach = rows + 2 * HALO
    smem = pl.BlockSpec(memory_space=pltpu.SMEM)
    return pl.pallas_call(
        smooth_kernel,
        out_shape=[jax.ShapeDtypeStruct((frames, planes, rows, width // parts), jnp.bfloat16)] * parts,
        in_specs=[smem, smem] + whole_vmem(3),
        out_specs=whole_vmem(parts),
        scratch_shapes=[
            pltpu.VMEM((2 * LANES, 2 * LANES), jnp.bfloat16),
            pltpu.VMEM((2 - frames % 2, planes, width // LANES, reach, LANES), jnp.float32),
        ],
        compiler_params=params(20 * MIB + 8 * movie.size),
        name="smooth",
    )(shifts, place, movie, other, pair)


def spread_kernel(part_frames, place_ref, kernel_ref, out_ref):
    planes, size, _ = out_ref.shape
    frames = size // GROUP
    me = place_ref[2]
    row = lax.broadcasted_iota(jnp.int32, (size, frames), 0)
    column = lax.broadcasted_iota(jnp.int32, (size, frames), 1)
    tall = (row % frames == column).astype(jnp.bfloat16)
    row = lax.broadcasted_iota(jnp.int32, (frames, size), 0)
    column = lax.broadcasted_iota(jnp.int32, (frames, size), 1) // GROUP
    last = frames // part_frames - 1
    column = ((last - column // part_frames) ^ me) * part_frames + column % part_frames
    flat = (column == row).astype(jnp.bfloat16)
    row = lax.broadcasted_iota(jnp.int32, (size, size), 0)
    column = lax.broadcasted_iota(jnp.int32, (size, size), 1)
    same = row // frames == column % GROUP
    for plane in range(planes):
        left = jnp.dot(tall, kernel_ref[plane], preferred_element_type=jnp.float32).astype(jnp.bfloat16)
        full = jnp.dot(left, flat, preferred_element_type=jnp.float32)
        out_ref[plane] = jnp.where(same, full, 0.0).astype(jnp.bfloat16)


def spread(kernel, place, part_frames):
    planes, frames, _ = kernel.shape
    size = frames * GROUP
    return pl.pallas_call(
        functools.partial(spread_kernel, part_frames),
        out_shape=jax.ShapeDtypeStruct((planes, size, size), jnp.bfloat16),
        in_specs=[pl.BlockSpec(memory_space=pltpu.SMEM)] + whole_vmem(1),
        out_specs=whole_vmem(1)[0],
        compiler_params=params(8 * MIB + 16 * size * size),
        name="spread_filters",
    )(place, kernel)


def swap_lanes(pieces):
    count = len(pieces)
    group = LANES // count
    half = count // 2
    lane = lax.broadcasted_iota(jnp.int32, pieces[0].shape, 1) // group
    while half >= 1:
        low = (lane & half) == 0
        result = list(pieces)
        for i in range(count):
            if i & half:
                continue
            a, b = pieces[i], pieces[i + half]
            if 2 * half == count:
                back = pltpu.roll(b, half * group, 1)
                ahead = pltpu.roll(a, half * group, 1)
            else:
                back = pltpu.roll(b, half * group, 1)
                ahead = pltpu.roll(a, LANES - half * group, 1)
            result[i] = jnp.where(low, a, back)
            result[i + half] = jnp.where(low, ahead, b)
        pieces = result
        half //= 2
    return pieces


def deconvolve_kernel(parts, spread_ref, *refs):
    data_refs, out_ref = refs[:parts], refs[-1]
    part_frames, planes, rows, width = data_refs[0].shape
    size = spread_ref.shape[1]
    frames = size // GROUP
    octets = rows // OCTET
    for q in range(width // LANES):
        lanes = slice(q * LANES, (q + 1) * LANES)
        for plane in range(planes):
            for first in range(0, rows // GROUP, 2):
                cells = []
                for a in (first, first + 1):
                    pieces = [ref[:, plane, a * GROUP : (a + 1) * GROUP, lanes] for ref in data_refs]
                    cells.append(jnp.concatenate(pieces, axis=0).reshape(size, LANES))
                cells = jnp.concatenate(cells, axis=1)
                spikes = jnp.dot(spread_ref[plane], cells, preferred_element_type=jnp.float32)
                spikes = jnp.maximum(spikes, 0.0)
                for a in (0, 1):
                    for half in (0, 1):
                        pieces = [
                            spikes[(half * OCTET + r) * frames : (half * OCTET + r + 1) * frames, a * LANES : (a + 1) * LANES]
                            for r in range(OCTET)
                        ]
                        octet = plane * octets + (first + a) * 2 + half
                        for j, piece in enumerate(swap_lanes(pieces)):
                            out_ref[q, octet, j * frames : (j + 1) * frames, :] = piece.astype(jnp.bfloat16)


def deconvolve(spread_filters, data, after):
    part_frames, planes, rows, width = data[0].shape
    frames = part_frames * len(data)
    shape = (width // LANES, planes * rows // OCTET, OCTET * frames, LANES)
    return pl.pallas_call(
        functools.partial(deconvolve_kernel, len(data)),
        out_shape=jax.ShapeDtypeStruct(shape, jnp.bfloat16),
        in_specs=whole_vmem(1 + len(data)) + [pl.BlockSpec(memory_space=pl.ANY)] * len(after),
        out_specs=whole_vmem(1)[0],
        compiler_params=params(12 * MIB + 4 * (spread_filters.size + 2 * len(data) * data[0].size)),
        name="deconvolve",
    )(spread_filters, *data, *after)


def pool_kernel(order, place_ref, spikes_ref, *refs):
    *weights_refs, out_ref = refs
    blocks, steps, height, _ = spikes_ref.shape
    tiles = len(weights_refs)
    me = place_ref[3]
    near = tiles // blocks
    frames = height // near
    tail = weights_refs[0].shape[0] - GROUP
    slots = tail // steps
    owners, owner_rows, _ = out_ref.shape
    owned = owners * owner_rows
    eye = lax.broadcasted_iota(jnp.int32, (slots, LANES), 0) == lax.broadcasted_iota(jnp.int32, (slots, LANES), 1)
    keys, groups = [], []
    for ref in weights_refs:
        ids = ref[tail : tail + GROUP, :].astype(jnp.float32)
        owner = jnp.sum(jnp.where(eye, ids[0:1, :], 0.0), axis=1, keepdims=True).astype(jnp.int32)
        local = jnp.sum(jnp.where(eye, ids[1:2, :], 0.0), axis=1, keepdims=True).astype(jnp.int32)
        keys.append(owner * owner_rows + local % owner_rows)
        groups.append(local // owner_rows)
    key = jnp.concatenate(keys, axis=0)
    group = jnp.concatenate(groups, axis=0)
    onehot = (lax.broadcasted_iota(jnp.int32, (tiles * slots, owned), 1) == key).astype(jnp.bfloat16)
    total = jnp.zeros((owned, LANES), jnp.float32)
    for q in range(blocks):
        pooled = jnp.zeros((tiles * slots, height), jnp.float32)
        for step in range(0, steps, 2):
            left = jnp.concatenate(
                [
                    jnp.concatenate([ref[at * slots : (at + 1) * slots, :] for ref in weights_refs], axis=0)
                    for at in (step, step + 1)
                ],
                axis=1,
            )
            right = jnp.concatenate([spikes_ref[q, step], spikes_ref[q, step + 1]], axis=1)
            pooled = pooled + lax.dot_general(
                left, right, (((1,), (1,)), ((), ())), preferred_element_type=jnp.float32
            )
        column = lax.broadcasted_iota(jnp.int32, (slots, height), 1) // frames + q * near
        pooled = jnp.concatenate(
            [jnp.where(column == me ^ k, pooled[i * slots : (i + 1) * slots], 0.0) for i, k in enumerate(order)], axis=0
        )
        partial = pooled[:, 0:LANES]
        for at in range(LANES, height, LANES):
            partial = partial + pooled[:, at : at + LANES]
        step = LANES // 2
        while step >= frames:
            partial = partial + pltpu.roll(partial, step, 1)
            step //= 2
        lane_group = lax.broadcasted_iota(jnp.int32, partial.shape, 1) // frames
        partial = jnp.where(lane_group == group, partial, 0.0)
        high = partial.astype(jnp.bfloat16)
        low = (partial - high.astype(jnp.float32)).astype(jnp.bfloat16)
        both = lax.dot_general(
            onehot,
            jnp.concatenate([high, low], axis=1),
            (((0,), (0,)), ((), ())),
            preferred_element_type=jnp.float32,
        )
        total = total + both[:, :LANES] + both[:, LANES:]
    out_ref[...] = total.reshape(owners, owner_rows, LANES)


def pool(spikes, weights, order, place, frames, owners):
    shape = (owners, COMP_DEV * frames // LANES, LANES)
    inputs = [spikes, *weights]
    return pl.pallas_call(
        functools.partial(pool_kernel, order),
        out_shape=jax.ShapeDtypeStruct(shape, jnp.float32),
        in_specs=[pl.BlockSpec(memory_space=pltpu.SMEM)] + whole_vmem(len(inputs)),
        out_specs=whole_vmem(1)[0],
        compiler_params=params(16 * MIB + 4 * sum(cells.size for cells in inputs)),
        name="pool",
    )(place, *inputs)


def finish_kernel(parts_ref, out_ref):
    sources, rows, _ = parts_ref.shape
    frames = out_ref.shape[1]
    total = jnp.sum(parts_ref[...], axis=0)
    for group in range(LANES // frames):
        out_ref[group * rows : (group + 1) * rows, :] = total[:, group * frames : (group + 1) * frames]


def finish(parts, frames):
    return pl.pallas_call(
        finish_kernel,
        out_shape=jax.ShapeDtypeStruct((COMP_DEV, frames), jnp.float32),
        in_specs=whole_vmem(1),
        out_specs=whole_vmem(1)[0],
        compiler_params=params(8 * MIB + 8 * parts.size),
        name="finish",
    )(parts)


def body(movie, shifts, filters, weights, slot_owner, slot_local):
    part_frames, planes, rows, width = movie.shape
    tiles = lax.axis_size("tile")
    parts = lax.axis_size("frame")
    frames = part_frames * parts
    slots = weights.shape[0]
    ends = tiles - 1
    tile = lax.axis_index("tile")
    place = jnp.stack([tile * rows, tiles * rows, lax.axis_index("frame"), tile]).astype(jnp.int32)
    far, close = list(range(tiles // 2, tiles)), list(range(1, tiles // 2))
    order = close[1:2] + far[-2:] + far[:1] + close[:1] + far[-3:0:-1] + close[2:] + [0]
    owner, local = slot_owner.reshape(1, slots), slot_local.reshape(1, slots)
    pair, other = edges(movie, place)
    swaps = [(i, i + 1) for i in range(1, ends, 2)]
    other = lax.ppermute(other, "tile", swaps + [(j, i) for i, j in swaps])
    pair = lax.ppermute(pair, "tile", [(i, i ^ 1) for i in range(tiles)])
    packed = pack(weights, owner, local, order[:3], tiles, planes, place)
    packed += pack(weights, owner, local, order[3:], tiles, planes, place, other)
    landed = [
        lax.ppermute(cells, "tile", [(i, i ^ k) for i in range(tiles)]) if k else cells
        for k, cells in zip(order, packed)
    ]
    pieces = smooth(movie, pair, other, shifts.T, place, parts)
    pieces = [
        lax.ppermute(pieces[k], "frame", [(i, i ^ k) for i in range(parts)]) for k in range(parts - 1, 0, -1)
    ] + [pieces[0]]
    spikes = deconvolve(spread(build_kernel(filters, frames), place, part_frames), pieces, landed[: len(far) + 1])
    traces = pool(spikes, landed, order, place, frames, parts * tiles)
    traces = lax.all_to_all(traces, ("frame", "tile"), split_axis=0, concat_axis=0, tiled=True)
    return finish(traces, frames)


def solution(mesh):
    in_specs = (
        P("frame", None, "tile", None),
        P("frame", None),
        P(),
        P(("frame", "tile"), None),
        P(("frame", "tile"), None),
        P(("frame", "tile"), None),
    )
    out_specs = P(("frame", "tile"), None)
    return jax.shard_map(body, mesh=mesh, in_specs=in_specs, out_specs=out_specs, check_vma=False)
```
